32 devices in a mesh: dp: 4 (over z), seq: 2 (over y), head: 4 (over x, core).
Axes of the slice: x: 2, y: 2, z: 4, core: 2. Of those that a mesh axis runs over, the one named last changes fastest.
Arguments:
- tokens: bfloat16 [8, 4096, 768], P('dp', ('seq', 'head')), may hold values from -6 to 6
- cotangent: bfloat16 [8, 4096, 768], P('dp', ('seq', 'head')), may hold values from -6 to 6
- rand_blocks: int32 [12, 64, 3], P('head', 'seq'), may hold values from 0 to 63
- global_blocks: int32 [2], replicated, may hold values from 0 to 63
- qkv_weight: float32 [768, 2304], P(('dp', 'seq'), 'head')
- out_weight: float32 [768, 768], P('head', ('dp', 'seq')), may hold values from -6 to 6
- up_weight: float32 [768, 3072], P(('dp', 'seq'), 'head')
- down_weight: float32 [3072, 768], P('head', ('dp', 'seq')), may hold values from -0.109375 to 0.109375
- norm_params: float32 [4, 768], replicated
- qkv_first: float32 [768, 2304], P(('dp', 'seq'), 'head'), may hold values from -0.00061035156 to 0.00061035156
- out_first: float32 [768, 768], P('head', ('dp', 'seq')), may hold values from -5.340576e-05 to 5.340576e-05
- up_first: float32 [768, 3072], P(('dp', 'seq'), 'head'), may hold values from -2.670288e-05 to 2.670288e-05
- down_first: float32 [3072, 768], P('head', ('dp', 'seq')), may hold values from -6.1035156e-05 to 6.1035156e-05
- norm_first: float32 [4, 768], replicated, may hold values from -0.0024414062 to 0.0024414062
- qkv_second: float32 [768, 2304], P(('dp', 'seq'), 'head'), may hold values from 1.4122378e-10 to 5.6489513e-10
- out_second: float32 [768, 768], P('head', ('dp', 'seq')), may hold values from 1.1037897e-12 to 4.4151588e-12
- up_second: float32 [768, 3072], P(('dp', 'seq'), 'head'), may hold values from 2.6490954e-13 to 1.1037897e-12
- down_second: float32 [3072, 768], P('head', ('dp', 'seq')), may hold values from 1.5453057e-12 to 6.1812226e-12
- norm_second: float32 [4, 768], replicated, may hold values from 2.2595805e-09 to 9.038322e-09
- qkv_average: float32 [768, 2304], P(('dp', 'seq'), 'head'), may hold values from -0.21875 to 0.21875
- out_average: float32 [768, 768], P('head', ('dp', 'seq')), may hold values from -6 to 6
- up_average: float32 [768, 3072], P(('dp', 'seq'), 'head'), may hold values from -0.21875 to 0.21875
- down_average: float32 [3072, 768], P('head', ('dp', 'seq')), may hold values from -0.109375 to 0.109375
- norm_average: float32 [4, 768], replicated, may hold values from 0.5 to 1.5
Outputs:
- block_out: bfloat16 [8, 4096, 768], P('dp', ('seq', 'head'))
- input_grad: bfloat16 [8, 4096, 768], P('dp', ('seq', 'head'))
- grad_norm: float32 [], replicated
- qkv_new: float32 [768, 2304], P(('dp', 'seq'), 'head')
- out_new: float32 [768, 768], P('head', ('dp', 'seq'))
- up_new: float32 [768, 3072], P(('dp', 'seq'), 'head')
- down_new: float32 [3072, 768], P('head', ('dp', 'seq'))
- norm_new: float32 [4, 768], replicated
- qkv_first_new: float32 [768, 2304], P(('dp', 'seq'), 'head')
- out_first_new: float32 [768, 768], P('head', ('dp', 'seq'))
- up_first_new: float32 [768, 3072], P(('dp', 'seq'), 'head')
- down_first_new: float32 [3072, 768], P('head', ('dp', 'seq'))
- norm_first_new: float32 [4, 768], replicated
- qkv_second_new: float32 [768, 2304], P(('dp', 'seq'), 'head')
- out_second_new: float32 [768, 768], P('head', ('dp', 'seq'))
- up_second_new: float32 [768, 3072], P(('dp', 'seq'), 'head')
- down_second_new: float32 [3072, 768], P('head', ('dp', 'seq'))
- norm_second_moment_next: float32 [4, 768], replicated
- qkv_average_new: float32 [768, 2304], P(('dp', 'seq'), 'head')
- out_average_new: float32 [768, 768], P('head', ('dp', 'seq'))
- up_average_new: float32 [768, 3072], P(('dp', 'seq'), 'head')
- down_average_new: float32 [3072, 768], P('head', ('dp', 'seq'))
- norm_average_new: float32 [4, 768], replicated
- qkv_copy: bfloat16 [768, 2304], P(('dp', 'seq'), 'head')
- out_copy: bfloat16 [768, 768], P('head', ('dp', 'seq'))
- up_copy: bfloat16 [768, 3072], P(('dp', 'seq'), 'head')
- down_copy: bfloat16 [3072, 768], P('head', ('dp', 'seq'))
- norm_two_grad: float32 [2, 768], replicated
The draws below stay inside these ranges and needn't reach their ends.
Inputs may be any that keep to these rules, and one draw needn't show every extreme that they name: `rand_blocks`: block numbers within a sequence. `global_blocks`: block numbers within a sequence.
All inputs are finite; a program needn't handle non-finite values.
Results may differ from the reference program's by a relative error of at most 0.014.
The reference program's roundings to bfloat16 on the way count: a program that leaves them out, or rounds other values in their place, can miss the bound.
Values may be sent and summed in bfloat16 or wider, within the bound.
No kernel may reach another device: no remote copies, remote signals or barrier semaphores. Data moves between devices by JAX's collectives and lax.ppermute only.
A program may use at most 512 MiB of HBM per device.

```python
import math
import jax
import jax.numpy as jnp
from jax import lax

D = 768
H = 12
DH = 64
FF = 3072
BLOCK = 64
STEP = 10
LENGTH = 4096
SEQS = 8
NBLK = 64
NPARAM = 7080960


def rising(length_cells, start_value, end_value):
    steps = jnp.arange(length_cells, dtype=jnp.float32) / (length_cells - 1)
    return start_value + (end_value - start_value) * steps


def draw_qkv_weight(key, part):
    key = jax.random.fold_in(key, 11)
    samples = jax.random.normal(key, (D, 3 * D), jnp.float32)
    column_scale = rising(3 * D, 0.6, 1.8)
    return samples * column_scale[None, :] * D ** (-0.5)


def draw_up_weight(key, part):
    key = jax.random.fold_in(key, 12)
    samples = jax.random.normal(key, (D, FF), jnp.float32)
    column_scale = rising(FF, 0.6, 1.8)
    return samples * column_scale[None, :] * D ** (-0.5)


def draw_norm_params(key, part):
    key = jax.random.fold_in(key, 13)
    column_scale = rising(D, 0.6, 1.8)
    jitter = jnp.clip(jax.random.normal(key, (4, D), jnp.float32), -3.0, 3.0) * 0.6
    gain_rows = column_scale[None, :] * (1.0 + 0.15 * jitter[0::2])
    shifts = 0.3 * jitter[1::2]
    return jnp.stack([gain_rows[0], shifts[0], gain_rows[1], shifts[1]])


def touch_ends(drawn, rng, smallest, largest):
    spot = [jax.random.randint(jax.random.fold_in(rng, axis), (), 0, length) for axis, length in enumerate(drawn.shape)]
    longest = drawn.shape.index(max(drawn.shape))
    beside = spot[:longest] + [(spot[longest] + 1) % drawn.shape[longest]] + spot[longest + 1:]
    return drawn.at[tuple(spot)].set(smallest).at[tuple(beside)].set(largest)


def shard_levels(stream_key, shape, cuts, least, high):
    gain = 1.0
    for axis_at, parts in cuts:
        draws = jax.random.uniform(jax.random.fold_in(jax.random.fold_in(stream_key, 6), axis_at), (parts,), jnp.float32, least / len(cuts), high / len(cuts))
        gain = gain * jnp.repeat(jnp.exp(draws), shape[axis_at] // parts).reshape((-1,) + (1,) * (len(shape) - 1 - axis_at))
    return gain


def centred(stream_key, shape, scale, most, cuts=(), kind=jnp.bfloat16):
    gain = shard_levels(stream_key, shape, cuts, -0.22, 0.18) if cuts else 1.0
    drawn = jax.random.normal(stream_key, shape, jnp.float32) * scale * gain
    return jnp.minimum(jnp.maximum(drawn, -most), most).astype(kind)


def setup_inputs(seed: int = 0) -> dict:
    arg_keys = jax.random.split(jax.random.key(seed), 25)
    return {
        "tokens": centred(arg_keys[0], (SEQS, LENGTH, D), 1.0, 6.0, ((0, 4), (1, 8))),
        "cotangent": centred(arg_keys[1], (SEQS, LENGTH, D), 1.0, 6.0, ((0, 4), (1, 8))),
        "rand_blocks": touch_ends(jax.random.randint(arg_keys[2], (H, NBLK, 3), 0, NBLK), jax.random.fold_in(arg_keys[2], 1), 0, NBLK - 1).astype(jnp.int32),
        "global_blocks": jax.random.randint(arg_keys[3], (2,), 0, NBLK).astype(jnp.int32),
        "qkv_weight": draw_qkv_weight(jax.random.fold_in(arg_keys[24], 71), 0),
        "out_weight": centred(arg_keys[5], (D, D), (max(1, D // (8 * BLOCK))) ** -0.5, 6.0, ((0, 4), (1, 8)), jnp.float32),
        "up_weight": draw_up_weight(jax.random.fold_in(arg_keys[24], 71), 0),
        "down_weight": centred(arg_keys[7], (FF, D), FF ** -0.5, 0.109375, ((0, 4), (1, 8)), jnp.float32),
        "norm_params": draw_norm_params(jax.random.fold_in(arg_keys[24], 71), 0),
        "qkv_first": centred(arg_keys[9], (D, 3 * D), (0.111 * NPARAM ** -0.5), 0.00061035156, ((0, 8), (1, 4)), jnp.float32),
        "out_first": centred(arg_keys[10], (D, D), (0.08 * D ** -1.5), 5.340576171875e-05, ((0, 4), (1, 8)), jnp.float32),
        "up_first": centred(arg_keys[11], (D, FF), (0.04 * D ** -1.5), 2.6702880859375e-05, ((0, 8), (1, 4)), jnp.float32),
        "down_first": centred(arg_keys[12], (FF, D), (0.09 * D ** -1.5), 6.103515625e-05, ((0, 4), (1, 8)), jnp.float32),
        "norm_first": centred(arg_keys[13], (4, D), (0.444 * NPARAM ** -0.5), 0.0024414062, (), jnp.float32),
        "qkv_second": jnp.clip(jnp.exp(math.log(5.648951306724825e-10) - 1.3862944 * jax.random.uniform(arg_keys[14], (D, 3 * D), jnp.float32) ** shard_levels(arg_keys[14], (D, 3 * D), ((0, 8), (1, 4)), -0.2, 0.2)), 1.4122378266812063e-10, 5.648951306724825e-10),
        "out_second": jnp.clip(jnp.exp(math.log(4.415158776777117e-12) - 1.3862944 * jax.random.uniform(arg_keys[15], (D, D), jnp.float32) ** shard_levels(arg_keys[15], (D, D), ((0, 4), (1, 8)), -0.2, 0.2)), 1.1037896941942793e-12, 4.415158776777117e-12),
        "up_second": jnp.clip(jnp.exp(math.log(1.1037896941942793e-12) - 1.4271163 * jax.random.uniform(arg_keys[16], (D, FF), jnp.float32) ** shard_levels(arg_keys[16], (D, FF), ((0, 8), (1, 4)), -0.2, 0.2)), 2.649095407012553e-13, 1.1037896941942793e-12),
        "down_second": jnp.clip(jnp.exp(math.log(6.181222634432659e-12) - 1.3862944 * jax.random.uniform(arg_keys[17], (FF, D), jnp.float32) ** shard_levels(arg_keys[17], (FF, D), ((0, 4), (1, 8)), -0.2, 0.2)), 1.5453056586081648e-12, 6.181222634432659e-12),
        "norm_second": jnp.clip(jnp.exp(jax.random.uniform(arg_keys[18], (4, D), jnp.float32, math.log(2.25958052268993e-09), math.log(9.03832209075972e-09))), 2.25958052268993e-09, 9.03832209075972e-09),
        "qkv_average": centred(arg_keys[19], (D, 3 * D), D ** -0.5, 0.21875, ((0, 8), (1, 4)), jnp.float32),
        "out_average": centred(arg_keys[20], (D, D), (max(1, D // (8 * BLOCK))) ** -0.5, 6.0, ((0, 4), (1, 8)), jnp.float32),
        "up_average": centred(arg_keys[21], (D, FF), D ** -0.5, 0.21875, ((0, 8), (1, 4)), jnp.float32),
        "down_average": centred(arg_keys[22], (FF, D), FF ** -0.5, 0.109375, ((0, 4), (1, 8)), jnp.float32),
        "norm_average": jnp.clip(1.0 + 0.1 * jax.random.normal(arg_keys[23], (4, D), jnp.float32), 0.5, 1.5),
    }


@jax.custom_vjp
def low(v):
    return lax.optimization_barrier(v.astype(jnp.bfloat16)).astype(jnp.float32)

@jax.custom_vjp
def low_back(v):
    return v

def low_keep(v):
    return (low(v), None)

def low_pass(kept, grad):
    return (grad,)

def back_keep(v):
    return (v, None)

def back_low(kept, grad):
    return (low(grad),)
low.defvjp(low_keep, low_pass)
low_back.defvjp(back_keep, back_low)
EPSILON = 1e-05
BETA_ONE = 0.9
BETA_TWO = 0.999
DECAY = 0.01
SMALL = 1e-08
CLIP_NORM = 1.0
AVERAGING = 0.999
NEGATIVE = -1e+30

def matmul(left_operand, right_operand):
    return jnp.dot(left_operand, right_operand, precision=lax.Precision.HIGHEST, preferred_element_type=jnp.float32)

def norm_rows(values, gain_row, shift_row):
    center = values - lax.optimization_barrier(jnp.mean(values, -1, keepdims=True))
    spread = lax.optimization_barrier(jnp.mean(center * center, -1, keepdims=True))
    return center * lax.rsqrt(spread + EPSILON) * gain_row + shift_row

def key_table(rand_local, global_blocks, first_block, blocks_total):
    head_count, local_blocks = (rand_local.shape[0], rand_local.shape[1])
    places = first_block + jnp.arange(local_blocks, dtype=jnp.int32)
    left_side = jnp.maximum(places - 1, 0)
    right_side = jnp.minimum(places + 1, blocks_total - 1)
    window = jnp.stack([left_side, places, right_side], -1)
    key_index = jnp.concatenate([jnp.broadcast_to(window[None], (head_count, local_blocks, 3)), rand_local.astype(jnp.int32), jnp.broadcast_to(global_blocks.astype(jnp.int32)[None, None], (head_count, local_blocks, 2))], -1).astype(jnp.int32)
    column_one = jnp.ones((local_blocks, 1), jnp.float32)
    key_valid = jnp.concatenate([(places > 0).astype(jnp.float32)[:, None], column_one, (places < blocks_total - 1).astype(jnp.float32)[:, None], jnp.ones((local_blocks, 5), jnp.float32)], -1)
    return (key_index, key_valid)

def attend(queries, key_part, value_part, key_index, key_valid):
    blocks = queries.shape[0] // BLOCK
    head_count = queries.shape[1]
    query_blocks = jnp.moveaxis(queries.reshape(blocks, BLOCK, head_count, DH), 2, 0)
    key_blocks = jnp.moveaxis(key_part.reshape(blocks, BLOCK, head_count, DH), 2, 0)
    value_block_rows = jnp.moveaxis(value_part.reshape(blocks, BLOCK, head_count, DH), 2, 0)
    group_size = 8

    def one_group(number):
        start_block = number * group_size
        query_group = lax.dynamic_slice_in_dim(query_blocks, start_block, group_size, 1)
        index_group = lax.dynamic_slice_in_dim(key_index, start_block, group_size, 1)
        valid_group = lax.dynamic_slice_in_dim(key_valid, start_block, group_size, 0)
        key_group = jax.vmap(lambda source, chosen: source[chosen])(key_blocks, index_group)
        value_group = jax.vmap(lambda source, chosen: source[chosen])(value_block_rows, index_group)
        raw_scores = jnp.einsum('hgbe,hgkce->hgbkc', query_group, key_group, precision=lax.Precision.HIGHEST) * DH ** (-0.5)
        raw_scores = low_back(raw_scores)
        raw_scores = jnp.where(valid_group[None, :, None, :, None] > 0, raw_scores, NEGATIVE)
        scores_flat = raw_scores.reshape(head_count, group_size, BLOCK, 8 * BLOCK)
        row_max = lax.optimization_barrier(jnp.max(scores_flat, -1, keepdims=True))
        exponent = jnp.exp(scores_flat - row_max)
        probabilities = low(exponent / lax.optimization_barrier(jnp.sum(exponent, -1, keepdims=True))).reshape(raw_scores.shape)
        return jnp.einsum('hgbkc,hgkce->hgbe', probabilities, value_group, precision=lax.Precision.HIGHEST)
    output = lax.map(jax.checkpoint(one_group), jnp.arange(blocks // group_size))
    return jnp.moveaxis(output, 1, 3).reshape(blocks * BLOCK, head_count, DH)

def block_layer(inputs, weights, key_index, key_valid):
    qkv_w, out_w, up_w, down_w, params = weights
    token_count = inputs.shape[0]
    normed = low(norm_rows(inputs, params[0], params[1]))
    qkv_all = low(low_back(matmul(normed, low(qkv_w)))).reshape(token_count, H, 3, DH)
    mixed_heads = attend(qkv_all[:, :, 0], qkv_all[:, :, 1], qkv_all[:, :, 2], key_index, key_valid)
    mixed_heads = low(low_back(mixed_heads.reshape(token_count, H * DH)))
    residual = inputs + low_back(matmul(mixed_heads, low(out_w)))
    normed_two = low(norm_rows(residual, params[2], params[3]))
    upward = low_back(matmul(normed_two, low(up_w)))
    active = low(jax.nn.gelu(upward))
    return residual + low_back(matmul(active, low(down_w)))

def rates():
    return (1.5 * D ** (-0.5), 1.5 * max(1, D // (8 * BLOCK)) ** (-0.5), 1.5 * D ** (-0.5), 1.5 * FF ** (-0.5), 0.5)

def adamw_moment_update(weight, gradient, moment_one, moment_two, average, rate, factor):
    decay_mean = min(AVERAGING, (1.0 + STEP) / (10.0 + STEP))
    clipped = gradient * factor
    first_new = BETA_ONE * moment_one + (1.0 - BETA_ONE) * clipped
    second_new = BETA_TWO * moment_two + (1.0 - BETA_TWO) * clipped * clipped
    update = first_new / (1.0 - BETA_ONE ** STEP) / (jnp.sqrt(second_new / (1.0 - BETA_TWO ** STEP)) + SMALL)
    weight_new = weight - rate * (update + DECAY * weight)
    average_new = decay_mean * average + (1.0 - decay_mean) * weight_new
    return (weight_new, first_new, second_new, average_new)

def reference(tokens, cotangent, rand_blocks, global_blocks, qkv_weight, out_weight, up_weight, down_weight, norm_params, qkv_first, out_first, up_first, down_first, norm_first, qkv_second, out_second, up_second, down_second, norm_second, qkv_average, out_average, up_average, down_average, norm_average):
    key_index, key_valid = key_table(rand_blocks, global_blocks, 0, rand_blocks.shape[1])
    weights = (qkv_weight, out_weight, up_weight, down_weight, norm_params)

    def per_sequence(running, seq_pair):
        seq_in, seq_grad = seq_pair

        def forward(inputs, params):
            return block_layer(inputs, params, key_index, key_valid)
        output, pullback = jax.vjp(forward, seq_in.astype(jnp.float32), weights)
        grad_in, grad_weights = pullback(seq_grad.astype(jnp.float32))
        return (jax.tree.map(jnp.add, running, grad_weights), (output.astype(jnp.bfloat16), grad_in.astype(jnp.bfloat16)))
    zeros = jax.tree.map(jnp.zeros_like, weights)
    reduced_total, outputs = lax.scan(per_sequence, zeros, (tokens, cotangent))
    block_out, input_grad = outputs
    squares = sum((jnp.sum(item * item) for item in reduced_total))
    grad_norm = jnp.sqrt(squares)
    factor = jnp.minimum(1.0, CLIP_NORM / (grad_norm + 1e-06))
    firsts = (qkv_first, out_first, up_first, down_first, norm_first)
    seconds = (qkv_second, out_second, up_second, down_second, norm_second)
    averages = (qkv_average, out_average, up_average, down_average, norm_average)
    results = [adamw_moment_update(weights[slot], reduced_total[slot], firsts[slot], seconds[slot], averages[slot], rates()[slot], factor) for slot in range(5)]
    news = tuple((item[0] for item in results))
    first_news = tuple((item[1] for item in results))
    second_news = tuple((item[2] for item in results))
    average_news = tuple((item[3] for item in results))
    return (block_out, input_grad, grad_norm, news[0], news[1], news[2], news[3], news[4], first_news[0], first_news[1], first_news[2], first_news[3], first_news[4], second_news[0], second_news[1], second_news[2], second_news[3], second_news[4], average_news[0], average_news[1], average_news[2], average_news[3], average_news[4], news[0].astype(jnp.bfloat16), news[1].astype(jnp.bfloat16), news[2].astype(jnp.bfloat16), news[3].astype(jnp.bfloat16), factor * reduced_total[4][2:])
```

```python
import jax
import jax.numpy as jnp
from jax import lax
from jax.experimental import pallas as pl
from jax.experimental.pallas import tpu as pltpu
from jax.sharding import PartitionSpec as P

D = 768
DH = 64
FF = 3072
BLOCK = 64
STEP = 10


EPSILON = 1e-05
BETA_ONE = 0.9
BETA_TWO = 0.999
DECAY = 0.01
SMALL = 1e-08
CLIP_NORM = 1.0
AVERAGING = 0.999
NEGATIVE = -1e30


def norm_rows(values, gain_row, shift_row):
    center = values - jnp.mean(values, -1, keepdims=True)
    spread = jnp.mean(center * center, -1, keepdims=True)
    return center * lax.rsqrt(spread + EPSILON) * gain_row + shift_row


def key_table(rand_local, global_blocks, first_block, blocks_total):
    head_count, local_blocks = (rand_local.shape[0], rand_local.shape[1])
    places = first_block + jnp.arange(local_blocks, dtype=jnp.int32)
    left_side = jnp.maximum(places - 1, 0)
    right_side = jnp.minimum(places + 1, blocks_total - 1)
    window = jnp.stack([left_side, places, right_side], -1)
    key_index = jnp.concatenate(
        [
            jnp.broadcast_to(window[None], (head_count, local_blocks, 3)),
            rand_local,
            jnp.broadcast_to(global_blocks[None, None], (head_count, local_blocks, 2)),
        ],
        -1,
    )
    column_one = jnp.ones((local_blocks, 1), jnp.float32)
    key_valid = jnp.concatenate(
        [
            (places > 0).astype(jnp.float32)[:, None],
            column_one,
            (places < blocks_total - 1).astype(jnp.float32)[:, None],
            jnp.ones((local_blocks, 5), jnp.float32),
        ],
        -1,
    )
    return (key_index, key_valid)


def gather_rows(values):
    return lax.all_gather(values, "head", axis=1, tiled=True)


def sum_rows(values):
    return lax.psum_scatter(values, "head", scatter_dimension=1, tiled=True)


def contract(left_operand, right_operand):
    return jnp.einsum(
        "enz,enf->zf", left_operand, right_operand, preferred_element_type=jnp.float32
    )


def to_heads(values, head_count):
    seq_count, token_count = (values.shape[0], values.shape[1])
    return jnp.moveaxis(
        values.reshape(seq_count, token_count // BLOCK, BLOCK, head_count, DH), 3, 0
    )


def from_heads(values):
    head_count, seq_count, blocks = (values.shape[0], values.shape[1], values.shape[2])
    return jnp.moveaxis(values, 0, 3).reshape(seq_count, blocks * BLOCK, head_count * DH)


def pick_keys(kv_all, key_index):
    seq_count, token_count = (kv_all.shape[0], kv_all.shape[1])
    head_count = key_index.shape[0]
    blocks = kv_all.reshape(seq_count, token_count // BLOCK, BLOCK, head_count, 2, DH)
    by_head = jnp.moveaxis(blocks, 3, 0)
    return jax.vmap(lambda source, chosen: source[:, chosen])(by_head, key_index)


def scores_of(queries, picked, key_valid):
    raw_scores = jnp.einsum(
        "hsnbe,hsnkce->hsnbkc", queries, picked[..., 0, :], preferred_element_type=jnp.float32
    ) * DH ** (-0.5)
    return jnp.where(key_valid[None, None, :, None, :, None] > 0, raw_scores, NEGATIVE)


def attend_forward(queries, picked, key_valid):
    raw_scores = scores_of(queries, picked, key_valid)
    score_shape = raw_scores.shape
    scores_flat = raw_scores.reshape(score_shape[:4] + (score_shape[4] * score_shape[5],))
    row_max = jnp.max(scores_flat, -1, keepdims=True)
    exponent = jnp.exp(scores_flat - row_max)
    row_total = jnp.sum(exponent, -1, keepdims=True)
    probabilities = (exponent / row_total).astype(jnp.bfloat16).reshape(score_shape)
    output = jnp.einsum(
        "hsnbkc,hsnkce->hsnbe", probabilities, picked[..., 1, :], preferred_element_type=jnp.float32
    )
    return (output, row_max + jnp.log(row_total))


def attend_backward(queries, picked, key_valid, log_total, grad_out):
    raw_scores = scores_of(queries, picked, key_valid)
    score_shape = raw_scores.shape
    scores_flat = raw_scores.reshape(score_shape[:4] + (score_shape[4] * score_shape[5],))
    probabilities = jnp.exp(scores_flat - log_total)
    grad_probs = jnp.einsum(
        "hsnbe,hsnkce->hsnbkc", grad_out, picked[..., 1, :], preferred_element_type=jnp.float32
    ).reshape(scores_flat.shape)
    row_delta = jnp.sum(probabilities * grad_probs, -1, keepdims=True)
    grad_scores = probabilities * (grad_probs - row_delta)
    grad_scores = grad_scores.astype(jnp.bfloat16).reshape(score_shape)
    low_probs = probabilities.astype(jnp.bfloat16).reshape(score_shape)
    grad_query = jnp.einsum(
        "hsnbkc,hsnkce->hsnbe", grad_scores, picked[..., 0, :], preferred_element_type=jnp.float32
    ) * DH ** (-0.5)
    grad_keys = jnp.einsum(
        "hsnbkc,hsnbe->hsnkce", grad_scores, queries, preferred_element_type=jnp.float32
    ) * DH ** (-0.5)
    grad_values = jnp.einsum(
        "hsnbkc,hsnbe->hsnkce", low_probs, grad_out, preferred_element_type=jnp.float32
    )
    return (grad_query, jnp.stack([grad_keys, grad_values], -2), row_delta)


def spread_back(grad_pairs, key_index, seq_count, blocks_total):
    head_count = key_index.shape[0]
    zero_grid = jnp.zeros((head_count, seq_count, blocks_total, BLOCK, 2, DH), jnp.float32)
    filled = jax.vmap(lambda source, chosen, addend: source.at[:, chosen].add(addend))(
        zero_grid, key_index, grad_pairs
    )
    return jnp.moveaxis(filled, 0, 3).reshape(seq_count, blocks_total * BLOCK, head_count * 2 * DH)


def rates():
    return (
        1.5 * D ** (-0.5),
        1.5 * max(1, D // (8 * BLOCK)) ** (-0.5),
        1.5 * D ** (-0.5),
        1.5 * FF ** (-0.5),
        0.5,
    )


def adamw_moment_update(weight, gradient, moment_one, moment_two, average, rate, factor):
    decay_mean = min(AVERAGING, (1.0 + STEP) / (10.0 + STEP))
    clipped = gradient * factor
    first_new = BETA_ONE * moment_one + (1.0 - BETA_ONE) * clipped
    second_new = BETA_TWO * moment_two + (1.0 - BETA_TWO) * clipped * clipped
    update = (
        first_new / (1.0 - BETA_ONE**STEP) / (jnp.sqrt(second_new / (1.0 - BETA_TWO**STEP)) + SMALL)
    )
    weight_new = weight - rate * (update + DECAY * weight)
    average_new = decay_mean * average + (1.0 - decay_mean) * weight_new
    return (weight_new, first_new, second_new, average_new)


def body(
    tokens,
    cotangent,
    rand_blocks,
    global_blocks,
    qkv_weight,
    out_weight,
    up_weight,
    down_weight,
    norm_params,
    qkv_first,
    out_first,
    up_first,
    down_first,
    norm_first,
    qkv_second,
    out_second,
    up_second,
    down_second,
    norm_second,
    qkv_average,
    out_average,
    up_average,
    down_average,
    norm_average,
):
    qkv_low, out_low, up_low, down_low = (
        lax.all_gather(qkv_weight.astype(jnp.bfloat16), ("dp", "seq"), axis=0, tiled=True),
        lax.all_gather(out_weight.astype(jnp.bfloat16), ("dp", "seq"), axis=1, tiled=True),
        lax.all_gather(up_weight.astype(jnp.bfloat16), ("dp", "seq"), axis=0, tiled=True),
        lax.all_gather(down_weight.astype(jnp.bfloat16), ("dp", "seq"), axis=1, tiled=True),
    )
    seq_count = tokens.shape[0]
    head_count = rand_blocks.shape[0]
    local_blocks = rand_blocks.shape[1]
    blocks_total = local_blocks * lax.axis_size("seq")
    first_block = lax.axis_index("seq") * local_blocks
    key_index, key_valid = key_table(rand_blocks, global_blocks, first_block, blocks_total)
    inputs = tokens.astype(jnp.float32)
    full_one = gather_rows(norm_rows(inputs, norm_params[0], norm_params[1]).astype(jnp.bfloat16))
    token_count = full_one.shape[1]
    qkv_all = jnp.dot(full_one, qkv_low, preferred_element_type=jnp.float32).astype(jnp.bfloat16)
    qkv_parts = qkv_all.reshape(seq_count, token_count, head_count, 3, DH)
    kv_local = qkv_parts[:, :, :, 1:, :].reshape(seq_count, token_count, head_count * 2 * DH)
    kv_all = lax.all_gather(kv_local, "seq", axis=1, tiled=True)
    picked = pick_keys(kv_all, key_index)
    queries = to_heads(qkv_parts[:, :, :, 0, :], head_count)
    attended, log_total = attend_forward(queries, picked, key_valid)
    mixed_heads = from_heads(attended.astype(jnp.bfloat16))
    residual = inputs + sum_rows(jnp.dot(mixed_heads, out_low, preferred_element_type=jnp.float32))
    full_two = gather_rows(norm_rows(residual, norm_params[2], norm_params[3]).astype(jnp.bfloat16))
    upward = jnp.dot(full_two, up_low, preferred_element_type=jnp.float32)
    active = jax.nn.gelu(upward).astype(jnp.bfloat16)
    result = residual + sum_rows(jnp.dot(active, down_low, preferred_element_type=jnp.float32))
    block_out = result.astype(jnp.bfloat16)
    grad_top = gather_rows(cotangent)
    grad_down = contract(active, grad_top)
    grad_active = jnp.dot(grad_top, down_low.T, preferred_element_type=jnp.float32)
    _, gelu_back = jax.vjp(jax.nn.gelu, upward)
    grad_upward = gelu_back(grad_active)[0].astype(jnp.bfloat16)
    grad_up = contract(full_two, grad_upward)
    part_two = sum_rows(jnp.dot(grad_upward, up_low.T, preferred_element_type=jnp.float32))
    _, norm_back_two = jax.vjp(norm_rows, residual, norm_params[2], norm_params[3])
    grad_residual_norm, grad_gain_two, grad_shift_two = norm_back_two(part_two)
    grad_residual = cotangent.astype(jnp.float32) + grad_residual_norm
    grad_middle = gather_rows(grad_residual.astype(jnp.bfloat16))
    grad_out = contract(mixed_heads, grad_middle)
    grad_mixed = jnp.dot(grad_middle, out_low.T, preferred_element_type=jnp.float32).astype(
        jnp.bfloat16
    )
    grad_query, grad_pairs, row_delta = attend_backward(
        queries, picked, key_valid, log_total, to_heads(grad_mixed, head_count)
    )
    grad_kv_full = spread_back(grad_pairs, key_index, seq_count, blocks_total)
    grad_kv = lax.psum_scatter(
        grad_kv_full.astype(jnp.bfloat16), "seq", scatter_dimension=1, tiled=True
    ).astype(jnp.float32)
    query_gradient = from_heads(grad_query).reshape(seq_count, token_count, head_count, 1, DH)
    grad_qkv_rows = jnp.concatenate(
        [query_gradient, grad_kv.reshape(seq_count, token_count, head_count, 2, DH)], 3
    )
    grad_qkv_rows = grad_qkv_rows.reshape(seq_count, token_count, head_count * 3 * DH).astype(
        jnp.bfloat16
    )
    grad_qkv = contract(full_one, grad_qkv_rows)
    part_one = sum_rows(jnp.dot(grad_qkv_rows, qkv_low.T, preferred_element_type=jnp.float32))
    _, norm_back_one = jax.vjp(norm_rows, inputs, norm_params[0], norm_params[1])
    grad_input_norm, grad_gain_one, grad_shift_one = norm_back_one(part_one)
    input_grad = (grad_residual + grad_input_norm).astype(jnp.bfloat16)
    grad_norm_local = jnp.stack([grad_gain_one, grad_shift_one, grad_gain_two, grad_shift_two])
    reduced_total = (
        lax.psum_scatter(grad_qkv, ("dp", "seq"), scatter_dimension=0, tiled=True),
        lax.psum_scatter(grad_out, ("dp", "seq"), scatter_dimension=1, tiled=True),
        lax.psum_scatter(grad_up, ("dp", "seq"), scatter_dimension=0, tiled=True),
        lax.psum_scatter(grad_down, ("dp", "seq"), scatter_dimension=1, tiled=True),
    )
    squares = sum((jnp.sum(item * item) for item in reduced_total))
    norm_grads = lax.psum(grad_norm_local, ("dp", "seq", "head"))
    matrix_squares = lax.psum(squares, ("dp", "seq", "head"))
    grad_norm = jnp.sqrt(matrix_squares + jnp.sum(norm_grads * norm_grads))
    factor = jnp.minimum(1.0, CLIP_NORM / (grad_norm + 1e-06))
    weights = (qkv_weight, out_weight, up_weight, down_weight, norm_params)
    gradients = (reduced_total[0], reduced_total[1], reduced_total[2], reduced_total[3], norm_grads)
    firsts = (qkv_first, out_first, up_first, down_first, norm_first)
    seconds = (qkv_second, out_second, up_second, down_second, norm_second)
    averages = (qkv_average, out_average, up_average, down_average, norm_average)
    results = [
        adamw_moment_update(
            weights[slot],
            gradients[slot],
            firsts[slot],
            seconds[slot],
            averages[slot],
            rates()[slot],
            factor,
        )
        for slot in range(5)
    ]
    news = tuple((item[0] for item in results))
    first_news = tuple((item[1] for item in results))
    second_news = tuple((item[2] for item in results))
    average_news = tuple((item[3] for item in results))
    return (
        block_out,
        input_grad,
        grad_norm,
        news[0],
        news[1],
        news[2],
        news[3],
        news[4],
        first_news[0],
        first_news[1],
        first_news[2],
        first_news[3],
        first_news[4],
        second_news[0],
        second_news[1],
        second_news[2],
        second_news[3],
        second_news[4],
        average_news[0],
        average_news[1],
        average_news[2],
        average_news[3],
        average_news[4],
        news[0].astype(jnp.bfloat16),
        news[1].astype(jnp.bfloat16),
        news[2].astype(jnp.bfloat16),
        news[3].astype(jnp.bfloat16),
        factor * norm_grads[2:],
    )


GROUP = ("seq", "head")
EVERY = ("dp", "seq", "head")
FULL = 4096
CHUNK = 512
MB = 1024 * 1024


def limits(megabytes):
    return pltpu.CompilerParams(vmem_limit_bytes=megabytes * MB)


def swap(values, distance):
    return lax.ppermute(values, GROUP, [(i, i ^ distance) for i in range(8)])


def swap_dp(values, distance, dp_size):
    count = dp_size * 2
    return lax.ppermute(values, ("dp", "seq"), [(i, i ^ distance) for i in range(count)])


def swap_every(values, distance, count):
    return lax.ppermute(values, EVERY, [(i, i ^ distance) for i in range(count)])


def nt(left, right):
    return lax.dot_general(left, right, (((1,), (1,)), ((), ())), preferred_element_type=jnp.float32)


def nn(left, right):
    return lax.dot_general(left, right, (((1,), (0,)), ((), ())), preferred_element_type=jnp.float32)


def tn(left, right):
    return lax.dot_general(left, right, (((0,), (0,)), ((), ())), preferred_element_type=jnp.float32)


def lane_low(shape):
    return lax.broadcasted_iota(jnp.int32, shape, len(shape) - 1) < 64


def roll64(values):
    return pltpu.roll(values, 64, 1)


def block_places(tab_ref, k, block):
    me = tab_ref[0]
    part = (block // 32) ^ (me // 4)
    base = 8 + ((part * 3 + k) * 32 + block % 32) * 3
    chosen = [
        jnp.maximum(block - 1, 0),
        block,
        jnp.minimum(block + 1, 63),
        tab_ref[base],
        tab_ref[base + 1],
        tab_ref[base + 2],
        tab_ref[1],
        tab_ref[2],
    ]
    return [pl.multiple_of((((b // 8) ^ me) * 8 + b % 8) * 64, 64) for b in chosen]


def softmax_parts(scores, block):
    lane = lax.broadcasted_iota(jnp.int32, scores.shape, 1)
    hidden = ((lane < 64) & (block == 0)) | ((lane >= 128) & (lane < 192) & (block == 63))
    scores = jnp.where(hidden, NEGATIVE, scores)
    top = jnp.max(scores, -1, keepdims=True)
    exponent = jnp.exp(scores - top)
    total = jnp.sum(exponent, -1, keepdims=True)
    return exponent * (1.0 / total)


def spread_heads(wide):
    tile = lambda j: wide[:, j * 128 : j * 128 + 128]
    low = lane_low((wide.shape[0], 128))
    last_half = jnp.concatenate([wide[:, 512:576], jnp.zeros((wide.shape[0], 64), jnp.float32)], 1)
    scale = DH ** (-0.5)
    return [
        jnp.where(low, tile(0) * scale, 0.0),
        jnp.where(low, roll64(tile(0)), roll64(tile(1))),
        jnp.where(low, roll64(tile(1)) * scale, 0.0),
        tile(2),
        jnp.where(low, tile(3) * scale, 0.0),
        jnp.where(low, roll64(tile(3)), roll64(last_half)),
    ]


def qkv_kernel(rows_ref, *refs):
    tok_refs, piece_refs, out_ref, weight_ref = refs[:8], refs[8:16], refs[16], refs[17]
    for j, piece in enumerate(piece_refs):
        at = pl.multiple_of((rows_ref[0] ^ j) * 96, 96)
        weight_ref[pl.ds(at, 96), :] = piece[...]
    for slot, tok_ref in enumerate(tok_refs):
        for n, part in enumerate(spread_heads(nn(tok_ref[...], weight_ref[...]))):
            out_ref[slot * CHUNK : slot * CHUNK + CHUNK, n * 128 : n * 128 + 128] = part.astype(jnp.bfloat16)


def project(me_rows, slots, pieces):
    return pl.pallas_call(
        qkv_kernel,
        grid_spec=pltpu.PrefetchScalarGridSpec(
            num_scalar_prefetch=1,
            grid=(1,),
            in_specs=[pl.BlockSpec((CHUNK, D), lambda i, t: (0, 0))] * 8 + [pl.BlockSpec((96, 576), lambda i, t: (0, 0))] * 8,
            out_specs=pl.BlockSpec((FULL, D), lambda i, t: (0, 0)),
            scratch_shapes=[pltpu.VMEM((D, 576), jnp.bfloat16)],
        ),
        out_shape=jax.ShapeDtypeStruct((FULL, D), jnp.bfloat16),
        compiler_params=limits(32),
        name="project",
        cost_estimate=pl.CostEstimate(flops=4 * 10**9, bytes_accessed=13 * MB, transcendentals=0),
    )(me_rows, *slots, *pieces)


def attend_kernel(k, tab_ref, qkv_ref, out_ref):
    me = tab_ref[0]

    def one(place):
        block = ((place // 8) ^ me) * 8 + place % 8
        places = block_places(tab_ref, k, block)
        keys = jnp.concatenate([qkv_ref[pl.ds(p, 64), 128:256] for p in places], 0)
        queries = qkv_ref[pl.ds(pl.multiple_of(place * 64, 64), 64), 0:128]
        probs = softmax_parts(nt(queries, keys), block).astype(jnp.bfloat16)
        return nn(probs, keys)

    def step(n, carry):
        slot, q = n // 4, n % 4
        low = one(slot * 8 + q)
        high = one(slot * 8 + q + 4)
        both = jnp.where(lane_low(low.shape), roll64(low), high)
        out_ref[slot ^ me, pl.ds(pl.multiple_of(q * 64, 64), 64), :] = both.astype(jnp.bfloat16)
        return carry

    lax.fori_loop(0, 32, step, 0, unroll=2)


def attend(k, table, qkv):
    return pl.pallas_call(
        lambda *refs: attend_kernel(k, *refs),
        grid_spec=pltpu.PrefetchScalarGridSpec(
            num_scalar_prefetch=1,
            grid=(1,),
            in_specs=[pl.BlockSpec((FULL, 256), lambda i, t: (0, k))],
            out_specs=pl.BlockSpec((8, 256, 128), lambda i, t: (0, 0, 0)),
        ),
        out_shape=jax.ShapeDtypeStruct((8, 256, 128), jnp.bfloat16),
        compiler_params=limits(24),
        name="attend",
        cost_estimate=pl.CostEstimate(flops=4 * 10**9, bytes_accessed=3 * MB, transcendentals=2 * 10**6),
    )(table, qkv)


def attend_back_kernel(k, tab_ref, qkv_ref, grad_ref, full_ref, pack_ref, acc_ref):
    me = tab_ref[0]
    acc_ref[...] = jnp.zeros_like(acc_ref)

    def one(place, grad):
        block = ((place // 8) ^ me) * 8 + place % 8
        places = block_places(tab_ref, k, block)
        keys = jnp.concatenate([qkv_ref[pl.ds(p, 64), 128:256] for p in places], 0)
        at = pl.multiple_of(place * 64, 64)
        queries = qkv_ref[pl.ds(at, 64), 0:128]
        stacked = jnp.concatenate([queries, grad], 0)
        both = nt(stacked, keys)
        probs = softmax_parts(both[:64], block)
        grad_probs = both[64:]
        delta = jnp.sum(probs * grad_probs, -1, keepdims=True)
        low_scores = (probs * (grad_probs - delta)).astype(jnp.bfloat16)
        grad_query = nn(low_scores, keys) * DH ** (-0.5)
        grad_query = jnp.where(lane_low(grad_query.shape), grad_query, 0.0)
        full_ref[pl.ds(at, 64), 0:128] = grad_query.astype(jnp.bfloat16)
        spread = tn(jnp.concatenate([low_scores, probs.astype(jnp.bfloat16)], 0), stacked)
        for j, p in enumerate(places):
            acc_ref[pl.ds(p, 64), :] += spread[j * 64 : j * 64 + 64]
        return grad_query

    def step(n, carry):
        slot, q = n // 4, n % 4
        rows = pl.ds(pl.multiple_of(q * 64, 64), 64)
        tile = grad_ref[slot ^ me, rows, :].astype(jnp.float32)
        low_lanes = lane_low(tile.shape)
        first = jnp.where(low_lanes, 0.0, roll64(tile)).astype(jnp.bfloat16)
        second = jnp.where(low_lanes, 0.0, tile).astype(jnp.bfloat16)
        grad_first = one(slot * 8 + q, first)
        grad_second = one(slot * 8 + q + 4, second)
        both = jnp.where(low_lanes, grad_first, roll64(grad_second))
        pack_ref[slot ^ me, rows, :] = both.astype(jnp.bfloat16)
        return carry

    lax.fori_loop(0, 32, step, 0)

    def finish(slot, carry):
        at = pl.ds(pl.multiple_of(slot * CHUNK, CHUNK), CHUNK)
        low = acc_ref[at, :].astype(jnp.bfloat16)
        full_ref[at, 128:256] = low
        pack_ref[slot ^ me, 256:768, :] = low
        return carry

    lax.fori_loop(0, 8, finish, 0)


def attend_back(k, table, qkv, grad):
    return pl.pallas_call(
        lambda *refs: attend_back_kernel(k, *refs),
        grid_spec=pltpu.PrefetchScalarGridSpec(
            num_scalar_prefetch=1,
            grid=(1,),
            in_specs=[
                pl.BlockSpec((FULL, 256), lambda i, t: (0, k)),
                pl.BlockSpec((8, 256, 128), lambda i, t: (0, 0, 0)),
            ],
            out_specs=[
                pl.BlockSpec((FULL, 256), lambda i, t: (0, 0)),
                pl.BlockSpec((8, 768, 128), lambda i, t: (0, 0, 0)),
            ],
            scratch_shapes=[pltpu.VMEM((FULL, 128), jnp.float32)],
        ),
        out_shape=[
            jax.ShapeDtypeStruct((FULL, 256), jnp.bfloat16),
            jax.ShapeDtypeStruct((8, 768, 128), jnp.bfloat16),
        ],
        compiler_params=limits(24),
        name="attend_back",
        cost_estimate=pl.CostEstimate(flops=10 * 10**9, bytes_accessed=6 * MB, transcendentals=2 * 10**6),
    )(table, qkv, grad)


def norm_stats(values):
    center = values - jnp.mean(values, -1, keepdims=True)
    spread = jnp.mean(center * center, -1, keepdims=True)
    scale = lax.rsqrt(spread + EPSILON)
    return center * scale, scale


ORDER = (0, 2, 1, 3)


def halves(first, second):
    low = lane_low(first.shape)
    upper = jnp.where(low, first, roll64(second))
    lower = jnp.where(low, roll64(first), second)
    return upper, lower


def mid_kernel(me_ref, o0_ref, o1_ref, o2_ref, wo_ref, tok_ref, par_ref, cat_ref, mid_ref, a2_ref):
    head = me_ref[0]
    group = [(head ^ r, ref) for r in ORDER for ref in (o0_ref, o1_ref, o2_ref)]
    for j in range(6):
        (ha, ra), (hb, rb) = group[2 * j], group[2 * j + 1]
        upper, lower = halves(ra[ha].astype(jnp.float32), rb[hb].astype(jnp.float32))
        cat_ref[0, 0:256, j * 128 : j * 128 + 128] = upper.astype(jnp.bfloat16)
        cat_ref[0, 256:512, j * 128 : j * 128 + 128] = lower.astype(jnp.bfloat16)
    middle = tok_ref[0].astype(jnp.float32) + nt(cat_ref[0], wo_ref[...])
    mid_ref[0] = middle
    normed, _ = norm_stats(middle)
    a2_ref[0] = (normed * par_ref[2:3, :] + par_ref[3:4, :]).astype(jnp.bfloat16)


def middle(me_head, o_parts, wo, tokens, params):
    seqs = tokens.shape[0]
    piece = pl.BlockSpec((4, 256, 128), lambda s, t: (s, 0, 0))
    rows = pl.BlockSpec((1, CHUNK, D), lambda s, t: (s, 0, 0))
    return pl.pallas_call(
        mid_kernel,
        grid_spec=pltpu.PrefetchScalarGridSpec(
            num_scalar_prefetch=1,
            grid=(seqs,),
            in_specs=[piece, piece, piece, pl.BlockSpec((D, D), lambda s, t: (0, 0)), rows,
                      pl.BlockSpec((4, D), lambda s, t: (0, 0))],
            out_specs=[rows, rows, rows],
        ),
        out_shape=[
            jax.ShapeDtypeStruct(tokens.shape, jnp.bfloat16),
            jax.ShapeDtypeStruct(tokens.shape, jnp.float32),
            jax.ShapeDtypeStruct(tokens.shape, jnp.bfloat16),
        ],
        compiler_params=limits(24),
        name="middle",
        cost_estimate=pl.CostEstimate(flops=2 * 10**9, bytes_accessed=12 * MB, transcendentals=0),
    )(me_head, *o_parts, wo, tokens, params)


HIDDEN = 384


def mlp_kernel(a2_ref, a2t_ref, dy_ref, dyt_ref, wu_ref, wd_ref, out_ref, back_ref, du_ref, dd_ref, g_ref, u_ref):
    @pl.when(pl.program_id(0) == 0)
    def _():
        out_ref[...] = jnp.zeros_like(out_ref)
        back_ref[...] = jnp.zeros_like(back_ref)

    wu, wd = wu_ref[0], wd_ref[0]
    rate, cubic = (2.0 / jnp.pi) ** 0.5, 0.044715
    rate = float(rate)
    for m in range(4):
        at = slice(m * 256, m * 256 + 256)
        up = nn(a2_ref[at, :], wu)
        grad = nn(dy_ref[at, :], wd)
        square = up * up
        bend = jnp.tanh(rate * up * (1.0 + cubic * square))
        half = 0.5 * (1.0 + bend)
        g_ref[at, :] = (up * half).astype(jnp.bfloat16)
        slope = half + 0.5 * up * (1.0 - bend * bend) * (rate * (1.0 + 3.0 * cubic * square))
        u_ref[at, :] = (grad * slope).astype(jnp.bfloat16)
        out_ref[at, :] += nt(g_ref[at, :], wd)
        back_ref[at, :] += nt(u_ref[at, :], wu)
    du_ref[0] = nn(a2t_ref[...], u_ref[...]).astype(du_ref.dtype)
    dd_ref[0] = nn(dyt_ref[...], g_ref[...]).astype(dd_ref.dtype)


def mlp(a2, a2t, dy, dyt, weights, grad_type):
    tokens = a2.shape[0]
    whole = lambda shape: pl.BlockSpec(shape, lambda i: (0, 0))
    per = D // HIDDEN
    grads = pl.BlockSpec((1, D, HIDDEN), lambda i: (i // per, 0, i % per))
    return pl.pallas_call(
        mlp_kernel,
        grid=(2 * per,),
        in_specs=[
            whole((tokens, D)), whole((D, tokens)), whole((tokens, D)), whole((D, tokens)),
            pl.BlockSpec((1, D, HIDDEN), lambda i: (i // per, 0, i % per)),
            pl.BlockSpec((1, D, HIDDEN), lambda i: (i // per, 0, per + i % per)),
        ],
        out_specs=[whole((tokens, D)), whole((tokens, D)), grads, grads],
        out_shape=[
            jax.ShapeDtypeStruct((tokens, D), jnp.float32),
            jax.ShapeDtypeStruct((tokens, D), jnp.float32),
            jax.ShapeDtypeStruct((2, D, D), grad_type),
            jax.ShapeDtypeStruct((2, D, D), grad_type),
        ],
        scratch_shapes=[pltpu.VMEM((tokens, HIDDEN), jnp.bfloat16), pltpu.VMEM((tokens, HIDDEN), jnp.bfloat16)],
        compiler_params=limits(32),
        name="mlp",
        cost_estimate=pl.CostEstimate(flops=15 * 10**9, bytes_accessed=20 * MB, transcendentals=2 * 10**6),
    )(a2, a2t, dy, dyt, weights, weights)


def norm_back(grad, values, gain):
    normed, scale = norm_stats(values)
    gain_grad = jnp.sum(grad * normed, 0, keepdims=True)
    shift_grad = jnp.sum(grad, 0, keepdims=True)
    inner = grad * gain
    across = jnp.mean(inner, -1, keepdims=True)
    along = jnp.mean(inner * normed, -1, keepdims=True)
    return scale * (inner - across - normed * along), gain_grad, shift_grad


def mid_back_kernel(me_ref, b0_ref, b1_ref, mid_ref, dy_ref, wo_ref, par_ref, grad_ref, low_ref, g0_ref, g1_ref, g2_ref, norm_ref):
    head = me_ref[0]
    grad, gain_grad, shift_grad = norm_back(b0_ref[...] + b1_ref[...], mid_ref[0], par_ref[2:3, :])
    total = dy_ref[0].astype(jnp.float32) + grad
    grad_ref[0] = total
    low = total.astype(jnp.bfloat16)
    low_ref[0] = low
    mixed = nn(low, wo_ref[...])
    group = [(head ^ r, ref) for r in ORDER for ref in (g0_ref, g1_ref, g2_ref)]
    for j in range(6):
        (ha, ra), (hb, rb) = group[2 * j], group[2 * j + 1]
        tile = mixed[:, j * 128 : j * 128 + 128]
        first, second = halves(tile[0:256], tile[256:512])
        ra[ha] = first.astype(jnp.bfloat16)
        rb[hb] = second.astype(jnp.bfloat16)

    @pl.when(pl.program_id(0) == 0)
    def _():
        norm_ref[...] = jnp.zeros_like(norm_ref)

    norm_ref[0:1, :] += gain_grad
    norm_ref[1:2, :] += shift_grad


def middle_back(me_head, backs, mid, dy, wo, params):
    seqs = dy.shape[0]
    piece = pl.BlockSpec((4, 256, 128), lambda s, t: (s, 0, 0))
    rows = pl.BlockSpec((1, CHUNK, D), lambda s, t: (s, 0, 0))
    flat = pl.BlockSpec((CHUNK, D), lambda s, t: (s, 0))
    low_piece = jax.ShapeDtypeStruct((8, 256, 128), jnp.bfloat16)
    return pl.pallas_call(
        mid_back_kernel,
        grid_spec=pltpu.PrefetchScalarGridSpec(
            num_scalar_prefetch=1,
            grid=(seqs,),
            in_specs=[flat, flat, rows, rows, pl.BlockSpec((D, D), lambda s, t: (0, 0)),
                      pl.BlockSpec((4, D), lambda s, t: (0, 0))],
            out_specs=[rows, rows, piece, piece, piece, pl.BlockSpec((8, D), lambda s, t: (0, 0))],
        ),
        out_shape=[
            jax.ShapeDtypeStruct(dy.shape, jnp.float32),
            jax.ShapeDtypeStruct(dy.shape, jnp.bfloat16),
            low_piece, low_piece, low_piece,
            jax.ShapeDtypeStruct((8, D), jnp.float32),
        ],
        compiler_params=limits(24),
        name="middle_back",
        cost_estimate=pl.CostEstimate(flops=2 * 10**9, bytes_accessed=16 * MB, transcendentals=0),
    )(me_head, *backs, mid, dy, wo, params)


def out_grad_kernel(low_ref, cat_ref, own_ref, mate_ref):
    full = tn(low_ref[...], cat_ref[...])
    own_ref[...] = full[:, 0:384]
    mate_ref[...] = full[:, 384:768].astype(jnp.bfloat16)


def out_weight_grad(low, cat):
    return pl.pallas_call(
        out_grad_kernel,
        out_shape=[jax.ShapeDtypeStruct((D, 384), jnp.float32), jax.ShapeDtypeStruct((D, 384), jnp.bfloat16)],
        compiler_params=limits(24),
        name="out_weight_grad",
        cost_estimate=pl.CostEstimate(flops=12 * 10**8, bytes_accessed=5 * MB, transcendentals=0),
    )(low, cat)


def qkv_grad_kernel(*refs):
    tok_refs, full_refs, out_ref = refs[:8], refs[8:11], refs[11]
    for slot, tok_ref in enumerate(tok_refs):
        at = slice(slot * CHUNK, slot * CHUNK + CHUNK)
        part = tn(tok_ref[...], jnp.concatenate([ref[at, :] for ref in full_refs], 1))
        out_ref[...] = part if slot == 0 else out_ref[...] + part


def qkv_weight_grad(slots, fulls):
    return pl.pallas_call(
        qkv_grad_kernel,
        out_shape=jax.ShapeDtypeStruct((D, D), jnp.float32),
        compiler_params=limits(32),
        name="qkv_weight_grad",
        cost_estimate=pl.CostEstimate(flops=5 * 10**9, bytes_accessed=14 * MB, transcendentals=0),
    )(*slots, *fulls)


def last_kernel(me_ref, p0_ref, p1_ref, p2_ref, own_ref, mate_ref, tok_ref, mid_ref, par_ref, out_ref, norm_ref):
    head = me_ref[0]
    low = lane_low((CHUNK, 128))
    grad = None
    for n, r in enumerate(ORDER):
        queries, pairs = [], []
        for ref in (p0_ref, p1_ref, p2_ref):
            both = ref[head ^ r, 0:256, :].astype(jnp.float32)
            queries.append(jnp.concatenate([both, roll64(both)], 0))
            pairs.append(ref[head ^ r, 256:768, :].astype(jnp.float32))
        tiles = [
            jnp.where(low, queries[0], roll64(pairs[0])),
            jnp.where(low, roll64(pairs[0]), roll64(queries[1])),
            pairs[1],
            jnp.where(low, queries[2], roll64(pairs[2])),
            jnp.where(low, roll64(pairs[2]), 0.0),
        ]
        wide = jnp.concatenate([tile.astype(jnp.bfloat16) for tile in tiles], 1)
        part = nt(wide, (own_ref, own_ref, mate_ref, mate_ref)[n][n % 2])
        grad = part if grad is None else grad + part
    back, gain_grad, shift_grad = norm_back(grad, tok_ref[0].astype(jnp.float32), par_ref[0:1, :])
    out_ref[0] = (mid_ref[0] + back).astype(jnp.bfloat16)

    @pl.when(pl.program_id(0) == 0)
    def _():
        norm_ref[...] = jnp.zeros_like(norm_ref)

    norm_ref[0:1, :] += gain_grad
    norm_ref[1:2, :] += shift_grad


def last(me_head, packs, own, mate, tokens, mid_grad, params):
    seqs = tokens.shape[0]
    piece = pl.BlockSpec((4, 768, 128), lambda s, t: (s, 0, 0))
    rows = pl.BlockSpec((1, CHUNK, D), lambda s, t: (s, 0, 0))
    weight = pl.BlockSpec((2, D, 640), lambda s, t: (0, 0, 0))
    return pl.pallas_call(
        last_kernel,
        grid_spec=pltpu.PrefetchScalarGridSpec(
            num_scalar_prefetch=1,
            grid=(seqs,),
            in_specs=[piece, piece, piece, weight, weight, rows, rows, pl.BlockSpec((4, D), lambda s, t: (0, 0))],
            out_specs=[rows, pl.BlockSpec((8, D), lambda s, t: (0, 0))],
        ),
        out_shape=[jax.ShapeDtypeStruct(tokens.shape, jnp.bfloat16), jax.ShapeDtypeStruct((8, D), jnp.float32)],
        compiler_params=limits(24),
        name="last",
        cost_estimate=pl.CostEstimate(flops=4 * 10**9, bytes_accessed=14 * MB, transcendentals=0),
    )(me_head, *packs, own, mate, tokens, mid_grad, params)


def join_seq(values, y):
    other = swap(values, 4)
    return jnp.concatenate(
        [jnp.where(y == 0, values, other), jnp.where(y == 0, other, values)], axis=values.ndim - 2
    )


def gather_core(shard, y):
    both = jnp.stack([shard, swap(shard, 2)])
    return lax.all_gather(join_seq(both, y), "dp", axis=1, tiled=True)


def pick(values, index, size, axis):
    return lax.dynamic_slice_in_dim(values, index * size, size, axis)


def scatter_core(mine, theirs, y):
    both = (mine + swap(theirs, 1).astype(jnp.float32)).astype(jnp.bfloat16)
    mixed = lax.psum_scatter(both, "dp", scatter_dimension=1, tiled=True)
    half = mixed.shape[1] // 2
    kept = pick(mixed, y, half, 1).astype(jnp.float32) + swap(pick(mixed, 1 - y, half, 1), 4).astype(jnp.float32)
    return kept[0] + swap(kept[1].astype(jnp.bfloat16), 2).astype(jnp.float32)


def fast_body(
    tokens, cotangent, rand_blocks, global_blocks, qkv_weight, out_weight, up_weight, down_weight, norm_params,
    qkv_first, out_first, up_first, down_first, norm_first,
    qkv_second, out_second, up_second, down_second, norm_second,
    qkv_average, out_average, up_average, down_average, norm_average,
):
    dp_size = lax.axis_size("dp")
    count = dp_size * 8
    y, head = lax.axis_index("seq"), lax.axis_index("head")
    me_rows = lax.axis_index("dp") * 2 + y
    me = y * 4 + head
    me_head = jnp.reshape(head, (1,)).astype(jnp.int32)

    turned = jnp.stack([pick(tokens, y, 1, 0)[0], pick(tokens, 1 - y, 1, 0)[0]])
    normed = norm_rows(turned.astype(jnp.float32), norm_params[0], norm_params[1]).astype(jnp.bfloat16)
    mine, theirs = normed[0], normed[1]
    even = [mine, swap(mine, 2), swap(theirs, 4), swap(theirs, 6)]
    odd = [swap(item, 1) for item in even]
    slots = [item for pair in zip(even, odd) for item in pair]

    low_qkv = qkv_weight.astype(jnp.bfloat16)
    pieces = [low_qkv] + [swap_dp(low_qkv, j, dp_size) for j in range(1, 8)]
    blank = jnp.zeros((96, 64), jnp.bfloat16)
    early = jnp.concatenate([up_weight, down_weight.T, out_weight.T], -1).astype(jnp.bfloat16)
    early_own = gather_core(early, y)
    early_mate = swap(early_own, 1)
    late_own = gather_core(jnp.concatenate([low_qkv, blank], -1), y)
    late_mate = swap(late_own, 1)
    wo = jnp.concatenate([early_own[0, :, 1536:], early_own[1, :, 1536:], early_mate[0, :, 1536:], early_mate[1, :, 1536:]], -1)

    both_rand = jnp.concatenate([rand_blocks.reshape(-1), swap(rand_blocks.reshape(-1), 4)])
    table = jnp.concatenate(
        [jnp.reshape(me, (1,)), global_blocks, jnp.zeros((5,), jnp.int32), both_rand]
    ).astype(jnp.int32)
    qkv = project(jnp.reshape(me_rows, (1,)).astype(jnp.int32), slots, pieces)

    def across(values):
        return lax.all_to_all(values, GROUP, 0, 0, tiled=True)

    o_parts = [across(attend(k, table, qkv)) for k in range(3)]
    mixed, mid, a2 = middle(me_head, o_parts, wo, tokens, norm_params)

    rows = a2.shape[0] * a2.shape[1]
    a2, dy, mixed = a2.reshape(rows, D), cotangent.reshape(rows, D), mixed.reshape(rows, D)
    a2t, dyt = a2.T, dy.T
    out_a, back_a, up_a, down_a = mlp(a2, a2t, dy, dyt, early_own, jnp.float32)
    out_b, back_b, up_b, down_b = mlp(a2, a2t, dy, dyt, early_mate, jnp.bfloat16)
    block_out = (mid + (out_a + out_b).reshape(mid.shape)).astype(jnp.bfloat16)
    up_grad = scatter_core(up_a, up_b, y)
    down_grad = scatter_core(down_a, down_b, y)

    mid_grad, low_grad, g0, g1, g2, norm_two = middle_back(me_head, (back_a, back_b), mid, cotangent, wo, norm_params)
    out_own, out_mate = out_weight_grad(low_grad.reshape(rows, D), mixed)
    pair = lambda item: jnp.stack([item[:, 0:192], item[:, 192:384]])
    out_grad = scatter_core(pair(out_own), pair(out_mate), y)

    fulls, packs = [], []
    for k, grad in enumerate((g0, g1, g2)):
        full, pack = attend_back(k, table, qkv, across(grad))
        fulls.append(full)
        packs.append(across(pack))
    input_grad, norm_one = last(me_head, packs, late_own, late_mate, tokens, mid_grad, norm_params)

    wide = qkv_weight_grad(slots, fulls)
    wide = jnp.concatenate([wide[:, k * 256 + at : k * 256 + to] for k in range(3) for at, to in ((0, 64), (128, 256))], -1)
    wide = wide.reshape(dp_size * 2, 96, 576)
    qkv_grad = lax.dynamic_index_in_dim(wide, me_rows, 0, False)
    for j in range(1, dp_size * 2):
        sent = lax.dynamic_index_in_dim(wide, me_rows ^ j, 0, False).astype(jnp.bfloat16)
        qkv_grad = qkv_grad + swap_dp(sent, j, dp_size).astype(jnp.float32)

    reduced = (qkv_grad, out_grad.T, up_grad, down_grad.T)
    squares = sum((jnp.sum(item * item) for item in reduced))
    shared = jnp.concatenate(
        [norm_one[0:2], norm_two[0:2], jnp.full((1, D), squares), jnp.zeros((3, D), jnp.float32)], 0
    )
    distance = 1
    while distance < count:
        shared = shared + swap_every(shared, distance, count)
        distance *= 2
    norm_grads = shared[0:4]
    grad_norm = jnp.sqrt(shared[4, 0] + jnp.sum(norm_grads * norm_grads))
    factor = jnp.minimum(1.0, CLIP_NORM / (grad_norm + 1e-06))
    weights = (qkv_weight, out_weight, up_weight, down_weight, norm_params)
    gradients = reduced + (norm_grads,)
    firsts = (qkv_first, out_first, up_first, down_first, norm_first)
    seconds = (qkv_second, out_second, up_second, down_second, norm_second)
    averages = (qkv_average, out_average, up_average, down_average, norm_average)
    results = [
        adamw_moment_update(
            weights[slot], gradients[slot], firsts[slot], seconds[slot], averages[slot], rates()[slot], factor
        )
        for slot in range(5)
    ]
    news, first_news, second_news, average_news = (tuple(item[n] for item in results) for n in range(4))
    copies = tuple(item.astype(jnp.bfloat16) for item in news[:4])
    return (block_out, input_grad, grad_norm) + news + first_news + second_news + average_news + copies + (factor * norm_grads[2:],)


def is_fast(mesh):
    sizes = dict(mesh.shape)
    return sizes["seq"] == 2 and sizes["head"] == 4 and sizes["dp"] == 4


def solution(mesh):
    return jax.shard_map(
        fast_body if is_fast(mesh) else body,
        mesh=mesh,
        in_specs=(
            P("dp", ("seq", "head"), None),
            P("dp", ("seq", "head"), None),
            P("head", "seq", None),
            P(),
            P(("dp", "seq"), "head"),
            P("head", ("dp", "seq")),
            P(("dp", "seq"), "head"),
            P("head", ("dp", "seq")),
            P(),
            P(("dp", "seq"), "head"),
            P("head", ("dp", "seq")),
            P(("dp", "seq"), "head"),
            P("head", ("dp", "seq")),
            P(),
            P(("dp", "seq"), "head"),
            P("head", ("dp", "seq")),
            P(("dp", "seq"), "head"),
            P("head", ("dp", "seq")),
            P(),
            P(("dp", "seq"), "head"),
            P("head", ("dp", "seq")),
            P(("dp", "seq"), "head"),
            P("head", ("dp", "seq")),
            P(),
        ),
        out_specs=(
            P("dp", ("seq", "head"), None),
            P("dp", ("seq", "head"), None),
            P(),
            P(("dp", "seq"), "head"),
            P("head", ("dp", "seq")),
            P(("dp", "seq"), "head"),
            P("head", ("dp", "seq")),
            P(),
            P(("dp", "seq"), "head"),
            P("head", ("dp", "seq")),
            P(("dp", "seq"), "head"),
            P("head", ("dp", "seq")),
            P(),
            P(("dp", "seq"), "head"),
            P("head", ("dp", "seq")),
            P(("dp", "seq"), "head"),
            P("head", ("dp", "seq")),
            P(),
            P(("dp", "seq"), "head"),
            P("head", ("dp", "seq")),
            P(("dp", "seq"), "head"),
            P("head", ("dp", "seq")),
            P(),
            P(("dp", "seq"), "head"),
            P("head", ("dp", "seq")),
            P(("dp", "seq"), "head"),
            P("head", ("dp", "seq")),
            P(),
        ),
        check_vma=False,
    )
```

```python
import jax
import jax.numpy as jnp
from jax import lax
from jax.experimental import pallas as pl
from jax.experimental.pallas import tpu as pltpu
from jax.sharding import PartitionSpec as P

D = 768
DH = 64
FF = 3072
BLOCK = 64
STEP = 10


EPSILON = 1e-05
BETA_ONE = 0.9
BETA_TWO = 0.999
DECAY = 0.01
SMALL = 1e-08
CLIP_NORM = 1.0
AVERAGING = 0.999
NEGATIVE = -1e30


def norm_rows(values, gain_row, shift_row):
    center = values - jnp.mean(values, -1, keepdims=True)
    spread = jnp.mean(center * center, -1, keepdims=True)
    return center * lax.rsqrt(spread + EPSILON) * gain_row + shift_row


def key_table(rand_local, global_blocks, first_block, blocks_total):
    head_count, local_blocks = (rand_local.shape[0], rand_local.shape[1])
    places = first_block + jnp.arange(local_blocks, dtype=jnp.int32)
    left_side = jnp.maximum(places - 1, 0)
    right_side = jnp.minimum(places + 1, blocks_total - 1)
    window = jnp.stack([left_side, places, right_side], -1)
    key_index = jnp.concatenate(
        [
            jnp.broadcast_to(window[None], (head_count, local_blocks, 3)),
            rand_local,
            jnp.broadcast_to(global_blocks[None, None], (head_count, local_blocks, 2)),
        ],
        -1,
    )
    column_one = jnp.ones((local_blocks, 1), jnp.float32)
    key_valid = jnp.concatenate(
        [
            (places > 0).astype(jnp.float32)[:, None],
            column_one,
            (places < blocks_total - 1).astype(jnp.float32)[:, None],
            jnp.ones((local_blocks, 5), jnp.float32),
        ],
        -1,
    )
    return (key_index, key_valid)


def gather_rows(values):
    return lax.all_gather(values, "head", axis=1, tiled=True)


def sum_rows(values):
    return lax.psum_scatter(values, "head", scatter_dimension=1, tiled=True)


def contract(left_operand, right_operand):
    return jnp.einsum(
        "enz,enf->zf", left_operand, right_operand, preferred_element_type=jnp.float32
    )


def to_heads(values, head_count):
    seq_count, token_count = (values.shape[0], values.shape[1])
    return jnp.moveaxis(
        values.reshape(seq_count, token_count // BLOCK, BLOCK, head_count, DH), 3, 0
    )


def from_heads(values):
    head_count, seq_count, blocks = (values.shape[0], values.shape[1], values.shape[2])
    return jnp.moveaxis(values, 0, 3).reshape(seq_count, blocks * BLOCK, head_count * DH)


def pick_keys(kv_all, key_index):
    seq_count, token_count = (kv_all.shape[0], kv_all.shape[1])
    head_count = key_index.shape[0]
    blocks = kv_all.reshape(seq_count, token_count // BLOCK, BLOCK, head_count, 2, DH)
    by_head = jnp.moveaxis(blocks, 3, 0)
    return jax.vmap(lambda source, chosen: source[:, chosen])(by_head, key_index)


def scores_of(queries, picked, key_valid):
    raw_scores = jnp.einsum(
        "hsnbe,hsnkce->hsnbkc", queries, picked[..., 0, :], preferred_element_type=jnp.float32
    ) * DH ** (-0.5)
    return jnp.where(key_valid[None, None, :, None, :, None] > 0, raw_scores, NEGATIVE)


def attend_forward(queries, picked, key_valid):
    raw_scores = scores_of(queries, picked, key_valid)
    score_shape = raw_scores.shape
    scores_flat = raw_scores.reshape(score_shape[:4] + (score_shape[4] * score_shape[5],))
    row_max = jnp.max(scores_flat, -1, keepdims=True)
    exponent = jnp.exp(scores_flat - row_max)
    row_total = jnp.sum(exponent, -1, keepdims=True)
    probabilities = (exponent / row_total).astype(jnp.bfloat16).reshape(score_shape)
    output = jnp.einsum(
        "hsnbkc,hsnkce->hsnbe", probabilities, picked[..., 1, :], preferred_element_type=jnp.float32
    )
    return (output, row_max + jnp.log(row_total))


def attend_backward(queries, picked, key_valid, log_total, grad_out):
    raw_scores = scores_of(queries, picked, key_valid)
    score_shape = raw_scores.shape
    scores_flat = raw_scores.reshape(score_shape[:4] + (score_shape[4] * score_shape[5],))
    probabilities = jnp.exp(scores_flat - log_total)
    grad_probs = jnp.einsum(
        "hsnbe,hsnkce->hsnbkc", grad_out, picked[..., 1, :], preferred_element_type=jnp.float32
    ).reshape(scores_flat.shape)
    row_delta = jnp.sum(probabilities * grad_probs, -1, keepdims=True)
    grad_scores = probabilities * (grad_probs - row_delta)
    grad_scores = grad_scores.astype(jnp.bfloat16).reshape(score_shape)
    low_probs = probabilities.astype(jnp.bfloat16).reshape(score_shape)
    grad_query = jnp.einsum(
        "hsnbkc,hsnkce->hsnbe", grad_scores, picked[..., 0, :], preferred_element_type=jnp.float32
    ) * DH ** (-0.5)
    grad_keys = jnp.einsum(
        "hsnbkc,hsnbe->hsnkce", grad_scores, queries, preferred_element_type=jnp.float32
    ) * DH ** (-0.5)
    grad_values = jnp.einsum(
        "hsnbkc,hsnbe->hsnkce", low_probs, grad_out, preferred_element_type=jnp.float32
    )
    return (grad_query, jnp.stack([grad_keys, grad_values], -2), row_delta)


def spread_back(grad_pairs, key_index, seq_count, blocks_total):
    head_count = key_index.shape[0]
    zero_grid = jnp.zeros((head_count, seq_count, blocks_total, BLOCK, 2, DH), jnp.float32)
    filled = jax.vmap(lambda source, chosen, addend: source.at[:, chosen].add(addend))(
        zero_grid, key_index, grad_pairs
    )
    return jnp.moveaxis(filled, 0, 3).reshape(seq_count, blocks_total * BLOCK, head_count * 2 * DH)


def rates():
    return (
        1.5 * D ** (-0.5),
        1.5 * max(1, D // (8 * BLOCK)) ** (-0.5),
        1.5 * D ** (-0.5),
        1.5 * FF ** (-0.5),
        0.5,
    )


def adamw_moment_update(weight, gradient, moment_one, moment_two, average, rate, factor):
    decay_mean = min(AVERAGING, (1.0 + STEP) / (10.0 + STEP))
    clipped = gradient * factor
    first_new = BETA_ONE * moment_one + (1.0 - BETA_ONE) * clipped
    second_new = BETA_TWO * moment_two + (1.0 - BETA_TWO) * clipped * clipped
    update = (
        first_new / (1.0 - BETA_ONE**STEP) / (jnp.sqrt(second_new / (1.0 - BETA_TWO**STEP)) + SMALL)
    )
    weight_new = weight - rate * (update + DECAY * weight)
    average_new = decay_mean * average + (1.0 - decay_mean) * weight_new
    return (weight_new, first_new, second_new, average_new)


def body(
    tokens,
    cotangent,
    rand_blocks,
    global_blocks,
    qkv_weight,
    out_weight,
    up_weight,
    down_weight,
    norm_params,
    qkv_first,
    out_first,
    up_first,
    down_first,
    norm_first,
    qkv_second,
    out_second,
    up_second,
    down_second,
    norm_second,
    qkv_average,
    out_average,
    up_average,
    down_average,
    norm_average,
):
    qkv_low, out_low, up_low, down_low = (
        lax.all_gather(qkv_weight.astype(jnp.bfloat16), ("dp", "seq"), axis=0, tiled=True),
        lax.all_gather(out_weight.astype(jnp.bfloat16), ("dp", "seq"), axis=1, tiled=True),
        lax.all_gather(up_weight.astype(jnp.bfloat16), ("dp", "seq"), axis=0, tiled=True),
        lax.all_gather(down_weight.astype(jnp.bfloat16), ("dp", "seq"), axis=1, tiled=True),
    )
    seq_count = tokens.shape[0]
    head_count = rand_blocks.shape[0]
    local_blocks = rand_blocks.shape[1]
    blocks_total = local_blocks * lax.axis_size("seq")
    first_block = lax.axis_index("seq") * local_blocks
    key_index, key_valid = key_table(rand_blocks, global_blocks, first_block, blocks_total)
    inputs = tokens.astype(jnp.float32)
    full_one = gather_rows(norm_rows(inputs, norm_params[0], norm_params[1]).astype(jnp.bfloat16))
    token_count = full_one.shape[1]
    qkv_all = jnp.dot(full_one, qkv_low, preferred_element_type=jnp.float32).astype(jnp.bfloat16)
    qkv_parts = qkv_all.reshape(seq_count, token_count, head_count, 3, DH)
    kv_local = qkv_parts[:, :, :, 1:, :].reshape(seq_count, token_count, head_count * 2 * DH)
    kv_all = lax.all_gather(kv_local, "seq", axis=1, tiled=True)
    picked = pick_keys(kv_all, key_index)
    queries = to_heads(qkv_parts[:, :, :, 0, :], head_count)
    attended, log_total = attend_forward(queries, picked, key_valid)
    mixed_heads = from_heads(attended.astype(jnp.bfloat16))
    residual = inputs + sum_rows(jnp.dot(mixed_heads, out_low, preferred_element_type=jnp.float32))
    full_two = gather_rows(norm_rows(residual, norm_params[2], norm_params[3]).astype(jnp.bfloat16))
    upward = jnp.dot(full_two, up_low, preferred_element_type=jnp.float32)
    active = jax.nn.gelu(upward).astype(jnp.bfloat16)
    result = residual + sum_rows(jnp.dot(active, down_low, preferred_element_type=jnp.float32))
    block_out = result.astype(jnp.bfloat16)
    grad_top = gather_rows(cotangent)
    grad_down = contract(active, grad_top)
    grad_active = jnp.dot(grad_top, down_low.T, preferred_element_type=jnp.float32)
    _, gelu_back = jax.vjp(jax.nn.gelu, upward)
    grad_upward = gelu_back(grad_active)[0].astype(jnp.bfloat16)
    grad_up = contract(full_two, grad_upward)
    part_two = sum_rows(jnp.dot(grad_upward, up_low.T, preferred_element_type=jnp.float32))
    _, norm_back_two = jax.vjp(norm_rows, residual, norm_params[2], norm_params[3])
    grad_residual_norm, grad_gain_two, grad_shift_two = norm_back_two(part_two)
    grad_residual = cotangent.astype(jnp.float32) + grad_residual_norm
    grad_middle = gather_rows(grad_residual.astype(jnp.bfloat16))
    grad_out = contract(mixed_heads, grad_middle)
    grad_mixed = jnp.dot(grad_middle, out_low.T, preferred_element_type=jnp.float32).astype(
        jnp.bfloat16
    )
    grad_query, grad_pairs, row_delta = attend_backward(
        queries, picked, key_valid, log_total, to_heads(grad_mixed, head_count)
    )
    grad_kv_full = spread_back(grad_pairs, key_index, seq_count, blocks_total)
    grad_kv = lax.psum_scatter(
        grad_kv_full.astype(jnp.bfloat16), "seq", scatter_dimension=1, tiled=True
    ).astype(jnp.float32)
    query_gradient = from_heads(grad_query).reshape(seq_count, token_count, head_count, 1, DH)
    grad_qkv_rows = jnp.concatenate(
        [query_gradient, grad_kv.reshape(seq_count, token_count, head_count, 2, DH)], 3
    )
    grad_qkv_rows = grad_qkv_rows.reshape(seq_count, token_count, head_count * 3 * DH).astype(
        jnp.bfloat16
    )
    grad_qkv = contract(full_one, grad_qkv_rows)
    part_one = sum_rows(jnp.dot(grad_qkv_rows, qkv_low.T, preferred_element_type=jnp.float32))
    _, norm_back_one = jax.vjp(norm_rows, inputs, norm_params[0], norm_params[1])
    grad_input_norm, grad_gain_one, grad_shift_one = norm_back_one(part_one)
    input_grad = (grad_residual + grad_input_norm).astype(jnp.bfloat16)
    grad_norm_local = jnp.stack([grad_gain_one, grad_shift_one, grad_gain_two, grad_shift_two])
    reduced_total = (
        lax.psum_scatter(grad_qkv, ("dp", "seq"), scatter_dimension=0, tiled=True),
        lax.psum_scatter(grad_out, ("dp", "seq"), scatter_dimension=1, tiled=True),
        lax.psum_scatter(grad_up, ("dp", "seq"), scatter_dimension=0, tiled=True),
        lax.psum_scatter(grad_down, ("dp", "seq"), scatter_dimension=1, tiled=True),
    )
    squares = sum((jnp.sum(item * item) for item in reduced_total))
    norm_grads = lax.psum(grad_norm_local, ("dp", "seq", "head"))
    matrix_squares = lax.psum(squares, ("dp", "seq", "head"))
    grad_norm = jnp.sqrt(matrix_squares + jnp.sum(norm_grads * norm_grads))
    factor = jnp.minimum(1.0, CLIP_NORM / (grad_norm + 1e-06))
    weights = (qkv_weight, out_weight, up_weight, down_weight, norm_params)
    gradients = (reduced_total[0], reduced_total[1], reduced_total[2], reduced_total[3], norm_grads)
    firsts = (qkv_first, out_first, up_first, down_first, norm_first)
    seconds = (qkv_second, out_second, up_second, down_second, norm_second)
    averages = (qkv_average, out_average, up_average, down_average, norm_average)
    results = [
        adamw_moment_update(
            weights[slot],
            gradients[slot],
            firsts[slot],
            seconds[slot],
            averages[slot],
            rates()[slot],
            factor,
        )
        for slot in range(5)
    ]
    news = tuple((item[0] for item in results))
    first_news = tuple((item[1] for item in results))
    second_news = tuple((item[2] for item in results))
    average_news = tuple((item[3] for item in results))
    return (
        block_out,
        input_grad,
        grad_norm,
        news[0],
        news[1],
        news[2],
        news[3],
        news[4],
        first_news[0],
        first_news[1],
        first_news[2],
        first_news[3],
        first_news[4],
        second_news[0],
        second_news[1],
        second_news[2],
        second_news[3],
        second_news[4],
        average_news[0],
        average_news[1],
        average_news[2],
        average_news[3],
        average_news[4],
        news[0].astype(jnp.bfloat16),
        news[1].astype(jnp.bfloat16),
        news[2].astype(jnp.bfloat16),
        news[3].astype(jnp.bfloat16),
        factor * norm_grads[2:],
    )


GROUP = ("seq", "head")
EVERY = ("dp", "seq", "head")
FULL = 4096
CHUNK = 512
MB = 1024 * 1024


def limits(megabytes):
    return pltpu.CompilerParams(vmem_limit_bytes=megabytes * MB)


def swap(values, distance):
    return lax.ppermute(values, GROUP, [(i, i ^ distance) for i in range(8)])


def swap_every(values, distance, count):
    return lax.ppermute(values, EVERY, [(i, i ^ distance) for i in range(count)])


def nt(left, right):
    return lax.dot_general(left, right, (((1,), (1,)), ((), ())), preferred_element_type=jnp.float32)


def nn(left, right):
    return lax.dot_general(left, right, (((1,), (0,)), ((), ())), preferred_element_type=jnp.float32)


def tn(left, right):
    return lax.dot_general(left, right, (((0,), (0,)), ((), ())), preferred_element_type=jnp.float32)


def lane_low(shape):
    return lax.broadcasted_iota(jnp.int32, shape, len(shape) - 1) < 64


def roll64(values):
    return pltpu.roll(values, 64, 1)


def block_places(tab_ref, k, block):
    me = tab_ref[0]
    part = (block // 32) ^ (me // 4)
    base = 8 + ((part * 3 + k) * 32 + block % 32) * 3
    chosen = [
        jnp.maximum(block - 1, 0),
        block,
        jnp.minimum(block + 1, 63),
        tab_ref[base],
        tab_ref[base + 1],
        tab_ref[base + 2],
        tab_ref[1],
        tab_ref[2],
    ]
    return [pl.multiple_of((((b // 8) ^ me) * 8 + b % 8) * 64, 64) for b in chosen]


def spread_heads(wide):
    tile = lambda j: wide[:, j * 128 : j * 128 + 128]
    low = lane_low((wide.shape[0], 128))
    scale = DH ** (-0.5)
    return [
        jnp.where(low, tile(0) * scale, 0.0),
        jnp.where(low, roll64(tile(0)), roll64(tile(1))),
        jnp.where(low, roll64(tile(1)) * scale, 0.0),
        tile(2),
        jnp.where(low, tile(3) * scale, 0.0),
        jnp.where(low, roll64(tile(3)), roll64(tile(4))),
    ]


def qkv_kernel(*refs):
    tok_refs, weight_ref, out_ref = refs[:8], refs[8], refs[9]
    for slot, tok_ref in enumerate(tok_refs):
        for n, part in enumerate(spread_heads(nn(tok_ref[...], weight_ref[...]))):
            out_ref[slot * CHUNK : slot * CHUNK + CHUNK, n * 128 : n * 128 + 128] = part.astype(jnp.bfloat16)


def project(slots, weights):
    return pl.pallas_call(
        qkv_kernel,
        grid=(1,),
        in_specs=[pl.BlockSpec((CHUNK, D), lambda i: (0, 0))] * 8 + [pl.BlockSpec((D, 640), lambda i: (0, 0))],
        out_specs=pl.BlockSpec((FULL, D), lambda i: (0, 0)),
        out_shape=jax.ShapeDtypeStruct((FULL, D), jnp.bfloat16),
        compiler_params=limits(40),
        name="project",
        cost_estimate=pl.CostEstimate(flops=4 * 10**9, bytes_accessed=13 * MB, transcendentals=0),
    )(*slots, weights)


def hide(scores, low, high):
    lane = lax.broadcasted_iota(jnp.int32, scores.shape, 1)
    return jnp.where((lane >= low) & (lane < high), NEGATIVE, scores)


def softmax_rows(scores, part, q):
    if q == 0:
        scores = jnp.where(part == 0, hide(scores, 0, 64), scores)
    if q == 7:
        scores = jnp.where(part == 7, hide(scores, 128, 192), scores)
    top = jnp.max(scores, -1, keepdims=True)
    exponent = jnp.exp(scores - top)
    total = jnp.sum(exponent, -1, keepdims=True)
    return exponent * (1.0 / total)


def attend_kernel(k, tab_ref, qkv_ref, out_ref):
    me = tab_ref[0]

    def step(slot, carry):
        part = slot ^ me
        keys, scores = [], []
        for q in range(8):
            places = block_places(tab_ref, k, part * 8 + q)
            keys.append(jnp.concatenate([qkv_ref[pl.ds(p, 64), 128:256] for p in places], 0))
            at = pl.multiple_of(slot * CHUNK + q * 64, 64)
            scores.append(nt(qkv_ref[pl.ds(at, 64), 0:128], keys[q]))
        probs = [softmax_rows(scores[q], part, q).astype(jnp.bfloat16) for q in range(8)]
        outs = [nn(probs[q], keys[q]) for q in range(8)]
        for q in range(4):
            both = jnp.where(lane_low(outs[q].shape), roll64(outs[q]), outs[q + 4])
            out_ref[part, q * 64 : q * 64 + 64, :] = both.astype(jnp.bfloat16)
        return carry

    lax.fori_loop(0, 8, step, 0)


def attend(heads, table, qkv):
    first, count = heads[0], len(heads)

    def kernel(tab_ref, qkv_ref, out_ref):
        attend_kernel(pl.program_id(0) + first, tab_ref, qkv_ref, out_ref)

    return pl.pallas_call(
        kernel,
        grid_spec=pltpu.PrefetchScalarGridSpec(
            num_scalar_prefetch=1,
            grid=(count,),
            in_specs=[pl.BlockSpec((FULL, 256), lambda i, t: (0, first + i))],
            out_specs=pl.BlockSpec((8, 256, 128), lambda i, t: (0, i, 0)),
        ),
        out_shape=jax.ShapeDtypeStruct((8, 256 * count, 128), jnp.bfloat16),
        compiler_params=limits(60),
        name="attend",
        cost_estimate=pl.CostEstimate(flops=4 * 10**9 * count, bytes_accessed=30 * MB * count, transcendentals=2 * 10**6),
    )(table, qkv)


def attend_back_kernel(k, tab_ref, qkv_ref, grad_ref, full_ref, pack_ref, acc_ref, shared_ref):
    me = tab_ref[0]
    acc_ref[...] = jnp.zeros_like(acc_ref)
    shared_ref[...] = jnp.zeros_like(shared_ref)

    def step(n, carry):
        slot, half = n // 2, n % 2
        part = slot ^ me
        picks = (0, 1, 4, 5)
        places, stacks, keys, both = [], [], [], []
        tiles = []
        for j in range(2):
            tile = grad_ref[part, pl.ds(pl.multiple_of(half * 128 + j * 64, 64), 64), :].astype(jnp.float32)
            low_lanes = lane_low(tile.shape)
            tiles.append(jnp.where(low_lanes, 0.0, roll64(tile)).astype(jnp.bfloat16))
            tiles.append(jnp.where(low_lanes, 0.0, tile).astype(jnp.bfloat16))
        grads = (tiles[0], tiles[2], tiles[1], tiles[3])
        for j, base in enumerate(picks):
            q = base + 2 * half
            places.append(block_places(tab_ref, k, part * 8 + q))
            keys.append(jnp.concatenate([qkv_ref[pl.ds(p, 64), 128:256] for p in places[j]], 0))
            at = pl.multiple_of(slot * CHUNK + q * 64, 64)
            stacks.append(jnp.concatenate([qkv_ref[pl.ds(at, 64), 0:128], grads[j]], 0))
            both.append(nt(stacks[j], keys[j]))
        lows, pairs = [], []
        for j in range(4):
            scores, grad_probs = both[j][:64], both[j][64:]
            if picks[j] == 0:
                scores = jnp.where((part == 0) & (half == 0), hide(scores, 0, 64), scores)
            if picks[j] == 5:
                scores = jnp.where((part == 7) & (half == 1), hide(scores, 128, 192), scores)
            probs = softmax_rows(scores, part, 1)
            delta = jnp.sum(probs * grad_probs, -1, keepdims=True)
            lows.append((probs * (grad_probs - delta)).astype(jnp.bfloat16))
            pairs.append(jnp.concatenate([lows[j], probs.astype(jnp.bfloat16)], 0))
        queries = []
        for j in range(4):
            grad_query = nn(lows[j], keys[j]) * DH ** (-0.5)
            queries.append(jnp.where(lane_low(grad_query.shape), grad_query, 0.0))
            at = pl.multiple_of(slot * CHUNK + (picks[j] + 2 * half) * 64, 64)
            full_ref[pl.ds(at, 64), 0:128] = queries[j].astype(jnp.bfloat16)
        spreads = [tn(pairs[j], stacks[j]) for j in range(4)]
        for j in range(4):
            for m in range(6):
                acc_ref[pl.ds(places[j][m], 64), :] += spreads[j][m * 64 : m * 64 + 64]
        shared_ref[...] += (spreads[0][384:] + spreads[1][384:]) + (spreads[2][384:] + spreads[3][384:])
        for j in range(2):
            packed = queries[j] + roll64(queries[j + 2])
            pack_ref[part, pl.ds(pl.multiple_of(half * 128 + j * 64, 64), 64), :] = packed.astype(jnp.bfloat16)
        return carry

    lax.fori_loop(0, 16, step, 0)
    for m in range(2):
        block = tab_ref[1 + m]
        at = pl.multiple_of((((block // 8) ^ me) * 8 + block % 8) * 64, 64)
        acc_ref[pl.ds(at, 64), :] += shared_ref[m * 64 : m * 64 + 64]

    def finish(slot, carry):
        at = pl.ds(pl.multiple_of(slot * CHUNK, CHUNK), CHUNK)
        low = acc_ref[at, :].astype(jnp.bfloat16)
        full_ref[at, 128:256] = low
        pack_ref[slot ^ me, 256:768, :] = low
        return carry

    lax.fori_loop(0, 8, finish, 0)


def attend_back(k, table, qkv, grad, row):
    return pl.pallas_call(
        lambda *refs: attend_back_kernel(k, *refs),
        grid_spec=pltpu.PrefetchScalarGridSpec(
            num_scalar_prefetch=1,
            grid=(1,),
            in_specs=[
                pl.BlockSpec((FULL, 256), lambda i, t: (0, k)),
                pl.BlockSpec((8, 256, 128), lambda i, t: (0, row, 0)),
            ],
            out_specs=[
                pl.BlockSpec((FULL, 256), lambda i, t: (0, 0)),
                pl.BlockSpec((8, 768, 128), lambda i, t: (0, 0, 0)),
            ],
            scratch_shapes=[pltpu.VMEM((FULL, 128), jnp.float32), pltpu.VMEM((128, 128), jnp.float32)],
        ),
        out_shape=[
            jax.ShapeDtypeStruct((FULL, 256), jnp.bfloat16),
            jax.ShapeDtypeStruct((8, 768, 128), jnp.bfloat16),
        ],
        compiler_params=limits(60),
        name="attend_back",
        cost_estimate=pl.CostEstimate(flops=10 * 10**9, bytes_accessed=60 * MB, transcendentals=2 * 10**6),
    )(table, qkv, grad)


def norm_stats(values):
    center = values - jnp.mean(values, -1, keepdims=True)
    spread = jnp.mean(center * center, -1, keepdims=True)
    scale = lax.rsqrt(spread + EPSILON)
    return center * scale, scale


def halves(first, second):
    low = lane_low(first.shape)
    upper = jnp.where(low, first, roll64(second))
    lower = jnp.where(low, roll64(first), second)
    return upper, lower


def mid_kernel(o0_ref, o1_ref, o2_ref, w_ref, tok_ref, par_ref, cat_ref, mid_ref, a2_ref, a2t_ref):
    middle = tok_ref[0].astype(jnp.float32)
    cat_ref[...] = jnp.zeros_like(cat_ref)
    for h in range(4):
        tiles = [ref[h, at : at + 256].astype(jnp.float32) for ref, at in ((o0_ref, 0), (o1_ref, 256), (o2_ref, 0))]
        upper, lower = halves(tiles[0], tiles[1])
        last_upper, last_lower = halves(tiles[2], jnp.zeros_like(tiles[2]))
        cat_ref[0:256, h * 256 : h * 256 + 128] = upper.astype(jnp.bfloat16)
        cat_ref[256:512, h * 256 : h * 256 + 128] = lower.astype(jnp.bfloat16)
        cat_ref[0:256, h * 256 + 128 : h * 256 + 256] = last_upper.astype(jnp.bfloat16)
        cat_ref[256:512, h * 256 + 128 : h * 256 + 256] = last_lower.astype(jnp.bfloat16)
        middle = middle + nt(cat_ref[:, h * 256 : h * 256 + 256], w_ref[h])
    mid_ref[0] = middle
    normed, _ = norm_stats(middle)
    low = normed * par_ref[2:3, :] + par_ref[3:4, :]
    a2_ref[...] = low.astype(jnp.bfloat16)
    a2t_ref[...] = low.T.astype(jnp.bfloat16)


def out_weight_spec():
    return pl.BlockSpec((4, D, 256), lambda s: (0, 0, 0))


def middle(o_pair, o_last, weights, tokens, params):
    seqs = tokens.shape[0]
    rows = pl.BlockSpec((1, CHUNK, D), lambda s: (s, 0, 0))
    return pl.pallas_call(
        mid_kernel,
        grid=(seqs,),
        in_specs=[
            pl.BlockSpec((4, 512, 128), lambda s: (s, 0, 0)),
            pl.BlockSpec((4, 512, 128), lambda s: (s, 0, 0)),
            pl.BlockSpec((4, 256, 128), lambda s: (s, 0, 0)),
            out_weight_spec(), rows, pl.BlockSpec((4, D), lambda s: (0, 0)),
        ],
        out_specs=[
            pl.BlockSpec((CHUNK, 1024), lambda s: (s, 0)), rows,
            pl.BlockSpec((CHUNK, D), lambda s: (s, 0)), pl.BlockSpec((D, CHUNK), lambda s: (0, s)),
        ],
        out_shape=[
            jax.ShapeDtypeStruct((seqs * CHUNK, 1024), jnp.bfloat16),
            jax.ShapeDtypeStruct(tokens.shape, jnp.float32),
            jax.ShapeDtypeStruct((seqs * CHUNK, D), jnp.bfloat16),
            jax.ShapeDtypeStruct((D, seqs * CHUNK), jnp.bfloat16),
        ],
        compiler_params=limits(40),
        name="middle",
        cost_estimate=pl.CostEstimate(flops=2 * 10**9, bytes_accessed=12 * MB, transcendentals=0),
    )(o_pair, o_pair, o_last, weights, tokens, params)


HIDDEN = 384


def mlp_kernel(a2_ref, a2t_ref, dy_ref, dyt_ref, wu_ref, wd_ref, out_ref, back_ref, du_ref, dd_ref, g_ref, u_ref):
    @pl.when(pl.program_id(0) == 0)
    def _():
        out_ref[...] = jnp.zeros_like(out_ref)
        back_ref[...] = jnp.zeros_like(back_ref)

    wu, wd = wu_ref[0], wd_ref[0]
    rate, cubic = (2.0 / jnp.pi) ** 0.5, 0.044715
    rate = float(rate)
    for m in range(4):
        at = slice(m * 256, m * 256 + 256)
        up = nn(a2_ref[at, :], wu)
        grad = nn(dy_ref[at, :], wd)
        square = up * up
        bend = jnp.tanh(rate * up * (1.0 + cubic * square))
        half = 0.5 * (1.0 + bend)
        g_ref[at, :] = (up * half).astype(jnp.bfloat16)
        slope = half + 0.5 * up * (1.0 - bend * bend) * (rate * (1.0 + 3.0 * cubic * square))
        u_ref[at, :] = (grad * slope).astype(jnp.bfloat16)
        out_ref[at, :] += nt(g_ref[at, :], wd)
        back_ref[at, :] += nt(u_ref[at, :], wu)
    du_ref[0] = nn(a2t_ref[...], u_ref[...]).astype(du_ref.dtype)
    dd_ref[0] = nn(dyt_ref[...], g_ref[...]).astype(dd_ref.dtype)


def mlp(a2, a2t, dy, dyt, up_weight, down_weight):
    tokens = a2.shape[0]
    whole = lambda shape: pl.BlockSpec(shape, lambda i: (0, 0))
    per = D // HIDDEN
    grads = pl.BlockSpec((1, D, HIDDEN), lambda i: (i // per, 0, i % per))
    return pl.pallas_call(
        mlp_kernel,
        grid=(4 * per,),
        in_specs=[
            whole((tokens, D)), whole((D, tokens)), whole((tokens, D)), whole((D, tokens)),
            grads, grads,
        ],
        out_specs=[whole((tokens, D)), whole((tokens, D)), grads, grads],
        out_shape=[
            jax.ShapeDtypeStruct((tokens, D), jnp.float32),
            jax.ShapeDtypeStruct((tokens, D), jnp.float32),
            jax.ShapeDtypeStruct((4, D, D), jnp.bfloat16),
            jax.ShapeDtypeStruct((4, D, D), jnp.bfloat16),
        ],
        scratch_shapes=[pltpu.VMEM((tokens, HIDDEN), jnp.bfloat16), pltpu.VMEM((tokens, HIDDEN), jnp.bfloat16)],
        compiler_params=limits(32),
        name="mlp",
        cost_estimate=pl.CostEstimate(flops=29 * 10**9, bytes_accessed=40 * MB, transcendentals=2 * 10**6),
    )(a2, a2t, dy, dyt, up_weight, down_weight)


def norm_back(grad, values, gain):
    normed, scale = norm_stats(values)
    gain_grad = jnp.sum(grad * normed, 0, keepdims=True)
    shift_grad = jnp.sum(grad, 0, keepdims=True)
    inner = grad * gain
    across = jnp.mean(inner, -1, keepdims=True)
    along = jnp.mean(inner * normed, -1, keepdims=True)
    return scale * (inner - across - normed * along), gain_grad, shift_grad


def mid_back_kernel(b_ref, mid_ref, dy_ref, w_ref, par_ref, grad_ref, low_ref, g0_ref, g1_ref, norm_ref):
    grad, gain_grad, shift_grad = norm_back(b_ref[...], mid_ref[0], par_ref[2:3, :])
    total = dy_ref[0].astype(jnp.float32) + grad
    grad_ref[0] = total
    low = total.astype(jnp.bfloat16)
    low_ref[...] = low
    for h in range(4):
        mixed = nn(low, w_ref[h])
        first, second = halves(mixed[0:256, 0:128], mixed[256:512, 0:128])
        third, _ = halves(mixed[0:256, 128:256], mixed[256:512, 128:256])
        g0_ref[h] = first.astype(jnp.bfloat16)
        g1_ref[h, 0:256] = second.astype(jnp.bfloat16)
        g1_ref[h, 256:512] = third.astype(jnp.bfloat16)

    @pl.when(pl.program_id(0) == 0)
    def _():
        norm_ref[...] = jnp.zeros_like(norm_ref)

    norm_ref[0:1, :] += gain_grad
    norm_ref[1:2, :] += shift_grad


def middle_back(back, mid, dy, weights, params):
    seqs = dy.shape[0]
    rows = pl.BlockSpec((1, CHUNK, D), lambda s: (s, 0, 0))
    flat = pl.BlockSpec((CHUNK, D), lambda s: (s, 0))
    return pl.pallas_call(
        mid_back_kernel,
        grid=(seqs,),
        in_specs=[flat, rows, rows, out_weight_spec(), pl.BlockSpec((4, D), lambda s: (0, 0))],
        out_specs=[
            rows, flat, pl.BlockSpec((4, 256, 128), lambda s: (s, 0, 0)),
            pl.BlockSpec((4, 512, 128), lambda s: (s, 0, 0)), pl.BlockSpec((8, D), lambda s: (0, 0)),
        ],
        out_shape=[
            jax.ShapeDtypeStruct(dy.shape, jnp.float32),
            jax.ShapeDtypeStruct((seqs * CHUNK, D), jnp.bfloat16),
            jax.ShapeDtypeStruct((8, 256, 128), jnp.bfloat16),
            jax.ShapeDtypeStruct((8, 512, 128), jnp.bfloat16),
            jax.ShapeDtypeStruct((8, D), jnp.float32),
        ],
        compiler_params=limits(40),
        name="middle_back",
        cost_estimate=pl.CostEstimate(flops=2 * 10**9, bytes_accessed=16 * MB, transcendentals=0),
    )(back, mid, dy, weights, params)


def out_grad_kernel(low_ref, cat_ref, out_ref):
    for h in range(4):
        out_ref[h] = tn(low_ref[...], cat_ref[:, h * 256 : h * 256 + 256]).astype(jnp.bfloat16)


def out_weight_grad(low, cat):
    return pl.pallas_call(
        out_grad_kernel,
        out_shape=jax.ShapeDtypeStruct((4, D, 256), jnp.bfloat16),
        compiler_params=limits(24),
        name="out_weight_grad",
        cost_estimate=pl.CostEstimate(flops=16 * 10**8, bytes_accessed=5 * MB, transcendentals=0),
    )(low, cat)


def merge_heads(queries, pairs):
    low = lane_low(queries[0].shape)
    return [
        jnp.where(low, queries[0], roll64(pairs[0])),
        jnp.where(low, roll64(pairs[0]), roll64(queries[1])),
        pairs[1],
        jnp.where(low, queries[2], roll64(pairs[2])),
        jnp.where(low, roll64(pairs[2]), 0.0),
    ]


def qkv_grad_kernel(*refs):
    tok_refs, full_refs, out_ref, acc_ref = refs[:8], refs[8:11], refs[11], refs[12]
    for slot, tok_ref in enumerate(tok_refs):
        at = slice(slot * CHUNK, slot * CHUNK + CHUNK)
        part = tn(tok_ref[...], jnp.concatenate([ref[at, :] for ref in full_refs], 1))
        acc_ref[...] = part if slot == 0 else acc_ref[...] + part
    tiles = merge_heads(
        [acc_ref[:, k * 256 : k * 256 + 128] for k in range(3)],
        [acc_ref[:, k * 256 + 128 : k * 256 + 256] for k in range(3)],
    )
    for j, tile in enumerate(tiles):
        out_ref[:, j * 128 : j * 128 + 128] = tile.astype(jnp.bfloat16)


def qkv_weight_grad(slots, fulls):
    return pl.pallas_call(
        qkv_grad_kernel,
        out_shape=jax.ShapeDtypeStruct((D, 640), jnp.bfloat16),
        scratch_shapes=[pltpu.VMEM((D, D), jnp.float32)],
        compiler_params=limits(40),
        name="qkv_weight_grad",
        cost_estimate=pl.CostEstimate(flops=5 * 10**9, bytes_accessed=14 * MB, transcendentals=0),
    )(*slots, *fulls)


def last_kernel(p0_ref, p1_ref, p2_ref, w_ref, tok_ref, mid_ref, par_ref, out_ref, norm_ref):
    grad = None
    for h in range(4):
        queries, pairs = [], []
        for ref in (p0_ref, p1_ref, p2_ref):
            both = ref[h, 0:256, :].astype(jnp.float32)
            queries.append(jnp.concatenate([both, roll64(both)], 0))
            pairs.append(ref[h, 256:768, :].astype(jnp.float32))
        wide = jnp.concatenate([tile.astype(jnp.bfloat16) for tile in merge_heads(queries, pairs)], 1)
        part = nt(wide, w_ref[h])
        grad = part if grad is None else grad + part
    back, gain_grad, shift_grad = norm_back(grad, tok_ref[0].astype(jnp.float32), par_ref[0:1, :])
    out_ref[0] = (mid_ref[0] + back).astype(jnp.bfloat16)

    @pl.when(pl.program_id(0) == 0)
    def _():
        norm_ref[...] = jnp.zeros_like(norm_ref)

    norm_ref[0:1, :] += gain_grad
    norm_ref[1:2, :] += shift_grad


def last(packs, weights, tokens, mid_grad, params):
    seqs = tokens.shape[0]
    piece = pl.BlockSpec((4, 768, 128), lambda s: (s, 0, 0))
    rows = pl.BlockSpec((1, CHUNK, D), lambda s: (s, 0, 0))
    return pl.pallas_call(
        last_kernel,
        grid=(seqs,),
        in_specs=[piece, piece, piece, pl.BlockSpec((4, D, 640), lambda s: (0, 0, 0)), rows, rows,
                  pl.BlockSpec((4, D), lambda s: (0, 0))],
        out_specs=[rows, pl.BlockSpec((8, D), lambda s: (0, 0))],
        out_shape=[jax.ShapeDtypeStruct(tokens.shape, jnp.bfloat16), jax.ShapeDtypeStruct((8, D), jnp.float32)],
        compiler_params=limits(40),
        name="last",
        cost_estimate=pl.CostEstimate(flops=4 * 10**9, bytes_accessed=14 * MB, transcendentals=0),
    )(*packs, weights, tokens, mid_grad, params)


def step_kernel(factor_ref, *refs):
    factor = factor_ref[0]
    for slot in range(4):
        weight, gradient, first, second, average = (ref[...] for ref in refs[slot * 5 : slot * 5 + 5])
        outs = refs[20 + slot * 5 : 25 + slot * 5]
        new, first, second, average = adamw_moment_update(
            weight, gradient, first, second, average, rates()[slot], factor
        )
        for ref, value in zip(outs, (new, first, second, average, new.astype(jnp.bfloat16))):
            ref[...] = value


def matrix_steps(factor, groups):
    shapes = [
        jax.ShapeDtypeStruct(group[0].shape, kind)
        for group in groups
        for kind in (jnp.float32,) * 4 + (jnp.bfloat16,)
    ]
    outs = pl.pallas_call(
        step_kernel,
        in_specs=[pl.BlockSpec(memory_space=pltpu.SMEM)] + [pl.BlockSpec(memory_space=pltpu.VMEM)] * 20,
        out_shape=shapes,
        compiler_params=limits(32),
        name="matrix_steps",
        cost_estimate=pl.CostEstimate(flops=5 * 10**6, bytes_accessed=10 * MB, transcendentals=10**5),
    )(factor, *(item for group in groups for item in group))
    return [outs[n * 5 : n * 5 + 5] for n in range(4)]


def pick(values, index, size, axis):
    return lax.dynamic_slice_in_dim(values, index * size, size, axis)


def gather_mine(shard):
    return lax.all_gather(shard, ("dp", "seq"), axis=0, tiled=True)


def gather_heads(mine):
    return lax.all_gather(mine, "head", axis=0)


def scatter_all(terms):
    mine = lax.psum_scatter(terms, "head", scatter_dimension=0)
    return lax.psum_scatter(mine, ("dp", "seq"), scatter_dimension=0, tiled=True).astype(jnp.float32)


def fast_body(
    tokens, cotangent, rand_blocks, global_blocks, qkv_weight, out_weight, up_weight, down_weight, norm_params,
    qkv_first, out_first, up_first, down_first, norm_first,
    qkv_second, out_second, up_second, down_second, norm_second,
    qkv_average, out_average, up_average, down_average, norm_average,
):
    dp_size = lax.axis_size("dp")
    count = dp_size * 8
    y, head = lax.axis_index("seq"), lax.axis_index("head")
    me = y * 4 + head

    turned = jnp.stack([pick(tokens, y, 1, 0)[0], pick(tokens, 1 - y, 1, 0)[0]])
    normed = norm_rows(turned.astype(jnp.float32), norm_params[0], norm_params[1]).astype(jnp.bfloat16)
    mine, theirs = normed[0], normed[1]
    even = [mine, swap(mine, 2), swap(theirs, 4), swap(theirs, 6)]
    odd = [swap(item, 1) for item in even]
    slots = [item for pair in zip(even, odd) for item in pair]

    low_qkv = qkv_weight.astype(jnp.bfloat16)
    blank = jnp.zeros((96, 64), jnp.bfloat16)
    low_out = out_weight.T.astype(jnp.bfloat16)
    mine_first = gather_mine(jnp.concatenate([low_qkv, blank, low_out, blank], -1))
    mine_up = gather_mine(up_weight.astype(jnp.bfloat16))
    mine_down = gather_mine(down_weight.T.astype(jnp.bfloat16))
    all_first, all_up, all_down = gather_heads(mine_first), gather_heads(mine_up), gather_heads(mine_down)
    all_out = all_first[:, :, 640:]

    both_rand = jnp.concatenate([rand_blocks.reshape(-1), swap(rand_blocks.reshape(-1), 4)])
    table = jnp.concatenate(
        [jnp.reshape(me, (1,)), global_blocks, jnp.zeros((5,), jnp.int32), both_rand]
    ).astype(jnp.int32)
    qkv = project(slots, mine_first)

    def across(values, axes=GROUP):
        return lax.all_to_all(values, axes, 0, 0, tiled=True)

    o_pair = across(attend((0, 1), table, qkv))
    o_last = across(attend((2,), table, qkv))
    mixed, mid, a2, a2t = middle(o_pair, o_last, all_out, tokens, norm_params)

    dy = cotangent.reshape(a2.shape)
    out_full, back, up_terms, down_terms = mlp(a2, a2t, dy, dy.T, all_up, all_down)
    up_grad, down_grad = scatter_all(up_terms), scatter_all(down_terms)
    block_out = (mid + out_full.reshape(mid.shape)).astype(jnp.bfloat16)

    mid_grad, low_grad, grad_first, grad_rest, norm_two = middle_back(back, mid, cotangent, all_out, norm_params)
    grad_first, grad_rest = across(grad_first), across(grad_rest)
    out_grad = scatter_all(out_weight_grad(low_grad, mixed))[:, 0:192]

    fulls, packs = [], []
    for k, (grad, row) in enumerate(((grad_first, 0), (grad_rest, 0), (grad_rest, 1))):
        full, pack = attend_back(k, table, qkv, grad, row)
        fulls.append(full)
        packs.append(across(pack))
    shares = across(qkv_weight_grad(slots, fulls).reshape(dp_size * 2, 96, 640), ("dp", "seq"))
    qkv_grad = jnp.sum(shares.astype(jnp.float32), 0)[:, 0:576]
    input_grad, norm_one = last(packs, all_first, tokens, mid_grad, norm_params)

    reduced = (qkv_grad, out_grad.T, up_grad, down_grad)
    squares = sum((jnp.sum(item * item) for item in reduced))
    shared = jnp.concatenate(
        [norm_one[0:2], norm_two[0:2], jnp.full((1, D), squares), jnp.zeros((3, D), jnp.float32)], 0
    )
    distance = 1
    while distance < count:
        shared = shared + swap_every(shared, distance, count)
        distance *= 2
    norm_grads = shared[0:4]
    grad_norm = jnp.sqrt(shared[4, 0] + jnp.sum(norm_grads * norm_grads))
    factor = jnp.minimum(1.0, CLIP_NORM / (grad_norm + 1e-06))
    groups = (
        (qkv_weight, reduced[0], qkv_first, qkv_second, qkv_average),
        (out_weight, reduced[1], out_first, out_second, out_average),
        (up_weight, reduced[2], up_first, up_second, up_average),
        (down_weight.T, reduced[3], down_first.T, down_second.T, down_average.T),
    )
    stepped = matrix_steps(jnp.reshape(factor, (1,)), groups)
    stepped[3] = [item.T for item in stepped[3]]
    norm_step = adamw_moment_update(
        norm_params, norm_grads, norm_first, norm_second, norm_average, rates()[4], factor
    )
    results = []
    for n in range(4):
        results += [item[n] for item in stepped] + [norm_step[n]]
    copies = [item[4] for item in stepped]
    return (block_out, input_grad, grad_norm, *results, *copies, factor * norm_grads[2:])


def is_fast(mesh):
    sizes = dict(mesh.shape)
    return sizes["seq"] == 2 and sizes["head"] == 4 and sizes["dp"] == 4


def solution(mesh):
    return jax.shard_map(
        fast_body if is_fast(mesh) else body,
        mesh=mesh,
        in_specs=(
            P("dp", ("seq", "head"), None),
            P("dp", ("seq", "head"), None),
            P("head", "seq", None),
            P(),
            P(("dp", "seq"), "head"),
            P("head", ("dp", "seq")),
            P(("dp", "seq"), "head"),
            P("head", ("dp", "seq")),
            P(),
            P(("dp", "seq"), "head"),
            P("head", ("dp", "seq")),
            P(("dp", "seq"), "head"),
            P("head", ("dp", "seq")),
            P(),
            P(("dp", "seq"), "head"),
            P("head", ("dp", "seq")),
            P(("dp", "seq"), "head"),
            P("head", ("dp", "seq")),
            P(),
            P(("dp", "seq"), "head"),
            P("head", ("dp", "seq")),
            P(("dp", "seq"), "head"),
            P("head", ("dp", "seq")),
            P(),
        ),
        out_specs=(
            P("dp", ("seq", "head"), None),
            P("dp", ("seq", "head"), None),
            P(),
            P(("dp", "seq"), "head"),
            P("head", ("dp", "seq")),
            P(("dp", "seq"), "head"),
            P("head", ("dp", "seq")),
            P(),
            P(("dp", "seq"), "head"),
            P("head", ("dp", "seq")),
            P(("dp", "seq"), "head"),
            P("head", ("dp", "seq")),
            P(),
            P(("dp", "seq"), "head"),
            P("head", ("dp", "seq")),
            P(("dp", "seq"), "head"),
            P("head", ("dp", "seq")),
            P(),
            P(("dp", "seq"), "head"),
            P("head", ("dp", "seq")),
            P(("dp", "seq"), "head"),
            P("head", ("dp", "seq")),
            P(),
            P(("dp", "seq"), "head"),
            P("head", ("dp", "seq")),
            P(("dp", "seq"), "head"),
            P("head", ("dp", "seq")),
            P(),
        ),
        check_vma=False,
    )
```

```python
import jax
import jax.numpy as jnp
from jax import lax
from jax.experimental import pallas as pl
from jax.experimental.pallas import tpu as pltpu
from jax.sharding import PartitionSpec as P

D = 768
DH = 64
FF = 3072
BLOCK = 64
STEP = 10


EPSILON = 1e-05
BETA_ONE = 0.9
BETA_TWO = 0.999
DECAY = 0.01
SMALL = 1e-08
CLIP_NORM = 1.0
AVERAGING = 0.999
NEGATIVE = -1e30


def norm_rows(values, gain_row, shift_row):
    center = values - jnp.mean(values, -1, keepdims=True)
    spread = jnp.mean(center * center, -1, keepdims=True)
    return center * lax.rsqrt(spread + EPSILON) * gain_row + shift_row


def key_table(rand_local, global_blocks, first_block, blocks_total):
    head_count, local_blocks = (rand_local.shape[0], rand_local.shape[1])
    places = first_block + jnp.arange(local_blocks, dtype=jnp.int32)
    left_side = jnp.maximum(places - 1, 0)
    right_side = jnp.minimum(places + 1, blocks_total - 1)
    window = jnp.stack([left_side, places, right_side], -1)
    key_index = jnp.concatenate(
        [
            jnp.broadcast_to(window[None], (head_count, local_blocks, 3)),
            rand_local,
            jnp.broadcast_to(global_blocks[None, None], (head_count, local_blocks, 2)),
        ],
        -1,
    )
    column_one = jnp.ones((local_blocks, 1), jnp.float32)
    key_valid = jnp.concatenate(
        [
            (places > 0).astype(jnp.float32)[:, None],
            column_one,
            (places < blocks_total - 1).astype(jnp.float32)[:, None],
            jnp.ones((local_blocks, 5), jnp.float32),
        ],
        -1,
    )
    return (key_index, key_valid)


def gather_rows(values):
    return lax.all_gather(values, "head", axis=1, tiled=True)


def sum_rows(values):
    return lax.psum_scatter(values, "head", scatter_dimension=1, tiled=True)


def contract(left_operand, right_operand):
    return jnp.einsum(
        "enz,enf->zf", left_operand, right_operand, preferred_element_type=jnp.float32
    )


def to_heads(values, head_count):
    seq_count, token_count = (values.shape[0], values.shape[1])
    return jnp.moveaxis(
        values.reshape(seq_count, token_count // BLOCK, BLOCK, head_count, DH), 3, 0
    )


def from_heads(values):
    head_count, seq_count, blocks = (values.shape[0], values.shape[1], values.shape[2])
    return jnp.moveaxis(values, 0, 3).reshape(seq_count, blocks * BLOCK, head_count * DH)


def pick_keys(kv_all, key_index):
    seq_count, token_count = (kv_all.shape[0], kv_all.shape[1])
    head_count = key_index.shape[0]
    blocks = kv_all.reshape(seq_count, token_count // BLOCK, BLOCK, head_count, 2, DH)
    by_head = jnp.moveaxis(blocks, 3, 0)
    return jax.vmap(lambda source, chosen: source[:, chosen])(by_head, key_index)


def scores_of(queries, picked, key_valid):
    raw_scores = jnp.einsum(
        "hsnbe,hsnkce->hsnbkc", queries, picked[..., 0, :], preferred_element_type=jnp.float32
    ) * DH ** (-0.5)
    return jnp.where(key_valid[None, None, :, None, :, None] > 0, raw_scores, NEGATIVE)


def attend_forward(queries, picked, key_valid):
    raw_scores = scores_of(queries, picked, key_valid)
    score_shape = raw_scores.shape
    scores_flat = raw_scores.reshape(score_shape[:4] + (score_shape[4] * score_shape[5],))
    row_max = jnp.max(scores_flat, -1, keepdims=True)
    exponent = jnp.exp(scores_flat - row_max)
    row_total = jnp.sum(exponent, -1, keepdims=True)
    probabilities = (exponent / row_total).astype(jnp.bfloat16).reshape(score_shape)
    output = jnp.einsum(
        "hsnbkc,hsnkce->hsnbe", probabilities, picked[..., 1, :], preferred_element_type=jnp.float32
    )
    return (output, row_max + jnp.log(row_total))


def attend_backward(queries, picked, key_valid, log_total, grad_out):
    raw_scores = scores_of(queries, picked, key_valid)
    score_shape = raw_scores.shape
    scores_flat = raw_scores.reshape(score_shape[:4] + (score_shape[4] * score_shape[5],))
    probabilities = jnp.exp(scores_flat - log_total)
    grad_probs = jnp.einsum(
        "hsnbe,hsnkce->hsnbkc", grad_out, picked[..., 1, :], preferred_element_type=jnp.float32
    ).reshape(scores_flat.shape)
    row_delta = jnp.sum(probabilities * grad_probs, -1, keepdims=True)
    grad_scores = probabilities * (grad_probs - row_delta)
    grad_scores = grad_scores.astype(jnp.bfloat16).reshape(score_shape)
    low_probs = probabilities.astype(jnp.bfloat16).reshape(score_shape)
    grad_query = jnp.einsum(
        "hsnbkc,hsnkce->hsnbe", grad_scores, picked[..., 0, :], preferred_element_type=jnp.float32
    ) * DH ** (-0.5)
    grad_keys = jnp.einsum(
        "hsnbkc,hsnbe->hsnkce", grad_scores, queries, preferred_element_type=jnp.float32
    ) * DH ** (-0.5)
    grad_values = jnp.einsum(
        "hsnbkc,hsnbe->hsnkce", low_probs, grad_out, preferred_element_type=jnp.float32
    )
    return (grad_query, jnp.stack([grad_keys, grad_values], -2), row_delta)


def spread_back(grad_pairs, key_index, seq_count, blocks_total):
    head_count = key_index.shape[0]
    zero_grid = jnp.zeros((head_count, seq_count, blocks_total, BLOCK, 2, DH), jnp.float32)
    filled = jax.vmap(lambda source, chosen, addend: source.at[:, chosen].add(addend))(
        zero_grid, key_index, grad_pairs
    )
    return jnp.moveaxis(filled, 0, 3).reshape(seq_count, blocks_total * BLOCK, head_count * 2 * DH)


def rates():
    return (
        1.5 * D ** (-0.5),
        1.5 * max(1, D // (8 * BLOCK)) ** (-0.5),
        1.5 * D ** (-0.5),
        1.5 * FF ** (-0.5),
        0.5,
    )


def adamw_moment_update(weight, gradient, moment_one, moment_two, average, rate, factor):
    decay_mean = min(AVERAGING, (1.0 + STEP) / (10.0 + STEP))
    clipped = gradient * factor
    first_new = BETA_ONE * moment_one + (1.0 - BETA_ONE) * clipped
    second_new = BETA_TWO * moment_two + (1.0 - BETA_TWO) * clipped * clipped
    update = (
        first_new / (1.0 - BETA_ONE**STEP) / (jnp.sqrt(second_new / (1.0 - BETA_TWO**STEP)) + SMALL)
    )
    weight_new = weight - rate * (update + DECAY * weight)
    average_new = decay_mean * average + (1.0 - decay_mean) * weight_new
    return (weight_new, first_new, second_new, average_new)


def body(
    tokens,
    cotangent,
    rand_blocks,
    global_blocks,
    qkv_weight,
    out_weight,
    up_weight,
    down_weight,
    norm_params,
    qkv_first,
    out_first,
    up_first,
    down_first,
    norm_first,
    qkv_second,
    out_second,
    up_second,
    down_second,
    norm_second,
    qkv_average,
    out_average,
    up_average,
    down_average,
    norm_average,
):
    qkv_low, out_low, up_low, down_low = (
        lax.all_gather(qkv_weight.astype(jnp.bfloat16), ("dp", "seq"), axis=0, tiled=True),
        lax.all_gather(out_weight.astype(jnp.bfloat16), ("dp", "seq"), axis=1, tiled=True),
        lax.all_gather(up_weight.astype(jnp.bfloat16), ("dp", "seq"), axis=0, tiled=True),
        lax.all_gather(down_weight.astype(jnp.bfloat16), ("dp", "seq"), axis=1, tiled=True),
    )
    seq_count = tokens.shape[0]
    head_count = rand_blocks.shape[0]
    local_blocks = rand_blocks.shape[1]
    blocks_total = local_blocks * lax.axis_size("seq")
    first_block = lax.axis_index("seq") * local_blocks
    key_index, key_valid = key_table(rand_blocks, global_blocks, first_block, blocks_total)
    inputs = tokens.astype(jnp.float32)
    full_one = gather_rows(norm_rows(inputs, norm_params[0], norm_params[1]).astype(jnp.bfloat16))
    token_count = full_one.shape[1]
    qkv_all = jnp.dot(full_one, qkv_low, preferred_element_type=jnp.float32).astype(jnp.bfloat16)
    qkv_parts = qkv_all.reshape(seq_count, token_count, head_count, 3, DH)
    kv_local = qkv_parts[:, :, :, 1:, :].reshape(seq_count, token_count, head_count * 2 * DH)
    kv_all = lax.all_gather(kv_local, "seq", axis=1, tiled=True)
    picked = pick_keys(kv_all, key_index)
    queries = to_heads(qkv_parts[:, :, :, 0, :], head_count)
    attended, log_total = attend_forward(queries, picked, key_valid)
    mixed_heads = from_heads(attended.astype(jnp.bfloat16))
    residual = inputs + sum_rows(jnp.dot(mixed_heads, out_low, preferred_element_type=jnp.float32))
    full_two = gather_rows(norm_rows(residual, norm_params[2], norm_params[3]).astype(jnp.bfloat16))
    upward = jnp.dot(full_two, up_low, preferred_element_type=jnp.float32)
    active = jax.nn.gelu(upward).astype(jnp.bfloat16)
    result = residual + sum_rows(jnp.dot(active, down_low, preferred_element_type=jnp.float32))
    block_out = result.astype(jnp.bfloat16)
    grad_top = gather_rows(cotangent)
    grad_down = contract(active, grad_top)
    grad_active = jnp.dot(grad_top, down_low.T, preferred_element_type=jnp.float32)
    _, gelu_back = jax.vjp(jax.nn.gelu, upward)
    grad_upward = gelu_back(grad_active)[0].astype(jnp.bfloat16)
    grad_up = contract(full_two, grad_upward)
    part_two = sum_rows(jnp.dot(grad_upward, up_low.T, preferred_element_type=jnp.float32))
    _, norm_back_two = jax.vjp(norm_rows, residual, norm_params[2], norm_params[3])
    grad_residual_norm, grad_gain_two, grad_shift_two = norm_back_two(part_two)
    grad_residual = cotangent.astype(jnp.float32) + grad_residual_norm
    grad_middle = gather_rows(grad_residual.astype(jnp.bfloat16))
    grad_out = contract(mixed_heads, grad_middle)
    grad_mixed = jnp.dot(grad_middle, out_low.T, preferred_element_type=jnp.float32).astype(
        jnp.bfloat16
    )
    grad_query, grad_pairs, row_delta = attend_backward(
        queries, picked, key_valid, log_total, to_heads(grad_mixed, head_count)
    )
    grad_kv_full = spread_back(grad_pairs, key_index, seq_count, blocks_total)
    grad_kv = lax.psum_scatter(
        grad_kv_full.astype(jnp.bfloat16), "seq", scatter_dimension=1, tiled=True
    ).astype(jnp.float32)
    query_gradient = from_heads(grad_query).reshape(seq_count, token_count, head_count, 1, DH)
    grad_qkv_rows = jnp.concatenate(
        [query_gradient, grad_kv.reshape(seq_count, token_count, head_count, 2, DH)], 3
    )
    grad_qkv_rows = grad_qkv_rows.reshape(seq_count, token_count, head_count * 3 * DH).astype(
        jnp.bfloat16
    )
    grad_qkv = contract(full_one, grad_qkv_rows)
    part_one = sum_rows(jnp.dot(grad_qkv_rows, qkv_low.T, preferred_element_type=jnp.float32))
    _, norm_back_one = jax.vjp(norm_rows, inputs, norm_params[0], norm_params[1])
    grad_input_norm, grad_gain_one, grad_shift_one = norm_back_one(part_one)
    input_grad = (grad_residual + grad_input_norm).astype(jnp.bfloat16)
    grad_norm_local = jnp.stack([grad_gain_one, grad_shift_one, grad_gain_two, grad_shift_two])
    reduced_total = (
        lax.psum_scatter(grad_qkv, ("dp", "seq"), scatter_dimension=0, tiled=True),
        lax.psum_scatter(grad_out, ("dp", "seq"), scatter_dimension=1, tiled=True),
        lax.psum_scatter(grad_up, ("dp", "seq"), scatter_dimension=0, tiled=True),
        lax.psum_scatter(grad_down, ("dp", "seq"), scatter_dimension=1, tiled=True),
    )
    squares = sum((jnp.sum(item * item) for item in reduced_total))
    norm_grads = lax.psum(grad_norm_local, ("dp", "seq", "head"))
    matrix_squares = lax.psum(squares, ("dp", "seq", "head"))
    grad_norm = jnp.sqrt(matrix_squares + jnp.sum(norm_grads * norm_grads))
    factor = jnp.minimum(1.0, CLIP_NORM / (grad_norm + 1e-06))
    weights = (qkv_weight, out_weight, up_weight, down_weight, norm_params)
    gradients = (reduced_total[0], reduced_total[1], reduced_total[2], reduced_total[3], norm_grads)
    firsts = (qkv_first, out_first, up_first, down_first, norm_first)
    seconds = (qkv_second, out_second, up_second, down_second, norm_second)
    averages = (qkv_average, out_average, up_average, down_average, norm_average)
    results = [
        adamw_moment_update(
            weights[slot],
            gradients[slot],
            firsts[slot],
            seconds[slot],
            averages[slot],
            rates()[slot],
            factor,
        )
        for slot in range(5)
    ]
    news = tuple((item[0] for item in results))
    first_news = tuple((item[1] for item in results))
    second_news = tuple((item[2] for item in results))
    average_news = tuple((item[3] for item in results))
    return (
        block_out,
        input_grad,
        grad_norm,
        news[0],
        news[1],
        news[2],
        news[3],
        news[4],
        first_news[0],
        first_news[1],
        first_news[2],
        first_news[3],
        first_news[4],
        second_news[0],
        second_news[1],
        second_news[2],
        second_news[3],
        second_news[4],
        average_news[0],
        average_news[1],
        average_news[2],
        average_news[3],
        average_news[4],
        news[0].astype(jnp.bfloat16),
        news[1].astype(jnp.bfloat16),
        news[2].astype(jnp.bfloat16),
        news[3].astype(jnp.bfloat16),
        factor * norm_grads[2:],
    )


GROUP = ("seq", "head")
EVERY = ("dp", "seq", "head")
FULL = 4096
CHUNK = 512
MB = 1024 * 1024
COST = pl.CostEstimate(flops=10**6, bytes_accessed=10**5, transcendentals=0)


def limits(megabytes):
    return pltpu.CompilerParams(vmem_limit_bytes=megabytes * MB)


def swap(values, distance):
    return lax.ppermute(values, GROUP, [(i, i ^ distance) for i in range(8)])


def swap_every(values, distance, count):
    return lax.ppermute(values, EVERY, [(i, i ^ distance) for i in range(count)])


def nt(left, right):
    return lax.dot_general(left, right, (((1,), (1,)), ((), ())), preferred_element_type=jnp.float32)


def nn(left, right):
    return lax.dot_general(left, right, (((1,), (0,)), ((), ())), preferred_element_type=jnp.float32)


def tn(left, right):
    return lax.dot_general(left, right, (((0,), (0,)), ((), ())), preferred_element_type=jnp.float32)


def lane_low(shape):
    return lax.broadcasted_iota(jnp.int32, shape, len(shape) - 1) < 64


def roll64(values):
    return pltpu.roll(values, 64, 1)


def block_places(tab_ref, k, block):
    me = tab_ref[0]
    part = (block // 32) ^ (me // 4)
    base = 8 + ((part * 3 + k) * 32 + block % 32) * 3
    chosen = [
        jnp.maximum(block - 1, 0),
        block,
        jnp.minimum(block + 1, 63),
        tab_ref[base],
        tab_ref[base + 1],
        tab_ref[base + 2],
        tab_ref[1],
        tab_ref[2],
    ]
    return [pl.multiple_of((((b // 8) ^ me) * 8 + b % 8) * 64, 64) for b in chosen]


def spread_heads(wide):
    tile = lambda j: wide[:, j * 128 : j * 128 + 128]
    low = lane_low((wide.shape[0], 128))
    scale = DH ** (-0.5)
    return [
        jnp.where(low, tile(0) * scale, 0.0),
        jnp.where(low, roll64(tile(0)), roll64(tile(1))),
        jnp.where(low, roll64(tile(1)) * scale, 0.0),
        tile(2),
        jnp.where(low, tile(3) * scale, 0.0),
        jnp.where(low, roll64(tile(3)), roll64(tile(4))),
    ]


def qkv_kernel(*refs):
    tok_refs, weight_ref, out_ref = refs[:8], refs[8], refs[9]
    for slot, tok_ref in enumerate(tok_refs):
        for n, part in enumerate(spread_heads(nn(tok_ref[...], weight_ref[...]))):
            out_ref[slot * CHUNK : slot * CHUNK + CHUNK, n * 128 : n * 128 + 128] = part.astype(jnp.bfloat16)


def project(slots, weights):
    return pl.pallas_call(
        qkv_kernel,
        grid=(1,),
        in_specs=[pl.BlockSpec((CHUNK, D), lambda i: (0, 0))] * 8 + [pl.BlockSpec((D, 640), lambda i: (0, 0))],
        out_specs=pl.BlockSpec((FULL, D), lambda i: (0, 0)),
        out_shape=jax.ShapeDtypeStruct((FULL, D), jnp.bfloat16),
        compiler_params=limits(60),
        name="project",
        cost_estimate=COST,
    )(*slots, weights)


def hide(scores, low, high):
    lane = lax.broadcasted_iota(jnp.int32, scores.shape, 1)
    return jnp.where((lane >= low) & (lane < high), NEGATIVE, scores)


def softmax_rows(scores, part, q):
    if q == 0:
        scores = jnp.where(part == 0, hide(scores, 0, 64), scores)
    if q == 7:
        scores = jnp.where(part == 7, hide(scores, 128, 192), scores)
    top = jnp.max(scores, -1, keepdims=True)
    exponent = jnp.exp(scores - top)
    total = jnp.sum(exponent, -1, keepdims=True)
    return exponent * (1.0 / total)


def attend_kernel(k, tab_ref, qkv_ref, out_ref):
    me = tab_ref[0]

    def step(slot, carry):
        part = slot ^ me
        keys, scores = [], []
        for q in range(8):
            places = block_places(tab_ref, k, part * 8 + q)
            keys.append(jnp.concatenate([qkv_ref[pl.ds(p, 64), 128:256] for p in places], 0))
            at = pl.multiple_of(slot * CHUNK + q * 64, 64)
            scores.append(nt(qkv_ref[pl.ds(at, 64), 0:128], keys[q]))
        probs = [softmax_rows(scores[q], part, q).astype(jnp.bfloat16) for q in range(8)]
        outs = [nn(probs[q], keys[q]) for q in range(8)]
        for q in range(4):
            both = jnp.where(lane_low(outs[q].shape), roll64(outs[q]), outs[q + 4])
            out_ref[part, q * 64 : q * 64 + 64, :] = both.astype(jnp.bfloat16)
        return carry

    lax.fori_loop(0, 8, step, 0)


def attend(heads, table, qkv):
    first, count = heads[0], len(heads)

    def kernel(tab_ref, qkv_ref, out_ref):
        attend_kernel(pl.program_id(0) + first, tab_ref, qkv_ref, out_ref)

    return pl.pallas_call(
        kernel,
        grid_spec=pltpu.PrefetchScalarGridSpec(
            num_scalar_prefetch=1,
            grid=(count,),
            in_specs=[pl.BlockSpec((FULL, 256), lambda i, t: (0, first + i))],
            out_specs=pl.BlockSpec((8, 256, 128), lambda i, t: (0, i, 0)),
        ),
        out_shape=jax.ShapeDtypeStruct((8, 256 * count, 128), jnp.bfloat16),
        compiler_params=limits(60),
        name="attend",
        cost_estimate=COST,
    )(table, qkv)


def attend_back_kernel(k, tab_ref, qkv_ref, grad_ref, full_ref, pack_ref, acc_ref, shared_ref):
    me = tab_ref[0]
    acc_ref[...] = jnp.zeros_like(acc_ref)
    shared_ref[...] = jnp.zeros_like(shared_ref)

    def step(n, carry):
        slot, half = n // 2, n % 2
        part = slot ^ me
        picks = (0, 1, 4, 5)
        places, stacks, keys, both = [], [], [], []
        tiles = []
        for j in range(2):
            tile = grad_ref[part, pl.ds(pl.multiple_of(half * 128 + j * 64, 64), 64), :].astype(jnp.float32)
            low_lanes = lane_low(tile.shape)
            tiles.append(jnp.where(low_lanes, 0.0, roll64(tile)).astype(jnp.bfloat16))
            tiles.append(jnp.where(low_lanes, 0.0, tile).astype(jnp.bfloat16))
        grads = (tiles[0], tiles[2], tiles[1], tiles[3])
        for j, base in enumerate(picks):
            q = base + 2 * half
            places.append(block_places(tab_ref, k, part * 8 + q))
            keys.append(jnp.concatenate([qkv_ref[pl.ds(p, 64), 128:256] for p in places[j]], 0))
            at = pl.multiple_of(slot * CHUNK + q * 64, 64)
            stacks.append(jnp.concatenate([qkv_ref[pl.ds(at, 64), 0:128], grads[j]], 0))
            both.append(nt(stacks[j], keys[j]))
        lows, pairs = [], []
        for j in range(4):
            scores, grad_probs = both[j][:64], both[j][64:]
            if picks[j] == 0:
                scores = jnp.where((part == 0) & (half == 0), hide(scores, 0, 64), scores)
            if picks[j] == 5:
                scores = jnp.where((part == 7) & (half == 1), hide(scores, 128, 192), scores)
            probs = softmax_rows(scores, part, 1)
            delta = jnp.sum(probs * grad_probs, -1, keepdims=True)
            lows.append((probs * (grad_probs - delta)).astype(jnp.bfloat16))
            pairs.append(jnp.concatenate([lows[j], probs.astype(jnp.bfloat16)], 0))
        queries = []
        for j in range(4):
            grad_query = nn(lows[j], keys[j]) * DH ** (-0.5)
            queries.append(jnp.where(lane_low(grad_query.shape), grad_query, 0.0))
            at = pl.multiple_of(slot * CHUNK + (picks[j] + 2 * half) * 64, 64)
            full_ref[pl.ds(at, 64), 0:128] = queries[j].astype(jnp.bfloat16)
        spreads = [tn(pairs[j], stacks[j]) for j in range(4)]
        for j in range(4):
            for m in range(6):
                acc_ref[pl.ds(places[j][m], 64), :] += spreads[j][m * 64 : m * 64 + 64]
        shared_ref[...] += (spreads[0][384:] + spreads[1][384:]) + (spreads[2][384:] + spreads[3][384:])
        for j in range(2):
            packed = queries[j] + roll64(queries[j + 2])
            pack_ref[part, pl.ds(pl.multiple_of(half * 128 + j * 64, 64), 64), :] = packed.astype(jnp.bfloat16)
        return carry

    lax.fori_loop(0, 16, step, 0)
    for m in range(2):
        block = tab_ref[1 + m]
        at = pl.multiple_of((((block // 8) ^ me) * 8 + block % 8) * 64, 64)
        acc_ref[pl.ds(at, 64), :] += shared_ref[m * 64 : m * 64 + 64]

    def finish(slot, carry):
        at = pl.ds(pl.multiple_of(slot * CHUNK, CHUNK), CHUNK)
        low = acc_ref[at, :].astype(jnp.bfloat16)
        full_ref[at, 128:256] = low
        pack_ref[slot ^ me, 256:768, :] = low
        return carry

    lax.fori_loop(0, 8, finish, 0)


def attend_back(k, table, qkv, grad, row):
    return pl.pallas_call(
        lambda *refs: attend_back_kernel(k, *refs),
        grid_spec=pltpu.PrefetchScalarGridSpec(
            num_scalar_prefetch=1,
            grid=(1,),
            in_specs=[
                pl.BlockSpec((FULL, 256), lambda i, t: (0, k)),
                pl.BlockSpec((8, 256, 128), lambda i, t: (0, row, 0)),
            ],
            out_specs=[
                pl.BlockSpec((FULL, 256), lambda i, t: (0, 0)),
                pl.BlockSpec((8, 768, 128), lambda i, t: (0, 0, 0)),
            ],
            scratch_shapes=[pltpu.VMEM((FULL, 128), jnp.float32), pltpu.VMEM((128, 128), jnp.float32)],
        ),
        out_shape=[
            jax.ShapeDtypeStruct((FULL, 256), jnp.bfloat16),
            jax.ShapeDtypeStruct((8, 768, 128), jnp.bfloat16),
        ],
        compiler_params=limits(60),
        name="attend_back",
        cost_estimate=COST,
    )(table, qkv, grad)


def norm_stats(values):
    center = values - jnp.mean(values, -1, keepdims=True)
    spread = jnp.mean(center * center, -1, keepdims=True)
    scale = lax.rsqrt(spread + EPSILON)
    return center * scale, scale


def halves(first, second):
    low = lane_low(first.shape)
    upper = jnp.where(low, first, roll64(second))
    lower = jnp.where(low, roll64(first), second)
    return upper, lower


def mid_kernel(o0_ref, o1_ref, o2_ref, w_ref, tok_ref, par_ref, cat_ref, mid_ref, a2_ref, a2t_ref):
    middle = tok_ref[0].astype(jnp.float32)
    cat_ref[...] = jnp.zeros_like(cat_ref)
    for h in range(4):
        tiles = [ref[h, at : at + 256].astype(jnp.float32) for ref, at in ((o0_ref, 0), (o1_ref, 256), (o2_ref, 0))]
        upper, lower = halves(tiles[0], tiles[1])
        last_upper, last_lower = halves(tiles[2], jnp.zeros_like(tiles[2]))
        cat_ref[0:256, h * 256 : h * 256 + 128] = upper.astype(jnp.bfloat16)
        cat_ref[256:512, h * 256 : h * 256 + 128] = lower.astype(jnp.bfloat16)
        cat_ref[0:256, h * 256 + 128 : h * 256 + 256] = last_upper.astype(jnp.bfloat16)
        cat_ref[256:512, h * 256 + 128 : h * 256 + 256] = last_lower.astype(jnp.bfloat16)
        middle = middle + nt(cat_ref[:, h * 256 : h * 256 + 256], w_ref[h])
    mid_ref[0] = middle
    normed, _ = norm_stats(middle)
    low = normed * par_ref[2:3, :] + par_ref[3:4, :]
    a2_ref[...] = low.astype(jnp.bfloat16)
    a2t_ref[...] = low.T.astype(jnp.bfloat16)


def out_weight_spec():
    return pl.BlockSpec((4, D, 256), lambda s: (0, 0, 0))


def middle(o_pair, o_last, weights, tokens, params):
    seqs = tokens.shape[0]
    rows = pl.BlockSpec((1, CHUNK, D), lambda s: (s, 0, 0))
    return pl.pallas_call(
        mid_kernel,
        grid=(seqs,),
        in_specs=[
            pl.BlockSpec((4, 512, 128), lambda s: (s, 0, 0)),
            pl.BlockSpec((4, 512, 128), lambda s: (s, 0, 0)),
            pl.BlockSpec((4, 256, 128), lambda s: (s, 0, 0)),
            out_weight_spec(), rows, pl.BlockSpec((4, D), lambda s: (0, 0)),
        ],
        out_specs=[
            pl.BlockSpec((CHUNK, 1024), lambda s: (s, 0)), rows,
            pl.BlockSpec((CHUNK, D), lambda s: (s, 0)), pl.BlockSpec((D, CHUNK), lambda s: (0, s)),
        ],
        out_shape=[
            jax.ShapeDtypeStruct((seqs * CHUNK, 1024), jnp.bfloat16),
            jax.ShapeDtypeStruct(tokens.shape, jnp.float32),
            jax.ShapeDtypeStruct((seqs * CHUNK, D), jnp.bfloat16),
            jax.ShapeDtypeStruct((D, seqs * CHUNK), jnp.bfloat16),
        ],
        compiler_params=limits(60),
        name="middle",
        cost_estimate=COST,
    )(o_pair, o_pair, o_last, weights, tokens, params)


def group_of(head, i):
    return head ^ (i % 2 * 2 + 1 - i // 2)


def mlp_kernel(head_ref, a2_ref, a2t_ref, dy_ref, dyt_ref, mid_ref, wu_ref, wd_ref, out_ref, back_ref,
               um_ref, dm_ref, uo_ref, do_ref, g_ref, u_ref, wut_ref, wdt_ref, acc_ref):
    step = pl.program_id(0)

    @pl.when(step == 0)
    def _():
        acc_ref[...] = mid_ref[...]
        back_ref[...] = jnp.zeros_like(back_ref)

    wut_ref[...] = wu_ref[0].T
    wdt_ref[...] = wd_ref[0].T
    rate, cubic = 0.7978845608028654, 0.044715
    for m in range(4):
        at = slice(m * 256, m * 256 + 256)
        up = nn(a2_ref[at, :], wu_ref[0])
        grad = nn(dy_ref[at, :], wd_ref[0])
        square = up * up
        bend = jnp.tanh(rate * up * (1.0 + cubic * square))
        half = 0.5 * (1.0 + bend)
        g_ref[at, :] = (up * half).astype(jnp.bfloat16)
        slope = half + 0.5 * up * (1.0 - bend * bend) * (rate * (1.0 + 3.0 * cubic * square))
        u_ref[at, :] = (grad * slope).astype(jnp.bfloat16)
        acc_ref[at, :] += nn(g_ref[at, :], wdt_ref[...])
        back_ref[at, :] += nn(u_ref[at, :], wut_ref[...])
    up_grad = nn(a2t_ref[...], u_ref[...]).astype(jnp.bfloat16)
    down_grad = nn(dyt_ref[...], g_ref[...]).astype(jnp.bfloat16)

    @pl.when(step < 2)
    def _():
        um_ref[0] = up_grad
        dm_ref[0] = down_grad

    @pl.when(step >= 2)
    def _():
        uo_ref[0] = up_grad
        do_ref[0] = down_grad

    @pl.when(step == 3)
    def _():
        out_ref[...] = acc_ref[...].astype(jnp.bfloat16)


def mlp(head, a2, a2t, dy, dyt, mid, weights):
    tokens = a2.shape[0]
    whole = lambda shape: pl.BlockSpec(shape, lambda i, t: (0, 0))
    weight = lambda part: pl.BlockSpec((1, D, D), lambda i, t: (group_of(t[0], i), 0, part))
    theirs = pl.BlockSpec((1, D, D), lambda i, t: (jnp.minimum(i, 1), 0, 0))
    ours = pl.BlockSpec((1, D, D), lambda i, t: (jnp.maximum(i - 2, 0), 0, 0))
    low = jax.ShapeDtypeStruct((2, D, D), jnp.bfloat16)
    return pl.pallas_call(
        mlp_kernel,
        grid_spec=pltpu.PrefetchScalarGridSpec(
            num_scalar_prefetch=1,
            grid=(4,),
            in_specs=[
                whole((tokens, D)), whole((D, tokens)), whole((tokens, D)), whole((D, tokens)), whole((tokens, D)),
                weight(0), weight(1),
            ],
            out_specs=[whole((tokens, D)), whole((tokens, D)), theirs, theirs, ours, ours],
            scratch_shapes=[
                pltpu.VMEM((tokens, D), jnp.bfloat16), pltpu.VMEM((tokens, D), jnp.bfloat16),
                pltpu.VMEM((D, D), jnp.bfloat16), pltpu.VMEM((D, D), jnp.bfloat16), pltpu.VMEM((tokens, D), jnp.float32),
            ],
        ),
        out_shape=[
            jax.ShapeDtypeStruct((tokens, D), jnp.bfloat16), jax.ShapeDtypeStruct((tokens, D), jnp.float32),
            low, low, low, low,
        ],
        compiler_params=limits(60),
        name="mlp",
        cost_estimate=COST,
    )(head, a2, a2t, dy, dyt, mid, weights, weights)


def norm_back(grad, values, gain):
    normed, scale = norm_stats(values)
    gain_grad = jnp.sum(grad * normed, 0, keepdims=True)
    shift_grad = jnp.sum(grad, 0, keepdims=True)
    inner = grad * gain
    across = jnp.mean(inner, -1, keepdims=True)
    along = jnp.mean(inner * normed, -1, keepdims=True)
    return scale * (inner - across - normed * along), gain_grad, shift_grad


def mid_back_kernel(b_ref, mid_ref, dy_ref, w_ref, par_ref, grad_ref, low_ref, g0_ref, g1_ref, norm_ref):
    grad, gain_grad, shift_grad = norm_back(b_ref[...], mid_ref[0], par_ref[2:3, :])
    total = dy_ref[0].astype(jnp.float32) + grad
    grad_ref[0] = total
    low = total.astype(jnp.bfloat16)
    low_ref[...] = low
    for h in range(4):
        mixed = nn(low, w_ref[h])
        first, second = halves(mixed[0:256, 0:128], mixed[256:512, 0:128])
        third, _ = halves(mixed[0:256, 128:256], mixed[256:512, 128:256])
        g0_ref[h] = first.astype(jnp.bfloat16)
        g1_ref[h, 0:256] = second.astype(jnp.bfloat16)
        g1_ref[h, 256:512] = third.astype(jnp.bfloat16)

    @pl.when(pl.program_id(0) == 0)
    def _():
        norm_ref[...] = jnp.zeros_like(norm_ref)

    norm_ref[0:1, :] += gain_grad
    norm_ref[1:2, :] += shift_grad


def middle_back(back, mid, dy, weights, params):
    seqs = dy.shape[0]
    rows = pl.BlockSpec((1, CHUNK, D), lambda s: (s, 0, 0))
    flat = pl.BlockSpec((CHUNK, D), lambda s: (s, 0))
    return pl.pallas_call(
        mid_back_kernel,
        grid=(seqs,),
        in_specs=[flat, rows, rows, out_weight_spec(), pl.BlockSpec((4, D), lambda s: (0, 0))],
        out_specs=[
            rows, flat, pl.BlockSpec((4, 256, 128), lambda s: (s, 0, 0)),
            pl.BlockSpec((4, 512, 128), lambda s: (s, 0, 0)), pl.BlockSpec((8, D), lambda s: (0, 0)),
        ],
        out_shape=[
            jax.ShapeDtypeStruct(dy.shape, jnp.float32),
            jax.ShapeDtypeStruct((seqs * CHUNK, D), jnp.bfloat16),
            jax.ShapeDtypeStruct((8, 256, 128), jnp.bfloat16),
            jax.ShapeDtypeStruct((8, 512, 128), jnp.bfloat16),
            jax.ShapeDtypeStruct((8, D), jnp.float32),
        ],
        compiler_params=limits(60),
        name="middle_back",
        cost_estimate=COST,
    )(back, mid, dy, weights, params)


def out_grad_kernel(head_ref, low_ref, cat_ref, out_ref):
    for h in range(4):
        r = head_ref[0] ^ h
        out_ref[(1 - r % 2) * 2 + r // 2] = tn(low_ref[...], cat_ref[:, h * 256 : h * 256 + 256]).astype(jnp.bfloat16)


def out_weight_grad(head, low, cat):
    return pl.pallas_call(
        out_grad_kernel,
        grid_spec=pltpu.PrefetchScalarGridSpec(
            num_scalar_prefetch=1,
            grid=(1,),
            in_specs=[pl.BlockSpec(low.shape, lambda i, t: (0, 0)), pl.BlockSpec(cat.shape, lambda i, t: (0, 0))],
            out_specs=pl.BlockSpec((4, D, 256), lambda i, t: (0, 0, 0)),
        ),
        out_shape=jax.ShapeDtypeStruct((4, D, 256), jnp.bfloat16),
        compiler_params=limits(60),
        name="out_weight_grad",
        cost_estimate=COST,
    )(head, low, cat)


def merge_heads(queries, pairs):
    low = lane_low(queries[0].shape)
    return [
        jnp.where(low, queries[0], roll64(pairs[0])),
        jnp.where(low, roll64(pairs[0]), roll64(queries[1])),
        pairs[1],
        jnp.where(low, queries[2], roll64(pairs[2])),
        jnp.where(low, roll64(pairs[2]), 0.0),
    ]


def qkv_grad_kernel(*refs):
    tok_refs, full_refs, out_ref, acc_ref = refs[:8], refs[8:11], refs[11], refs[12]
    for slot, tok_ref in enumerate(tok_refs):
        at = slice(slot * CHUNK, slot * CHUNK + CHUNK)
        part = tn(tok_ref[...], jnp.concatenate([ref[at, :] for ref in full_refs], 1))
        acc_ref[...] = part if slot == 0 else acc_ref[...] + part
    tiles = merge_heads(
        [acc_ref[:, k * 256 : k * 256 + 128] for k in range(3)],
        [acc_ref[:, k * 256 + 128 : k * 256 + 256] for k in range(3)],
    )
    for j, tile in enumerate(tiles):
        out_ref[:, j * 128 : j * 128 + 128] = tile.astype(jnp.bfloat16)


def qkv_weight_grad(slots, fulls):
    return pl.pallas_call(
        qkv_grad_kernel,
        out_shape=jax.ShapeDtypeStruct((D, 640), jnp.bfloat16),
        scratch_shapes=[pltpu.VMEM((D, D), jnp.float32)],
        compiler_params=limits(60),
        name="qkv_weight_grad",
        cost_estimate=COST,
    )(*slots, *fulls)


def last_kernel(p0_ref, p1_ref, p2_ref, w_ref, tok_ref, mid_ref, par_ref, out_ref, norm_ref):
    grad = None
    for h in range(4):
        queries, pairs = [], []
        for ref in (p0_ref, p1_ref, p2_ref):
            both = ref[h, 0:256, :].astype(jnp.float32)
            queries.append(jnp.concatenate([both, roll64(both)], 0))
            pairs.append(ref[h, 256:768, :].astype(jnp.float32))
        wide = jnp.concatenate([tile.astype(jnp.bfloat16) for tile in merge_heads(queries, pairs)], 1)
        part = nt(wide, w_ref[h])
        grad = part if grad is None else grad + part
    back, gain_grad, shift_grad = norm_back(grad, tok_ref[0].astype(jnp.float32), par_ref[0:1, :])
    out_ref[0] = (mid_ref[0] + back).astype(jnp.bfloat16)

    @pl.when(pl.program_id(0) == 0)
    def _():
        norm_ref[...] = jnp.zeros_like(norm_ref)

    norm_ref[0:1, :] += gain_grad
    norm_ref[1:2, :] += shift_grad


def last(packs, weights, tokens, mid_grad, params):
    seqs = tokens.shape[0]
    piece = pl.BlockSpec((4, 768, 128), lambda s: (s, 0, 0))
    rows = pl.BlockSpec((1, CHUNK, D), lambda s: (s, 0, 0))
    return pl.pallas_call(
        last_kernel,
        grid=(seqs,),
        in_specs=[piece, piece, piece, pl.BlockSpec((4, D, 640), lambda s: (0, 0, 0)), rows, rows,
                  pl.BlockSpec((4, D), lambda s: (0, 0))],
        out_specs=[rows, pl.BlockSpec((8, D), lambda s: (0, 0))],
        out_shape=[jax.ShapeDtypeStruct(tokens.shape, jnp.bfloat16), jax.ShapeDtypeStruct((8, D), jnp.float32)],
        compiler_params=limits(60),
        name="last",
        cost_estimate=COST,
    )(*packs, weights, tokens, mid_grad, params)


def step_kernel(factor_ref, *refs):
    factor = factor_ref[0]
    for slot in range(4):
        weight, gradient, first, second, average = (ref[...] for ref in refs[slot * 5 : slot * 5 + 5])
        outs = refs[20 + slot * 5 : 25 + slot * 5]
        new, first, second, average = adamw_moment_update(
            weight, gradient, first, second, average, rates()[slot], factor
        )
        for ref, value in zip(outs, (new, first, second, average, new.astype(jnp.bfloat16))):
            ref[...] = value


def matrix_steps(factor, groups):
    blocks = [pl.BlockSpec((group[0].shape[0] // 3, group[0].shape[1]), lambda i, t: (i, 0)) for group in groups for _ in range(5)]
    shapes = [
        jax.ShapeDtypeStruct(group[0].shape, kind)
        for group in groups
        for kind in (jnp.float32,) * 4 + (jnp.bfloat16,)
    ]
    outs = pl.pallas_call(
        step_kernel,
        grid_spec=pltpu.PrefetchScalarGridSpec(num_scalar_prefetch=1, grid=(3,), in_specs=blocks, out_specs=blocks),
        out_shape=shapes,
        compiler_params=limits(60),
        name="matrix_steps",
        cost_estimate=COST,
    )(factor, *(item for group in groups for item in group))
    return [outs[n * 5 : n * 5 + 5] for n in range(4)]


def gather_mine(shard):
    return lax.all_gather(shard, ("dp", "seq"), axis=0, tiled=True)


def gather_heads(mine):
    return lax.all_gather(mine, "head", axis=0)


def pick(values, index, size, axis):
    return lax.dynamic_slice_in_dim(values, index * size, size, axis)


def after(value, *others):
    return lax.optimization_barrier((value, others))[0]


def add_low(left, right):
    return (left.astype(jnp.float32) + right.astype(jnp.float32)).astype(jnp.bfloat16)


def fast_body(
    tokens, cotangent, rand_blocks, global_blocks, qkv_weight, out_weight, up_weight, down_weight, norm_params,
    qkv_first, out_first, up_first, down_first, norm_first,
    qkv_second, out_second, up_second, down_second, norm_second,
    qkv_average, out_average, up_average, down_average, norm_average,
):
    dp_size = lax.axis_size("dp")
    count = dp_size * 8
    y, head = lax.axis_index("seq"), lax.axis_index("head")
    me = y * 4 + head

    head_word = jnp.reshape(head, (1,)).astype(jnp.int32)

    turned = jnp.stack([pick(tokens, y, 1, 0)[0], pick(tokens, 1 - y, 1, 0)[0]])
    normed = norm_rows(turned.astype(jnp.float32), norm_params[0], norm_params[1]).astype(jnp.bfloat16)
    mine, theirs = normed[0], normed[1]
    even = [mine, swap(mine, 2), swap(theirs, 4), swap(theirs, 6)]
    odd = [swap(item, 1) for item in even]
    slots = [item for pair in zip(even, odd) for item in pair]

    low_qkv = qkv_weight.astype(jnp.bfloat16)
    blank = jnp.zeros((96, 64), jnp.bfloat16)
    low_out = out_weight.T.astype(jnp.bfloat16)
    mine_first = gather_mine(jnp.concatenate([low_qkv, blank, low_out, blank], -1))
    low_mlp = jnp.concatenate([up_weight.astype(jnp.bfloat16), down_weight.T.astype(jnp.bfloat16)], -1)
    mine_mlp = gather_mine(after(low_mlp, even[1]))
    both_rand = jnp.concatenate([rand_blocks.reshape(-1), swap(rand_blocks.reshape(-1), 4)])
    table = jnp.concatenate(
        [jnp.reshape(me, (1,)), global_blocks, jnp.zeros((5,), jnp.int32), both_rand]
    ).astype(jnp.int32)
    qkv = project(slots, mine_first)
    all_first = gather_heads(after(mine_first, qkv))
    all_out = all_first[:, :, 640:]

    def across(values, axes=GROUP):
        return lax.all_to_all(values, axes, 0, 0, tiled=True)

    o_pair = attend((0, 1), table, qkv)
    all_mlp = gather_heads(after(mine_mlp, o_pair))
    o_pair = across(o_pair)
    o_last = across(after(attend((2,), table, qkv), o_pair))
    mixed, mid, a2, a2t = middle(o_pair, o_last, all_out, tokens, norm_params)

    dy = cotangent.reshape(a2.shape)
    block_out, back, up_mate, down_mate, up_own, down_own = mlp(
        head_word, a2, a2t, dy, dy.T, mid.reshape(a2.shape), all_mlp
    )
    block_out = block_out.reshape(tokens.shape)
    up_mate, down_mate = swap(up_mate, 1), swap(down_mate, 1)

    mid_grad, low_grad, grad_first, grad_rest, norm_two = middle_back(back, mid, cotangent, all_out, norm_params)
    grad_first, grad_rest = across(grad_first), across(grad_rest)
    out_terms = out_weight_grad(head_word, low_grad, mixed)
    out_mate = swap(out_terms[0:2], 1)

    fulls, packs = [], []

    def back_step(k, grad, row, *ahead):
        full, pack = attend_back(k, after(table, *ahead), qkv, grad, row)
        fulls.append(full)
        packs.append(across(pack))

    down_both = add_low(down_own, down_mate)
    back_step(0, grad_first, 0, down_both, out_terms)
    down_terms = lax.psum_scatter(down_both, "dp", scatter_dimension=1, tiled=True)
    rest_terms = jnp.concatenate([add_low(up_own, up_mate), add_low(out_terms[2:4], out_mate)], -1)
    rest_other = swap(rest_terms[1], 2)
    back_step(1, grad_rest, 0, rest_terms)
    rest_mine = add_low(rest_terms[0], after(rest_other, fulls[0])).reshape(dp_size, 192, 1024)
    rest_kept, rest_sent = pick(rest_mine, y, 96, 1), pick(rest_mine, 1 - y, 96, 1)
    rest_sent = swap(rest_sent, 4)
    down_terms = after(down_terms, fulls[0])
    down_kept, down_sent = pick(down_terms, y, 96, 1), pick(down_terms, 1 - y, 96, 1)
    down_sent = swap(down_sent, 4)
    back_step(2, grad_rest, 1, rest_kept, down_kept)
    rest_half = add_low(rest_kept, after(rest_sent, fulls[2]))
    down_half = add_low(down_kept, after(down_sent, fulls[2]))
    rest_grad = lax.psum_scatter(rest_half, "dp", scatter_dimension=0).astype(jnp.float32)
    up_grad, out_grad = rest_grad[:, 0:D], rest_grad[:, D : D + 192]
    down_grad = down_half[0].astype(jnp.float32) + swap(down_half[1], 2).astype(jnp.float32)
    fulls[2] = after(fulls[2], rest_half, down_half)

    shares = across(qkv_weight_grad(slots, fulls).reshape(dp_size * 2, 96, 640), ("dp", "seq"))
    qkv_grad = jnp.sum(shares.astype(jnp.float32), 0)[:, 0:576]
    input_grad, norm_one = last(packs, all_first, tokens, mid_grad, norm_params)

    reduced = (qkv_grad, out_grad.T, up_grad, down_grad)
    squares = sum((jnp.sum(item * item) for item in reduced))
    shared = jnp.concatenate(
        [norm_one[0:2], norm_two[0:2], jnp.full((1, D), squares), jnp.zeros((3, D), jnp.float32)], 0
    )
    distance = 1
    while distance < count:
        shared = shared + swap_every(shared, distance, count)
        distance *= 2
    norm_grads = shared[0:4]
    grad_norm = jnp.sqrt(shared[4, 0] + jnp.sum(norm_grads * norm_grads))
    factor = jnp.minimum(1.0, CLIP_NORM / (grad_norm + 1e-06))
    groups = (
        (qkv_weight, reduced[0], qkv_first, qkv_second, qkv_average),
        (out_weight, reduced[1], out_first, out_second, out_average),
        (up_weight, reduced[2], up_first, up_second, up_average),
        (down_weight.T, reduced[3], down_first.T, down_second.T, down_average.T),
    )
    stepped = matrix_steps(jnp.reshape(factor, (1,)), groups)
    stepped[3] = [item.T for item in stepped[3]]
    norm_step = adamw_moment_update(
        norm_params, norm_grads, norm_first, norm_second, norm_average, rates()[4], factor
    )
    results = []
    for n in range(4):
        results += [item[n] for item in stepped] + [norm_step[n]]
    copies = [item[4] for item in stepped]
    return (block_out, input_grad, grad_norm, *results, *copies, factor * norm_grads[2:])


def is_fast(mesh):
    sizes = dict(mesh.shape)
    return sizes["seq"] == 2 and sizes["head"] == 4 and sizes["dp"] == 4


def solution(mesh):
    return jax.shard_map(
        fast_body if is_fast(mesh) else body,
        mesh=mesh,
        in_specs=(
            P("dp", ("seq", "head"), None),
            P("dp", ("seq", "head"), None),
            P("head", "seq", None),
            P(),
            P(("dp", "seq"), "head"),
            P("head", ("dp", "seq")),
            P(("dp", "seq"), "head"),
            P("head", ("dp", "seq")),
            P(),
            P(("dp", "seq"), "head"),
            P("head", ("dp", "seq")),
            P(("dp", "seq"), "head"),
            P("head", ("dp", "seq")),
            P(),
            P(("dp", "seq"), "head"),
            P("head", ("dp", "seq")),
            P(("dp", "seq"), "head"),
            P("head", ("dp", "seq")),
            P(),
            P(("dp", "seq"), "head"),
            P("head", ("dp", "seq")),
            P(("dp", "seq"), "head"),
            P("head", ("dp", "seq")),
            P(),
        ),
        out_specs=(
            P("dp", ("seq", "head"), None),
            P("dp", ("seq", "head"), None),
            P(),
            P(("dp", "seq"), "head"),
            P("head", ("dp", "seq")),
            P(("dp", "seq"), "head"),
            P("head", ("dp", "seq")),
            P(),
            P(("dp", "seq"), "head"),
            P("head", ("dp", "seq")),
            P(("dp", "seq"), "head"),
            P("head", ("dp", "seq")),
            P(),
            P(("dp", "seq"), "head"),
            P("head", ("dp", "seq")),
            P(("dp", "seq"), "head"),
            P("head", ("dp", "seq")),
            P(),
            P(("dp", "seq"), "head"),
            P("head", ("dp", "seq")),
            P(("dp", "seq"), "head"),
            P("head", ("dp", "seq")),
            P(),
            P(("dp", "seq"), "head"),
            P("head", ("dp", "seq")),
            P(("dp", "seq"), "head"),
            P("head", ("dp", "seq")),
            P(),
        ),
        check_vma=False,
    )
```

```python
import jax
import jax.numpy as jnp
from jax import lax
from jax.experimental import pallas as pl
from jax.experimental.pallas import tpu as pltpu
from jax.sharding import PartitionSpec as P

D = 768
DH = 64
FF = 3072
BLOCK = 64
STEP = 10


EPSILON = 1e-05
BETA_ONE = 0.9
BETA_TWO = 0.999
DECAY = 0.01
SMALL = 1e-08
CLIP_NORM = 1.0
AVERAGING = 0.999
NEGATIVE = -1e30


def norm_rows(values, gain_row, shift_row):
    center = values - jnp.mean(values, -1, keepdims=True)
    spread = jnp.mean(center * center, -1, keepdims=True)
    return center * lax.rsqrt(spread + EPSILON) * gain_row + shift_row


def key_table(rand_local, global_blocks, first_block, blocks_total):
    head_count, local_blocks = (rand_local.shape[0], rand_local.shape[1])
    places = first_block + jnp.arange(local_blocks, dtype=jnp.int32)
    left_side = jnp.maximum(places - 1, 0)
    right_side = jnp.minimum(places + 1, blocks_total - 1)
    window = jnp.stack([left_side, places, right_side], -1)
    key_index = jnp.concatenate(
        [
            jnp.broadcast_to(window[None], (head_count, local_blocks, 3)),
            rand_local,
            jnp.broadcast_to(global_blocks[None, None], (head_count, local_blocks, 2)),
        ],
        -1,
    )
    column_one = jnp.ones((local_blocks, 1), jnp.float32)
    key_valid = jnp.concatenate(
        [
            (places > 0).astype(jnp.float32)[:, None],
            column_one,
            (places < blocks_total - 1).astype(jnp.float32)[:, None],
            jnp.ones((local_blocks, 5), jnp.float32),
        ],
        -1,
    )
    return (key_index, key_valid)


def gather_rows(values):
    return lax.all_gather(values, "head", axis=1, tiled=True)


def sum_rows(values):
    return lax.psum_scatter(values, "head", scatter_dimension=1, tiled=True)


def contract(left_operand, right_operand):
    return jnp.einsum(
        "enz,enf->zf", left_operand, right_operand, preferred_element_type=jnp.float32
    )


def to_heads(values, head_count):
    seq_count, token_count = (values.shape[0], values.shape[1])
    return jnp.moveaxis(
        values.reshape(seq_count, token_count // BLOCK, BLOCK, head_count, DH), 3, 0
    )


def from_heads(values):
    head_count, seq_count, blocks = (values.shape[0], values.shape[1], values.shape[2])
    return jnp.moveaxis(values, 0, 3).reshape(seq_count, blocks * BLOCK, head_count * DH)


def pick_keys(kv_all, key_index):
    seq_count, token_count = (kv_all.shape[0], kv_all.shape[1])
    head_count = key_index.shape[0]
    blocks = kv_all.reshape(seq_count, token_count // BLOCK, BLOCK, head_count, 2, DH)
    by_head = jnp.moveaxis(blocks, 3, 0)
    return jax.vmap(lambda source, chosen: source[:, chosen])(by_head, key_index)


def scores_of(queries, picked, key_valid):
    raw_scores = jnp.einsum(
        "hsnbe,hsnkce->hsnbkc", queries, picked[..., 0, :], preferred_element_type=jnp.float32
    ) * DH ** (-0.5)
    return jnp.where(key_valid[None, None, :, None, :, None] > 0, raw_scores, NEGATIVE)


def attend_forward(queries, picked, key_valid):
    raw_scores = scores_of(queries, picked, key_valid)
    score_shape = raw_scores.shape
    scores_flat = raw_scores.reshape(score_shape[:4] + (score_shape[4] * score_shape[5],))
    row_max = jnp.max(scores_flat, -1, keepdims=True)
    exponent = jnp.exp(scores_flat - row_max)
    row_total = jnp.sum(exponent, -1, keepdims=True)
    probabilities = (exponent / row_total).astype(jnp.bfloat16).reshape(score_shape)
    output = jnp.einsum(
        "hsnbkc,hsnkce->hsnbe", probabilities, picked[..., 1, :], preferred_element_type=jnp.float32
    )
    return (output, row_max + jnp.log(row_total))


def attend_backward(queries, picked, key_valid, log_total, grad_out):
    raw_scores = scores_of(queries, picked, key_valid)
    score_shape = raw_scores.shape
    scores_flat = raw_scores.reshape(score_shape[:4] + (score_shape[4] * score_shape[5],))
    probabilities = jnp.exp(scores_flat - log_total)
    grad_probs = jnp.einsum(
        "hsnbe,hsnkce->hsnbkc", grad_out, picked[..., 1, :], preferred_element_type=jnp.float32
    ).reshape(scores_flat.shape)
    row_delta = jnp.sum(probabilities * grad_probs, -1, keepdims=True)
    grad_scores = probabilities * (grad_probs - row_delta)
    grad_scores = grad_scores.astype(jnp.bfloat16).reshape(score_shape)
    low_probs = probabilities.astype(jnp.bfloat16).reshape(score_shape)
    grad_query = jnp.einsum(
        "hsnbkc,hsnkce->hsnbe", grad_scores, picked[..., 0, :], preferred_element_type=jnp.float32
    ) * DH ** (-0.5)
    grad_keys = jnp.einsum(
        "hsnbkc,hsnbe->hsnkce", grad_scores, queries, preferred_element_type=jnp.float32
    ) * DH ** (-0.5)
    grad_values = jnp.einsum(
        "hsnbkc,hsnbe->hsnkce", low_probs, grad_out, preferred_element_type=jnp.float32
    )
    return (grad_query, jnp.stack([grad_keys, grad_values], -2), row_delta)


def spread_back(grad_pairs, key_index, seq_count, blocks_total):
    head_count = key_index.shape[0]
    zero_grid = jnp.zeros((head_count, seq_count, blocks_total, BLOCK, 2, DH), jnp.float32)
    filled = jax.vmap(lambda source, chosen, addend: source.at[:, chosen].add(addend))(
        zero_grid, key_index, grad_pairs
    )
    return jnp.moveaxis(filled, 0, 3).reshape(seq_count, blocks_total * BLOCK, head_count * 2 * DH)


def rates():
    return (
        1.5 * D ** (-0.5),
        1.5 * max(1, D // (8 * BLOCK)) ** (-0.5),
        1.5 * D ** (-0.5),
        1.5 * FF ** (-0.5),
        0.5,
    )


def adamw_moment_update(weight, gradient, moment_one, moment_two, average, rate, factor):
    decay_mean = min(AVERAGING, (1.0 + STEP) / (10.0 + STEP))
    clipped = gradient * factor
    first_new = BETA_ONE * moment_one + (1.0 - BETA_ONE) * clipped
    second_new = BETA_TWO * moment_two + (1.0 - BETA_TWO) * clipped * clipped
    update = (
        first_new / (1.0 - BETA_ONE**STEP) / (jnp.sqrt(second_new / (1.0 - BETA_TWO**STEP)) + SMALL)
    )
    weight_new = weight - rate * (update + DECAY * weight)
    average_new = decay_mean * average + (1.0 - decay_mean) * weight_new
    return (weight_new, first_new, second_new, average_new)


def body(
    tokens,
    cotangent,
    rand_blocks,
    global_blocks,
    qkv_weight,
    out_weight,
    up_weight,
    down_weight,
    norm_params,
    qkv_first,
    out_first,
    up_first,
    down_first,
    norm_first,
    qkv_second,
    out_second,
    up_second,
    down_second,
    norm_second,
    qkv_average,
    out_average,
    up_average,
    down_average,
    norm_average,
):
    qkv_low, out_low, up_low, down_low = (
        lax.all_gather(qkv_weight.astype(jnp.bfloat16), ("dp", "seq"), axis=0, tiled=True),
        lax.all_gather(out_weight.astype(jnp.bfloat16), ("dp", "seq"), axis=1, tiled=True),
        lax.all_gather(up_weight.astype(jnp.bfloat16), ("dp", "seq"), axis=0, tiled=True),
        lax.all_gather(down_weight.astype(jnp.bfloat16), ("dp", "seq"), axis=1, tiled=True),
    )
    seq_count = tokens.shape[0]
    head_count = rand_blocks.shape[0]
    local_blocks = rand_blocks.shape[1]
    blocks_total = local_blocks * lax.axis_size("seq")
    first_block = lax.axis_index("seq") * local_blocks
    key_index, key_valid = key_table(rand_blocks, global_blocks, first_block, blocks_total)
    inputs = tokens.astype(jnp.float32)
    full_one = gather_rows(norm_rows(inputs, norm_params[0], norm_params[1]).astype(jnp.bfloat16))
    token_count = full_one.shape[1]
    qkv_all = jnp.dot(full_one, qkv_low, preferred_element_type=jnp.float32).astype(jnp.bfloat16)
    qkv_parts = qkv_all.reshape(seq_count, token_count, head_count, 3, DH)
    kv_local = qkv_parts[:, :, :, 1:, :].reshape(seq_count, token_count, head_count * 2 * DH)
    kv_all = lax.all_gather(kv_local, "seq", axis=1, tiled=True)
    picked = pick_keys(kv_all, key_index)
    queries = to_heads(qkv_parts[:, :, :, 0, :], head_count)
    attended, log_total = attend_forward(queries, picked, key_valid)
    mixed_heads = from_heads(attended.astype(jnp.bfloat16))
    residual = inputs + sum_rows(jnp.dot(mixed_heads, out_low, preferred_element_type=jnp.float32))
    full_two = gather_rows(norm_rows(residual, norm_params[2], norm_params[3]).astype(jnp.bfloat16))
    upward = jnp.dot(full_two, up_low, preferred_element_type=jnp.float32)
    active = jax.nn.gelu(upward).astype(jnp.bfloat16)
    result = residual + sum_rows(jnp.dot(active, down_low, preferred_element_type=jnp.float32))
    block_out = result.astype(jnp.bfloat16)
    grad_top = gather_rows(cotangent)
    grad_down = contract(active, grad_top)
    grad_active = jnp.dot(grad_top, down_low.T, preferred_element_type=jnp.float32)
    _, gelu_back = jax.vjp(jax.nn.gelu, upward)
    grad_upward = gelu_back(grad_active)[0].astype(jnp.bfloat16)
    grad_up = contract(full_two, grad_upward)
    part_two = sum_rows(jnp.dot(grad_upward, up_low.T, preferred_element_type=jnp.float32))
    _, norm_back_two = jax.vjp(norm_rows, residual, norm_params[2], norm_params[3])
    grad_residual_norm, grad_gain_two, grad_shift_two = norm_back_two(part_two)
    grad_residual = cotangent.astype(jnp.float32) + grad_residual_norm
    grad_middle = gather_rows(grad_residual.astype(jnp.bfloat16))
    grad_out = contract(mixed_heads, grad_middle)
    grad_mixed = jnp.dot(grad_middle, out_low.T, preferred_element_type=jnp.float32).astype(
        jnp.bfloat16
    )
    grad_query, grad_pairs, row_delta = attend_backward(
        queries, picked, key_valid, log_total, to_heads(grad_mixed, head_count)
    )
    grad_kv_full = spread_back(grad_pairs, key_index, seq_count, blocks_total)
    grad_kv = lax.psum_scatter(
        grad_kv_full.astype(jnp.bfloat16), "seq", scatter_dimension=1, tiled=True
    ).astype(jnp.float32)
    query_gradient = from_heads(grad_query).reshape(seq_count, token_count, head_count, 1, DH)
    grad_qkv_rows = jnp.concatenate(
        [query_gradient, grad_kv.reshape(seq_count, token_count, head_count, 2, DH)], 3
    )
    grad_qkv_rows = grad_qkv_rows.reshape(seq_count, token_count, head_count * 3 * DH).astype(
        jnp.bfloat16
    )
    grad_qkv = contract(full_one, grad_qkv_rows)
    part_one = sum_rows(jnp.dot(grad_qkv_rows, qkv_low.T, preferred_element_type=jnp.float32))
    _, norm_back_one = jax.vjp(norm_rows, inputs, norm_params[0], norm_params[1])
    grad_input_norm, grad_gain_one, grad_shift_one = norm_back_one(part_one)
    input_grad = (grad_residual + grad_input_norm).astype(jnp.bfloat16)
    grad_norm_local = jnp.stack([grad_gain_one, grad_shift_one, grad_gain_two, grad_shift_two])
    reduced_total = (
        lax.psum_scatter(grad_qkv, ("dp", "seq"), scatter_dimension=0, tiled=True),
        lax.psum_scatter(grad_out, ("dp", "seq"), scatter_dimension=1, tiled=True),
        lax.psum_scatter(grad_up, ("dp", "seq"), scatter_dimension=0, tiled=True),
        lax.psum_scatter(grad_down, ("dp", "seq"), scatter_dimension=1, tiled=True),
    )
    squares = sum((jnp.sum(item * item) for item in reduced_total))
    norm_grads = lax.psum(grad_norm_local, ("dp", "seq", "head"))
    matrix_squares = lax.psum(squares, ("dp", "seq", "head"))
    grad_norm = jnp.sqrt(matrix_squares + jnp.sum(norm_grads * norm_grads))
    factor = jnp.minimum(1.0, CLIP_NORM / (grad_norm + 1e-06))
    weights = (qkv_weight, out_weight, up_weight, down_weight, norm_params)
    gradients = (reduced_total[0], reduced_total[1], reduced_total[2], reduced_total[3], norm_grads)
    firsts = (qkv_first, out_first, up_first, down_first, norm_first)
    seconds = (qkv_second, out_second, up_second, down_second, norm_second)
    averages = (qkv_average, out_average, up_average, down_average, norm_average)
    results = [
        adamw_moment_update(
            weights[slot],
            gradients[slot],
            firsts[slot],
            seconds[slot],
            averages[slot],
            rates()[slot],
            factor,
        )
        for slot in range(5)
    ]
    news = tuple((item[0] for item in results))
    first_news = tuple((item[1] for item in results))
    second_news = tuple((item[2] for item in results))
    average_news = tuple((item[3] for item in results))
    return (
        block_out,
        input_grad,
        grad_norm,
        news[0],
        news[1],
        news[2],
        news[3],
        news[4],
        first_news[0],
        first_news[1],
        first_news[2],
        first_news[3],
        first_news[4],
        second_news[0],
        second_news[1],
        second_news[2],
        second_news[3],
        second_news[4],
        average_news[0],
        average_news[1],
        average_news[2],
        average_news[3],
        average_news[4],
        news[0].astype(jnp.bfloat16),
        news[1].astype(jnp.bfloat16),
        news[2].astype(jnp.bfloat16),
        news[3].astype(jnp.bfloat16),
        factor * norm_grads[2:],
    )


GROUP = ("seq", "head")
EVERY = ("dp", "seq", "head")
FULL = 4096
CHUNK = 512
MB = 1024 * 1024
COST = pl.CostEstimate(flops=10**6, bytes_accessed=10**5, transcendentals=0)


def limits(megabytes):
    return pltpu.CompilerParams(vmem_limit_bytes=megabytes * MB)


def swap(values, distance):
    return lax.ppermute(values, GROUP, [(i, i ^ distance) for i in range(8)])


def swap_every(values, distance, count):
    return lax.ppermute(values, EVERY, [(i, i ^ distance) for i in range(count)])


def nt(left, right):
    return lax.dot_general(left, right, (((1,), (1,)), ((), ())), preferred_element_type=jnp.float32)


def nn(left, right):
    return lax.dot_general(left, right, (((1,), (0,)), ((), ())), preferred_element_type=jnp.float32)


def tn(left, right):
    return lax.dot_general(left, right, (((0,), (0,)), ((), ())), preferred_element_type=jnp.float32)


def lane_low(shape):
    return lax.broadcasted_iota(jnp.int32, shape, len(shape) - 1) < 64


def roll64(values):
    return pltpu.roll(values, 64, 1)


def block_places(tab_ref, k, block):
    me = tab_ref[0]
    part = (block // 32) ^ (me // 4)
    base = 8 + ((part * 3 + k) * 32 + block % 32) * 3
    chosen = [
        jnp.maximum(block - 1, 0),
        block,
        jnp.minimum(block + 1, 63),
        tab_ref[base],
        tab_ref[base + 1],
        tab_ref[base + 2],
        tab_ref[1],
        tab_ref[2],
    ]
    return [pl.multiple_of((((b // 8) ^ me) * 8 + b % 8) * 64, 64) for b in chosen]


def spread_heads(wide):
    tile = lambda j: wide[:, j * 128 : j * 128 + 128]
    low = lane_low((wide.shape[0], 128))
    scale = DH ** (-0.5)
    return [
        jnp.where(low, tile(0) * scale, 0.0),
        jnp.where(low, roll64(tile(0)), roll64(tile(1))),
        jnp.where(low, roll64(tile(1)) * scale, 0.0),
        tile(2),
        jnp.where(low, tile(3) * scale, 0.0),
        jnp.where(low, roll64(tile(3)), roll64(tile(4))),
    ]


def qkv_kernel(*refs):
    tok_refs, weight_ref, out_ref = refs[:8], refs[8], refs[9]
    for slot, tok_ref in enumerate(tok_refs):
        for n, part in enumerate(spread_heads(nn(tok_ref[...], weight_ref[...]))):
            out_ref[slot * CHUNK : slot * CHUNK + CHUNK, n * 128 : n * 128 + 128] = part.astype(jnp.bfloat16)


def project(slots, weights):
    return pl.pallas_call(
        qkv_kernel,
        grid=(1,),
        in_specs=[pl.BlockSpec((CHUNK, D), lambda i: (0, 0))] * 8 + [pl.BlockSpec((D, 640), lambda i: (0, 0))],
        out_specs=pl.BlockSpec((FULL, D), lambda i: (0, 0)),
        out_shape=jax.ShapeDtypeStruct((FULL, D), jnp.bfloat16),
        compiler_params=limits(60),
        name="project",
        cost_estimate=COST,
    )(*slots, weights)


def hide(scores, low, high):
    lane = lax.broadcasted_iota(jnp.int32, scores.shape, 1)
    return jnp.where((lane >= low) & (lane < high), NEGATIVE, scores)


def softmax_rows(scores, part, q):
    if q == 0:
        scores = jnp.where(part == 0, hide(scores, 0, 64), scores)
    if q == 7:
        scores = jnp.where(part == 7, hide(scores, 128, 192), scores)
    top = jnp.max(scores, -1, keepdims=True)
    exponent = jnp.exp(scores - top)
    total = jnp.sum(exponent, -1, keepdims=True)
    return exponent * (1.0 / total)


def attend_kernel(k, tab_ref, qkv_ref, out_ref):
    me = tab_ref[0]

    def step(slot, carry):
        part = slot ^ me
        keys, scores = [], []
        for q in range(8):
            places = block_places(tab_ref, k, part * 8 + q)
            keys.append(jnp.concatenate([qkv_ref[pl.ds(p, 64), 128:256] for p in places], 0))
            at = pl.multiple_of(slot * CHUNK + q * 64, 64)
            scores.append(nt(qkv_ref[pl.ds(at, 64), 0:128], keys[q]))
        probs = [softmax_rows(scores[q], part, q).astype(jnp.bfloat16) for q in range(8)]
        outs = [nn(probs[q], keys[q]) for q in range(8)]
        for q in range(4):
            both = jnp.where(lane_low(outs[q].shape), roll64(outs[q]), outs[q + 4])
            out_ref[part, q * 64 : q * 64 + 64, :] = both.astype(jnp.bfloat16)
        return carry

    lax.fori_loop(0, 8, step, 0)


def attend(heads, table, qkv):
    first, count = heads[0], len(heads)

    def kernel(tab_ref, qkv_ref, out_ref):
        attend_kernel(pl.program_id(0) + first, tab_ref, qkv_ref, out_ref)

    return pl.pallas_call(
        kernel,
        grid_spec=pltpu.PrefetchScalarGridSpec(
            num_scalar_prefetch=1,
            grid=(count,),
            in_specs=[pl.BlockSpec((FULL, 256), lambda i, t: (0, first + i))],
            out_specs=pl.BlockSpec((8, 256, 128), lambda i, t: (0, i, 0)),
        ),
        out_shape=jax.ShapeDtypeStruct((8, 256 * count, 128), jnp.bfloat16),
        compiler_params=limits(60),
        name="attend",
        cost_estimate=COST,
    )(table, qkv)


def attend_back_kernel(k, tab_ref, qkv_ref, grad_ref, full_ref, pack_ref, acc_ref, shared_ref):
    me = tab_ref[0]
    acc_ref[...] = jnp.zeros_like(acc_ref)
    shared_ref[...] = jnp.zeros_like(shared_ref)

    def step(n, carry):
        slot, half = n // 2, n % 2
        part = slot ^ me
        picks = (0, 1, 4, 5)
        places, stacks, keys, both = [], [], [], []
        tiles = []
        for j in range(2):
            tile = grad_ref[part, pl.ds(pl.multiple_of(half * 128 + j * 64, 64), 64), :].astype(jnp.float32)
            low_lanes = lane_low(tile.shape)
            tiles.append(jnp.where(low_lanes, 0.0, roll64(tile)).astype(jnp.bfloat16))
            tiles.append(jnp.where(low_lanes, 0.0, tile).astype(jnp.bfloat16))
        grads = (tiles[0], tiles[2], tiles[1], tiles[3])
        for j, base in enumerate(picks):
            q = base + 2 * half
            places.append(block_places(tab_ref, k, part * 8 + q))
            keys.append(jnp.concatenate([qkv_ref[pl.ds(p, 64), 128:256] for p in places[j]], 0))
            at = pl.multiple_of(slot * CHUNK + q * 64, 64)
            stacks.append(jnp.concatenate([qkv_ref[pl.ds(at, 64), 0:128], grads[j]], 0))
            both.append(nt(stacks[j], keys[j]))
        lows, pairs = [], []
        for j in range(4):
            scores, grad_probs = both[j][:64], both[j][64:]
            if picks[j] == 0:
                scores = jnp.where((part == 0) & (half == 0), hide(scores, 0, 64), scores)
            if picks[j] == 5:
                scores = jnp.where((part == 7) & (half == 1), hide(scores, 128, 192), scores)
            probs = softmax_rows(scores, part, 1)
            delta = jnp.sum(probs * grad_probs, -1, keepdims=True)
            lows.append((probs * (grad_probs - delta)).astype(jnp.bfloat16))
            pairs.append(jnp.concatenate([lows[j], probs.astype(jnp.bfloat16)], 0))
        queries = []
        for j in range(4):
            grad_query = nn(lows[j], keys[j]) * DH ** (-0.5)
            queries.append(jnp.where(lane_low(grad_query.shape), grad_query, 0.0))
            at = pl.multiple_of(slot * CHUNK + (picks[j] + 2 * half) * 64, 64)
            full_ref[pl.ds(at, 64), 0:128] = queries[j].astype(jnp.bfloat16)
        spreads = [tn(pairs[j], stacks[j]) for j in range(4)]
        for j in range(4):
            for m in range(6):
                acc_ref[pl.ds(places[j][m], 64), :] += spreads[j][m * 64 : m * 64 + 64]
        shared_ref[...] += (spreads[0][384:] + spreads[1][384:]) + (spreads[2][384:] + spreads[3][384:])
        for j in range(2):
            packed = queries[j] + roll64(queries[j + 2])
            pack_ref[part, pl.ds(pl.multiple_of(half * 128 + j * 64, 64), 64), :] = packed.astype(jnp.bfloat16)
        return carry

    lax.fori_loop(0, 16, step, 0)
    for m in range(2):
        block = tab_ref[1 + m]
        at = pl.multiple_of((((block // 8) ^ me) * 8 + block % 8) * 64, 64)
        acc_ref[pl.ds(at, 64), :] += shared_ref[m * 64 : m * 64 + 64]

    def finish(slot, carry):
        at = pl.ds(pl.multiple_of(slot * CHUNK, CHUNK), CHUNK)
        low = acc_ref[at, :].astype(jnp.bfloat16)
        full_ref[at, 128:256] = low
        pack_ref[slot ^ me, 256:768, :] = low
        return carry

    lax.fori_loop(0, 8, finish, 0)


def attend_back(k, table, qkv, grad, row):
    return pl.pallas_call(
        lambda *refs: attend_back_kernel(k, *refs),
        grid_spec=pltpu.PrefetchScalarGridSpec(
            num_scalar_prefetch=1,
            grid=(1,),
            in_specs=[
                pl.BlockSpec((FULL, 256), lambda i, t: (0, k)),
                pl.BlockSpec((8, 256, 128), lambda i, t: (0, row, 0)),
            ],
            out_specs=[
                pl.BlockSpec((FULL, 256), lambda i, t: (0, 0)),
                pl.BlockSpec((8, 768, 128), lambda i, t: (0, 0, 0)),
            ],
            scratch_shapes=[pltpu.VMEM((FULL, 128), jnp.float32), pltpu.VMEM((128, 128), jnp.float32)],
        ),
        out_shape=[
            jax.ShapeDtypeStruct((FULL, 256), jnp.bfloat16),
            jax.ShapeDtypeStruct((8, 768, 128), jnp.bfloat16),
        ],
        compiler_params=limits(60),
        name="attend_back",
        cost_estimate=COST,
    )(table, qkv, grad)


def norm_stats(values):
    center = values - jnp.mean(values, -1, keepdims=True)
    spread = jnp.mean(center * center, -1, keepdims=True)
    scale = lax.rsqrt(spread + EPSILON)
    return center * scale, scale


def halves(first, second):
    low = lane_low(first.shape)
    upper = jnp.where(low, first, roll64(second))
    lower = jnp.where(low, roll64(first), second)
    return upper, lower


def mid_kernel(o0_ref, o1_ref, o2_ref, w_ref, tok_ref, par_ref, cat_ref, mid_ref, a2_ref, a2t_ref):
    middle = tok_ref[0].astype(jnp.float32)
    cat_ref[...] = jnp.zeros_like(cat_ref)
    for h in range(4):
        tiles = [ref[h, at : at + 256].astype(jnp.float32) for ref, at in ((o0_ref, 0), (o1_ref, 256), (o2_ref, 0))]
        upper, lower = halves(tiles[0], tiles[1])
        last_upper, last_lower = halves(tiles[2], jnp.zeros_like(tiles[2]))
        cat_ref[0:256, h * 256 : h * 256 + 128] = upper.astype(jnp.bfloat16)
        cat_ref[256:512, h * 256 : h * 256 + 128] = lower.astype(jnp.bfloat16)
        cat_ref[0:256, h * 256 + 128 : h * 256 + 256] = last_upper.astype(jnp.bfloat16)
        cat_ref[256:512, h * 256 + 128 : h * 256 + 256] = last_lower.astype(jnp.bfloat16)
        middle = middle + nt(cat_ref[:, h * 256 : h * 256 + 256], w_ref[h])
    mid_ref[0] = middle
    normed, _ = norm_stats(middle)
    low = normed * par_ref[2:3, :] + par_ref[3:4, :]
    a2_ref[...] = low.astype(jnp.bfloat16)
    a2t_ref[...] = low.T.astype(jnp.bfloat16)


def out_weight_spec():
    return pl.BlockSpec((4, D, 256), lambda s: (0, 0, 6))


def middle(o_pair, o_last, weights, tokens, params):
    seqs = tokens.shape[0]
    rows = pl.BlockSpec((1, CHUNK, D), lambda s: (s, 0, 0))
    return pl.pallas_call(
        mid_kernel,
        grid=(seqs,),
        in_specs=[
            pl.BlockSpec((4, 512, 128), lambda s: (s, 0, 0)),
            pl.BlockSpec((4, 512, 128), lambda s: (s, 0, 0)),
            pl.BlockSpec((4, 256, 128), lambda s: (s, 0, 0)),
            out_weight_spec(), rows, pl.BlockSpec((4, D), lambda s: (0, 0)),
        ],
        out_specs=[
            pl.BlockSpec((CHUNK, 1024), lambda s: (s, 0)), rows,
            pl.BlockSpec((CHUNK, D), lambda s: (s, 0)), pl.BlockSpec((D, CHUNK), lambda s: (0, s)),
        ],
        out_shape=[
            jax.ShapeDtypeStruct((seqs * CHUNK, 1024), jnp.bfloat16),
            jax.ShapeDtypeStruct(tokens.shape, jnp.float32),
            jax.ShapeDtypeStruct((seqs * CHUNK, D), jnp.bfloat16),
            jax.ShapeDtypeStruct((D, seqs * CHUNK), jnp.bfloat16),
        ],
        compiler_params=limits(60),
        name="middle",
        cost_estimate=COST,
    )(o_pair, o_pair, o_last, weights, tokens, params)


def group_of(head, i):
    return head ^ (i % 2 * 2 + 1 - i // 2)


def mlp_kernel(head_ref, a2_ref, a2t_ref, dy_ref, dyt_ref, mid_ref, wu_ref, wd_ref, out_ref, back_ref,
               um_ref, dm_ref, uo_ref, do_ref, g_ref, u_ref, wut_ref, wdt_ref, acc_ref):
    step = pl.program_id(0)

    @pl.when(step == 0)
    def _():
        acc_ref[...] = mid_ref[...]
        back_ref[...] = jnp.zeros_like(back_ref)

    wut_ref[...] = wu_ref[0].T
    wdt_ref[...] = wd_ref[0].T
    rate, cubic = 0.7978845608028654, 0.044715
    rows = [slice(m * 256, m * 256 + 256) for m in range(4)]
    products = lambda m: (nn(a2_ref[rows[m], :], wu_ref[0]), nn(dy_ref[rows[m], :], wd_ref[0]))
    ahead = products(0)
    for m in range(4):
        up, grad = ahead
        if m < 3:
            ahead = products(m + 1)
        at = rows[m]
        square = up * up
        bend = jnp.tanh(up * (rate + rate * cubic * square))
        half = 0.5 + 0.5 * bend
        g_ref[at, :] = (up * half).astype(jnp.bfloat16)
        slope = half + (0.5 * up) * (1.0 - bend * bend) * (rate + 3.0 * rate * cubic * square)
        u_ref[at, :] = (grad * slope).astype(jnp.bfloat16)
        acc_ref[at, :] += nn(g_ref[at, :], wdt_ref[...])
        back_ref[at, :] += nn(u_ref[at, :], wut_ref[...])
    up_grad = nn(a2t_ref[...], u_ref[...]).astype(jnp.bfloat16)
    down_grad = nn(dyt_ref[...], g_ref[...]).astype(jnp.bfloat16)

    @pl.when(step < 2)
    def _():
        um_ref[0] = up_grad
        dm_ref[0] = down_grad

    @pl.when(step >= 2)
    def _():
        uo_ref[0] = up_grad
        do_ref[0] = down_grad

    @pl.when(step == 3)
    def _():
        out_ref[...] = acc_ref[...].astype(jnp.bfloat16)


def mlp(head, a2, a2t, dy, dyt, mid, weights):
    tokens = a2.shape[0]
    whole = lambda shape: pl.BlockSpec(shape, lambda i, t: (0, 0))
    weight = lambda part: pl.BlockSpec((1, D, D), lambda i, t: (group_of(t[0], i), 0, part))
    theirs = pl.BlockSpec((1, D, D), lambda i, t: (jnp.minimum(i, 1), 0, 0))
    ours = pl.BlockSpec((1, D, D), lambda i, t: (jnp.maximum(i - 2, 0), 0, 0))
    low = jax.ShapeDtypeStruct((2, D, D), jnp.bfloat16)
    return pl.pallas_call(
        mlp_kernel,
        grid_spec=pltpu.PrefetchScalarGridSpec(
            num_scalar_prefetch=1,
            grid=(4,),
            in_specs=[
                whole((tokens, D)), whole((D, tokens)), whole((tokens, D)), whole((D, tokens)), whole((tokens, D)),
                weight(0), weight(1),
            ],
            out_specs=[whole((tokens, D)), whole((tokens, D)), theirs, theirs, ours, ours],
            scratch_shapes=[
                pltpu.VMEM((tokens, D), jnp.bfloat16), pltpu.VMEM((tokens, D), jnp.bfloat16),
                pltpu.VMEM((D, D), jnp.bfloat16), pltpu.VMEM((D, D), jnp.bfloat16), pltpu.VMEM((tokens, D), jnp.float32),
            ],
        ),
        out_shape=[
            jax.ShapeDtypeStruct((tokens, D), jnp.bfloat16), jax.ShapeDtypeStruct((tokens, D), jnp.float32),
            low, low, low, low,
        ],
        compiler_params=limits(60),
        name="mlp",
        cost_estimate=COST,
    )(head, a2, a2t, dy, dyt, mid, weights, weights)


def norm_back(grad, values, gain):
    normed, scale = norm_stats(values)
    gain_grad = jnp.sum(grad * normed, 0, keepdims=True)
    shift_grad = jnp.sum(grad, 0, keepdims=True)
    inner = grad * gain
    across = jnp.mean(inner, -1, keepdims=True)
    along = jnp.mean(inner * normed, -1, keepdims=True)
    return scale * (inner - across - normed * along), gain_grad, shift_grad


def mid_back_kernel(b_ref, mid_ref, dy_ref, w_ref, par_ref, grad_ref, low_ref, g0_ref, g1_ref, norm_ref):
    grad, gain_grad, shift_grad = norm_back(b_ref[...], mid_ref[0], par_ref[2:3, :])
    total = dy_ref[0].astype(jnp.float32) + grad
    grad_ref[0] = total
    low = total.astype(jnp.bfloat16)
    low_ref[...] = low
    for h in range(4):
        mixed = nn(low, w_ref[h])
        first, second = halves(mixed[0:256, 0:128], mixed[256:512, 0:128])
        third, _ = halves(mixed[0:256, 128:256], mixed[256:512, 128:256])
        g0_ref[h] = first.astype(jnp.bfloat16)
        g1_ref[h, 0:256] = second.astype(jnp.bfloat16)
        g1_ref[h, 256:512] = third.astype(jnp.bfloat16)

    @pl.when(pl.program_id(0) == 0)
    def _():
        norm_ref[...] = jnp.zeros_like(norm_ref)

    norm_ref[0:1, :] += gain_grad
    norm_ref[1:2, :] += shift_grad


def middle_back(back, mid, dy, weights, params):
    seqs = dy.shape[0]
    rows = pl.BlockSpec((1, CHUNK, D), lambda s: (s, 0, 0))
    flat = pl.BlockSpec((CHUNK, D), lambda s: (s, 0))
    return pl.pallas_call(
        mid_back_kernel,
        grid=(seqs,),
        in_specs=[flat, rows, rows, out_weight_spec(), pl.BlockSpec((4, D), lambda s: (0, 0))],
        out_specs=[
            rows, flat, pl.BlockSpec((4, 256, 128), lambda s: (s, 0, 0)),
            pl.BlockSpec((4, 512, 128), lambda s: (s, 0, 0)), pl.BlockSpec((8, D), lambda s: (0, 0)),
        ],
        out_shape=[
            jax.ShapeDtypeStruct(dy.shape, jnp.float32),
            jax.ShapeDtypeStruct((seqs * CHUNK, D), jnp.bfloat16),
            jax.ShapeDtypeStruct((8, 256, 128), jnp.bfloat16),
            jax.ShapeDtypeStruct((8, 512, 128), jnp.bfloat16),
            jax.ShapeDtypeStruct((8, D), jnp.float32),
        ],
        compiler_params=limits(60),
        name="middle_back",
        cost_estimate=COST,
    )(back, mid, dy, weights, params)


def out_grad_kernel(head_ref, low_ref, cat_ref, out_ref):
    for h in range(4):
        r = head_ref[0] ^ h
        out_ref[(1 - r % 2) * 2 + r // 2] = tn(low_ref[...], cat_ref[:, h * 256 : h * 256 + 256]).astype(jnp.bfloat16)


def out_weight_grad(head, low, cat):
    return pl.pallas_call(
        out_grad_kernel,
        grid_spec=pltpu.PrefetchScalarGridSpec(
            num_scalar_prefetch=1,
            grid=(1,),
            in_specs=[pl.BlockSpec(low.shape, lambda i, t: (0, 0)), pl.BlockSpec(cat.shape, lambda i, t: (0, 0))],
            out_specs=pl.BlockSpec((4, D, 256), lambda i, t: (0, 0, 0)),
        ),
        out_shape=jax.ShapeDtypeStruct((4, D, 256), jnp.bfloat16),
        compiler_params=limits(60),
        name="out_weight_grad",
        cost_estimate=COST,
    )(head, low, cat)


def merge_heads(queries, pairs):
    low = lane_low(queries[0].shape)
    return [
        jnp.where(low, queries[0], roll64(pairs[0])),
        jnp.where(low, roll64(pairs[0]), roll64(queries[1])),
        pairs[1],
        jnp.where(low, queries[2], roll64(pairs[2])),
        jnp.where(low, roll64(pairs[2]), 0.0),
    ]


def qkv_grad_kernel(*refs):
    tok_refs, full_refs, out_ref, acc_ref = refs[:8], refs[8:11], refs[11], refs[12]
    for slot, tok_ref in enumerate(tok_refs):
        at = slice(slot * CHUNK, slot * CHUNK + CHUNK)
        part = tn(tok_ref[...], jnp.concatenate([ref[at, :] for ref in full_refs], 1))
        acc_ref[...] = part if slot == 0 else acc_ref[...] + part
    tiles = merge_heads(
        [acc_ref[:, k * 256 : k * 256 + 128] for k in range(3)],
        [acc_ref[:, k * 256 + 128 : k * 256 + 256] for k in range(3)],
    )
    for j, tile in enumerate(tiles):
        out_ref[:, j * 128 : j * 128 + 128] = tile.astype(jnp.bfloat16)


def qkv_weight_grad(slots, fulls):
    return pl.pallas_call(
        qkv_grad_kernel,
        out_shape=jax.ShapeDtypeStruct((D, 640), jnp.bfloat16),
        scratch_shapes=[pltpu.VMEM((D, D), jnp.float32)],
        compiler_params=limits(60),
        name="qkv_weight_grad",
        cost_estimate=COST,
    )(*slots, *fulls)


def last_kernel(p0_ref, p1_ref, p2_ref, w_ref, tok_ref, mid_ref, par_ref, out_ref, norm_ref):
    grad = None
    for h in range(4):
        queries, pairs = [], []
        for ref in (p0_ref, p1_ref, p2_ref):
            both = ref[h, 0:256, :].astype(jnp.float32)
            queries.append(jnp.concatenate([both, roll64(both)], 0))
            pairs.append(ref[h, 256:768, :].astype(jnp.float32))
        wide = jnp.concatenate([tile.astype(jnp.bfloat16) for tile in merge_heads(queries, pairs)], 1)
        part = nt(wide, w_ref[h])
        grad = part if grad is None else grad + part
    back, gain_grad, shift_grad = norm_back(grad, tok_ref[0].astype(jnp.float32), par_ref[0:1, :])
    out_ref[0] = (mid_ref[0] + back).astype(jnp.bfloat16)

    @pl.when(pl.program_id(0) == 0)
    def _():
        norm_ref[...] = jnp.zeros_like(norm_ref)

    norm_ref[0:1, :] += gain_grad
    norm_ref[1:2, :] += shift_grad


def last(packs, weights, tokens, mid_grad, params):
    seqs = tokens.shape[0]
    piece = pl.BlockSpec((4, 768, 128), lambda s: (s, 0, 0))
    rows = pl.BlockSpec((1, CHUNK, D), lambda s: (s, 0, 0))
    return pl.pallas_call(
        last_kernel,
        grid=(seqs,),
        in_specs=[piece, piece, piece, pl.BlockSpec((4, D, 640), lambda s: (0, 0, 0)), rows, rows,
                  pl.BlockSpec((4, D), lambda s: (0, 0))],
        out_specs=[rows, pl.BlockSpec((8, D), lambda s: (0, 0))],
        out_shape=[jax.ShapeDtypeStruct(tokens.shape, jnp.bfloat16), jax.ShapeDtypeStruct((8, D), jnp.float32)],
        compiler_params=limits(60),
        name="last",
        cost_estimate=COST,
    )(*packs, weights, tokens, mid_grad, params)


def step_kernel(factor_ref, *refs):
    factor = factor_ref[0]
    for slot in range(4):
        weight, gradient, first, second, average = (ref[...] for ref in refs[slot * 5 : slot * 5 + 5])
        outs = refs[20 + slot * 5 : 25 + slot * 5]
        new, first, second, average = adamw_moment_update(
            weight, gradient, first, second, average, rates()[slot], factor
        )
        for ref, value in zip(outs, (new, first, second, average, new.astype(jnp.bfloat16))):
            ref[...] = value


def matrix_steps(factor, groups):
    blocks = [pl.BlockSpec((group[0].shape[0] // 3, group[0].shape[1]), lambda i, t: (i, 0)) for group in groups for _ in range(5)]
    shapes = [
        jax.ShapeDtypeStruct(group[0].shape, kind)
        for group in groups
        for kind in (jnp.float32,) * 4 + (jnp.bfloat16,)
    ]
    outs = pl.pallas_call(
        step_kernel,
        grid_spec=pltpu.PrefetchScalarGridSpec(num_scalar_prefetch=1, grid=(3,), in_specs=blocks, out_specs=blocks),
        out_shape=shapes,
        compiler_params=limits(60),
        name="matrix_steps",
        cost_estimate=COST,
    )(factor, *(item for group in groups for item in group))
    return [outs[n * 5 : n * 5 + 5] for n in range(4)]


def gather_mine(shard):
    return lax.all_gather(shard, ("dp", "seq"), axis=0, tiled=True)


def gather_heads(mine):
    return lax.all_gather(mine, "head", axis=0)


def pick(values, index, size, axis):
    return lax.dynamic_slice_in_dim(values, index * size, size, axis)


def after(value, *others):
    return lax.optimization_barrier((value, others))[0]


def add_low(left, right):
    return (left.astype(jnp.float32) + right.astype(jnp.float32)).astype(jnp.bfloat16)


def across(values, axes=GROUP):
    return lax.all_to_all(values, axes, 0, 0, tiled=True)


def fast_body(
    tokens, cotangent, rand_blocks, global_blocks, qkv_weight, out_weight, up_weight, down_weight, norm_params,
    qkv_first, out_first, up_first, down_first, norm_first,
    qkv_second, out_second, up_second, down_second, norm_second,
    qkv_average, out_average, up_average, down_average, norm_average,
):
    dp_size = lax.axis_size("dp")
    count = dp_size * 8
    y, head = lax.axis_index("seq"), lax.axis_index("head")
    me = y * 4 + head

    head_word = jnp.reshape(head, (1,)).astype(jnp.int32)

    turned = jnp.stack([pick(tokens, y, 1, 0)[0], pick(tokens, 1 - y, 1, 0)[0]])
    normed = norm_rows(turned.astype(jnp.float32), norm_params[0], norm_params[1]).astype(jnp.bfloat16)
    mine, theirs = normed[0], normed[1]
    even = [mine, swap(mine, 2), swap(theirs, 4), swap(theirs, 6)]
    odd = [swap(item, 1) for item in even]
    slots = [item for pair in zip(even, odd) for item in pair]

    low_qkv = qkv_weight.astype(jnp.bfloat16)
    blank = jnp.zeros((96, 64), jnp.bfloat16)
    shard = jnp.concatenate([low_qkv, blank], -1)
    count_rows = dp_size * 2
    mine_qkv = across(jnp.broadcast_to(shard[None], (count_rows,) + shard.shape), ("dp", "seq")).reshape(D, 640)
    rest = (up_weight, down_weight.T, out_weight.T)
    mine_rest = gather_mine(jnp.concatenate([item.astype(jnp.bfloat16) for item in rest] + [blank], -1))

    both_rand = jnp.concatenate([rand_blocks.reshape(-1), swap(rand_blocks.reshape(-1), 4)])
    table = jnp.concatenate(
        [jnp.reshape(me, (1,)), global_blocks, jnp.zeros((5,), jnp.int32), both_rand]
    ).astype(jnp.int32)
    qkv = project(slots, mine_qkv)
    all_rest = gather_heads(after(mine_rest, qkv))

    o_pair = attend((0, 1), table, qkv)
    o_pair = across(o_pair)
    o_last = across(after(attend((2,), table, qkv), o_pair))
    mixed, mid, a2, a2t = middle(o_pair, o_last, all_rest, tokens, norm_params)
    all_qkv = gather_heads(after(mine_qkv, a2))

    dy = cotangent.reshape(a2.shape)
    block_out, back, up_mate, down_mate, up_own, down_own = mlp(
        head_word, a2, a2t, dy, dy.T, mid.reshape(a2.shape), all_rest
    )
    block_out = block_out.reshape(tokens.shape)
    up_mate, down_mate = swap(up_mate, 1), swap(down_mate, 1)

    mid_grad, low_grad, grad_first, grad_rest, norm_two = middle_back(
        back, mid, cotangent, all_rest, after(norm_params, all_qkv)
    )
    up_mate, down_mate = after(up_mate, grad_first), after(down_mate, grad_first)
    grad_first, grad_rest = across(grad_first), across(grad_rest)
    out_terms = out_weight_grad(head_word, low_grad, mixed)
    out_mate = swap(out_terms[0:2], 1)

    fulls, packs = [], []

    def back_step(k, grad, row, *ahead):
        full, pack = attend_back(k, after(table, *ahead), qkv, grad, row)
        fulls.append(full)
        packs.append(across(pack))

    down_both = add_low(down_own, down_mate)
    down_terms = lax.psum_scatter(down_both, "dp", scatter_dimension=1, tiled=True)
    rest_terms = jnp.concatenate([add_low(up_own, up_mate), add_low(out_terms[2:4], out_mate)], -1)
    rest_other = swap(rest_terms[1], 2)
    back_step(0, grad_first, 0, down_both, rest_terms)
    back_step(1, grad_rest, 0, fulls[0])
    rest_mine = add_low(rest_terms[0], after(rest_other, fulls[1])).reshape(dp_size, 192, 1024)
    rest_kept, rest_sent = pick(rest_mine, y, 96, 1), pick(rest_mine, 1 - y, 96, 1)
    rest_sent = swap(rest_sent, 4)
    down_terms = after(down_terms, fulls[1])
    down_kept, down_sent = pick(down_terms, y, 96, 1), pick(down_terms, 1 - y, 96, 1)
    down_sent = swap(down_sent, 4)
    back_step(2, grad_rest, 1, rest_kept, down_kept)
    rest_half = add_low(rest_kept, after(rest_sent, fulls[2]))
    down_half = add_low(down_kept, after(down_sent, fulls[2]))
    rest_grad = lax.psum_scatter(rest_half, "dp", scatter_dimension=0).astype(jnp.float32)
    up_grad, out_grad = rest_grad[:, 0:D], rest_grad[:, D : D + 192]
    down_grad = down_half[0].astype(jnp.float32) + swap(down_half[1], 2).astype(jnp.float32)
    fulls[2] = after(fulls[2], rest_half, down_half)

    shares = across(qkv_weight_grad(slots, fulls).reshape(dp_size * 2, 96, 640), ("dp", "seq"))
    qkv_grad = jnp.sum(shares.astype(jnp.float32), 0)[:, 0:576]
    input_grad, norm_one = last(packs, all_qkv, tokens, mid_grad, norm_params)

    reduced = (qkv_grad, out_grad.T, up_grad, down_grad)
    squares = sum((jnp.sum(item * item) for item in reduced))
    shared = jnp.concatenate(
        [norm_one[0:2], norm_two[0:2], jnp.full((1, D), squares), jnp.zeros((3, D), jnp.float32)], 0
    )
    distance = 1
    while distance < count:
        shared = shared + swap_every(shared, distance, count)
        distance *= 2
    norm_grads = shared[0:4]
    grad_norm = jnp.sqrt(shared[4, 0] + jnp.sum(norm_grads * norm_grads))
    factor = jnp.minimum(1.0, CLIP_NORM / (grad_norm + 1e-06))
    groups = (
        (qkv_weight, reduced[0], qkv_first, qkv_second, qkv_average),
        (out_weight, reduced[1], out_first, out_second, out_average),
        (up_weight, reduced[2], up_first, up_second, up_average),
        (down_weight.T, reduced[3], down_first.T, down_second.T, down_average.T),
    )
    stepped = matrix_steps(jnp.reshape(factor, (1,)), groups)
    stepped[3] = [item.T for item in stepped[3]]
    norm_step = adamw_moment_update(
        norm_params, norm_grads, norm_first, norm_second, norm_average, rates()[4], factor
    )
    results = []
    for n in range(4):
        results += [item[n] for item in stepped] + [norm_step[n]]
    copies = [item[4] for item in stepped]
    return (block_out, input_grad, grad_norm, *results, *copies, factor * norm_grads[2:])


def is_fast(mesh):
    sizes = dict(mesh.shape)
    return sizes["seq"] == 2 and sizes["head"] == 4 and sizes["dp"] == 4


def solution(mesh):
    return jax.shard_map(
        fast_body if is_fast(mesh) else body,
        mesh=mesh,
        in_specs=(
            P("dp", ("seq", "head"), None),
            P("dp", ("seq", "head"), None),
            P("head", "seq", None),
            P(),
            P(("dp", "seq"), "head"),
            P("head", ("dp", "seq")),
            P(("dp", "seq"), "head"),
            P("head", ("dp", "seq")),
            P(),
            P(("dp", "seq"), "head"),
            P("head", ("dp", "seq")),
            P(("dp", "seq"), "head"),
            P("head", ("dp", "seq")),
            P(),
            P(("dp", "seq"), "head"),
            P("head", ("dp", "seq")),
            P(("dp", "seq"), "head"),
            P("head", ("dp", "seq")),
            P(),
            P(("dp", "seq"), "head"),
            P("head", ("dp", "seq")),
            P(("dp", "seq"), "head"),
            P("head", ("dp", "seq")),
            P(),
        ),
        out_specs=(
            P("dp", ("seq", "head"), None),
            P("dp", ("seq", "head"), None),
            P(),
            P(("dp", "seq"), "head"),
            P("head", ("dp", "seq")),
            P(("dp", "seq"), "head"),
            P("head", ("dp", "seq")),
            P(),
            P(("dp", "seq"), "head"),
            P("head", ("dp", "seq")),
            P(("dp", "seq"), "head"),
            P("head", ("dp", "seq")),
            P(),
            P(("dp", "seq"), "head"),
            P("head", ("dp", "seq")),
            P(("dp", "seq"), "head"),
            P("head", ("dp", "seq")),
            P(),
            P(("dp", "seq"), "head"),
            P("head", ("dp", "seq")),
            P(("dp", "seq"), "head"),
            P("head", ("dp", "seq")),
            P(),
            P(("dp", "seq"), "head"),
            P("head", ("dp", "seq")),
            P(("dp", "seq"), "head"),
            P("head", ("dp", "seq")),
            P(),
        ),
        check_vma=False,
    )
```

```python
import jax
import jax.numpy as jnp
from jax import lax
from jax.experimental import pallas as pl
from jax.experimental.pallas import tpu as pltpu
from jax.sharding import PartitionSpec as P

D = 768
DH = 64
FF = 3072
BLOCK = 64
STEP = 10


EPSILON = 1e-05
BETA_ONE = 0.9
BETA_TWO = 0.999
DECAY = 0.01
SMALL = 1e-08
CLIP_NORM = 1.0
AVERAGING = 0.999
NEGATIVE = -1e30


def norm_rows(values, gain_row, shift_row):
    center = values - jnp.mean(values, -1, keepdims=True)
    spread = jnp.mean(center * center, -1, keepdims=True)
    return center * lax.rsqrt(spread + EPSILON) * gain_row + shift_row


def key_table(rand_local, global_blocks, first_block, blocks_total):
    head_count, local_blocks = (rand_local.shape[0], rand_local.shape[1])
    places = first_block + jnp.arange(local_blocks, dtype=jnp.int32)
    left_side = jnp.maximum(places - 1, 0)
    right_side = jnp.minimum(places + 1, blocks_total - 1)
    window = jnp.stack([left_side, places, right_side], -1)
    key_index = jnp.concatenate(
        [
            jnp.broadcast_to(window[None], (head_count, local_blocks, 3)),
            rand_local,
            jnp.broadcast_to(global_blocks[None, None], (head_count, local_blocks, 2)),
        ],
        -1,
    )
    column_one = jnp.ones((local_blocks, 1), jnp.float32)
    key_valid = jnp.concatenate(
        [
            (places > 0).astype(jnp.float32)[:, None],
            column_one,
            (places < blocks_total - 1).astype(jnp.float32)[:, None],
            jnp.ones((local_blocks, 5), jnp.float32),
        ],
        -1,
    )
    return (key_index, key_valid)


def gather_rows(values):
    return lax.all_gather(values, "head", axis=1, tiled=True)


def sum_rows(values):
    return lax.psum_scatter(values, "head", scatter_dimension=1, tiled=True)


def contract(left_operand, right_operand):
    return jnp.einsum(
        "enz,enf->zf", left_operand, right_operand, preferred_element_type=jnp.float32
    )


def to_heads(values, head_count):
    seq_count, token_count = (values.shape[0], values.shape[1])
    return jnp.moveaxis(
        values.reshape(seq_count, token_count // BLOCK, BLOCK, head_count, DH), 3, 0
    )


def from_heads(values):
    head_count, seq_count, blocks = (values.shape[0], values.shape[1], values.shape[2])
    return jnp.moveaxis(values, 0, 3).reshape(seq_count, blocks * BLOCK, head_count * DH)


def pick_keys(kv_all, key_index):
    seq_count, token_count = (kv_all.shape[0], kv_all.shape[1])
    head_count = key_index.shape[0]
    blocks = kv_all.reshape(seq_count, token_count // BLOCK, BLOCK, head_count, 2, DH)
    by_head = jnp.moveaxis(blocks, 3, 0)
    return jax.vmap(lambda source, chosen: source[:, chosen])(by_head, key_index)


def scores_of(queries, picked, key_valid):
    raw_scores = jnp.einsum(
        "hsnbe,hsnkce->hsnbkc", queries, picked[..., 0, :], preferred_element_type=jnp.float32
    ) * DH ** (-0.5)
    return jnp.where(key_valid[None, None, :, None, :, None] > 0, raw_scores, NEGATIVE)


def attend_forward(queries, picked, key_valid):
    raw_scores = scores_of(queries, picked, key_valid)
    score_shape = raw_scores.shape
    scores_flat = raw_scores.reshape(score_shape[:4] + (score_shape[4] * score_shape[5],))
    row_max = jnp.max(scores_flat, -1, keepdims=True)
    exponent = jnp.exp(scores_flat - row_max)
    row_total = jnp.sum(exponent, -1, keepdims=True)
    probabilities = (exponent / row_total).astype(jnp.bfloat16).reshape(score_shape)
    output = jnp.einsum(
        "hsnbkc,hsnkce->hsnbe", probabilities, picked[..., 1, :], preferred_element_type=jnp.float32
    )
    return (output, row_max + jnp.log(row_total))


def attend_backward(queries, picked, key_valid, log_total, grad_out):
    raw_scores = scores_of(queries, picked, key_valid)
    score_shape = raw_scores.shape
    scores_flat = raw_scores.reshape(score_shape[:4] + (score_shape[4] * score_shape[5],))
    probabilities = jnp.exp(scores_flat - log_total)
    grad_probs = jnp.einsum(
        "hsnbe,hsnkce->hsnbkc", grad_out, picked[..., 1, :], preferred_element_type=jnp.float32
    ).reshape(scores_flat.shape)
    row_delta = jnp.sum(probabilities * grad_probs, -1, keepdims=True)
    grad_scores = probabilities * (grad_probs - row_delta)
    grad_scores = grad_scores.astype(jnp.bfloat16).reshape(score_shape)
    low_probs = probabilities.astype(jnp.bfloat16).reshape(score_shape)
    grad_query = jnp.einsum(
        "hsnbkc,hsnkce->hsnbe", grad_scores, picked[..., 0, :], preferred_element_type=jnp.float32
    ) * DH ** (-0.5)
    grad_keys = jnp.einsum(
        "hsnbkc,hsnbe->hsnkce", grad_scores, queries, preferred_element_type=jnp.float32
    ) * DH ** (-0.5)
    grad_values = jnp.einsum(
        "hsnbkc,hsnbe->hsnkce", low_probs, grad_out, preferred_element_type=jnp.float32
    )
    return (grad_query, jnp.stack([grad_keys, grad_values], -2), row_delta)


def spread_back(grad_pairs, key_index, seq_count, blocks_total):
    head_count = key_index.shape[0]
    zero_grid = jnp.zeros((head_count, seq_count, blocks_total, BLOCK, 2, DH), jnp.float32)
    filled = jax.vmap(lambda source, chosen, addend: source.at[:, chosen].add(addend))(
        zero_grid, key_index, grad_pairs
    )
    return jnp.moveaxis(filled, 0, 3).reshape(seq_count, blocks_total * BLOCK, head_count * 2 * DH)


def rates():
    return (
        1.5 * D ** (-0.5),
        1.5 * max(1, D // (8 * BLOCK)) ** (-0.5),
        1.5 * D ** (-0.5),
        1.5 * FF ** (-0.5),
        0.5,
    )


def adamw_moment_update(weight, gradient, moment_one, moment_two, average, rate, factor):
    decay_mean = min(AVERAGING, (1.0 + STEP) / (10.0 + STEP))
    clipped = gradient * factor
    first_new = BETA_ONE * moment_one + (1.0 - BETA_ONE) * clipped
    second_new = BETA_TWO * moment_two + (1.0 - BETA_TWO) * clipped * clipped
    update = (
        first_new / (1.0 - BETA_ONE**STEP) / (jnp.sqrt(second_new / (1.0 - BETA_TWO**STEP)) + SMALL)
    )
    weight_new = weight - rate * (update + DECAY * weight)
    average_new = decay_mean * average + (1.0 - decay_mean) * weight_new
    return (weight_new, first_new, second_new, average_new)


def body(
    tokens,
    cotangent,
    rand_blocks,
    global_blocks,
    qkv_weight,
    out_weight,
    up_weight,
    down_weight,
    norm_params,
    qkv_first,
    out_first,
    up_first,
    down_first,
    norm_first,
    qkv_second,
    out_second,
    up_second,
    down_second,
    norm_second,
    qkv_average,
    out_average,
    up_average,
    down_average,
    norm_average,
):
    qkv_low, out_low, up_low, down_low = (
        lax.all_gather(qkv_weight.astype(jnp.bfloat16), ("dp", "seq"), axis=0, tiled=True),
        lax.all_gather(out_weight.astype(jnp.bfloat16), ("dp", "seq"), axis=1, tiled=True),
        lax.all_gather(up_weight.astype(jnp.bfloat16), ("dp", "seq"), axis=0, tiled=True),
        lax.all_gather(down_weight.astype(jnp.bfloat16), ("dp", "seq"), axis=1, tiled=True),
    )
    seq_count = tokens.shape[0]
    head_count = rand_blocks.shape[0]
    local_blocks = rand_blocks.shape[1]
    blocks_total = local_blocks * lax.axis_size("seq")
    first_block = lax.axis_index("seq") * local_blocks
    key_index, key_valid = key_table(rand_blocks, global_blocks, first_block, blocks_total)
    inputs = tokens.astype(jnp.float32)
    full_one = gather_rows(norm_rows(inputs, norm_params[0], norm_params[1]).astype(jnp.bfloat16))
    token_count = full_one.shape[1]
    qkv_all = jnp.dot(full_one, qkv_low, preferred_element_type=jnp.float32).astype(jnp.bfloat16)
    qkv_parts = qkv_all.reshape(seq_count, token_count, head_count, 3, DH)
    kv_local = qkv_parts[:, :, :, 1:, :].reshape(seq_count, token_count, head_count * 2 * DH)
    kv_all = lax.all_gather(kv_local, "seq", axis=1, tiled=True)
    picked = pick_keys(kv_all, key_index)
    queries = to_heads(qkv_parts[:, :, :, 0, :], head_count)
    attended, log_total = attend_forward(queries, picked, key_valid)
    mixed_heads = from_heads(attended.astype(jnp.bfloat16))
    residual = inputs + sum_rows(jnp.dot(mixed_heads, out_low, preferred_element_type=jnp.float32))
    full_two = gather_rows(norm_rows(residual, norm_params[2], norm_params[3]).astype(jnp.bfloat16))
    upward = jnp.dot(full_two, up_low, preferred_element_type=jnp.float32)
    active = jax.nn.gelu(upward).astype(jnp.bfloat16)
    result = residual + sum_rows(jnp.dot(active, down_low, preferred_element_type=jnp.float32))
    block_out = result.astype(jnp.bfloat16)
    grad_top = gather_rows(cotangent)
    grad_down = contract(active, grad_top)
    grad_active = jnp.dot(grad_top, down_low.T, preferred_element_type=jnp.float32)
    _, gelu_back = jax.vjp(jax.nn.gelu, upward)
    grad_upward = gelu_back(grad_active)[0].astype(jnp.bfloat16)
    grad_up = contract(full_two, grad_upward)
    part_two = sum_rows(jnp.dot(grad_upward, up_low.T, preferred_element_type=jnp.float32))
    _, norm_back_two = jax.vjp(norm_rows, residual, norm_params[2], norm_params[3])
    grad_residual_norm, grad_gain_two, grad_shift_two = norm_back_two(part_two)
    grad_residual = cotangent.astype(jnp.float32) + grad_residual_norm
    grad_middle = gather_rows(grad_residual.astype(jnp.bfloat16))
    grad_out = contract(mixed_heads, grad_middle)
    grad_mixed = jnp.dot(grad_middle, out_low.T, preferred_element_type=jnp.float32).astype(
        jnp.bfloat16
    )
    grad_query, grad_pairs, row_delta = attend_backward(
        queries, picked, key_valid, log_total, to_heads(grad_mixed, head_count)
    )
    grad_kv_full = spread_back(grad_pairs, key_index, seq_count, blocks_total)
    grad_kv = lax.psum_scatter(
        grad_kv_full.astype(jnp.bfloat16), "seq", scatter_dimension=1, tiled=True
    ).astype(jnp.float32)
    query_gradient = from_heads(grad_query).reshape(seq_count, token_count, head_count, 1, DH)
    grad_qkv_rows = jnp.concatenate(
        [query_gradient, grad_kv.reshape(seq_count, token_count, head_count, 2, DH)], 3
    )
    grad_qkv_rows = grad_qkv_rows.reshape(seq_count, token_count, head_count * 3 * DH).astype(
        jnp.bfloat16
    )
    grad_qkv = contract(full_one, grad_qkv_rows)
    part_one = sum_rows(jnp.dot(grad_qkv_rows, qkv_low.T, preferred_element_type=jnp.float32))
    _, norm_back_one = jax.vjp(norm_rows, inputs, norm_params[0], norm_params[1])
    grad_input_norm, grad_gain_one, grad_shift_one = norm_back_one(part_one)
    input_grad = (grad_residual + grad_input_norm).astype(jnp.bfloat16)
    grad_norm_local = jnp.stack([grad_gain_one, grad_shift_one, grad_gain_two, grad_shift_two])
    reduced_total = (
        lax.psum_scatter(grad_qkv, ("dp", "seq"), scatter_dimension=0, tiled=True),
        lax.psum_scatter(grad_out, ("dp", "seq"), scatter_dimension=1, tiled=True),
        lax.psum_scatter(grad_up, ("dp", "seq"), scatter_dimension=0, tiled=True),
        lax.psum_scatter(grad_down, ("dp", "seq"), scatter_dimension=1, tiled=True),
    )
    squares = sum((jnp.sum(item * item) for item in reduced_total))
    norm_grads = lax.psum(grad_norm_local, ("dp", "seq", "head"))
    matrix_squares = lax.psum(squares, ("dp", "seq", "head"))
    grad_norm = jnp.sqrt(matrix_squares + jnp.sum(norm_grads * norm_grads))
    factor = jnp.minimum(1.0, CLIP_NORM / (grad_norm + 1e-06))
    weights = (qkv_weight, out_weight, up_weight, down_weight, norm_params)
    gradients = (reduced_total[0], reduced_total[1], reduced_total[2], reduced_total[3], norm_grads)
    firsts = (qkv_first, out_first, up_first, down_first, norm_first)
    seconds = (qkv_second, out_second, up_second, down_second, norm_second)
    averages = (qkv_average, out_average, up_average, down_average, norm_average)
    results = [
        adamw_moment_update(
            weights[slot],
            gradients[slot],
            firsts[slot],
            seconds[slot],
            averages[slot],
            rates()[slot],
            factor,
        )
        for slot in range(5)
    ]
    news = tuple((item[0] for item in results))
    first_news = tuple((item[1] for item in results))
    second_news = tuple((item[2] for item in results))
    average_news = tuple((item[3] for item in results))
    return (
        block_out,
        input_grad,
        grad_norm,
        news[0],
        news[1],
        news[2],
        news[3],
        news[4],
        first_news[0],
        first_news[1],
        first_news[2],
        first_news[3],
        first_news[4],
        second_news[0],
        second_news[1],
        second_news[2],
        second_news[3],
        second_news[4],
        average_news[0],
        average_news[1],
        average_news[2],
        average_news[3],
        average_news[4],
        news[0].astype(jnp.bfloat16),
        news[1].astype(jnp.bfloat16),
        news[2].astype(jnp.bfloat16),
        news[3].astype(jnp.bfloat16),
        factor * norm_grads[2:],
    )


GROUP = ("seq", "head")
EVERY = ("dp", "seq", "head")
FULL = 4096
CHUNK = 512
MB = 1024 * 1024
COST = pl.CostEstimate(flops=10**6, bytes_accessed=10**5, transcendentals=0)


def limits(megabytes):
    return pltpu.CompilerParams(vmem_limit_bytes=megabytes * MB)


def swap(values, distance):
    return lax.ppermute(values, GROUP, [(i, i ^ distance) for i in range(8)])


def swap_every(values, distance, count):
    return lax.ppermute(values, EVERY, [(i, i ^ distance) for i in range(count)])


def nt(left, right):
    return lax.dot_general(left, right, (((1,), (1,)), ((), ())), preferred_element_type=jnp.float32)


def nn(left, right):
    return lax.dot_general(left, right, (((1,), (0,)), ((), ())), preferred_element_type=jnp.float32)


def tn(left, right):
    return lax.dot_general(left, right, (((0,), (0,)), ((), ())), preferred_element_type=jnp.float32)


def lane_low(shape):
    return lax.broadcasted_iota(jnp.int32, shape, len(shape) - 1) < 64


def roll64(values):
    return pltpu.roll(values, 64, 1)


def block_places(tab_ref, k, block):
    me = tab_ref[0]
    part = (block // 32) ^ (me // 4)
    base = 8 + ((part * 3 + k) * 32 + block % 32) * 3
    chosen = [
        jnp.maximum(block - 1, 0),
        block,
        jnp.minimum(block + 1, 63),
        tab_ref[base],
        tab_ref[base + 1],
        tab_ref[base + 2],
        tab_ref[1],
        tab_ref[2],
    ]
    return [pl.multiple_of((((b // 8) ^ me) * 8 + b % 8) * 64, 64) for b in chosen]


def spread_heads(wide):
    tile = lambda j: wide[:, j * 128 : j * 128 + 128]
    low = lane_low((wide.shape[0], 128))
    scale = DH ** (-0.5)
    return [
        jnp.where(low, tile(0) * scale, 0.0),
        jnp.where(low, roll64(tile(0)), roll64(tile(1))),
        jnp.where(low, roll64(tile(1)) * scale, 0.0),
        tile(2),
        jnp.where(low, tile(3) * scale, 0.0),
        jnp.where(low, roll64(tile(3)), roll64(tile(4))),
    ]


def qkv_kernel(*refs):
    tok_refs, weight_ref, out_ref = refs[:8], refs[8], refs[9]

    def one(tok_ref):
        for n, part in enumerate(spread_heads(nn(tok_ref[...], weight_ref[...]))):
            out_ref[:, n * 128 : n * 128 + 128] = part.astype(jnp.bfloat16)

    for slot, tok_ref in enumerate(tok_refs):
        pl.when(pl.program_id(0) == slot)(lambda tok_ref=tok_ref: one(tok_ref))


def project(slots, weights):
    return pl.pallas_call(
        qkv_kernel,
        grid=(8,),
        in_specs=[pl.BlockSpec((CHUNK, D), lambda i: (0, 0))] * 8 + [pl.BlockSpec((D, 640), lambda i: (0, 0))],
        out_specs=pl.BlockSpec((CHUNK, D), lambda i: (i, 0)),
        out_shape=jax.ShapeDtypeStruct((FULL, D), jnp.bfloat16),
        compiler_params=limits(60),
        name="project",
        cost_estimate=COST,
    )(*slots, weights)


def hide(scores, low, high):
    lane = lax.broadcasted_iota(jnp.int32, scores.shape, 1)
    return jnp.where((lane >= low) & (lane < high), NEGATIVE, scores)


def softmax_rows(scores, part, q):
    if q == 0:
        scores = jnp.where(part == 0, hide(scores, 0, 64), scores)
    if q == 7:
        scores = jnp.where(part == 7, hide(scores, 128, 192), scores)
    top = jnp.max(scores, -1, keepdims=True)
    exponent = jnp.exp(scores - top)
    total = jnp.sum(exponent, -1, keepdims=True)
    return exponent * (1.0 / total)


def attend_kernel(k, tab_ref, qkv_ref, out_ref):
    me = tab_ref[0]

    def step(slot, carry):
        part = slot ^ me
        keys, scores = [], []
        for q in range(8):
            places = block_places(tab_ref, k, part * 8 + q)
            keys.append(jnp.concatenate([qkv_ref[pl.ds(p, 64), 128:256] for p in places], 0))
            at = pl.multiple_of(slot * CHUNK + q * 64, 64)
            scores.append(nt(qkv_ref[pl.ds(at, 64), 0:128], keys[q]))
        probs = [softmax_rows(scores[q], part, q).astype(jnp.bfloat16) for q in range(8)]
        outs = [nn(probs[q], keys[q]) for q in range(8)]
        for q in range(4):
            both = jnp.where(lane_low(outs[q].shape), roll64(outs[q]), outs[q + 4])
            out_ref[part, q * 64 : q * 64 + 64, :] = both.astype(jnp.bfloat16)
        return carry

    lax.fori_loop(0, 8, step, 0)


def attend(table, qkv):
    return pl.pallas_call(
        lambda *refs: attend_kernel(pl.program_id(0), *refs),
        grid_spec=pltpu.PrefetchScalarGridSpec(
            num_scalar_prefetch=1,
            grid=(3,),
            in_specs=[pl.BlockSpec((FULL, 256), lambda i, t: (0, i))],
            out_specs=pl.BlockSpec((8, 256, 128), lambda i, t: (0, i, 0)),
        ),
        out_shape=jax.ShapeDtypeStruct((8, D, 128), jnp.bfloat16),
        compiler_params=limits(60),
        name="attend",
        cost_estimate=COST,
    )(table, qkv)


def attend_back_kernel(k, tab_ref, qkv_ref, grad_ref, full_ref, pack_ref, acc_ref, shared_ref):
    me = tab_ref[0]
    acc_ref[...] = jnp.zeros_like(acc_ref)
    shared_ref[...] = jnp.zeros_like(shared_ref)

    def step(n, carry):
        slot, half = n // 2, n % 2
        part = slot ^ me
        picks = (0, 1, 4, 5)
        places, stacks, keys, both = [], [], [], []
        tiles = []
        for j in range(2):
            tile = grad_ref[part, pl.ds(pl.multiple_of(half * 128 + j * 64, 64), 64), :].astype(jnp.float32)
            low_lanes = lane_low(tile.shape)
            tiles.append(jnp.where(low_lanes, 0.0, roll64(tile)).astype(jnp.bfloat16))
            tiles.append(jnp.where(low_lanes, 0.0, tile).astype(jnp.bfloat16))
        grads = (tiles[0], tiles[2], tiles[1], tiles[3])
        for j, base in enumerate(picks):
            q = base + 2 * half
            places.append(block_places(tab_ref, k, part * 8 + q))
            keys.append(jnp.concatenate([qkv_ref[pl.ds(p, 64), 128:256] for p in places[j]], 0))
            at = pl.multiple_of(slot * CHUNK + q * 64, 64)
            stacks.append(jnp.concatenate([qkv_ref[pl.ds(at, 64), 0:128], grads[j]], 0))
            both.append(nt(stacks[j], keys[j]))
        lows, pairs = [], []
        for j in range(4):
            scores, grad_probs = both[j][:64], both[j][64:]
            if picks[j] == 0:
                scores = jnp.where((part == 0) & (half == 0), hide(scores, 0, 64), scores)
            if picks[j] == 5:
                scores = jnp.where((part == 7) & (half == 1), hide(scores, 128, 192), scores)
            probs = softmax_rows(scores, part, 1)
            delta = jnp.sum(probs * grad_probs, -1, keepdims=True)
            lows.append((probs * (grad_probs - delta)).astype(jnp.bfloat16))
            pairs.append(jnp.concatenate([lows[j], probs.astype(jnp.bfloat16)], 0))
        queries = []
        for j in range(4):
            grad_query = nn(lows[j], keys[j]) * DH ** (-0.5)
            queries.append(jnp.where(lane_low(grad_query.shape), grad_query, 0.0))
            at = pl.multiple_of(slot * CHUNK + (picks[j] + 2 * half) * 64, 64)
            full_ref[pl.ds(at, 64), 0:128] = queries[j].astype(jnp.bfloat16)
        spreads = [tn(pairs[j], stacks[j]) for j in range(4)]
        for j in range(4):
            for m in range(6):
                acc_ref[pl.ds(places[j][m], 64), :] += spreads[j][m * 64 : m * 64 + 64]
        shared_ref[...] += (spreads[0][384:] + spreads[1][384:]) + (spreads[2][384:] + spreads[3][384:])
        for j in range(2):
            packed = queries[j] + roll64(queries[j + 2])
            pack_ref[part, pl.ds(pl.multiple_of(half * 128 + j * 64, 64), 64), :] = packed.astype(jnp.bfloat16)
        return carry

    lax.fori_loop(0, 16, step, 0)
    for m in range(2):
        block = tab_ref[1 + m]
        at = pl.multiple_of((((block // 8) ^ me) * 8 + block % 8) * 64, 64)
        acc_ref[pl.ds(at, 64), :] += shared_ref[m * 64 : m * 64 + 64]

    def finish(slot, carry):
        at = pl.ds(pl.multiple_of(slot * CHUNK, CHUNK), CHUNK)
        low = acc_ref[at, :].astype(jnp.bfloat16)
        full_ref[at, 128:256] = low
        pack_ref[slot ^ me, 256:768, :] = low
        return carry

    lax.fori_loop(0, 8, finish, 0)


def attend_back(k, table, qkv, grad):
    return pl.pallas_call(
        lambda *refs: attend_back_kernel(k, *refs),
        grid_spec=pltpu.PrefetchScalarGridSpec(
            num_scalar_prefetch=1,
            grid=(1,),
            in_specs=[
                pl.BlockSpec((FULL, 256), lambda i, t: (0, k)),
                pl.BlockSpec((8, 256, 128), lambda i, t: (0, k, 0)),
            ],
            out_specs=[
                pl.BlockSpec((FULL, 256), lambda i, t: (0, 0)),
                pl.BlockSpec((8, 768, 128), lambda i, t: (0, 0, 0)),
            ],
            scratch_shapes=[pltpu.VMEM((FULL, 128), jnp.float32), pltpu.VMEM((128, 128), jnp.float32)],
        ),
        out_shape=[
            jax.ShapeDtypeStruct((FULL, 256), jnp.bfloat16),
            jax.ShapeDtypeStruct((8, 768, 128), jnp.bfloat16),
        ],
        compiler_params=limits(60),
        name="attend_back",
        cost_estimate=COST,
    )(table, qkv, grad)


def norm_stats(values):
    center = values - jnp.mean(values, -1, keepdims=True)
    spread = jnp.mean(center * center, -1, keepdims=True)
    scale = lax.rsqrt(spread + EPSILON)
    return center * scale, scale


def halves(first, second):
    low = lane_low(first.shape)
    upper = jnp.where(low, first, roll64(second))
    lower = jnp.where(low, roll64(first), second)
    return upper, lower


def mid_kernel(o_ref, w_ref, tok_ref, par_ref, cat_ref, mid_ref, a2_ref, a2t_ref):
    middle = tok_ref[0].astype(jnp.float32)
    cat_ref[...] = jnp.zeros_like(cat_ref)
    for h in range(4):
        tiles = [o_ref[h, at : at + 256].astype(jnp.float32) for at in (0, 256, 512)]
        upper, lower = halves(tiles[0], tiles[1])
        last_upper, last_lower = halves(tiles[2], jnp.zeros_like(tiles[2]))
        cat_ref[0:256, h * 256 : h * 256 + 128] = upper.astype(jnp.bfloat16)
        cat_ref[256:512, h * 256 : h * 256 + 128] = lower.astype(jnp.bfloat16)
        cat_ref[0:256, h * 256 + 128 : h * 256 + 256] = last_upper.astype(jnp.bfloat16)
        cat_ref[256:512, h * 256 + 128 : h * 256 + 256] = last_lower.astype(jnp.bfloat16)
        middle = middle + nt(cat_ref[:, h * 256 : h * 256 + 256], ordered(w_ref, h))
    mid_ref[0] = middle
    normed, _ = norm_stats(middle)
    low = normed * par_ref[2:3, :] + par_ref[3:4, :]
    a2_ref[...] = low.astype(jnp.bfloat16)
    a2t_ref[...] = low.T.astype(jnp.bfloat16)


def ordered(ref, h):
    return jnp.concatenate([ref[y, h, d] for d in range(ref.shape[2]) for y in range(2)], 0)


def out_weight_spec(dp_size):
    return pl.BlockSpec((2, 4, dp_size, 96, 256), lambda s: (0, 0, 0, 0, 6))


def middle(o_parts, weights, tokens, params):
    seqs = tokens.shape[0]
    rows = pl.BlockSpec((1, CHUNK, D), lambda s: (s, 0, 0))
    return pl.pallas_call(
        mid_kernel,
        grid=(seqs,),
        in_specs=[
            pl.BlockSpec((4, D, 128), lambda s: (s, 0, 0)),
            out_weight_spec(weights.shape[2]), rows, pl.BlockSpec((4, D), lambda s: (0, 0)),
        ],
        out_specs=[
            pl.BlockSpec((CHUNK, 1024), lambda s: (s, 0)), rows,
            pl.BlockSpec((CHUNK, D), lambda s: (s, 0)), pl.BlockSpec((D, CHUNK), lambda s: (0, s)),
        ],
        out_shape=[
            jax.ShapeDtypeStruct((seqs * CHUNK, 1024), jnp.bfloat16),
            jax.ShapeDtypeStruct(tokens.shape, jnp.float32),
            jax.ShapeDtypeStruct((seqs * CHUNK, D), jnp.bfloat16),
            jax.ShapeDtypeStruct((D, seqs * CHUNK), jnp.bfloat16),
        ],
        compiler_params=limits(60),
        name="middle",
        cost_estimate=COST,
    )(o_parts, weights, tokens, params)


def group_of(head, i):
    return head ^ (i % 2 * 2 + 1 - i // 2)


def mlp_kernel(head_ref, a2_ref, a2t_ref, dy_ref, dyt_ref, mid_ref, wu_ref, wd_ref, out_ref, back_ref,
               um_ref, dm_ref, uo_ref, do_ref, g_ref, u_ref, wuo_ref, wdo_ref, wut_ref, wdt_ref, acc_ref):
    step = pl.program_id(0)

    @pl.when(step == 0)
    def _():
        acc_ref[...] = mid_ref[...]
        back_ref[...] = jnp.zeros_like(back_ref)

    wuo_ref[...] = ordered(wu_ref, 0)
    wdo_ref[...] = ordered(wd_ref, 0)
    wut_ref[...] = wuo_ref[...].T
    wdt_ref[...] = wdo_ref[...].T
    rate, cubic = 0.7978845608028654, 0.044715
    rows = [slice(m * 256, m * 256 + 256) for m in range(4)]
    products = lambda m: (nn(a2_ref[rows[m], :], wuo_ref[...]), nn(dy_ref[rows[m], :], wdo_ref[...]))
    ahead = products(0)
    for m in range(4):
        up, grad = ahead
        if m < 3:
            ahead = products(m + 1)
        at = rows[m]
        square = up * up
        bend = jnp.tanh(up * (rate + rate * cubic * square))
        half = 0.5 + 0.5 * bend
        g_ref[at, :] = (up * half).astype(jnp.bfloat16)
        slope = half + (0.5 * up) * (1.0 - bend * bend) * (rate + 3.0 * rate * cubic * square)
        u_ref[at, :] = (grad * slope).astype(jnp.bfloat16)
        acc_ref[at, :] += nn(g_ref[at, :], wdt_ref[...])
        back_ref[at, :] += nn(u_ref[at, :], wut_ref[...])
    up_grad = nn(a2t_ref[...], u_ref[...]).astype(jnp.bfloat16)
    down_grad = nn(dyt_ref[...], g_ref[...]).astype(jnp.bfloat16)

    @pl.when(step < 2)
    def _():
        um_ref[0] = up_grad
        dm_ref[0] = down_grad

    @pl.when(step >= 2)
    def _():
        uo_ref[0] = up_grad
        do_ref[0] = down_grad

    @pl.when(step == 3)
    def _():
        out_ref[...] = acc_ref[...].astype(jnp.bfloat16)


def mlp(head, a2, a2t, dy, dyt, mid, weights):
    tokens = a2.shape[0]
    whole = lambda shape: pl.BlockSpec(shape, lambda i, t: (0, 0))
    weight = lambda part: pl.BlockSpec(
        (2, 1, weights.shape[2], 96, D), lambda i, t: (0, group_of(t[0], i), 0, 0, part)
    )
    theirs = pl.BlockSpec((1, D, D), lambda i, t: (jnp.minimum(i, 1), 0, 0))
    ours = pl.BlockSpec((1, D, D), lambda i, t: (jnp.maximum(i - 2, 0), 0, 0))
    low = jax.ShapeDtypeStruct((2, D, D), jnp.bfloat16)
    return pl.pallas_call(
        mlp_kernel,
        grid_spec=pltpu.PrefetchScalarGridSpec(
            num_scalar_prefetch=1,
            grid=(4,),
            in_specs=[
                whole((tokens, D)), whole((D, tokens)), whole((tokens, D)), whole((D, tokens)), whole((tokens, D)),
                weight(0), weight(1),
            ],
            out_specs=[whole((tokens, D)), whole((tokens, D)), theirs, theirs, ours, ours],
            scratch_shapes=[
                pltpu.VMEM((tokens, D), jnp.bfloat16), pltpu.VMEM((tokens, D), jnp.bfloat16),
                *(pltpu.VMEM((D, D), jnp.bfloat16) for _ in range(4)), pltpu.VMEM((tokens, D), jnp.float32),
            ],
        ),
        out_shape=[
            jax.ShapeDtypeStruct((tokens, D), jnp.bfloat16), jax.ShapeDtypeStruct((tokens, D), jnp.float32),
            low, low, low, low,
        ],
        compiler_params=limits(60),
        name="mlp",
        cost_estimate=COST,
    )(head, a2, a2t, dy, dyt, mid, weights, weights)


def norm_back(grad, values, gain):
    normed, scale = norm_stats(values)
    gain_grad = jnp.sum(grad * normed, 0, keepdims=True)
    shift_grad = jnp.sum(grad, 0, keepdims=True)
    inner = grad * gain
    across = jnp.mean(inner, -1, keepdims=True)
    along = jnp.mean(inner * normed, -1, keepdims=True)
    return scale * (inner - across - normed * along), gain_grad, shift_grad


def mid_back_kernel(b_ref, mid_ref, dy_ref, w_ref, par_ref, grad_ref, low_ref, parts_ref, norm_ref):
    grad, gain_grad, shift_grad = norm_back(b_ref[...], mid_ref[0], par_ref[2:3, :])
    total = dy_ref[0].astype(jnp.float32) + grad
    grad_ref[0] = total
    low = total.astype(jnp.bfloat16)
    low_ref[...] = low
    for h in range(4):
        mixed = nn(low, ordered(w_ref, h))
        first, second = halves(mixed[0:256, 0:128], mixed[256:512, 0:128])
        third, _ = halves(mixed[0:256, 128:256], mixed[256:512, 128:256])
        for k, tile in enumerate((first, second, third)):
            parts_ref[h, k * 256 : k * 256 + 256] = tile.astype(jnp.bfloat16)

    @pl.when(pl.program_id(0) == 0)
    def _():
        norm_ref[...] = jnp.zeros_like(norm_ref)

    norm_ref[0:1, :] += gain_grad
    norm_ref[1:2, :] += shift_grad


def middle_back(back, mid, dy, weights, params):
    seqs = dy.shape[0]
    rows = pl.BlockSpec((1, CHUNK, D), lambda s: (s, 0, 0))
    flat = pl.BlockSpec((CHUNK, D), lambda s: (s, 0))
    return pl.pallas_call(
        mid_back_kernel,
        grid=(seqs,),
        in_specs=[flat, rows, rows, out_weight_spec(weights.shape[2]), pl.BlockSpec((4, D), lambda s: (0, 0))],
        out_specs=[
            rows, flat, pl.BlockSpec((4, D, 128), lambda s: (s, 0, 0)), pl.BlockSpec((8, D), lambda s: (0, 0)),
        ],
        out_shape=[
            jax.ShapeDtypeStruct(dy.shape, jnp.float32),
            jax.ShapeDtypeStruct((seqs * CHUNK, D), jnp.bfloat16),
            jax.ShapeDtypeStruct((8, D, 128), jnp.bfloat16),
            jax.ShapeDtypeStruct((8, D), jnp.float32),
        ],
        compiler_params=limits(60),
        name="middle_back",
        cost_estimate=COST,
    )(back, mid, dy, weights, params)


def out_grad_kernel(head_ref, low_ref, cat_ref, out_ref):
    for h in range(4):
        r = head_ref[0] ^ h
        out_ref[(1 - r % 2) * 2 + r // 2] = tn(low_ref[...], cat_ref[:, h * 256 : h * 256 + 256]).astype(jnp.bfloat16)


def out_weight_grad(head, low, cat):
    return pl.pallas_call(
        out_grad_kernel,
        grid_spec=pltpu.PrefetchScalarGridSpec(
            num_scalar_prefetch=1,
            grid=(1,),
            in_specs=[pl.BlockSpec(low.shape, lambda i, t: (0, 0)), pl.BlockSpec(cat.shape, lambda i, t: (0, 0))],
            out_specs=pl.BlockSpec((4, D, 256), lambda i, t: (0, 0, 0)),
        ),
        out_shape=jax.ShapeDtypeStruct((4, D, 256), jnp.bfloat16),
        compiler_params=limits(60),
        name="out_weight_grad",
        cost_estimate=COST,
    )(head, low, cat)


def merge_heads(queries, pairs):
    low = lane_low(queries[0].shape)
    return [
        jnp.where(low, queries[0], roll64(pairs[0])),
        jnp.where(low, roll64(pairs[0]), roll64(queries[1])),
        pairs[1],
        jnp.where(low, queries[2], roll64(pairs[2])),
        jnp.where(low, roll64(pairs[2]), 0.0),
    ]


def qkv_grad_kernel(*refs):
    tok_refs, full_refs, out_ref, acc_ref = refs[:8], refs[8:11], refs[11], refs[12]
    step = pl.program_id(0)

    @pl.when(step == 0)
    def _():
        acc_ref[...] = jnp.zeros_like(acc_ref)

    def one(tok_ref):
        acc_ref[...] += tn(tok_ref[...], jnp.concatenate([ref[...] for ref in full_refs], 1))

    for slot, tok_ref in enumerate(tok_refs):
        pl.when(step == slot)(lambda tok_ref=tok_ref: one(tok_ref))

    @pl.when(step == 7)
    def _():
        tiles = merge_heads(
            [acc_ref[:, k * 256 : k * 256 + 128] for k in range(3)],
            [acc_ref[:, k * 256 + 128 : k * 256 + 256] for k in range(3)],
        )
        for j, tile in enumerate(tiles):
            out_ref[:, j * 128 : j * 128 + 128] = tile.astype(jnp.bfloat16)


def qkv_weight_grad(slots, fulls):
    return pl.pallas_call(
        qkv_grad_kernel,
        grid=(8,),
        in_specs=[pl.BlockSpec((CHUNK, D), lambda i: (0, 0))] * 8 + [pl.BlockSpec((CHUNK, 256), lambda i: (i, 0))] * 3,
        out_specs=pl.BlockSpec((D, 640), lambda i: (0, 0)),
        out_shape=jax.ShapeDtypeStruct((D, 640), jnp.bfloat16),
        scratch_shapes=[pltpu.VMEM((D, D), jnp.float32)],
        compiler_params=limits(60),
        name="qkv_weight_grad",
        cost_estimate=COST,
    )(*slots, *fulls)


def last_kernel(p0_ref, p1_ref, p2_ref, w_ref, tok_ref, mid_ref, par_ref, out_ref, norm_ref):
    grad = None
    for h in range(4):
        queries, pairs = [], []
        for ref in (p0_ref, p1_ref, p2_ref):
            both = ref[h, 0:256, :].astype(jnp.float32)
            queries.append(jnp.concatenate([both, roll64(both)], 0))
            pairs.append(ref[h, 256:768, :].astype(jnp.float32))
        wide = jnp.concatenate([tile.astype(jnp.bfloat16) for tile in merge_heads(queries, pairs)], 1)
        part = nt(wide, w_ref[h])
        grad = part if grad is None else grad + part
    back, gain_grad, shift_grad = norm_back(grad, tok_ref[0].astype(jnp.float32), par_ref[0:1, :])
    out_ref[0] = (mid_ref[0] + back).astype(jnp.bfloat16)

    @pl.when(pl.program_id(0) == 0)
    def _():
        norm_ref[...] = jnp.zeros_like(norm_ref)

    norm_ref[0:1, :] += gain_grad
    norm_ref[1:2, :] += shift_grad


def last(packs, weights, tokens, mid_grad, params):
    seqs = tokens.shape[0]
    piece = pl.BlockSpec((4, 768, 128), lambda s: (s, 0, 0))
    rows = pl.BlockSpec((1, CHUNK, D), lambda s: (s, 0, 0))
    return pl.pallas_call(
        last_kernel,
        grid=(seqs,),
        in_specs=[piece, piece, piece, pl.BlockSpec((4, D, 640), lambda s: (0, 0, 0)), rows, rows,
                  pl.BlockSpec((4, D), lambda s: (0, 0))],
        out_specs=[rows, pl.BlockSpec((8, D), lambda s: (0, 0))],
        out_shape=[jax.ShapeDtypeStruct(tokens.shape, jnp.bfloat16), jax.ShapeDtypeStruct((8, D), jnp.float32)],
        compiler_params=limits(60),
        name="last",
        cost_estimate=COST,
    )(*packs, weights, tokens, mid_grad, params)


def step_kernel(factor_ref, *refs):
    factor = factor_ref[0]
    for slot in range(4):
        weight, gradient, first, second, average = (ref[...] for ref in refs[slot * 5 : slot * 5 + 5])
        outs = refs[20 + slot * 5 : 25 + slot * 5]
        new, first, second, average = adamw_moment_update(
            weight, gradient, first, second, average, rates()[slot], factor
        )
        for ref, value in zip(outs, (new, first, second, average, new.astype(jnp.bfloat16))):
            ref[...] = value


def matrix_steps(factor, groups):
    blocks = [pl.BlockSpec((group[0].shape[0] // 3, group[0].shape[1]), lambda i, t: (i, 0)) for group in groups for _ in range(5)]
    shapes = [
        jax.ShapeDtypeStruct(group[0].shape, kind)
        for group in groups
        for kind in (jnp.float32,) * 4 + (jnp.bfloat16,)
    ]
    outs = pl.pallas_call(
        step_kernel,
        grid_spec=pltpu.PrefetchScalarGridSpec(num_scalar_prefetch=1, grid=(3,), in_specs=blocks, out_specs=blocks),
        out_shape=shapes,
        compiler_params=limits(60),
        name="matrix_steps",
        cost_estimate=COST,
    )(factor, *(item for group in groups for item in group))
    return [outs[n * 5 : n * 5 + 5] for n in range(4)]


def gather_heads(mine):
    return lax.all_gather(mine, "head", axis=0)


def pick(values, index, size, axis):
    return lax.dynamic_slice_in_dim(values, index * size, size, axis)


def after(value, *others):
    return lax.optimization_barrier((value, others))[0]


def add_low(left, right):
    return (left.astype(jnp.float32) + right.astype(jnp.float32)).astype(jnp.bfloat16)


def across(values, axes=GROUP):
    return lax.all_to_all(values, axes, 0, 0, tiled=True)


def fast_body(
    tokens, cotangent, rand_blocks, global_blocks, qkv_weight, out_weight, up_weight, down_weight, norm_params,
    qkv_first, out_first, up_first, down_first, norm_first,
    qkv_second, out_second, up_second, down_second, norm_second,
    qkv_average, out_average, up_average, down_average, norm_average,
):
    dp_size = lax.axis_size("dp")
    count = dp_size * 8
    y, head = lax.axis_index("seq"), lax.axis_index("head")
    me = y * 4 + head

    head_word = jnp.reshape(head, (1,)).astype(jnp.int32)

    turned = jnp.stack([pick(tokens, y, 1, 0)[0], pick(tokens, 1 - y, 1, 0)[0]])
    normed = norm_rows(turned.astype(jnp.float32), norm_params[0], norm_params[1]).astype(jnp.bfloat16)
    mine, theirs = normed[0], normed[1]
    beyond = swap(theirs, 4)
    even = [mine, swap(mine, 2), beyond, swap(beyond, 2)]
    odd = [swap(item, 1) for item in even]
    slots = [item for pair in zip(even, odd) for item in pair]

    low_qkv = qkv_weight.astype(jnp.bfloat16)
    blank = jnp.zeros((96, 64), jnp.bfloat16)
    shard = jnp.concatenate([low_qkv, blank], -1)
    count_rows = dp_size * 2
    mine_qkv = across(jnp.broadcast_to(shard[None], (count_rows,) + shard.shape), ("dp", "seq")).reshape(D, 640)
    rest = (up_weight, down_weight.T, out_weight.T)
    along_dp = lax.all_gather(jnp.concatenate([item.astype(jnp.bfloat16) for item in rest] + [blank], -1), "dp", axis=0)
    all_rest = lax.all_gather(after(along_dp, even[1], even[3], mine_qkv), GROUP, axis=0).reshape((2, 4) + along_dp.shape)

    both_rand = jnp.concatenate([rand_blocks.reshape(-1), swap(rand_blocks.reshape(-1), 4)])
    table = jnp.concatenate(
        [jnp.reshape(me, (1,)), global_blocks, jnp.zeros((5,), jnp.int32), both_rand]
    ).astype(jnp.int32)
    qkv = project(slots, mine_qkv)

    o_parts = across(attend(table, qkv))
    mixed, mid, a2, a2t = middle(o_parts, all_rest, tokens, norm_params)
    all_qkv = gather_heads(after(mine_qkv, a2))

    dy = cotangent.reshape(a2.shape)
    block_out, back, up_mate, down_mate, up_own, down_own = mlp(
        head_word, a2, a2t, dy, dy.T, mid.reshape(a2.shape), all_rest
    )
    block_out = block_out.reshape(tokens.shape)
    up_mate, down_mate = swap(up_mate, 1), swap(down_mate, 1)

    mid_grad, low_grad, grad_parts, norm_two = middle_back(
        back, mid, cotangent, all_rest, after(norm_params, all_qkv)
    )
    down_mate = after(down_mate, grad_parts)
    grad_parts = across(grad_parts)

    fulls, packs = [], []

    def back_step(k, *ahead):
        full, pack = attend_back(k, after(table, *ahead), qkv, grad_parts)
        fulls.append(full)
        packs.append(across(pack))

    down_both = add_low(down_own, down_mate)
    down_terms = lax.psum_scatter(down_both, "dp", scatter_dimension=1, tiled=True)
    back_step(0, down_both)
    out_terms = out_weight_grad(head_word, after(low_grad, fulls[0]), mixed)
    out_mate = swap(out_terms[0:2], 1)
    rest_both = jnp.concatenate([add_low(up_own, after(up_mate, fulls[0])), add_low(out_terms[2:4], out_mate)], -1)
    rest_terms = lax.psum_scatter(rest_both, "dp", scatter_dimension=1, tiled=True)
    back_step(1, fulls[0], rest_both)
    back_step(2, fulls[1], packs[0])
    fulls[2] = after(fulls[2], packs[1])
    wide = qkv_weight_grad(slots, fulls)
    all_terms = jnp.concatenate([after(down_terms, wide), after(rest_terms, wide)], -1)
    kept, sent = pick(all_terms, y, 96, 1), pick(all_terms, 1 - y, 96, 1)
    shares = across(wide.reshape(dp_size * 2, 96, 640), ("dp", "seq"))
    qkv_grad = jnp.sum(shares.astype(jnp.float32), 0)[:, 0:576]
    half = add_low(kept, swap(sent, 4))
    matrix_grad = half[0].astype(jnp.float32) + swap(half[1], 2).astype(jnp.float32)
    down_grad, up_grad, out_grad = matrix_grad[:, 0:D], matrix_grad[:, D : 2 * D], matrix_grad[:, 2 * D : 2 * D + 192]
    input_grad, norm_one = last(packs, all_qkv, tokens, mid_grad, norm_params)

    reduced = (qkv_grad, out_grad.T, up_grad, down_grad)
    squares = sum((jnp.sum(item * item) for item in reduced))
    shared = jnp.concatenate(
        [norm_one[0:2], norm_two[0:2], jnp.full((1, D), squares), jnp.zeros((3, D), jnp.float32)], 0
    )
    distance = 1
    while distance < count:
        shared = shared + swap_every(shared, distance, count)
        distance *= 2
    norm_grads = shared[0:4]
    grad_norm = jnp.sqrt(shared[4, 0] + jnp.sum(norm_grads * norm_grads))
    factor = jnp.minimum(1.0, CLIP_NORM / (grad_norm + 1e-06))
    groups = (
        (qkv_weight, reduced[0], qkv_first, qkv_second, qkv_average),
        (out_weight, reduced[1], out_first, out_second, out_average),
        (up_weight, reduced[2], up_first, up_second, up_average),
        (down_weight.T, reduced[3], down_first.T, down_second.T, down_average.T),
    )
    stepped = matrix_steps(jnp.reshape(factor, (1,)), groups)
    stepped[3] = [item.T for item in stepped[3]]
    norm_step = adamw_moment_update(
        norm_params, norm_grads, norm_first, norm_second, norm_average, rates()[4], factor
    )
    results = []
    for n in range(4):
        results += [item[n] for item in stepped] + [norm_step[n]]
    copies = [item[4] for item in stepped]
    return (block_out, input_grad, grad_norm, *results, *copies, factor * norm_grads[2:])


def is_fast(mesh):
    sizes = dict(mesh.shape)
    return sizes["seq"] == 2 and sizes["head"] == 4 and sizes["dp"] == 4


def solution(mesh):
    return jax.shard_map(
        fast_body if is_fast(mesh) else body,
        mesh=mesh,
        in_specs=(
            P("dp", ("seq", "head"), None),
            P("dp", ("seq", "head"), None),
            P("head", "seq", None),
            P(),
            P(("dp", "seq"), "head"),
            P("head", ("dp", "seq")),
            P(("dp", "seq"), "head"),
            P("head", ("dp", "seq")),
            P(),
            P(("dp", "seq"), "head"),
            P("head", ("dp", "seq")),
            P(("dp", "seq"), "head"),
            P("head", ("dp", "seq")),
            P(),
            P(("dp", "seq"), "head"),
            P("head", ("dp", "seq")),
            P(("dp", "seq"), "head"),
            P("head", ("dp", "seq")),
            P(),
            P(("dp", "seq"), "head"),
            P("head", ("dp", "seq")),
            P(("dp", "seq"), "head"),
            P("head", ("dp", "seq")),
            P(),
        ),
        out_specs=(
            P("dp", ("seq", "head"), None),
            P("dp", ("seq", "head"), None),
            P(),
            P(("dp", "seq"), "head"),
            P("head", ("dp", "seq")),
            P(("dp", "seq"), "head"),
            P("head", ("dp", "seq")),
            P(),
            P(("dp", "seq"), "head"),
            P("head", ("dp", "seq")),
            P(("dp", "seq"), "head"),
            P("head", ("dp", "seq")),
            P(),
            P(("dp", "seq"), "head"),
            P("head", ("dp", "seq")),
            P(("dp", "seq"), "head"),
            P("head", ("dp", "seq")),
            P(),
            P(("dp", "seq"), "head"),
            P("head", ("dp", "seq")),
            P(("dp", "seq"), "head"),
            P("head", ("dp", "seq")),
            P(),
            P(("dp", "seq"), "head"),
            P("head", ("dp", "seq")),
            P(("dp", "seq"), "head"),
            P("head", ("dp", "seq")),
            P(),
        ),
        check_vma=False,
    )
```

```python
import jax
import jax.numpy as jnp
from jax import lax
from jax.experimental import pallas as pl
from jax.experimental.pallas import tpu as pltpu
from jax.sharding import PartitionSpec as P

D = 768
DH = 64
FF = 3072
BLOCK = 64
STEP = 10


EPSILON = 1e-05
BETA_ONE = 0.9
BETA_TWO = 0.999
DECAY = 0.01
SMALL = 1e-08
CLIP_NORM = 1.0
AVERAGING = 0.999
NEGATIVE = -1e30


def norm_rows(values, gain_row, shift_row):
    center = values - jnp.mean(values, -1, keepdims=True)
    spread = jnp.mean(center * center, -1, keepdims=True)
    return center * lax.rsqrt(spread + EPSILON) * gain_row + shift_row


def key_table(rand_local, global_blocks, first_block, blocks_total):
    head_count, local_blocks = (rand_local.shape[0], rand_local.shape[1])
    places = first_block + jnp.arange(local_blocks, dtype=jnp.int32)
    left_side = jnp.maximum(places - 1, 0)
    right_side = jnp.minimum(places + 1, blocks_total - 1)
    window = jnp.stack([left_side, places, right_side], -1)
    key_index = jnp.concatenate(
        [
            jnp.broadcast_to(window[None], (head_count, local_blocks, 3)),
            rand_local,
            jnp.broadcast_to(global_blocks[None, None], (head_count, local_blocks, 2)),
        ],
        -1,
    )
    column_one = jnp.ones((local_blocks, 1), jnp.float32)
    key_valid = jnp.concatenate(
        [
            (places > 0).astype(jnp.float32)[:, None],
            column_one,
            (places < blocks_total - 1).astype(jnp.float32)[:, None],
            jnp.ones((local_blocks, 5), jnp.float32),
        ],
        -1,
    )
    return (key_index, key_valid)


def gather_rows(values):
    return lax.all_gather(values, "head", axis=1, tiled=True)


def sum_rows(values):
    return lax.psum_scatter(values, "head", scatter_dimension=1, tiled=True)


def contract(left_operand, right_operand):
    return jnp.einsum(
        "enz,enf->zf", left_operand, right_operand, preferred_element_type=jnp.float32
    )


def to_heads(values, head_count):
    seq_count, token_count = (values.shape[0], values.shape[1])
    return jnp.moveaxis(
        values.reshape(seq_count, token_count // BLOCK, BLOCK, head_count, DH), 3, 0
    )


def from_heads(values):
    head_count, seq_count, blocks = (values.shape[0], values.shape[1], values.shape[2])
    return jnp.moveaxis(values, 0, 3).reshape(seq_count, blocks * BLOCK, head_count * DH)


def pick_keys(kv_all, key_index):
    seq_count, token_count = (kv_all.shape[0], kv_all.shape[1])
    head_count = key_index.shape[0]
    blocks = kv_all.reshape(seq_count, token_count // BLOCK, BLOCK, head_count, 2, DH)
    by_head = jnp.moveaxis(blocks, 3, 0)
    return jax.vmap(lambda source, chosen: source[:, chosen])(by_head, key_index)


def scores_of(queries, picked, key_valid):
    raw_scores = jnp.einsum(
        "hsnbe,hsnkce->hsnbkc", queries, picked[..., 0, :], preferred_element_type=jnp.float32
    ) * DH ** (-0.5)
    return jnp.where(key_valid[None, None, :, None, :, None] > 0, raw_scores, NEGATIVE)


def attend_forward(queries, picked, key_valid):
    raw_scores = scores_of(queries, picked, key_valid)
    score_shape = raw_scores.shape
    scores_flat = raw_scores.reshape(score_shape[:4] + (score_shape[4] * score_shape[5],))
    row_max = jnp.max(scores_flat, -1, keepdims=True)
    exponent = jnp.exp(scores_flat - row_max)
    row_total = jnp.sum(exponent, -1, keepdims=True)
    probabilities = (exponent / row_total).astype(jnp.bfloat16).reshape(score_shape)
    output = jnp.einsum(
        "hsnbkc,hsnkce->hsnbe", probabilities, picked[..., 1, :], preferred_element_type=jnp.float32
    )
    return (output, row_max + jnp.log(row_total))


def attend_backward(queries, picked, key_valid, log_total, grad_out):
    raw_scores = scores_of(queries, picked, key_valid)
    score_shape = raw_scores.shape
    scores_flat = raw_scores.reshape(score_shape[:4] + (score_shape[4] * score_shape[5],))
    probabilities = jnp.exp(scores_flat - log_total)
    grad_probs = jnp.einsum(
        "hsnbe,hsnkce->hsnbkc", grad_out, picked[..., 1, :], preferred_element_type=jnp.float32
    ).reshape(scores_flat.shape)
    row_delta = jnp.sum(probabilities * grad_probs, -1, keepdims=True)
    grad_scores = probabilities * (grad_probs - row_delta)
    grad_scores = grad_scores.astype(jnp.bfloat16).reshape(score_shape)
    low_probs = probabilities.astype(jnp.bfloat16).reshape(score_shape)
    grad_query = jnp.einsum(
        "hsnbkc,hsnkce->hsnbe", grad_scores, picked[..., 0, :], preferred_element_type=jnp.float32
    ) * DH ** (-0.5)
    grad_keys = jnp.einsum(
        "hsnbkc,hsnbe->hsnkce", grad_scores, queries, preferred_element_type=jnp.float32
    ) * DH ** (-0.5)
    grad_values = jnp.einsum(
        "hsnbkc,hsnbe->hsnkce", low_probs, grad_out, preferred_element_type=jnp.float32
    )
    return (grad_query, jnp.stack([grad_keys, grad_values], -2), row_delta)


def spread_back(grad_pairs, key_index, seq_count, blocks_total):
    head_count = key_index.shape[0]
    zero_grid = jnp.zeros((head_count, seq_count, blocks_total, BLOCK, 2, DH), jnp.float32)
    filled = jax.vmap(lambda source, chosen, addend: source.at[:, chosen].add(addend))(
        zero_grid, key_index, grad_pairs
    )
    return jnp.moveaxis(filled, 0, 3).reshape(seq_count, blocks_total * BLOCK, head_count * 2 * DH)


def rates():
    return (
        1.5 * D ** (-0.5),
        1.5 * max(1, D // (8 * BLOCK)) ** (-0.5),
        1.5 * D ** (-0.5),
        1.5 * FF ** (-0.5),
        0.5,
    )


def adamw_moment_update(weight, gradient, moment_one, moment_two, average, rate, factor):
    decay_mean = min(AVERAGING, (1.0 + STEP) / (10.0 + STEP))
    clipped = gradient * factor
    first_new = BETA_ONE * moment_one + (1.0 - BETA_ONE) * clipped
    second_new = BETA_TWO * moment_two + (1.0 - BETA_TWO) * clipped * clipped
    update = (
        first_new / (1.0 - BETA_ONE**STEP) / (jnp.sqrt(second_new / (1.0 - BETA_TWO**STEP)) + SMALL)
    )
    weight_new = weight - rate * (update + DECAY * weight)
    average_new = decay_mean * average + (1.0 - decay_mean) * weight_new
    return (weight_new, first_new, second_new, average_new)


def body(
    tokens,
    cotangent,
    rand_blocks,
    global_blocks,
    qkv_weight,
    out_weight,
    up_weight,
    down_weight,
    norm_params,
    qkv_first,
    out_first,
    up_first,
    down_first,
    norm_first,
    qkv_second,
    out_second,
    up_second,
    down_second,
    norm_second,
    qkv_average,
    out_average,
    up_average,
    down_average,
    norm_average,
):
    qkv_low, out_low, up_low, down_low = (
        lax.all_gather(qkv_weight.astype(jnp.bfloat16), ("dp", "seq"), axis=0, tiled=True),
        lax.all_gather(out_weight.astype(jnp.bfloat16), ("dp", "seq"), axis=1, tiled=True),
        lax.all_gather(up_weight.astype(jnp.bfloat16), ("dp", "seq"), axis=0, tiled=True),
        lax.all_gather(down_weight.astype(jnp.bfloat16), ("dp", "seq"), axis=1, tiled=True),
    )
    seq_count = tokens.shape[0]
    head_count = rand_blocks.shape[0]
    local_blocks = rand_blocks.shape[1]
    blocks_total = local_blocks * lax.axis_size("seq")
    first_block = lax.axis_index("seq") * local_blocks
    key_index, key_valid = key_table(rand_blocks, global_blocks, first_block, blocks_total)
    inputs = tokens.astype(jnp.float32)
    full_one = gather_rows(norm_rows(inputs, norm_params[0], norm_params[1]).astype(jnp.bfloat16))
    token_count = full_one.shape[1]
    qkv_all = jnp.dot(full_one, qkv_low, preferred_element_type=jnp.float32).astype(jnp.bfloat16)
    qkv_parts = qkv_all.reshape(seq_count, token_count, head_count, 3, DH)
    kv_local = qkv_parts[:, :, :, 1:, :].reshape(seq_count, token_count, head_count * 2 * DH)
    kv_all = lax.all_gather(kv_local, "seq", axis=1, tiled=True)
    picked = pick_keys(kv_all, key_index)
    queries = to_heads(qkv_parts[:, :, :, 0, :], head_count)
    attended, log_total = attend_forward(queries, picked, key_valid)
    mixed_heads = from_heads(attended.astype(jnp.bfloat16))
    residual = inputs + sum_rows(jnp.dot(mixed_heads, out_low, preferred_element_type=jnp.float32))
    full_two = gather_rows(norm_rows(residual, norm_params[2], norm_params[3]).astype(jnp.bfloat16))
    upward = jnp.dot(full_two, up_low, preferred_element_type=jnp.float32)
    active = jax.nn.gelu(upward).astype(jnp.bfloat16)
    result = residual + sum_rows(jnp.dot(active, down_low, preferred_element_type=jnp.float32))
    block_out = result.astype(jnp.bfloat16)
    grad_top = gather_rows(cotangent)
    grad_down = contract(active, grad_top)
    grad_active = jnp.dot(grad_top, down_low.T, preferred_element_type=jnp.float32)
    _, gelu_back = jax.vjp(jax.nn.gelu, upward)
    grad_upward = gelu_back(grad_active)[0].astype(jnp.bfloat16)
    grad_up = contract(full_two, grad_upward)
    part_two = sum_rows(jnp.dot(grad_upward, up_low.T, preferred_element_type=jnp.float32))
    _, norm_back_two = jax.vjp(norm_rows, residual, norm_params[2], norm_params[3])
    grad_residual_norm, grad_gain_two, grad_shift_two = norm_back_two(part_two)
    grad_residual = cotangent.astype(jnp.float32) + grad_residual_norm
    grad_middle = gather_rows(grad_residual.astype(jnp.bfloat16))
    grad_out = contract(mixed_heads, grad_middle)
    grad_mixed = jnp.dot(grad_middle, out_low.T, preferred_element_type=jnp.float32).astype(
        jnp.bfloat16
    )
    grad_query, grad_pairs, row_delta = attend_backward(
        queries, picked, key_valid, log_total, to_heads(grad_mixed, head_count)
    )
    grad_kv_full = spread_back(grad_pairs, key_index, seq_count, blocks_total)
    grad_kv = lax.psum_scatter(
        grad_kv_full.astype(jnp.bfloat16), "seq", scatter_dimension=1, tiled=True
    ).astype(jnp.float32)
    query_gradient = from_heads(grad_query).reshape(seq_count, token_count, head_count, 1, DH)
    grad_qkv_rows = jnp.concatenate(
        [query_gradient, grad_kv.reshape(seq_count, token_count, head_count, 2, DH)], 3
    )
    grad_qkv_rows = grad_qkv_rows.reshape(seq_count, token_count, head_count * 3 * DH).astype(
        jnp.bfloat16
    )
    grad_qkv = contract(full_one, grad_qkv_rows)
    part_one = sum_rows(jnp.dot(grad_qkv_rows, qkv_low.T, preferred_element_type=jnp.float32))
    _, norm_back_one = jax.vjp(norm_rows, inputs, norm_params[0], norm_params[1])
    grad_input_norm, grad_gain_one, grad_shift_one = norm_back_one(part_one)
    input_grad = (grad_residual + grad_input_norm).astype(jnp.bfloat16)
    grad_norm_local = jnp.stack([grad_gain_one, grad_shift_one, grad_gain_two, grad_shift_two])
    reduced_total = (
        lax.psum_scatter(grad_qkv, ("dp", "seq"), scatter_dimension=0, tiled=True),
        lax.psum_scatter(grad_out, ("dp", "seq"), scatter_dimension=1, tiled=True),
        lax.psum_scatter(grad_up, ("dp", "seq"), scatter_dimension=0, tiled=True),
        lax.psum_scatter(grad_down, ("dp", "seq"), scatter_dimension=1, tiled=True),
    )
    squares = sum((jnp.sum(item * item) for item in reduced_total))
    norm_grads = lax.psum(grad_norm_local, ("dp", "seq", "head"))
    matrix_squares = lax.psum(squares, ("dp", "seq", "head"))
    grad_norm = jnp.sqrt(matrix_squares + jnp.sum(norm_grads * norm_grads))
    factor = jnp.minimum(1.0, CLIP_NORM / (grad_norm + 1e-06))
    weights = (qkv_weight, out_weight, up_weight, down_weight, norm_params)
    gradients = (reduced_total[0], reduced_total[1], reduced_total[2], reduced_total[3], norm_grads)
    firsts = (qkv_first, out_first, up_first, down_first, norm_first)
    seconds = (qkv_second, out_second, up_second, down_second, norm_second)
    averages = (qkv_average, out_average, up_average, down_average, norm_average)
    results = [
        adamw_moment_update(
            weights[slot],
            gradients[slot],
            firsts[slot],
            seconds[slot],
            averages[slot],
            rates()[slot],
            factor,
        )
        for slot in range(5)
    ]
    news = tuple((item[0] for item in results))
    first_news = tuple((item[1] for item in results))
    second_news = tuple((item[2] for item in results))
    average_news = tuple((item[3] for item in results))
    return (
        block_out,
        input_grad,
        grad_norm,
        news[0],
        news[1],
        news[2],
        news[3],
        news[4],
        first_news[0],
        first_news[1],
        first_news[2],
        first_news[3],
        first_news[4],
        second_news[0],
        second_news[1],
        second_news[2],
        second_news[3],
        second_news[4],
        average_news[0],
        average_news[1],
        average_news[2],
        average_news[3],
        average_news[4],
        news[0].astype(jnp.bfloat16),
        news[1].astype(jnp.bfloat16),
        news[2].astype(jnp.bfloat16),
        news[3].astype(jnp.bfloat16),
        factor * norm_grads[2:],
    )


GROUP = ("seq", "head")
EVERY = ("dp", "seq", "head")
FULL = 4096
CHUNK = 512
MB = 1024 * 1024
COST = pl.CostEstimate(flops=10**6, bytes_accessed=10**5, transcendentals=0)


def limits(megabytes):
    return pltpu.CompilerParams(vmem_limit_bytes=megabytes * MB)


def swap(values, distance):
    return lax.ppermute(values, GROUP, [(i, i ^ distance) for i in range(8)])


def swap_every(values, distance, count):
    return lax.ppermute(values, EVERY, [(i, i ^ distance) for i in range(count)])


def nt(left, right):
    return lax.dot_general(left, right, (((1,), (1,)), ((), ())), preferred_element_type=jnp.float32)


def nn(left, right):
    return lax.dot_general(left, right, (((1,), (0,)), ((), ())), preferred_element_type=jnp.float32)


def tn(left, right):
    return lax.dot_general(left, right, (((0,), (0,)), ((), ())), preferred_element_type=jnp.float32)


def lane_low(shape):
    return lax.broadcasted_iota(jnp.int32, shape, len(shape) - 1) < 64


def roll64(values):
    return pltpu.roll(values, 64, 1)


def block_places(tab_ref, k, block):
    me = tab_ref[0]
    part = (block // 32) ^ (me // 4)
    base = 8 + ((part * 3 + k) * 32 + block % 32) * 3
    chosen = [
        jnp.maximum(block - 1, 0),
        block,
        jnp.minimum(block + 1, 63),
        tab_ref[base],
        tab_ref[base + 1],
        tab_ref[base + 2],
        tab_ref[1],
        tab_ref[2],
    ]
    return [pl.multiple_of((((b // 8) ^ me) * 8 + b % 8) * 64, 64) for b in chosen]


def spread_kernel(in_ref, out_ref):
    low = lane_low((96, 128))
    tiles = [in_ref[:, j * 128 : j * 128 + 128] for j in range(4)]
    tiles.append(jnp.concatenate([in_ref[:, 512:576], jnp.zeros((96, 64), jnp.float32)], 1))
    scale = DH ** (-0.5)
    parts = [
        jnp.where(low, tiles[0] * scale, 0.0),
        jnp.where(low, roll64(tiles[0]), roll64(tiles[1])),
        jnp.where(low, roll64(tiles[1]) * scale, 0.0),
        tiles[2],
        jnp.where(low, tiles[3] * scale, 0.0),
        jnp.where(low, roll64(tiles[3]), roll64(tiles[4])),
    ]
    for n, part in enumerate(parts):
        out_ref[:, n * 128 : n * 128 + 128] = part.astype(jnp.bfloat16)


def spread_heads(shard):
    return pl.pallas_call(
        spread_kernel,
        out_shape=jax.ShapeDtypeStruct((96, D), jnp.bfloat16),
        compiler_params=limits(60),
        name="spread_heads",
        cost_estimate=COST,
    )(shard)


def qkv_kernel(*refs):
    tok_refs, weight_ref, out_ref = refs[:8], refs[8], refs[9]

    def one(tok_ref):
        out_ref[...] = nn(tok_ref[...], weight_ref[...]).astype(jnp.bfloat16)

    for slot, tok_ref in enumerate(tok_refs):
        pl.when(pl.program_id(0) == slot)(lambda tok_ref=tok_ref: one(tok_ref))


def project(slots, weights):
    return pl.pallas_call(
        qkv_kernel,
        grid=(8,),
        in_specs=[pl.BlockSpec((CHUNK, D), lambda i: (0, 0))] * 8 + [pl.BlockSpec((D, D), lambda i: (0, 0))],
        out_specs=pl.BlockSpec((CHUNK, D), lambda i: (i, 0)),
        out_shape=jax.ShapeDtypeStruct((FULL, D), jnp.bfloat16),
        compiler_params=limits(60),
        name="project",
        cost_estimate=COST,
    )(*slots, weights)


def hide(scores, low, high):
    lane = lax.broadcasted_iota(jnp.int32, scores.shape, 1)
    return jnp.where((lane >= low) & (lane < high), NEGATIVE, scores)


def softmax_rows(scores, part, q):
    if q == 0:
        scores = jnp.where(part == 0, hide(scores, 0, 64), scores)
    if q == 7:
        scores = jnp.where(part == 7, hide(scores, 128, 192), scores)
    top = jnp.max(scores, -1, keepdims=True)
    exponent = jnp.exp(scores - top)
    total = jnp.sum(exponent, -1, keepdims=True)
    return exponent * (1.0 / total)


def attend_kernel(k, tab_ref, qkv_ref, out_ref):
    me = tab_ref[0]

    def step(pair, carry):
        blocks = [(pair * 2 + n, q) for n in range(2) for q in range(8)]
        keys, scores = [], []
        for slot, q in blocks:
            places = block_places(tab_ref, k, (slot ^ me) * 8 + q)
            keys.append(jnp.concatenate([qkv_ref[pl.ds(p, 64), 128:256] for p in places], 0))
            at = pl.multiple_of(slot * CHUNK + q * 64, 64)
            scores.append(nt(qkv_ref[pl.ds(at, 64), 0:128], keys[-1]))
        probs = [
            softmax_rows(score, slot ^ me, q).astype(jnp.bfloat16) for score, (slot, q) in zip(scores, blocks)
        ]
        outs = [nn(prob, key) for prob, key in zip(probs, keys)]
        for n, (slot, q) in enumerate(blocks):
            if q < 4:
                both = jnp.where(lane_low(outs[n].shape), roll64(outs[n]), outs[n + 4])
                out_ref[slot ^ me, q * 64 : q * 64 + 64, :] = both.astype(jnp.bfloat16)
        return carry

    lax.fori_loop(0, 4, step, 0)


def attend(table, qkv):
    return pl.pallas_call(
        lambda *refs: attend_kernel(pl.program_id(0), *refs),
        grid_spec=pltpu.PrefetchScalarGridSpec(
            num_scalar_prefetch=1,
            grid=(3,),
            in_specs=[pl.BlockSpec((FULL, 256), lambda i, t: (0, i))],
            out_specs=pl.BlockSpec((8, 256, 128), lambda i, t: (0, i, 0)),
        ),
        out_shape=jax.ShapeDtypeStruct((8, D, 128), jnp.bfloat16),
        compiler_params=limits(60),
        name="attend",
        cost_estimate=COST,
    )(table, qkv)


def attend_back_kernel(k, tab_ref, qkv_ref, grad_ref, full_ref, pack_ref, acc_ref, shared_ref):
    me = tab_ref[0]
    acc_ref[...] = jnp.zeros_like(acc_ref)
    shared_ref[...] = jnp.zeros_like(shared_ref)

    def step(slot, carry):
        part = slot ^ me
        grads = [None] * 8
        for j in range(4):
            tile = grad_ref[part, j * 64 : j * 64 + 64, :].astype(jnp.float32)
            low_lanes = lane_low(tile.shape)
            grads[j] = jnp.where(low_lanes, 0.0, roll64(tile)).astype(jnp.bfloat16)
            grads[j + 4] = jnp.where(low_lanes, 0.0, tile).astype(jnp.bfloat16)
        places, stacks, keys, both = [], [], [], []
        for q in range(8):
            places.append(block_places(tab_ref, k, part * 8 + q))
            keys.append(jnp.concatenate([qkv_ref[pl.ds(p, 64), 128:256] for p in places[q]], 0))
            at = pl.multiple_of(slot * CHUNK + q * 64, 64)
            stacks.append(jnp.concatenate([qkv_ref[pl.ds(at, 64), 0:128], grads[q]], 0))
            both.append(nt(stacks[q], keys[q]))
        lows, pairs = [], []
        for q in range(8):
            probs, grad_probs = softmax_rows(both[q][:64], part, q), both[q][64:]
            delta = jnp.sum(probs * grad_probs, -1, keepdims=True)
            lows.append((probs * (grad_probs - delta)).astype(jnp.bfloat16))
            pairs.append(jnp.concatenate([lows[q], probs.astype(jnp.bfloat16)], 0))
        queries = []
        for q in range(8):
            grad_query = nn(lows[q], keys[q]) * DH ** (-0.5)
            queries.append(jnp.where(lane_low(grad_query.shape), grad_query, 0.0))
            at = pl.multiple_of(slot * CHUNK + q * 64, 64)
            full_ref[pl.ds(at, 64), 0:128] = queries[q].astype(jnp.bfloat16)
        spreads = [tn(pairs[q], stacks[q]) for q in range(8)]
        shared = spreads[0][384:]
        for q in range(8):
            if q:
                shared = shared + spreads[q][384:]
            for m in range(6):
                acc_ref[pl.ds(places[q][m], 64), :] += spreads[q][m * 64 : m * 64 + 64]
        shared_ref[...] += shared
        for j in range(4):
            packed = queries[j] + roll64(queries[j + 4])
            pack_ref[part, j * 64 : j * 64 + 64, :] = packed.astype(jnp.bfloat16)
        return carry

    lax.fori_loop(0, 8, step, 0)
    for m in range(2):
        block = tab_ref[1 + m]
        at = pl.multiple_of((((block // 8) ^ me) * 8 + block % 8) * 64, 64)
        acc_ref[pl.ds(at, 64), :] += shared_ref[m * 64 : m * 64 + 64]

    def finish(slot, carry):
        at = pl.ds(pl.multiple_of(slot * CHUNK, CHUNK), CHUNK)
        low = acc_ref[at, :].astype(jnp.bfloat16)
        full_ref[at, 128:256] = low
        pack_ref[slot ^ me, 256:768, :] = low
        return carry

    lax.fori_loop(0, 8, finish, 0)


def attend_back(k, table, qkv, grad, row):
    return pl.pallas_call(
        lambda *refs: attend_back_kernel(k, *refs),
        grid_spec=pltpu.PrefetchScalarGridSpec(
            num_scalar_prefetch=1,
            grid=(1,),
            in_specs=[
                pl.BlockSpec((FULL, 256), lambda i, t: (0, k)),
                pl.BlockSpec((8, 256, 128), lambda i, t: (0, row, 0)),
            ],
            out_specs=[
                pl.BlockSpec((FULL, 256), lambda i, t: (0, 0)),
                pl.BlockSpec((8, 768, 128), lambda i, t: (0, 0, 0)),
            ],
            scratch_shapes=[pltpu.VMEM((FULL, 128), jnp.float32), pltpu.VMEM((128, 128), jnp.float32)],
        ),
        out_shape=[
            jax.ShapeDtypeStruct((FULL, 256), jnp.bfloat16),
            jax.ShapeDtypeStruct((8, 768, 128), jnp.bfloat16),
        ],
        compiler_params=limits(60),
        name="attend_back",
        cost_estimate=COST,
    )(table, qkv, grad)


def norm_stats(values):
    center = values - jnp.mean(values, -1, keepdims=True)
    spread = jnp.mean(center * center, -1, keepdims=True)
    scale = lax.rsqrt(spread + EPSILON)
    return center * scale, scale


def halves(first, second):
    low = lane_low(first.shape)
    upper = jnp.where(low, first, roll64(second))
    lower = jnp.where(low, roll64(first), second)
    return upper, lower


def mid_kernel(o_ref, w_ref, tok_ref, par_ref, cat_ref, mid_ref, a2_ref, a2t_ref):
    middle = tok_ref[0].astype(jnp.float32)
    cat_ref[...] = jnp.zeros_like(cat_ref)
    for h in range(4):
        tiles = [o_ref[h, at : at + 256].astype(jnp.float32) for at in (0, 256, 512)]
        upper, lower = halves(tiles[0], tiles[1])
        last_upper, last_lower = halves(tiles[2], jnp.zeros_like(tiles[2]))
        cat_ref[0:256, h * 256 : h * 256 + 128] = upper.astype(jnp.bfloat16)
        cat_ref[256:512, h * 256 : h * 256 + 128] = lower.astype(jnp.bfloat16)
        cat_ref[0:256, h * 256 + 128 : h * 256 + 256] = last_upper.astype(jnp.bfloat16)
        cat_ref[256:512, h * 256 + 128 : h * 256 + 256] = last_lower.astype(jnp.bfloat16)
        middle = middle + nt(cat_ref[:, h * 256 : h * 256 + 256], ordered(w_ref, h))
    mid_ref[0] = middle
    normed, _ = norm_stats(middle)
    low = normed * par_ref[2:3, :] + par_ref[3:4, :]
    a2_ref[...] = low.astype(jnp.bfloat16)
    a2t_ref[...] = low.T.astype(jnp.bfloat16)


def ordered(ref, h):
    return jnp.concatenate([ref[y, h, d] for d in range(ref.shape[2]) for y in range(2)], 0)


def out_weight_spec(dp_size):
    return pl.BlockSpec((2, 4, dp_size, 96, 256), lambda s: (0, 0, 0, 0, 6))


def middle(o_parts, weights, tokens, params):
    seqs = tokens.shape[0]
    rows = pl.BlockSpec((1, CHUNK, D), lambda s: (s, 0, 0))
    return pl.pallas_call(
        mid_kernel,
        grid=(seqs,),
        in_specs=[
            pl.BlockSpec((4, D, 128), lambda s: (s, 0, 0)),
            out_weight_spec(weights.shape[2]), rows, pl.BlockSpec((4, D), lambda s: (0, 0)),
        ],
        out_specs=[
            pl.BlockSpec((CHUNK, 1024), lambda s: (s, 0)), rows,
            pl.BlockSpec((CHUNK, D), lambda s: (s, 0)), pl.BlockSpec((D, CHUNK), lambda s: (0, s)),
        ],
        out_shape=[
            jax.ShapeDtypeStruct((seqs * CHUNK, 1024), jnp.bfloat16),
            jax.ShapeDtypeStruct(tokens.shape, jnp.float32),
            jax.ShapeDtypeStruct((seqs * CHUNK, D), jnp.bfloat16),
            jax.ShapeDtypeStruct((D, seqs * CHUNK), jnp.bfloat16),
        ],
        compiler_params=limits(60),
        name="middle",
        cost_estimate=COST,
    )(o_parts, weights, tokens, params)


def group_of(head, i):
    return head ^ (i % 2 * 2 + 1 - i // 2)


def mlp_kernel(head_ref, a2_ref, a2t_ref, dy_ref, dyt_ref, mid_ref, wu_ref, wd_ref, out_ref, back_ref,
               um_ref, dm_ref, uo_ref, do_ref, g_ref, u_ref, wuo_ref, wdo_ref, wut_ref, wdt_ref, acc_ref):
    step = pl.program_id(0)

    @pl.when(step == 0)
    def _():
        acc_ref[...] = mid_ref[...]
        back_ref[...] = jnp.zeros_like(back_ref)

    wuo_ref[...] = ordered(wu_ref, 0)
    wdo_ref[...] = ordered(wd_ref, 0)
    wut_ref[...] = wuo_ref[...].T
    wdt_ref[...] = wdo_ref[...].T
    rate, cubic = 0.7978845608028654, 0.044715
    rows = [slice(m * 256, m * 256 + 256) for m in range(4)]
    products = lambda m: (nn(a2_ref[rows[m], :], wuo_ref[...]), nn(dy_ref[rows[m], :], wdo_ref[...]))
    ahead = products(0)
    for m in range(4):
        up, grad = ahead
        if m < 3:
            ahead = products(m + 1)
        at = rows[m]
        square = up * up
        bend = jnp.tanh(up * (rate + rate * cubic * square))
        half = 0.5 + 0.5 * bend
        g_ref[at, :] = (up * half).astype(jnp.bfloat16)
        slope = half + (0.5 * up) * (1.0 - bend * bend) * (rate + 3.0 * rate * cubic * square)
        u_ref[at, :] = (grad * slope).astype(jnp.bfloat16)
        acc_ref[at, :] += nn(g_ref[at, :], wdt_ref[...])
        back_ref[at, :] += nn(u_ref[at, :], wut_ref[...])
    up_grad = nn(a2t_ref[...], u_ref[...]).astype(jnp.bfloat16)
    down_grad = nn(dyt_ref[...], g_ref[...]).astype(jnp.bfloat16)

    @pl.when(step < 2)
    def _():
        um_ref[0] = up_grad
        dm_ref[0] = down_grad

    @pl.when(step >= 2)
    def _():
        uo_ref[0] = up_grad
        do_ref[0] = down_grad

    @pl.when(step == 3)
    def _():
        out_ref[...] = acc_ref[...].astype(jnp.bfloat16)


def mlp(head, a2, a2t, dy, dyt, mid, weights):
    tokens = a2.shape[0]
    whole = lambda shape: pl.BlockSpec(shape, lambda i, t: (0, 0))
    weight = lambda part: pl.BlockSpec(
        (2, 1, weights.shape[2], 96, D), lambda i, t: (0, group_of(t[0], i), 0, 0, part)
    )
    theirs = pl.BlockSpec((1, D, D), lambda i, t: (jnp.minimum(i, 1), 0, 0))
    ours = pl.BlockSpec((1, D, D), lambda i, t: (jnp.maximum(i - 2, 0), 0, 0))
    low = jax.ShapeDtypeStruct((2, D, D), jnp.bfloat16)
    return pl.pallas_call(
        mlp_kernel,
        grid_spec=pltpu.PrefetchScalarGridSpec(
            num_scalar_prefetch=1,
            grid=(4,),
            in_specs=[
                whole((tokens, D)), whole((D, tokens)), whole((tokens, D)), whole((D, tokens)), whole((tokens, D)),
                weight(0), weight(1),
            ],
            out_specs=[whole((tokens, D)), whole((tokens, D)), theirs, theirs, ours, ours],
            scratch_shapes=[
                pltpu.VMEM((tokens, D), jnp.bfloat16), pltpu.VMEM((tokens, D), jnp.bfloat16),
                *(pltpu.VMEM((D, D), jnp.bfloat16) for _ in range(4)), pltpu.VMEM((tokens, D), jnp.float32),
            ],
        ),
        out_shape=[
            jax.ShapeDtypeStruct((tokens, D), jnp.bfloat16), jax.ShapeDtypeStruct((tokens, D), jnp.float32),
            low, low, low, low,
        ],
        compiler_params=limits(60),
        name="mlp",
        cost_estimate=COST,
    )(head, a2, a2t, dy, dyt, mid, weights, weights)


def norm_back(grad, values, gain):
    normed, scale = norm_stats(values)
    gain_grad = jnp.sum(grad * normed, 0, keepdims=True)
    shift_grad = jnp.sum(grad, 0, keepdims=True)
    inner = grad * gain
    across = jnp.mean(inner, -1, keepdims=True)
    along = jnp.mean(inner * normed, -1, keepdims=True)
    return scale * (inner - across - normed * along), gain_grad, shift_grad


def mid_back_kernel(b_ref, mid_ref, dy_ref, w_ref, par_ref, grad_ref, low_ref, first_ref, rest_ref, norm_ref):
    grad, gain_grad, shift_grad = norm_back(b_ref[...], mid_ref[0], par_ref[2:3, :])
    total = dy_ref[0].astype(jnp.float32) + grad
    grad_ref[0] = total
    low = total.astype(jnp.bfloat16)
    low_ref[...] = low
    for h in range(4):
        mixed = nn(low, ordered(w_ref, h))
        first, second = halves(mixed[0:256, 0:128], mixed[256:512, 0:128])
        third, _ = halves(mixed[0:256, 128:256], mixed[256:512, 128:256])
        first_ref[h] = first.astype(jnp.bfloat16)
        rest_ref[h, 0:256] = second.astype(jnp.bfloat16)
        rest_ref[h, 256:512] = third.astype(jnp.bfloat16)

    @pl.when(pl.program_id(0) == 0)
    def _():
        norm_ref[...] = jnp.zeros_like(norm_ref)

    norm_ref[0:1, :] += gain_grad
    norm_ref[1:2, :] += shift_grad


def middle_back(back, mid, dy, weights, params):
    seqs = dy.shape[0]
    rows = pl.BlockSpec((1, CHUNK, D), lambda s: (s, 0, 0))
    flat = pl.BlockSpec((CHUNK, D), lambda s: (s, 0))
    return pl.pallas_call(
        mid_back_kernel,
        grid=(seqs,),
        in_specs=[flat, rows, rows, out_weight_spec(weights.shape[2]), pl.BlockSpec((4, D), lambda s: (0, 0))],
        out_specs=[
            rows, flat, pl.BlockSpec((4, 256, 128), lambda s: (s, 0, 0)),
            pl.BlockSpec((4, 512, 128), lambda s: (s, 0, 0)), pl.BlockSpec((8, D), lambda s: (0, 0)),
        ],
        out_shape=[
            jax.ShapeDtypeStruct(dy.shape, jnp.float32),
            jax.ShapeDtypeStruct((seqs * CHUNK, D), jnp.bfloat16),
            jax.ShapeDtypeStruct((8, 256, 128), jnp.bfloat16),
            jax.ShapeDtypeStruct((8, 512, 128), jnp.bfloat16),
            jax.ShapeDtypeStruct((8, D), jnp.float32),
        ],
        compiler_params=limits(60),
        name="middle_back",
        cost_estimate=COST,
    )(back, mid, dy, weights, params)


def out_grad_kernel(head_ref, low_ref, cat_ref, out_ref):
    for h in range(4):
        r = head_ref[0] ^ h
        out_ref[(1 - r % 2) * 2 + r // 2] = tn(low_ref[...], cat_ref[:, h * 256 : h * 256 + 256]).astype(jnp.bfloat16)


def out_weight_grad(head, low, cat):
    return pl.pallas_call(
        out_grad_kernel,
        grid_spec=pltpu.PrefetchScalarGridSpec(
            num_scalar_prefetch=1,
            grid=(1,),
            in_specs=[pl.BlockSpec(low.shape, lambda i, t: (0, 0)), pl.BlockSpec(cat.shape, lambda i, t: (0, 0))],
            out_specs=pl.BlockSpec((4, D, 256), lambda i, t: (0, 0, 0)),
        ),
        out_shape=jax.ShapeDtypeStruct((4, D, 256), jnp.bfloat16),
        compiler_params=limits(60),
        name="out_weight_grad",
        cost_estimate=COST,
    )(head, low, cat)


def merge_heads(queries, pairs):
    low = lane_low(queries[0].shape)
    return [
        jnp.where(low, queries[0], roll64(pairs[0])),
        jnp.where(low, roll64(pairs[0]), roll64(queries[1])),
        pairs[1],
        jnp.where(low, queries[2], roll64(pairs[2])),
        jnp.where(low, roll64(pairs[2]), 0.0),
    ]


def qkv_grad_kernel(*refs):
    tok_refs, full_refs, out_ref, acc_ref = refs[:8], refs[8:11], refs[11], refs[12]
    step = pl.program_id(0)

    @pl.when(step == 0)
    def _():
        acc_ref[...] = jnp.zeros_like(acc_ref)

    def one(tok_ref):
        acc_ref[...] += tn(tok_ref[...], jnp.concatenate([ref[...] for ref in full_refs], 1))

    for slot, tok_ref in enumerate(tok_refs):
        pl.when(step == slot)(lambda tok_ref=tok_ref: one(tok_ref))

    @pl.when(step == 7)
    def _():
        tiles = merge_heads(
            [acc_ref[:, k * 256 : k * 256 + 128] for k in range(3)],
            [acc_ref[:, k * 256 + 128 : k * 256 + 256] for k in range(3)],
        )
        for j, tile in enumerate(tiles):
            out_ref[:, j * 128 : j * 128 + 128] = tile.astype(jnp.bfloat16)


def qkv_weight_grad(slots, fulls):
    return pl.pallas_call(
        qkv_grad_kernel,
        grid=(8,),
        in_specs=[pl.BlockSpec((CHUNK, D), lambda i: (0, 0))] * 8 + [pl.BlockSpec((CHUNK, 256), lambda i: (i, 0))] * 3,
        out_specs=pl.BlockSpec((D, 640), lambda i: (0, 0)),
        out_shape=jax.ShapeDtypeStruct((D, 640), jnp.bfloat16),
        scratch_shapes=[pltpu.VMEM((D, D), jnp.float32)],
        compiler_params=limits(60),
        name="qkv_weight_grad",
        cost_estimate=COST,
    )(*slots, *fulls)


def last_kernel(p0_ref, p1_ref, p2_ref, w_ref, tok_ref, mid_ref, par_ref, out_ref, norm_ref):
    grad = None
    low = lane_low((CHUNK, 128))
    for h in range(4):
        tiles = []
        for ref in (p0_ref, p1_ref, p2_ref):
            both = ref[h, 0:256, :].astype(jnp.float32) * DH**0.5
            tiles.append(jnp.where(low, jnp.concatenate([both, roll64(both)], 0), 0.0).astype(jnp.bfloat16))
            tiles.append(ref[h, 256:768, :])
        part = nt(jnp.concatenate(tiles, 1), w_ref[h])
        grad = part if grad is None else grad + part
    back, gain_grad, shift_grad = norm_back(grad, tok_ref[0].astype(jnp.float32), par_ref[0:1, :])
    out_ref[0] = (mid_ref[0] + back).astype(jnp.bfloat16)

    @pl.when(pl.program_id(0) == 0)
    def _():
        norm_ref[...] = jnp.zeros_like(norm_ref)

    norm_ref[0:1, :] += gain_grad
    norm_ref[1:2, :] += shift_grad


def last(packs, weights, tokens, mid_grad, params):
    seqs = tokens.shape[0]
    piece = pl.BlockSpec((4, 768, 128), lambda s: (s, 0, 0))
    rows = pl.BlockSpec((1, CHUNK, D), lambda s: (s, 0, 0))
    return pl.pallas_call(
        last_kernel,
        grid=(seqs,),
        in_specs=[piece, piece, piece, pl.BlockSpec((4, D, D), lambda s: (0, 0, 0)), rows, rows,
                  pl.BlockSpec((4, D), lambda s: (0, 0))],
        out_specs=[rows, pl.BlockSpec((8, D), lambda s: (0, 0))],
        out_shape=[jax.ShapeDtypeStruct(tokens.shape, jnp.bfloat16), jax.ShapeDtypeStruct((8, D), jnp.float32)],
        compiler_params=limits(60),
        name="last",
        cost_estimate=COST,
    )(*packs, weights, tokens, mid_grad, params)


def step_kernel(factor_ref, *refs):
    factor = factor_ref[0]
    for slot in range(4):
        weight, gradient, first, second, average = (ref[...] for ref in refs[slot * 5 : slot * 5 + 5])
        outs = refs[20 + slot * 5 : 25 + slot * 5]
        new, first, second, average = adamw_moment_update(
            weight, gradient, first, second, average, rates()[slot], factor
        )
        for ref, value in zip(outs, (new, first, second, average, new.astype(jnp.bfloat16))):
            ref[...] = value


def matrix_steps(factor, groups):
    blocks = [pl.BlockSpec((group[0].shape[0] // 3, group[0].shape[1]), lambda i, t: (i, 0)) for group in groups for _ in range(5)]
    shapes = [
        jax.ShapeDtypeStruct(group[0].shape, kind)
        for group in groups
        for kind in (jnp.float32,) * 4 + (jnp.bfloat16,)
    ]
    outs = pl.pallas_call(
        step_kernel,
        grid_spec=pltpu.PrefetchScalarGridSpec(num_scalar_prefetch=1, grid=(3,), in_specs=blocks, out_specs=blocks),
        out_shape=shapes,
        compiler_params=limits(60),
        name="matrix_steps",
        cost_estimate=COST,
    )(factor, *(item for group in groups for item in group))
    return [outs[n * 5 : n * 5 + 5] for n in range(4)]


def gather_heads(mine):
    return lax.all_gather(mine, "head", axis=0)


def pick(values, index, size, axis):
    return lax.dynamic_slice_in_dim(values, index * size, size, axis)


def after(value, *others):
    return lax.optimization_barrier((value, others))[0]


def add_low(left, right):
    return (left.astype(jnp.float32) + right.astype(jnp.float32)).astype(jnp.bfloat16)


def across(values, axes=GROUP):
    return lax.all_to_all(values, axes, 0, 0, tiled=True)


def fast_body(
    tokens, cotangent, rand_blocks, global_blocks, qkv_weight, out_weight, up_weight, down_weight, norm_params,
    qkv_first, out_first, up_first, down_first, norm_first,
    qkv_second, out_second, up_second, down_second, norm_second,
    qkv_average, out_average, up_average, down_average, norm_average,
):
    dp_size = lax.axis_size("dp")
    count = dp_size * 8
    y, head = lax.axis_index("seq"), lax.axis_index("head")
    me = y * 4 + head

    head_word = jnp.reshape(head, (1,)).astype(jnp.int32)

    turned = jnp.stack([pick(tokens, y, 1, 0)[0], pick(tokens, 1 - y, 1, 0)[0]])
    normed = norm_rows(turned.astype(jnp.float32), norm_params[0], norm_params[1]).astype(jnp.bfloat16)
    mine, theirs = normed[0], normed[1]
    beyond = swap(theirs, 4)
    even = [mine, swap(mine, 2), beyond, swap(beyond, 2)]
    odd = [swap(item, 1) for item in even]
    slots = [item for pair in zip(even, odd) for item in pair]

    blank = jnp.zeros((96, 64), jnp.bfloat16)
    shard = after(spread_heads(qkv_weight), beyond, even[1])
    count_rows = dp_size * 2
    mine_qkv = across(jnp.broadcast_to(shard[None], (count_rows,) + shard.shape), ("dp", "seq")).reshape(D, D)
    rest = (up_weight, down_weight.T, out_weight.T)
    along_dp = lax.all_gather(jnp.concatenate([item.astype(jnp.bfloat16) for item in rest] + [blank], -1), "dp", axis=0)
    all_rest = lax.all_gather(after(along_dp, even[1], even[3], mine_qkv), GROUP, axis=0).reshape((2, 4) + along_dp.shape)

    both_rand = jnp.concatenate([rand_blocks.reshape(-1), swap(rand_blocks.reshape(-1), 4)])
    table = jnp.concatenate(
        [jnp.reshape(me, (1,)), global_blocks, jnp.zeros((5,), jnp.int32), both_rand]
    ).astype(jnp.int32)
    qkv = project(slots, mine_qkv)

    o_parts = across(attend(table, qkv))
    mixed, mid, a2, a2t = middle(o_parts, all_rest, tokens, norm_params)
    all_qkv = gather_heads(after(mine_qkv, a2))

    dy = cotangent.reshape(a2.shape)
    block_out, back, up_mate, down_mate, up_own, down_own = mlp(
        head_word, a2, a2t, dy, dy.T, mid.reshape(a2.shape), all_rest
    )
    block_out = block_out.reshape(tokens.shape)
    up_mate, down_mate = swap(up_mate, 1), swap(down_mate, 1)

    mid_grad, low_grad, grad_first, grad_rest, norm_two = middle_back(
        back, mid, cotangent, all_rest, after(norm_params, all_qkv)
    )
    down_mate = after(down_mate, grad_first)
    grad_first, grad_rest = across(grad_first), across(grad_rest)

    fulls, packs = [], []

    def back_step(k, *ahead):
        grad, row = (grad_first, 0) if k == 0 else (grad_rest, k - 1)
        full, pack = attend_back(k, after(table, *ahead), qkv, grad, row)
        fulls.append(full)
        packs.append(across(pack))

    down_both = add_low(down_own, down_mate)
    down_terms = lax.psum_scatter(down_both, "dp", scatter_dimension=1, tiled=True)
    back_step(0, down_both)
    out_terms = out_weight_grad(head_word, after(low_grad, fulls[0], grad_rest), mixed)
    out_mate = swap(out_terms[0:2], 1)
    rest_both = jnp.concatenate([add_low(up_own, after(up_mate, fulls[0])), add_low(out_terms[2:4], out_mate)], -1)
    rest_terms = lax.psum_scatter(rest_both, "dp", scatter_dimension=1, tiled=True)
    back_step(1, fulls[0], rest_both)
    back_step(2, fulls[1], packs[0])
    fulls[2] = after(fulls[2], packs[1])
    wide = qkv_weight_grad(slots, fulls)
    all_terms = jnp.concatenate([after(down_terms, wide), after(rest_terms, wide)], -1)
    kept, sent = pick(all_terms, y, 96, 1), pick(all_terms, 1 - y, 96, 1)
    shares = across(wide.reshape(dp_size * 2, 96, 640), ("dp", "seq"))
    qkv_grad = jnp.sum(shares.astype(jnp.float32), 0)[:, 0:576]
    half = add_low(kept, swap(sent, 4))
    matrix_grad = half[0].astype(jnp.float32) + swap(half[1], 2).astype(jnp.float32)
    down_grad, up_grad, out_grad = matrix_grad[:, 0:D], matrix_grad[:, D : 2 * D], matrix_grad[:, 2 * D : 2 * D + 192]
    input_grad, norm_one = last(packs, all_qkv, tokens, mid_grad, norm_params)

    reduced = (qkv_grad, out_grad.T, up_grad, down_grad)
    squares = sum((jnp.sum(item * item) for item in reduced))
    shared = jnp.concatenate(
        [norm_one[0:2], norm_two[0:2], jnp.full((1, D), squares), jnp.zeros((3, D), jnp.float32)], 0
    )
    distance = 1
    while distance < count:
        shared = shared + swap_every(shared, distance, count)
        distance *= 2
    norm_grads = shared[0:4]
    grad_norm = jnp.sqrt(shared[4, 0] + jnp.sum(norm_grads * norm_grads))
    factor = jnp.minimum(1.0, CLIP_NORM / (grad_norm + 1e-06))
    groups = (
        (qkv_weight, reduced[0], qkv_first, qkv_second, qkv_average),
        (out_weight, reduced[1], out_first, out_second, out_average),
        (up_weight, reduced[2], up_first, up_second, up_average),
        (down_weight.T, reduced[3], down_first.T, down_second.T, down_average.T),
    )
    stepped = matrix_steps(jnp.reshape(factor, (1,)), groups)
    stepped[3] = [item.T for item in stepped[3]]
    norm_step = adamw_moment_update(
        norm_params, norm_grads, norm_first, norm_second, norm_average, rates()[4], factor
    )
    results = []
    for n in range(4):
        results += [item[n] for item in stepped] + [norm_step[n]]
    copies = [item[4] for item in stepped]
    return (block_out, input_grad, grad_norm, *results, *copies, factor * norm_grads[2:])


def is_fast(mesh):
    sizes = dict(mesh.shape)
    return sizes["seq"] == 2 and sizes["head"] == 4 and sizes["dp"] == 4


def solution(mesh):
    return jax.shard_map(
        fast_body if is_fast(mesh) else body,
        mesh=mesh,
        in_specs=(
            P("dp", ("seq", "head"), None),
            P("dp", ("seq", "head"), None),
            P("head", "seq", None),
            P(),
            P(("dp", "seq"), "head"),
            P("head", ("dp", "seq")),
            P(("dp", "seq"), "head"),
            P("head", ("dp", "seq")),
            P(),
            P(("dp", "seq"), "head"),
            P("head", ("dp", "seq")),
            P(("dp", "seq"), "head"),
            P("head", ("dp", "seq")),
            P(),
            P(("dp", "seq"), "head"),
            P("head", ("dp", "seq")),
            P(("dp", "seq"), "head"),
            P("head", ("dp", "seq")),
            P(),
            P(("dp", "seq"), "head"),
            P("head", ("dp", "seq")),
            P(("dp", "seq"), "head"),
            P("head", ("dp", "seq")),
            P(),
        ),
        out_specs=(
            P("dp", ("seq", "head"), None),
            P("dp", ("seq", "head"), None),
            P(),
            P(("dp", "seq"), "head"),
            P("head", ("dp", "seq")),
            P(("dp", "seq"), "head"),
            P("head", ("dp", "seq")),
            P(),
            P(("dp", "seq"), "head"),
            P("head", ("dp", "seq")),
            P(("dp", "seq"), "head"),
            P("head", ("dp", "seq")),
            P(),
            P(("dp", "seq"), "head"),
            P("head", ("dp", "seq")),
            P(("dp", "seq"), "head"),
            P("head", ("dp", "seq")),
            P(),
            P(("dp", "seq"), "head"),
            P("head", ("dp", "seq")),
            P(("dp", "seq"), "head"),
            P("head", ("dp", "seq")),
            P(),
            P(("dp", "seq"), "head"),
            P("head", ("dp", "seq")),
            P(("dp", "seq"), "head"),
            P("head", ("dp", "seq")),
            P(),
        ),
        check_vma=False,
    )
```

```python
import jax
import jax.numpy as jnp
from jax import lax
from jax.experimental import pallas as pl
from jax.experimental.pallas import tpu as pltpu
from jax.sharding import PartitionSpec as P

D = 768
DH = 64
FF = 3072
BLOCK = 64
STEP = 10


EPSILON = 1e-05
BETA_ONE = 0.9
BETA_TWO = 0.999
DECAY = 0.01
SMALL = 1e-08
CLIP_NORM = 1.0
AVERAGING = 0.999
NEGATIVE = -1e30


def norm_rows(values, gain_row, shift_row):
    center = values - jnp.mean(values, -1, keepdims=True)
    spread = jnp.mean(center * center, -1, keepdims=True)
    return center * lax.rsqrt(spread + EPSILON) * gain_row + shift_row


def key_table(rand_local, global_blocks, first_block, blocks_total):
    head_count, local_blocks = (rand_local.shape[0], rand_local.shape[1])
    places = first_block + jnp.arange(local_blocks, dtype=jnp.int32)
    left_side = jnp.maximum(places - 1, 0)
    right_side = jnp.minimum(places + 1, blocks_total - 1)
    window = jnp.stack([left_side, places, right_side], -1)
    key_index = jnp.concatenate(
        [
            jnp.broadcast_to(window[None], (head_count, local_blocks, 3)),
            rand_local,
            jnp.broadcast_to(global_blocks[None, None], (head_count, local_blocks, 2)),
        ],
        -1,
    )
    column_one = jnp.ones((local_blocks, 1), jnp.float32)
    key_valid = jnp.concatenate(
        [
            (places > 0).astype(jnp.float32)[:, None],
            column_one,
            (places < blocks_total - 1).astype(jnp.float32)[:, None],
            jnp.ones((local_blocks, 5), jnp.float32),
        ],
        -1,
    )
    return (key_index, key_valid)


def gather_rows(values):
    return lax.all_gather(values, "head", axis=1, tiled=True)


def sum_rows(values):
    return lax.psum_scatter(values, "head", scatter_dimension=1, tiled=True)


def contract(left_operand, right_operand):
    return jnp.einsum(
        "enz,enf->zf", left_operand, right_operand, preferred_element_type=jnp.float32
    )


def to_heads(values, head_count):
    seq_count, token_count = (values.shape[0], values.shape[1])
    return jnp.moveaxis(
        values.reshape(seq_count, token_count // BLOCK, BLOCK, head_count, DH), 3, 0
    )


def from_heads(values):
    head_count, seq_count, blocks = (values.shape[0], values.shape[1], values.shape[2])
    return jnp.moveaxis(values, 0, 3).reshape(seq_count, blocks * BLOCK, head_count * DH)


def pick_keys(kv_all, key_index):
    seq_count, token_count = (kv_all.shape[0], kv_all.shape[1])
    head_count = key_index.shape[0]
    blocks = kv_all.reshape(seq_count, token_count // BLOCK, BLOCK, head_count, 2, DH)
    by_head = jnp.moveaxis(blocks, 3, 0)
    return jax.vmap(lambda source, chosen: source[:, chosen])(by_head, key_index)


def scores_of(queries, picked, key_valid):
    raw_scores = jnp.einsum(
        "hsnbe,hsnkce->hsnbkc", queries, picked[..., 0, :], preferred_element_type=jnp.float32
    ) * DH ** (-0.5)
    return jnp.where(key_valid[None, None, :, None, :, None] > 0, raw_scores, NEGATIVE)


def attend_forward(queries, picked, key_valid):
    raw_scores = scores_of(queries, picked, key_valid)
    score_shape = raw_scores.shape
    scores_flat = raw_scores.reshape(score_shape[:4] + (score_shape[4] * score_shape[5],))
    row_max = jnp.max(scores_flat, -1, keepdims=True)
    exponent = jnp.exp(scores_flat - row_max)
    row_total = jnp.sum(exponent, -1, keepdims=True)
    probabilities = (exponent / row_total).astype(jnp.bfloat16).reshape(score_shape)
    output = jnp.einsum(
        "hsnbkc,hsnkce->hsnbe", probabilities, picked[..., 1, :], preferred_element_type=jnp.float32
    )
    return (output, row_max + jnp.log(row_total))


def attend_backward(queries, picked, key_valid, log_total, grad_out):
    raw_scores = scores_of(queries, picked, key_valid)
    score_shape = raw_scores.shape
    scores_flat = raw_scores.reshape(score_shape[:4] + (score_shape[4] * score_shape[5],))
    probabilities = jnp.exp(scores_flat - log_total)
    grad_probs = jnp.einsum(
        "hsnbe,hsnkce->hsnbkc", grad_out, picked[..., 1, :], preferred_element_type=jnp.float32
    ).reshape(scores_flat.shape)
    row_delta = jnp.sum(probabilities * grad_probs, -1, keepdims=True)
    grad_scores = probabilities * (grad_probs - row_delta)
    grad_scores = grad_scores.astype(jnp.bfloat16).reshape(score_shape)
    low_probs = probabilities.astype(jnp.bfloat16).reshape(score_shape)
    grad_query = jnp.einsum(
        "hsnbkc,hsnkce->hsnbe", grad_scores, picked[..., 0, :], preferred_element_type=jnp.float32
    ) * DH ** (-0.5)
    grad_keys = jnp.einsum(
        "hsnbkc,hsnbe->hsnkce", grad_scores, queries, preferred_element_type=jnp.float32
    ) * DH ** (-0.5)
    grad_values = jnp.einsum(
        "hsnbkc,hsnbe->hsnkce", low_probs, grad_out, preferred_element_type=jnp.float32
    )
    return (grad_query, jnp.stack([grad_keys, grad_values], -2), row_delta)


def spread_back(grad_pairs, key_index, seq_count, blocks_total):
    head_count = key_index.shape[0]
    zero_grid = jnp.zeros((head_count, seq_count, blocks_total, BLOCK, 2, DH), jnp.float32)
    filled = jax.vmap(lambda source, chosen, addend: source.at[:, chosen].add(addend))(
        zero_grid, key_index, grad_pairs
    )
    return jnp.moveaxis(filled, 0, 3).reshape(seq_count, blocks_total * BLOCK, head_count * 2 * DH)


def rates():
    return (
        1.5 * D ** (-0.5),
        1.5 * max(1, D // (8 * BLOCK)) ** (-0.5),
        1.5 * D ** (-0.5),
        1.5 * FF ** (-0.5),
        0.5,
    )


def adamw_moment_update(weight, gradient, moment_one, moment_two, average, rate, factor):
    decay_mean = min(AVERAGING, (1.0 + STEP) / (10.0 + STEP))
    clipped = gradient * factor
    first_new = BETA_ONE * moment_one + (1.0 - BETA_ONE) * clipped
    second_new = BETA_TWO * moment_two + (1.0 - BETA_TWO) * clipped * clipped
    update = (
        first_new / (1.0 - BETA_ONE**STEP) / (jnp.sqrt(second_new / (1.0 - BETA_TWO**STEP)) + SMALL)
    )
    weight_new = weight - rate * (update + DECAY * weight)
    average_new = decay_mean * average + (1.0 - decay_mean) * weight_new
    return (weight_new, first_new, second_new, average_new)


def body(
    tokens,
    cotangent,
    rand_blocks,
    global_blocks,
    qkv_weight,
    out_weight,
    up_weight,
    down_weight,
    norm_params,
    qkv_first,
    out_first,
    up_first,
    down_first,
    norm_first,
    qkv_second,
    out_second,
    up_second,
    down_second,
    norm_second,
    qkv_average,
    out_average,
    up_average,
    down_average,
    norm_average,
):
    qkv_low, out_low, up_low, down_low = (
        lax.all_gather(qkv_weight.astype(jnp.bfloat16), ("dp", "seq"), axis=0, tiled=True),
        lax.all_gather(out_weight.astype(jnp.bfloat16), ("dp", "seq"), axis=1, tiled=True),
        lax.all_gather(up_weight.astype(jnp.bfloat16), ("dp", "seq"), axis=0, tiled=True),
        lax.all_gather(down_weight.astype(jnp.bfloat16), ("dp", "seq"), axis=1, tiled=True),
    )
    seq_count = tokens.shape[0]
    head_count = rand_blocks.shape[0]
    local_blocks = rand_blocks.shape[1]
    blocks_total = local_blocks * lax.axis_size("seq")
    first_block = lax.axis_index("seq") * local_blocks
    key_index, key_valid = key_table(rand_blocks, global_blocks, first_block, blocks_total)
    inputs = tokens.astype(jnp.float32)
    full_one = gather_rows(norm_rows(inputs, norm_params[0], norm_params[1]).astype(jnp.bfloat16))
    token_count = full_one.shape[1]
    qkv_all = jnp.dot(full_one, qkv_low, preferred_element_type=jnp.float32).astype(jnp.bfloat16)
    qkv_parts = qkv_all.reshape(seq_count, token_count, head_count, 3, DH)
    kv_local = qkv_parts[:, :, :, 1:, :].reshape(seq_count, token_count, head_count * 2 * DH)
    kv_all = lax.all_gather(kv_local, "seq", axis=1, tiled=True)
    picked = pick_keys(kv_all, key_index)
    queries = to_heads(qkv_parts[:, :, :, 0, :], head_count)
    attended, log_total = attend_forward(queries, picked, key_valid)
    mixed_heads = from_heads(attended.astype(jnp.bfloat16))
    residual = inputs + sum_rows(jnp.dot(mixed_heads, out_low, preferred_element_type=jnp.float32))
    full_two = gather_rows(norm_rows(residual, norm_params[2], norm_params[3]).astype(jnp.bfloat16))
    upward = jnp.dot(full_two, up_low, preferred_element_type=jnp.float32)
    active = jax.nn.gelu(upward).astype(jnp.bfloat16)
    result = residual + sum_rows(jnp.dot(active, down_low, preferred_element_type=jnp.float32))
    block_out = result.astype(jnp.bfloat16)
    grad_top = gather_rows(cotangent)
    grad_down = contract(active, grad_top)
    grad_active = jnp.dot(grad_top, down_low.T, preferred_element_type=jnp.float32)
    _, gelu_back = jax.vjp(jax.nn.gelu, upward)
    grad_upward = gelu_back(grad_active)[0].astype(jnp.bfloat16)
    grad_up = contract(full_two, grad_upward)
    part_two = sum_rows(jnp.dot(grad_upward, up_low.T, preferred_element_type=jnp.float32))
    _, norm_back_two = jax.vjp(norm_rows, residual, norm_params[2], norm_params[3])
    grad_residual_norm, grad_gain_two, grad_shift_two = norm_back_two(part_two)
    grad_residual = cotangent.astype(jnp.float32) + grad_residual_norm
    grad_middle = gather_rows(grad_residual.astype(jnp.bfloat16))
    grad_out = contract(mixed_heads, grad_middle)
    grad_mixed = jnp.dot(grad_middle, out_low.T, preferred_element_type=jnp.float32).astype(
        jnp.bfloat16
    )
    grad_query, grad_pairs, row_delta = attend_backward(
        queries, picked, key_valid, log_total, to_heads(grad_mixed, head_count)
    )
    grad_kv_full = spread_back(grad_pairs, key_index, seq_count, blocks_total)
    grad_kv = lax.psum_scatter(
        grad_kv_full.astype(jnp.bfloat16), "seq", scatter_dimension=1, tiled=True
    ).astype(jnp.float32)
    query_gradient = from_heads(grad_query).reshape(seq_count, token_count, head_count, 1, DH)
    grad_qkv_rows = jnp.concatenate(
        [query_gradient, grad_kv.reshape(seq_count, token_count, head_count, 2, DH)], 3
    )
    grad_qkv_rows = grad_qkv_rows.reshape(seq_count, token_count, head_count * 3 * DH).astype(
        jnp.bfloat16
    )
    grad_qkv = contract(full_one, grad_qkv_rows)
    part_one = sum_rows(jnp.dot(grad_qkv_rows, qkv_low.T, preferred_element_type=jnp.float32))
    _, norm_back_one = jax.vjp(norm_rows, inputs, norm_params[0], norm_params[1])
    grad_input_norm, grad_gain_one, grad_shift_one = norm_back_one(part_one)
    input_grad = (grad_residual + grad_input_norm).astype(jnp.bfloat16)
    grad_norm_local = jnp.stack([grad_gain_one, grad_shift_one, grad_gain_two, grad_shift_two])
    reduced_total = (
        lax.psum_scatter(grad_qkv, ("dp", "seq"), scatter_dimension=0, tiled=True),
        lax.psum_scatter(grad_out, ("dp", "seq"), scatter_dimension=1, tiled=True),
        lax.psum_scatter(grad_up, ("dp", "seq"), scatter_dimension=0, tiled=True),
        lax.psum_scatter(grad_down, ("dp", "seq"), scatter_dimension=1, tiled=True),
    )
    squares = sum((jnp.sum(item * item) for item in reduced_total))
    norm_grads = lax.psum(grad_norm_local, ("dp", "seq", "head"))
    matrix_squares = lax.psum(squares, ("dp", "seq", "head"))
    grad_norm = jnp.sqrt(matrix_squares + jnp.sum(norm_grads * norm_grads))
    factor = jnp.minimum(1.0, CLIP_NORM / (grad_norm + 1e-06))
    weights = (qkv_weight, out_weight, up_weight, down_weight, norm_params)
    gradients = (reduced_total[0], reduced_total[1], reduced_total[2], reduced_total[3], norm_grads)
    firsts = (qkv_first, out_first, up_first, down_first, norm_first)
    seconds = (qkv_second, out_second, up_second, down_second, norm_second)
    averages = (qkv_average, out_average, up_average, down_average, norm_average)
    results = [
        adamw_moment_update(
            weights[slot],
            gradients[slot],
            firsts[slot],
            seconds[slot],
            averages[slot],
            rates()[slot],
            factor,
        )
        for slot in range(5)
    ]
    news = tuple((item[0] for item in results))
    first_news = tuple((item[1] for item in results))
    second_news = tuple((item[2] for item in results))
    average_news = tuple((item[3] for item in results))
    return (
        block_out,
        input_grad,
        grad_norm,
        news[0],
        news[1],
        news[2],
        news[3],
        news[4],
        first_news[0],
        first_news[1],
        first_news[2],
        first_news[3],
        first_news[4],
        second_news[0],
        second_news[1],
        second_news[2],
        second_news[3],
        second_news[4],
        average_news[0],
        average_news[1],
        average_news[2],
        average_news[3],
        average_news[4],
        news[0].astype(jnp.bfloat16),
        news[1].astype(jnp.bfloat16),
        news[2].astype(jnp.bfloat16),
        news[3].astype(jnp.bfloat16),
        factor * norm_grads[2:],
    )


GROUP = ("seq", "head")
EVERY = ("dp", "seq", "head")
FULL = 4096
CHUNK = 512
MB = 1024 * 1024
COST = pl.CostEstimate(flops=10**6, bytes_accessed=10**5, transcendentals=0)


def limits(megabytes):
    return pltpu.CompilerParams(vmem_limit_bytes=megabytes * MB)


def swap(values, distance):
    return lax.ppermute(values, GROUP, [(i, i ^ distance) for i in range(8)])


def swap_every(values, distance, count):
    return lax.ppermute(values, EVERY, [(i, i ^ distance) for i in range(count)])


def nt(left, right):
    return lax.dot_general(left, right, (((1,), (1,)), ((), ())), preferred_element_type=jnp.float32)


def nn(left, right):
    return lax.dot_general(left, right, (((1,), (0,)), ((), ())), preferred_element_type=jnp.float32)


def tn(left, right):
    return lax.dot_general(left, right, (((0,), (0,)), ((), ())), preferred_element_type=jnp.float32)


def lane_low(shape):
    return lax.broadcasted_iota(jnp.int32, shape, len(shape) - 1) < 64


def roll64(values):
    return pltpu.roll(values, 64, 1)


def block_places(tab_ref, k, block):
    me = tab_ref[0]
    part = (block // 32) ^ (me // 4)
    base = 8 + ((part * 3 + k) * 32 + block % 32) * 3
    chosen = [
        jnp.maximum(block - 1, 0),
        block,
        jnp.minimum(block + 1, 63),
        tab_ref[base],
        tab_ref[base + 1],
        tab_ref[base + 2],
        tab_ref[1],
        tab_ref[2],
    ]
    return [pl.multiple_of((((b // 8) ^ me) * 8 + b % 8) * 64, 64) for b in chosen]


def spread_kernel(in_ref, out_ref):
    low = lane_low((96, 128))
    tiles = [in_ref[:, j * 128 : j * 128 + 128] for j in range(4)]
    tiles.append(jnp.concatenate([in_ref[:, 512:576], jnp.zeros((96, 64), jnp.float32)], 1))
    scale = DH ** (-0.5)
    parts = [
        jnp.where(low, tiles[0] * scale, 0.0),
        jnp.where(low, roll64(tiles[0]), roll64(tiles[1])),
        jnp.where(low, roll64(tiles[1]) * scale, 0.0),
        tiles[2],
        jnp.where(low, tiles[3] * scale, 0.0),
        jnp.where(low, roll64(tiles[3]), roll64(tiles[4])),
    ]
    for n, part in enumerate(parts):
        out_ref[:, n * 128 : n * 128 + 128] = part.astype(jnp.bfloat16)


def spread_heads(shard):
    return pl.pallas_call(
        spread_kernel,
        out_shape=jax.ShapeDtypeStruct((96, D), jnp.bfloat16),
        compiler_params=limits(60),
        name="spread_heads",
        cost_estimate=COST,
    )(shard)


def qkv_kernel(*refs):
    tok_refs, weight_ref, out_ref = refs[:8], refs[8], refs[9]

    def one(tok_ref):
        out_ref[...] = nn(tok_ref[...], weight_ref[...]).astype(jnp.bfloat16)

    for slot, tok_ref in enumerate(tok_refs):
        pl.when(pl.program_id(0) == slot)(lambda tok_ref=tok_ref: one(tok_ref))


def project(slots, weights):
    return pl.pallas_call(
        qkv_kernel,
        grid=(8,),
        in_specs=[pl.BlockSpec((CHUNK, D), lambda i: (0, 0))] * 8 + [pl.BlockSpec((D, D), lambda i: (0, 0))],
        out_specs=pl.BlockSpec((CHUNK, D), lambda i: (i, 0)),
        out_shape=jax.ShapeDtypeStruct((FULL, D), jnp.bfloat16),
        compiler_params=limits(60),
        name="project",
        cost_estimate=COST,
    )(*slots, weights)


def hide(scores, low, high):
    lane = lax.broadcasted_iota(jnp.int32, scores.shape, 1)
    return jnp.where((lane >= low) & (lane < high), NEGATIVE, scores)


def softmax_rows(scores, part, q):
    if q == 0:
        scores = jnp.where(part == 0, hide(scores, 0, 64), scores)
    if q == 7:
        scores = jnp.where(part == 7, hide(scores, 128, 192), scores)
    top = jnp.max(scores, -1, keepdims=True)
    exponent = jnp.exp(scores - top)
    total = jnp.sum(exponent, -1, keepdims=True)
    return exponent * (1.0 / total)


def attend_kernel(k, tab_ref, qkv_ref, out_ref):
    me = tab_ref[0]

    def step(pair, carry):
        blocks = [(pair * 2 + n, q) for n in range(2) for q in range(8)]
        keys, scores = [], []
        for slot, q in blocks:
            places = block_places(tab_ref, k, (slot ^ me) * 8 + q)
            keys.append(jnp.concatenate([qkv_ref[pl.ds(p, 64), 128:256] for p in places], 0))
            at = pl.multiple_of(slot * CHUNK + q * 64, 64)
            scores.append(nt(qkv_ref[pl.ds(at, 64), 0:128], keys[-1]))
        probs = [
            softmax_rows(score, slot ^ me, q).astype(jnp.bfloat16) for score, (slot, q) in zip(scores, blocks)
        ]
        outs = [nn(prob, key) for prob, key in zip(probs, keys)]
        for n, (slot, q) in enumerate(blocks):
            if q < 4:
                both = jnp.where(lane_low(outs[n].shape), roll64(outs[n]), outs[n + 4])
                out_ref[slot ^ me, q * 64 : q * 64 + 64, :] = both.astype(jnp.bfloat16)
        return carry

    lax.fori_loop(0, 4, step, 0)


def attend(table, qkv):
    return pl.pallas_call(
        lambda *refs: attend_kernel(pl.program_id(0), *refs),
        grid_spec=pltpu.PrefetchScalarGridSpec(
            num_scalar_prefetch=1,
            grid=(3,),
            in_specs=[pl.BlockSpec((FULL, 256), lambda i, t: (0, i))],
            out_specs=pl.BlockSpec((8, 256, 128), lambda i, t: (0, i, 0)),
        ),
        out_shape=jax.ShapeDtypeStruct((8, D, 128), jnp.bfloat16),
        compiler_params=limits(60),
        name="attend",
        cost_estimate=COST,
    )(table, qkv)


def attend_back_kernel(k, tab_ref, qkv_ref, grad_ref, full_ref, pack_ref, acc_ref, shared_ref):
    me = tab_ref[0]
    acc_ref[...] = jnp.zeros_like(acc_ref)
    shared_ref[...] = jnp.zeros_like(shared_ref)

    def step(slot, carry):
        part = slot ^ me
        grads = [None] * 8
        for j in range(4):
            tile = grad_ref[part, j * 64 : j * 64 + 64, :].astype(jnp.float32)
            low_lanes = lane_low(tile.shape)
            grads[j] = jnp.where(low_lanes, 0.0, roll64(tile)).astype(jnp.bfloat16)
            grads[j + 4] = jnp.where(low_lanes, 0.0, tile).astype(jnp.bfloat16)
        places, stacks, keys, both = [], [], [], []
        for q in range(8):
            places.append(block_places(tab_ref, k, part * 8 + q))
            keys.append(jnp.concatenate([qkv_ref[pl.ds(p, 64), 128:256] for p in places[q]], 0))
            at = pl.multiple_of(slot * CHUNK + q * 64, 64)
            stacks.append(jnp.concatenate([qkv_ref[pl.ds(at, 64), 0:128], grads[q]], 0))
            both.append(nt(stacks[q], keys[q]))
        lows, pairs = [], []
        for q in range(8):
            probs, grad_probs = softmax_rows(both[q][:64], part, q), both[q][64:]
            delta = jnp.sum(probs * grad_probs, -1, keepdims=True)
            lows.append((probs * (grad_probs - delta)).astype(jnp.bfloat16))
            pairs.append(jnp.concatenate([lows[q], probs.astype(jnp.bfloat16)], 0))
        queries = []
        for q in range(8):
            grad_query = nn(lows[q], keys[q]) * DH ** (-0.5)
            queries.append(jnp.where(lane_low(grad_query.shape), grad_query, 0.0))
            at = pl.multiple_of(slot * CHUNK + q * 64, 64)
            full_ref[pl.ds(at, 64), 0:128] = queries[q].astype(jnp.bfloat16)
        spreads = [tn(pairs[q], stacks[q]) for q in range(8)]
        shared = spreads[0][384:]
        for q in range(8):
            if q:
                shared = shared + spreads[q][384:]
            for m in range(6):
                acc_ref[pl.ds(places[q][m], 64), :] += spreads[q][m * 64 : m * 64 + 64]
        shared_ref[...] += shared
        for j in range(4):
            packed = queries[j] + roll64(queries[j + 4])
            pack_ref[part, j * 64 : j * 64 + 64, :] = packed.astype(jnp.bfloat16)
        return carry

    lax.fori_loop(0, 8, step, 0)
    for m in range(2):
        block = tab_ref[1 + m]
        at = pl.multiple_of((((block // 8) ^ me) * 8 + block % 8) * 64, 64)
        acc_ref[pl.ds(at, 64), :] += shared_ref[m * 64 : m * 64 + 64]

    def finish(slot, carry):
        at = pl.ds(pl.multiple_of(slot * CHUNK, CHUNK), CHUNK)
        low = acc_ref[at, :].astype(jnp.bfloat16)
        full_ref[at, 128:256] = low
        pack_ref[slot ^ me, 256:768, :] = low
        return carry

    lax.fori_loop(0, 8, finish, 0)


def attend_back(k, table, qkv, grad, row):
    return pl.pallas_call(
        lambda *refs: attend_back_kernel(k, *refs),
        grid_spec=pltpu.PrefetchScalarGridSpec(
            num_scalar_prefetch=1,
            grid=(1,),
            in_specs=[
                pl.BlockSpec((FULL, 256), lambda i, t: (0, k)),
                pl.BlockSpec((8, 256, 128), lambda i, t: (0, row, 0)),
            ],
            out_specs=[
                pl.BlockSpec((FULL, 256), lambda i, t: (0, 0)),
                pl.BlockSpec((8, 768, 128), lambda i, t: (0, 0, 0)),
            ],
            scratch_shapes=[pltpu.VMEM((FULL, 128), jnp.float32), pltpu.VMEM((128, 128), jnp.float32)],
        ),
        out_shape=[
            jax.ShapeDtypeStruct((FULL, 256), jnp.bfloat16),
            jax.ShapeDtypeStruct((8, 768, 128), jnp.bfloat16),
        ],
        compiler_params=limits(60),
        name="attend_back",
        cost_estimate=COST,
    )(table, qkv, grad)


def norm_stats(values):
    center = values - jnp.mean(values, -1, keepdims=True)
    spread = jnp.mean(center * center, -1, keepdims=True)
    scale = lax.rsqrt(spread + EPSILON)
    return center * scale, scale


def halves(first, second):
    low = lane_low(first.shape)
    upper = jnp.where(low, first, roll64(second))
    lower = jnp.where(low, roll64(first), second)
    return upper, lower


def mid_kernel(head_ref, o_ref, w0_ref, w1_ref, w2_ref, w3_ref, tok_ref, par_ref, cat_ref, mid_ref, a2_ref, a2t_ref):
    middle = tok_ref[0].astype(jnp.float32)
    cat_ref[...] = jnp.zeros_like(cat_ref)
    for h, w_ref in enumerate((w0_ref, w1_ref, w2_ref, w3_ref)):
        group = head_ref[0] ^ NEAR[h]
        tiles = [o_ref[group, at : at + 256].astype(jnp.float32) for at in (0, 256, 512)]
        upper, lower = halves(tiles[0], tiles[1])
        last_upper, last_lower = halves(tiles[2], jnp.zeros_like(tiles[2]))
        cat_ref[0:256, h * 256 : h * 256 + 128] = upper.astype(jnp.bfloat16)
        cat_ref[256:512, h * 256 : h * 256 + 128] = lower.astype(jnp.bfloat16)
        cat_ref[0:256, h * 256 + 128 : h * 256 + 256] = last_upper.astype(jnp.bfloat16)
        cat_ref[256:512, h * 256 + 128 : h * 256 + 256] = last_lower.astype(jnp.bfloat16)
        middle = middle + nt(cat_ref[:, h * 256 : h * 256 + 256], w_ref[...])
    mid_ref[0] = middle
    normed, _ = norm_stats(middle)
    low = normed * par_ref[2:3, :] + par_ref[3:4, :]
    a2_ref[...] = low.astype(jnp.bfloat16)
    a2t_ref[...] = low.T.astype(jnp.bfloat16)


NEAR = (0, 2, 1, 3)


def middle(head, o_parts, weights, tokens, params):
    seqs = tokens.shape[0]
    rows = pl.BlockSpec((1, CHUNK, D), lambda s, t: (s, 0, 0))
    return pl.pallas_call(
        mid_kernel,
        grid_spec=pltpu.PrefetchScalarGridSpec(
            num_scalar_prefetch=1,
            grid=(seqs,),
            in_specs=[
                pl.BlockSpec((4, D, 128), lambda s, t: (s, 0, 0)),
                *(pl.BlockSpec((D, 256), lambda s, t: (0, 3)) for _ in range(4)),
                rows, pl.BlockSpec((4, D), lambda s, t: (0, 0)),
            ],
            out_specs=[
                pl.BlockSpec((CHUNK, 1024), lambda s, t: (s, 0)), rows,
                pl.BlockSpec((CHUNK, D), lambda s, t: (s, 0)), pl.BlockSpec((D, CHUNK), lambda s, t: (0, s)),
            ],
        ),
        out_shape=[
            jax.ShapeDtypeStruct((seqs * CHUNK, 1024), jnp.bfloat16),
            jax.ShapeDtypeStruct(tokens.shape, jnp.float32),
            jax.ShapeDtypeStruct((seqs * CHUNK, D), jnp.bfloat16),
            jax.ShapeDtypeStruct((D, seqs * CHUNK), jnp.bfloat16),
        ],
        compiler_params=limits(60),
        name="middle",
        cost_estimate=COST,
    )(head, o_parts, *weights, tokens, params)


def mlp_kernel(a2_ref, a2t_ref, dy_ref, dyt_ref, mid_ref, u0_ref, u1_ref, u2_ref, u3_ref, d0_ref, d1_ref, d2_ref, d3_ref, out_ref, back_ref,
               um_ref, dm_ref, uo_ref, do_ref, g_ref, u_ref, wuo_ref, wdo_ref, wut_ref, wdt_ref, acc_ref):
    step = pl.program_id(0)

    @pl.when(step == 0)
    def _():
        acc_ref[...] = mid_ref[...]
        back_ref[...] = jnp.zeros_like(back_ref)

    for n, (wu_ref, wd_ref) in enumerate(((u2_ref, d2_ref), (u3_ref, d3_ref), (u0_ref, d0_ref), (u1_ref, d1_ref))):
        @pl.when(step == n)
        def _(wu_ref=wu_ref, wd_ref=wd_ref):
            wuo_ref[...] = wu_ref[...]
            wdo_ref[...] = wd_ref[...]

    wut_ref[...] = wuo_ref[...].T
    wdt_ref[...] = wdo_ref[...].T
    rate, cubic = 0.7978845608028654, 0.044715
    rows = [slice(m * 256, m * 256 + 256) for m in range(4)]
    products = lambda m: (nn(a2_ref[rows[m], :], wuo_ref[...]), nn(dy_ref[rows[m], :], wdo_ref[...]))
    ahead = products(0)
    for m in range(4):
        up, grad = ahead
        if m < 3:
            ahead = products(m + 1)
        at = rows[m]
        square = up * up
        bend = jnp.tanh(up * (rate + rate * cubic * square))
        half = 0.5 + 0.5 * bend
        g_ref[at, :] = (up * half).astype(jnp.bfloat16)
        slope = half + (0.5 * up) * (1.0 - bend * bend) * (rate + 3.0 * rate * cubic * square)
        u_ref[at, :] = (grad * slope).astype(jnp.bfloat16)
        acc_ref[at, :] += nn(g_ref[at, :], wdt_ref[...])
        back_ref[at, :] += nn(u_ref[at, :], wut_ref[...])
    up_grad = nn(a2t_ref[...], u_ref[...]).astype(jnp.bfloat16)
    down_grad = nn(dyt_ref[...], g_ref[...]).astype(jnp.bfloat16)

    @pl.when(step < 2)
    def _():
        um_ref[0] = up_grad
        dm_ref[0] = down_grad

    @pl.when(step >= 2)
    def _():
        uo_ref[0] = up_grad
        do_ref[0] = down_grad

    @pl.when(step == 3)
    def _():
        out_ref[...] = acc_ref[...].astype(jnp.bfloat16)


def mlp(a2, a2t, dy, dyt, mid, up_weights, down_weights):
    tokens = a2.shape[0]
    whole = lambda shape: pl.BlockSpec(shape, lambda i: (0, 0))
    theirs = pl.BlockSpec((1, D, D), lambda i: (jnp.minimum(i, 1), 0, 0))
    ours = pl.BlockSpec((1, D, D), lambda i: (jnp.maximum(i - 2, 0), 0, 0))
    low = jax.ShapeDtypeStruct((2, D, D), jnp.bfloat16)
    return pl.pallas_call(
        mlp_kernel,
        grid=(4,),
        in_specs=[
            whole((tokens, D)), whole((D, tokens)), whole((tokens, D)), whole((D, tokens)), whole((tokens, D)),
            *(whole((D, D)) for _ in range(8)),
        ],
        out_specs=[whole((tokens, D)), whole((tokens, D)), theirs, theirs, ours, ours],
        out_shape=[
            jax.ShapeDtypeStruct((tokens, D), jnp.bfloat16), jax.ShapeDtypeStruct((tokens, D), jnp.float32),
            low, low, low, low,
        ],
        scratch_shapes=[
            pltpu.VMEM((tokens, D), jnp.bfloat16), pltpu.VMEM((tokens, D), jnp.bfloat16),
            *(pltpu.VMEM((D, D), jnp.bfloat16) for _ in range(4)), pltpu.VMEM((tokens, D), jnp.float32),
        ],
        compiler_params=limits(60),
        name="mlp",
        cost_estimate=COST,
    )(a2, a2t, dy, dyt, mid, *up_weights, *down_weights)


def norm_back(grad, values, gain):
    normed, scale = norm_stats(values)
    gain_grad = jnp.sum(grad * normed, 0, keepdims=True)
    shift_grad = jnp.sum(grad, 0, keepdims=True)
    inner = grad * gain
    across = jnp.mean(inner, -1, keepdims=True)
    along = jnp.mean(inner * normed, -1, keepdims=True)
    return scale * (inner - across - normed * along), gain_grad, shift_grad


def mid_back_kernel(head_ref, b_ref, mid_ref, dy_ref, w0_ref, w1_ref, w2_ref, w3_ref, par_ref, grad_ref, low_ref, first_ref, rest_ref, norm_ref):
    grad, gain_grad, shift_grad = norm_back(b_ref[...], mid_ref[0], par_ref[2:3, :])
    total = dy_ref[0].astype(jnp.float32) + grad
    grad_ref[0] = total
    low = total.astype(jnp.bfloat16)
    low_ref[...] = low
    for h, w_ref in zip(NEAR, (w0_ref, w1_ref, w2_ref, w3_ref)):
        group = head_ref[0] ^ h
        mixed = nn(low, w_ref[...])
        first, second = halves(mixed[0:256, 0:128], mixed[256:512, 0:128])
        third, _ = halves(mixed[0:256, 128:256], mixed[256:512, 128:256])
        first_ref[group] = first.astype(jnp.bfloat16)
        rest_ref[group, 0:256] = second.astype(jnp.bfloat16)
        rest_ref[group, 256:512] = third.astype(jnp.bfloat16)

    @pl.when(pl.program_id(0) == 0)
    def _():
        norm_ref[...] = jnp.zeros_like(norm_ref)

    norm_ref[0:1, :] += gain_grad
    norm_ref[1:2, :] += shift_grad


def middle_back(head, back, mid, dy, weights, params):
    seqs = dy.shape[0]
    rows = pl.BlockSpec((1, CHUNK, D), lambda s, t: (s, 0, 0))
    flat = pl.BlockSpec((CHUNK, D), lambda s, t: (s, 0))
    return pl.pallas_call(
        mid_back_kernel,
        grid_spec=pltpu.PrefetchScalarGridSpec(
            num_scalar_prefetch=1,
            grid=(seqs,),
            in_specs=[
                flat, rows, rows, *(pl.BlockSpec((D, 256), lambda s, t: (0, 3)) for _ in range(4)),
                pl.BlockSpec((4, D), lambda s, t: (0, 0)),
            ],
            out_specs=[
                rows, flat, pl.BlockSpec((4, 256, 128), lambda s, t: (s, 0, 0)),
                pl.BlockSpec((4, 512, 128), lambda s, t: (s, 0, 0)), pl.BlockSpec((8, D), lambda s, t: (0, 0)),
            ],
        ),
        out_shape=[
            jax.ShapeDtypeStruct(dy.shape, jnp.float32),
            jax.ShapeDtypeStruct((seqs * CHUNK, D), jnp.bfloat16),
            jax.ShapeDtypeStruct((8, 256, 128), jnp.bfloat16),
            jax.ShapeDtypeStruct((8, 512, 128), jnp.bfloat16),
            jax.ShapeDtypeStruct((8, D), jnp.float32),
        ],
        compiler_params=limits(60),
        name="middle_back",
        cost_estimate=COST,
    )(head, back, mid, dy, *weights, params)


def out_grad_kernel(low_ref, cat_ref, out_ref):
    for n, h in enumerate((2, 3, 0, 1)):
        out_ref[n] = tn(low_ref[...], cat_ref[:, h * 256 : h * 256 + 256]).astype(jnp.bfloat16)


def out_weight_grad(low, cat):
    return pl.pallas_call(
        out_grad_kernel,
        out_shape=jax.ShapeDtypeStruct((4, D, 256), jnp.bfloat16),
        compiler_params=limits(60),
        name="out_weight_grad",
        cost_estimate=COST,
    )(low, cat)


def merge_heads(queries, pairs):
    low = lane_low(queries[0].shape)
    return [
        jnp.where(low, queries[0], roll64(pairs[0])),
        jnp.where(low, roll64(pairs[0]), roll64(queries[1])),
        pairs[1],
        jnp.where(low, queries[2], roll64(pairs[2])),
        jnp.where(low, roll64(pairs[2]), 0.0),
    ]


def qkv_grad_kernel(*refs):
    tok_refs, full_refs, out_ref, acc_ref = refs[:8], refs[8:11], refs[11], refs[12]
    step = pl.program_id(0)

    @pl.when(step == 0)
    def _():
        acc_ref[...] = jnp.zeros_like(acc_ref)

    def one(tok_ref):
        acc_ref[...] += tn(tok_ref[...], jnp.concatenate([ref[...] for ref in full_refs], 1))

    for slot, tok_ref in enumerate(tok_refs):
        pl.when(step == slot)(lambda tok_ref=tok_ref: one(tok_ref))

    @pl.when(step == 7)
    def _():
        tiles = merge_heads(
            [acc_ref[:, k * 256 : k * 256 + 128] for k in range(3)],
            [acc_ref[:, k * 256 + 128 : k * 256 + 256] for k in range(3)],
        )
        for j, tile in enumerate(tiles):
            out_ref[:, j * 128 : j * 128 + 128] = tile.astype(jnp.bfloat16)


def qkv_weight_grad(slots, fulls):
    return pl.pallas_call(
        qkv_grad_kernel,
        grid=(8,),
        in_specs=[pl.BlockSpec((CHUNK, D), lambda i: (0, 0))] * 8 + [pl.BlockSpec((CHUNK, 256), lambda i: (i, 0))] * 3,
        out_specs=pl.BlockSpec((D, 640), lambda i: (0, 0)),
        out_shape=jax.ShapeDtypeStruct((D, 640), jnp.bfloat16),
        scratch_shapes=[pltpu.VMEM((D, D), jnp.float32)],
        compiler_params=limits(60),
        name="qkv_weight_grad",
        cost_estimate=COST,
    )(*slots, *fulls)


def last_kernel(p0_ref, p1_ref, p2_ref, w_ref, tok_ref, mid_ref, par_ref, out_ref, norm_ref):
    grad = None
    low = lane_low((CHUNK, 128))
    for h in range(4):
        tiles = []
        for ref in (p0_ref, p1_ref, p2_ref):
            both = ref[h, 0:256, :].astype(jnp.float32) * DH**0.5
            tiles.append(jnp.where(low, jnp.concatenate([both, roll64(both)], 0), 0.0).astype(jnp.bfloat16))
            tiles.append(ref[h, 256:768, :])
        part = nt(jnp.concatenate(tiles, 1), w_ref[h])
        grad = part if grad is None else grad + part
    back, gain_grad, shift_grad = norm_back(grad, tok_ref[0].astype(jnp.float32), par_ref[0:1, :])
    out_ref[0] = (mid_ref[0] + back).astype(jnp.bfloat16)

    @pl.when(pl.program_id(0) == 0)
    def _():
        norm_ref[...] = jnp.zeros_like(norm_ref)

    norm_ref[0:1, :] += gain_grad
    norm_ref[1:2, :] += shift_grad


def last(packs, weights, tokens, mid_grad, params):
    seqs = tokens.shape[0]
    piece = pl.BlockSpec((4, 768, 128), lambda s: (s, 0, 0))
    rows = pl.BlockSpec((1, CHUNK, D), lambda s: (s, 0, 0))
    return pl.pallas_call(
        last_kernel,
        grid=(seqs,),
        in_specs=[piece, piece, piece, pl.BlockSpec((4, D, D), lambda s: (0, 0, 0)), rows, rows,
                  pl.BlockSpec((4, D), lambda s: (0, 0))],
        out_specs=[rows, pl.BlockSpec((8, D), lambda s: (0, 0))],
        out_shape=[jax.ShapeDtypeStruct(tokens.shape, jnp.bfloat16), jax.ShapeDtypeStruct((8, D), jnp.float32)],
        compiler_params=limits(60),
        name="last",
        cost_estimate=COST,
    )(*packs, weights, tokens, mid_grad, params)


def step_kernel(factor_ref, *refs):
    factor = factor_ref[0]
    for slot in range(4):
        weight, gradient, first, second, average = (ref[...] for ref in refs[slot * 5 : slot * 5 + 5])
        outs = refs[20 + slot * 5 : 25 + slot * 5]
        new, first, second, average = adamw_moment_update(
            weight, gradient, first, second, average, rates()[slot], factor
        )
        for ref, value in zip(outs, (new, first, second, average, new.astype(jnp.bfloat16))):
            ref[...] = value


def matrix_steps(factor, groups):
    blocks = [pl.BlockSpec((group[0].shape[0] // 3, group[0].shape[1]), lambda i, t: (i, 0)) for group in groups for _ in range(5)]
    shapes = [
        jax.ShapeDtypeStruct(group[0].shape, kind)
        for group in groups
        for kind in (jnp.float32,) * 4 + (jnp.bfloat16,)
    ]
    outs = pl.pallas_call(
        step_kernel,
        grid_spec=pltpu.PrefetchScalarGridSpec(num_scalar_prefetch=1, grid=(3,), in_specs=blocks, out_specs=blocks),
        out_shape=shapes,
        compiler_params=limits(60),
        name="matrix_steps",
        cost_estimate=COST,
    )(factor, *(item for group in groups for item in group))
    return [outs[n * 5 : n * 5 + 5] for n in range(4)]


def gather_heads(mine):
    return lax.all_gather(mine, "head", axis=0)


def pick(values, index, size, axis):
    return lax.dynamic_slice_in_dim(values, index * size, size, axis)


def after(value, *others):
    return lax.optimization_barrier((value, others))[0]


def add_low(left, right):
    return (left.astype(jnp.float32) + right.astype(jnp.float32)).astype(jnp.bfloat16)


def across(values, axes=GROUP):
    return lax.all_to_all(values, axes, 0, 0, tiled=True)


def fast_body(
    tokens, cotangent, rand_blocks, global_blocks, qkv_weight, out_weight, up_weight, down_weight, norm_params,
    qkv_first, out_first, up_first, down_first, norm_first,
    qkv_second, out_second, up_second, down_second, norm_second,
    qkv_average, out_average, up_average, down_average, norm_average,
):
    dp_size = lax.axis_size("dp")
    count = dp_size * 8
    y, head = lax.axis_index("seq"), lax.axis_index("head")
    me = y * 4 + head

    head_word = jnp.reshape(head, (1,)).astype(jnp.int32)

    turned = jnp.stack([pick(tokens, y, 1, 0)[0], pick(tokens, 1 - y, 1, 0)[0]])
    normed = norm_rows(turned.astype(jnp.float32), norm_params[0], norm_params[1]).astype(jnp.bfloat16)
    mine, theirs = normed[0], normed[1]
    beyond = swap(theirs, 4)
    even = [mine, swap(mine, 2), beyond, swap(beyond, 2)]
    odd = [swap(item, 1) for item in even]
    slots = [item for pair in zip(even, odd) for item in pair]

    blank = jnp.zeros((96, 64), jnp.bfloat16)
    shard = after(spread_heads(qkv_weight), beyond, even[1])
    count_rows = dp_size * 2
    mine_qkv = across(jnp.broadcast_to(shard[None], (count_rows,) + shard.shape), ("dp", "seq")).reshape(D, D)
    rest = (up_weight, down_weight.T, out_weight.T)
    gather = lambda item: lax.all_gather(item, ("dp", "seq"), axis=0, tiled=True)
    first_own = gather(jnp.concatenate([rest[0].astype(jnp.bfloat16), rest[2].astype(jnp.bfloat16), blank], -1))
    second_own = gather(rest[1].astype(jnp.bfloat16))
    first_over = swap(after(first_own, *even), 2)

    both_rand = jnp.concatenate([rand_blocks.reshape(-1), swap(rand_blocks.reshape(-1), 4)])
    table = jnp.concatenate(
        [jnp.reshape(me, (1,)), global_blocks, jnp.zeros((5,), jnp.int32), both_rand]
    ).astype(jnp.int32)
    qkv = project(slots, mine_qkv)
    attended = attend(table, qkv)
    second_over = swap(after(second_own, attended), 2)
    attended = after(attended, second_own)
    first = [first_own, first_over] + [swap(after(item, attended), 1) for item in (first_own, first_over)]

    o_parts = across(attended)
    second = [second_own, second_over, swap(after(second_own, attended), 1), swap(after(second_over, o_parts), 1)]
    mixed, mid, a2, a2t = middle(head_word, after(o_parts, second_over), first, tokens, norm_params)
    all_qkv = gather_heads(after(mine_qkv, a2))

    dy = cotangent.reshape(a2.shape)
    block_out, back, up_mate, down_mate, up_own, down_own = mlp(
        a2, a2t, dy, dy.T, mid.reshape(a2.shape), first, second
    )
    block_out = block_out.reshape(tokens.shape)
    up_mate, down_mate = swap(up_mate, 1), swap(down_mate, 1)

    mid_grad, low_grad, grad_first, grad_rest, norm_two = middle_back(
        head_word, back, mid, cotangent, first, after(norm_params, all_qkv)
    )
    down_mate = after(down_mate, grad_first)
    grad_first, grad_rest = across(grad_first), across(grad_rest)

    fulls, packs = [], []

    def back_step(k, *ahead):
        grad, row = (grad_first, 0) if k == 0 else (grad_rest, k - 1)
        full, pack = attend_back(k, after(table, *ahead), qkv, grad, row)
        fulls.append(full)
        packs.append(across(pack))

    down_both = add_low(down_own, down_mate)
    down_terms = lax.psum_scatter(down_both, "dp", scatter_dimension=1, tiled=True)
    back_step(0, down_both)
    out_terms = out_weight_grad(after(low_grad, fulls[0], grad_rest), mixed)
    out_mate = swap(out_terms[0:2], 1)
    rest_both = jnp.concatenate([add_low(up_own, after(up_mate, fulls[0])), add_low(out_terms[2:4], out_mate)], -1)
    rest_terms = lax.psum_scatter(rest_both, "dp", scatter_dimension=1, tiled=True)
    back_step(1, fulls[0], rest_both)
    back_step(2, fulls[1], packs[0])
    fulls[2] = after(fulls[2], packs[1])
    wide = qkv_weight_grad(slots, fulls)
    all_terms = jnp.concatenate([after(down_terms, wide), after(rest_terms, wide)], -1)
    shares = across(after(wide, packs[2]).reshape(dp_size * 2, 96, 640), ("dp", "seq"))
    term = lambda over, row: pick(all_terms, row, 96, 1)[over]
    terms = [term(0, y), term(0, 1 - y), term(1, y), term(1, 1 - y)]
    last_params = after(norm_params, *terms)
    terms = [terms[0]] + [swap(item, distance) for item, distance in zip(terms[1:], (4, 2, 6))]
    input_grad, norm_one = last(packs, all_qkv, tokens, mid_grad, last_params)
    qkv_grad = jnp.sum(after(shares, norm_one).astype(jnp.float32), 0)[:, 0:576]
    matrix_grad = sum(item.astype(jnp.float32) for item in after(terms, norm_one))
    down_grad, up_grad, out_grad = matrix_grad[:, 0:D], matrix_grad[:, D : 2 * D], matrix_grad[:, 2 * D : 2 * D + 192]

    reduced = (qkv_grad, out_grad.T, up_grad, down_grad)
    squares = sum((jnp.sum(item * item) for item in reduced))
    shared = jnp.concatenate(
        [norm_one[0:2], norm_two[0:2], jnp.full((1, D), squares), jnp.zeros((3, D), jnp.float32)], 0
    )
    distance = 1
    while distance < count:
        shared = shared + swap_every(shared, distance, count)
        distance *= 2
    norm_grads = shared[0:4]
    grad_norm = jnp.sqrt(shared[4, 0] + jnp.sum(norm_grads * norm_grads))
    factor = jnp.minimum(1.0, CLIP_NORM / (grad_norm + 1e-06))
    groups = (
        (qkv_weight, reduced[0], qkv_first, qkv_second, qkv_average),
        (out_weight, reduced[1], out_first, out_second, out_average),
        (up_weight, reduced[2], up_first, up_second, up_average),
        (down_weight.T, reduced[3], down_first.T, down_second.T, down_average.T),
    )
    stepped = matrix_steps(jnp.reshape(factor, (1,)), groups)
    stepped[3] = [item.T for item in stepped[3]]
    norm_step = adamw_moment_update(
        norm_params, norm_grads, norm_first, norm_second, norm_average, rates()[4], factor
    )
    results = []
    for n in range(4):
        results += [item[n] for item in stepped] + [norm_step[n]]
    copies = [item[4] for item in stepped]
    return (block_out, input_grad, grad_norm, *results, *copies, factor * norm_grads[2:])


def is_fast(mesh):
    sizes = dict(mesh.shape)
    return sizes["seq"] == 2 and sizes["head"] == 4 and sizes["dp"] == 4


def solution(mesh):
    return jax.shard_map(
        fast_body if is_fast(mesh) else body,
        mesh=mesh,
        in_specs=(
            P("dp", ("seq", "head"), None),
            P("dp", ("seq", "head"), None),
            P("head", "seq", None),
            P(),
            P(("dp", "seq"), "head"),
            P("head", ("dp", "seq")),
            P(("dp", "seq"), "head"),
            P("head", ("dp", "seq")),
            P(),
            P(("dp", "seq"), "head"),
            P("head", ("dp", "seq")),
            P(("dp", "seq"), "head"),
            P("head", ("dp", "seq")),
            P(),
            P(("dp", "seq"), "head"),
            P("head", ("dp", "seq")),
            P(("dp", "seq"), "head"),
            P("head", ("dp", "seq")),
            P(),
            P(("dp", "seq"), "head"),
            P("head", ("dp", "seq")),
            P(("dp", "seq"), "head"),
            P("head", ("dp", "seq")),
            P(),
        ),
        out_specs=(
            P("dp", ("seq", "head"), None),
            P("dp", ("seq", "head"), None),
            P(),
            P(("dp", "seq"), "head"),
            P("head", ("dp", "seq")),
            P(("dp", "seq"), "head"),
            P("head", ("dp", "seq")),
            P(),
            P(("dp", "seq"), "head"),
            P("head", ("dp", "seq")),
            P(("dp", "seq"), "head"),
            P("head", ("dp", "seq")),
            P(),
            P(("dp", "seq"), "head"),
            P("head", ("dp", "seq")),
            P(("dp", "seq"), "head"),
            P("head", ("dp", "seq")),
            P(),
            P(("dp", "seq"), "head"),
            P("head", ("dp", "seq")),
            P(("dp", "seq"), "head"),
            P("head", ("dp", "seq")),
            P(),
            P(("dp", "seq"), "head"),
            P("head", ("dp", "seq")),
            P(("dp", "seq"), "head"),
            P("head", ("dp", "seq")),
            P(),
        ),
        check_vma=False,
    )
```

```python
import jax
import jax.numpy as jnp
from jax import lax
from jax.experimental import pallas as pl
from jax.experimental.pallas import tpu as pltpu
from jax.sharding import PartitionSpec as P

D = 768
DH = 64
FF = 3072
BLOCK = 64
STEP = 10


EPSILON = 1e-05
BETA_ONE = 0.9
BETA_TWO = 0.999
DECAY = 0.01
SMALL = 1e-08
CLIP_NORM = 1.0
AVERAGING = 0.999
NEGATIVE = -1e30


def norm_rows(values, gain_row, shift_row):
    center = values - jnp.mean(values, -1, keepdims=True)
    spread = jnp.mean(center * center, -1, keepdims=True)
    return center * lax.rsqrt(spread + EPSILON) * gain_row + shift_row


def key_table(rand_local, global_blocks, first_block, blocks_total):
    head_count, local_blocks = (rand_local.shape[0], rand_local.shape[1])
    places = first_block + jnp.arange(local_blocks, dtype=jnp.int32)
    left_side = jnp.maximum(places - 1, 0)
    right_side = jnp.minimum(places + 1, blocks_total - 1)
    window = jnp.stack([left_side, places, right_side], -1)
    key_index = jnp.concatenate(
        [
            jnp.broadcast_to(window[None], (head_count, local_blocks, 3)),
            rand_local,
            jnp.broadcast_to(global_blocks[None, None], (head_count, local_blocks, 2)),
        ],
        -1,
    )
    column_one = jnp.ones((local_blocks, 1), jnp.float32)
    key_valid = jnp.concatenate(
        [
            (places > 0).astype(jnp.float32)[:, None],
            column_one,
            (places < blocks_total - 1).astype(jnp.float32)[:, None],
            jnp.ones((local_blocks, 5), jnp.float32),
        ],
        -1,
    )
    return (key_index, key_valid)


def gather_rows(values):
    return lax.all_gather(values, "head", axis=1, tiled=True)


def sum_rows(values):
    return lax.psum_scatter(values, "head", scatter_dimension=1, tiled=True)


def contract(left_operand, right_operand):
    return jnp.einsum(
        "enz,enf->zf", left_operand, right_operand, preferred_element_type=jnp.float32
    )


def to_heads(values, head_count):
    seq_count, token_count = (values.shape[0], values.shape[1])
    return jnp.moveaxis(
        values.reshape(seq_count, token_count // BLOCK, BLOCK, head_count, DH), 3, 0
    )


def from_heads(values):
    head_count, seq_count, blocks = (values.shape[0], values.shape[1], values.shape[2])
    return jnp.moveaxis(values, 0, 3).reshape(seq_count, blocks * BLOCK, head_count * DH)


def pick_keys(kv_all, key_index):
    seq_count, token_count = (kv_all.shape[0], kv_all.shape[1])
    head_count = key_index.shape[0]
    blocks = kv_all.reshape(seq_count, token_count // BLOCK, BLOCK, head_count, 2, DH)
    by_head = jnp.moveaxis(blocks, 3, 0)
    return jax.vmap(lambda source, chosen: source[:, chosen])(by_head, key_index)


def scores_of(queries, picked, key_valid):
    raw_scores = jnp.einsum(
        "hsnbe,hsnkce->hsnbkc", queries, picked[..., 0, :], preferred_element_type=jnp.float32
    ) * DH ** (-0.5)
    return jnp.where(key_valid[None, None, :, None, :, None] > 0, raw_scores, NEGATIVE)


def attend_forward(queries, picked, key_valid):
    raw_scores = scores_of(queries, picked, key_valid)
    score_shape = raw_scores.shape
    scores_flat = raw_scores.reshape(score_shape[:4] + (score_shape[4] * score_shape[5],))
    row_max = jnp.max(scores_flat, -1, keepdims=True)
    exponent = jnp.exp(scores_flat - row_max)
    row_total = jnp.sum(exponent, -1, keepdims=True)
    probabilities = (exponent / row_total).astype(jnp.bfloat16).reshape(score_shape)
    output = jnp.einsum(
        "hsnbkc,hsnkce->hsnbe", probabilities, picked[..., 1, :], preferred_element_type=jnp.float32
    )
    return (output, row_max + jnp.log(row_total))


def attend_backward(queries, picked, key_valid, log_total, grad_out):
    raw_scores = scores_of(queries, picked, key_valid)
    score_shape = raw_scores.shape
    scores_flat = raw_scores.reshape(score_shape[:4] + (score_shape[4] * score_shape[5],))
    probabilities = jnp.exp(scores_flat - log_total)
    grad_probs = jnp.einsum(
        "hsnbe,hsnkce->hsnbkc", grad_out, picked[..., 1, :], preferred_element_type=jnp.float32
    ).reshape(scores_flat.shape)
    row_delta = jnp.sum(probabilities * grad_probs, -1, keepdims=True)
    grad_scores = probabilities * (grad_probs - row_delta)
    grad_scores = grad_scores.astype(jnp.bfloat16).reshape(score_shape)
    low_probs = probabilities.astype(jnp.bfloat16).reshape(score_shape)
    grad_query = jnp.einsum(
        "hsnbkc,hsnkce->hsnbe", grad_scores, picked[..., 0, :], preferred_element_type=jnp.float32
    ) * DH ** (-0.5)
    grad_keys = jnp.einsum(
        "hsnbkc,hsnbe->hsnkce", grad_scores, queries, preferred_element_type=jnp.float32
    ) * DH ** (-0.5)
    grad_values = jnp.einsum(
        "hsnbkc,hsnbe->hsnkce", low_probs, grad_out, preferred_element_type=jnp.float32
    )
    return (grad_query, jnp.stack([grad_keys, grad_values], -2), row_delta)


def spread_back(grad_pairs, key_index, seq_count, blocks_total):
    head_count = key_index.shape[0]
    zero_grid = jnp.zeros((head_count, seq_count, blocks_total, BLOCK, 2, DH), jnp.float32)
    filled = jax.vmap(lambda source, chosen, addend: source.at[:, chosen].add(addend))(
        zero_grid, key_index, grad_pairs
    )
    return jnp.moveaxis(filled, 0, 3).reshape(seq_count, blocks_total * BLOCK, head_count * 2 * DH)


def rates():
    return (
        1.5 * D ** (-0.5),
        1.5 * max(1, D // (8 * BLOCK)) ** (-0.5),
        1.5 * D ** (-0.5),
        1.5 * FF ** (-0.5),
        0.5,
    )


def adamw_moment_update(weight, gradient, moment_one, moment_two, average, rate, factor):
    decay_mean = min(AVERAGING, (1.0 + STEP) / (10.0 + STEP))
    clipped = gradient * factor
    first_new = BETA_ONE * moment_one + (1.0 - BETA_ONE) * clipped
    second_new = BETA_TWO * moment_two + (1.0 - BETA_TWO) * clipped * clipped
    update = (
        first_new / (1.0 - BETA_ONE**STEP) / (jnp.sqrt(second_new / (1.0 - BETA_TWO**STEP)) + SMALL)
    )
    weight_new = weight - rate * (update + DECAY * weight)
    average_new = decay_mean * average + (1.0 - decay_mean) * weight_new
    return (weight_new, first_new, second_new, average_new)


def body(
    tokens,
    cotangent,
    rand_blocks,
    global_blocks,
    qkv_weight,
    out_weight,
    up_weight,
    down_weight,
    norm_params,
    qkv_first,
    out_first,
    up_first,
    down_first,
    norm_first,
    qkv_second,
    out_second,
    up_second,
    down_second,
    norm_second,
    qkv_average,
    out_average,
    up_average,
    down_average,
    norm_average,
):
    qkv_low, out_low, up_low, down_low = (
        lax.all_gather(qkv_weight.astype(jnp.bfloat16), ("dp", "seq"), axis=0, tiled=True),
        lax.all_gather(out_weight.astype(jnp.bfloat16), ("dp", "seq"), axis=1, tiled=True),
        lax.all_gather(up_weight.astype(jnp.bfloat16), ("dp", "seq"), axis=0, tiled=True),
        lax.all_gather(down_weight.astype(jnp.bfloat16), ("dp", "seq"), axis=1, tiled=True),
    )
    seq_count = tokens.shape[0]
    head_count = rand_blocks.shape[0]
    local_blocks = rand_blocks.shape[1]
    blocks_total = local_blocks * lax.axis_size("seq")
    first_block = lax.axis_index("seq") * local_blocks
    key_index, key_valid = key_table(rand_blocks, global_blocks, first_block, blocks_total)
    inputs = tokens.astype(jnp.float32)
    full_one = gather_rows(norm_rows(inputs, norm_params[0], norm_params[1]).astype(jnp.bfloat16))
    token_count = full_one.shape[1]
    qkv_all = jnp.dot(full_one, qkv_low, preferred_element_type=jnp.float32).astype(jnp.bfloat16)
    qkv_parts = qkv_all.reshape(seq_count, token_count, head_count, 3, DH)
    kv_local = qkv_parts[:, :, :, 1:, :].reshape(seq_count, token_count, head_count * 2 * DH)
    kv_all = lax.all_gather(kv_local, "seq", axis=1, tiled=True)
    picked = pick_keys(kv_all, key_index)
    queries = to_heads(qkv_parts[:, :, :, 0, :], head_count)
    attended, log_total = attend_forward(queries, picked, key_valid)
    mixed_heads = from_heads(attended.astype(jnp.bfloat16))
    residual = inputs + sum_rows(jnp.dot(mixed_heads, out_low, preferred_element_type=jnp.float32))
    full_two = gather_rows(norm_rows(residual, norm_params[2], norm_params[3]).astype(jnp.bfloat16))
    upward = jnp.dot(full_two, up_low, preferred_element_type=jnp.float32)
    active = jax.nn.gelu(upward).astype(jnp.bfloat16)
    result = residual + sum_rows(jnp.dot(active, down_low, preferred_element_type=jnp.float32))
    block_out = result.astype(jnp.bfloat16)
    grad_top = gather_rows(cotangent)
    grad_down = contract(active, grad_top)
    grad_active = jnp.dot(grad_top, down_low.T, preferred_element_type=jnp.float32)
    _, gelu_back = jax.vjp(jax.nn.gelu, upward)
    grad_upward = gelu_back(grad_active)[0].astype(jnp.bfloat16)
    grad_up = contract(full_two, grad_upward)
    part_two = sum_rows(jnp.dot(grad_upward, up_low.T, preferred_element_type=jnp.float32))
    _, norm_back_two = jax.vjp(norm_rows, residual, norm_params[2], norm_params[3])
    grad_residual_norm, grad_gain_two, grad_shift_two = norm_back_two(part_two)
    grad_residual = cotangent.astype(jnp.float32) + grad_residual_norm
    grad_middle = gather_rows(grad_residual.astype(jnp.bfloat16))
    grad_out = contract(mixed_heads, grad_middle)
    grad_mixed = jnp.dot(grad_middle, out_low.T, preferred_element_type=jnp.float32).astype(
        jnp.bfloat16
    )
    grad_query, grad_pairs, row_delta = attend_backward(
        queries, picked, key_valid, log_total, to_heads(grad_mixed, head_count)
    )
    grad_kv_full = spread_back(grad_pairs, key_index, seq_count, blocks_total)
    grad_kv = lax.psum_scatter(
        grad_kv_full.astype(jnp.bfloat16), "seq", scatter_dimension=1, tiled=True
    ).astype(jnp.float32)
    query_gradient = from_heads(grad_query).reshape(seq_count, token_count, head_count, 1, DH)
    grad_qkv_rows = jnp.concatenate(
        [query_gradient, grad_kv.reshape(seq_count, token_count, head_count, 2, DH)], 3
    )
    grad_qkv_rows = grad_qkv_rows.reshape(seq_count, token_count, head_count * 3 * DH).astype(
        jnp.bfloat16
    )
    grad_qkv = contract(full_one, grad_qkv_rows)
    part_one = sum_rows(jnp.dot(grad_qkv_rows, qkv_low.T, preferred_element_type=jnp.float32))
    _, norm_back_one = jax.vjp(norm_rows, inputs, norm_params[0], norm_params[1])
    grad_input_norm, grad_gain_one, grad_shift_one = norm_back_one(part_one)
    input_grad = (grad_residual + grad_input_norm).astype(jnp.bfloat16)
    grad_norm_local = jnp.stack([grad_gain_one, grad_shift_one, grad_gain_two, grad_shift_two])
    reduced_total = (
        lax.psum_scatter(grad_qkv, ("dp", "seq"), scatter_dimension=0, tiled=True),
        lax.psum_scatter(grad_out, ("dp", "seq"), scatter_dimension=1, tiled=True),
        lax.psum_scatter(grad_up, ("dp", "seq"), scatter_dimension=0, tiled=True),
        lax.psum_scatter(grad_down, ("dp", "seq"), scatter_dimension=1, tiled=True),
    )
    squares = sum((jnp.sum(item * item) for item in reduced_total))
    norm_grads = lax.psum(grad_norm_local, ("dp", "seq", "head"))
    matrix_squares = lax.psum(squares, ("dp", "seq", "head"))
    grad_norm = jnp.sqrt(matrix_squares + jnp.sum(norm_grads * norm_grads))
    factor = jnp.minimum(1.0, CLIP_NORM / (grad_norm + 1e-06))
    weights = (qkv_weight, out_weight, up_weight, down_weight, norm_params)
    gradients = (reduced_total[0], reduced_total[1], reduced_total[2], reduced_total[3], norm_grads)
    firsts = (qkv_first, out_first, up_first, down_first, norm_first)
    seconds = (qkv_second, out_second, up_second, down_second, norm_second)
    averages = (qkv_average, out_average, up_average, down_average, norm_average)
    results = [
        adamw_moment_update(
            weights[slot],
            gradients[slot],
            firsts[slot],
            seconds[slot],
            averages[slot],
            rates()[slot],
            factor,
        )
        for slot in range(5)
    ]
    news = tuple((item[0] for item in results))
    first_news = tuple((item[1] for item in results))
    second_news = tuple((item[2] for item in results))
    average_news = tuple((item[3] for item in results))
    return (
        block_out,
        input_grad,
        grad_norm,
        news[0],
        news[1],
        news[2],
        news[3],
        news[4],
        first_news[0],
        first_news[1],
        first_news[2],
        first_news[3],
        first_news[4],
        second_news[0],
        second_news[1],
        second_news[2],
        second_news[3],
        second_news[4],
        average_news[0],
        average_news[1],
        average_news[2],
        average_news[3],
        average_news[4],
        news[0].astype(jnp.bfloat16),
        news[1].astype(jnp.bfloat16),
        news[2].astype(jnp.bfloat16),
        news[3].astype(jnp.bfloat16),
        factor * norm_grads[2:],
    )


GROUP = ("seq", "head")
EVERY = ("dp", "seq", "head")
FULL = 4096
CHUNK = 512
MB = 1024 * 1024
COST = pl.CostEstimate(flops=10**6, bytes_accessed=10**5, transcendentals=0)


def limits(megabytes):
    return pltpu.CompilerParams(vmem_limit_bytes=megabytes * MB)


def swap(values, distance):
    return lax.ppermute(values, GROUP, [(i, i ^ distance) for i in range(8)])


def swap_every(values, distance, count):
    return lax.ppermute(values, EVERY, [(i, i ^ distance) for i in range(count)])


def nt(left, right):
    return lax.dot_general(left, right, (((1,), (1,)), ((), ())), preferred_element_type=jnp.float32)


def nn(left, right):
    return lax.dot_general(left, right, (((1,), (0,)), ((), ())), preferred_element_type=jnp.float32)


def tn(left, right):
    return lax.dot_general(left, right, (((0,), (0,)), ((), ())), preferred_element_type=jnp.float32)


def lane_low(shape):
    return lax.broadcasted_iota(jnp.int32, shape, len(shape) - 1) < 64


def roll64(values):
    return pltpu.roll(values, 64, 1)


def block_places(tab_ref, k, block):
    me = tab_ref[0]
    part = (block // 32) ^ (me // 4)
    base = 8 + ((part * 3 + k) * 32 + block % 32) * 3
    chosen = [
        jnp.maximum(block - 1, 0),
        block,
        jnp.minimum(block + 1, 63),
        tab_ref[base],
        tab_ref[base + 1],
        tab_ref[base + 2],
        tab_ref[1],
        tab_ref[2],
    ]
    return [pl.multiple_of((((b // 8) ^ me) * 8 + b % 8) * 64, 64) for b in chosen]


def spread_kernel(in_ref, out_ref):
    low = lane_low((96, 128))
    tiles = [in_ref[:, j * 128 : j * 128 + 128] for j in range(4)]
    tiles.append(jnp.concatenate([in_ref[:, 512:576], jnp.zeros((96, 64), jnp.float32)], 1))
    scale = DH ** (-0.5)
    parts = [
        jnp.where(low, tiles[0] * scale, 0.0),
        jnp.where(low, roll64(tiles[0]), roll64(tiles[1])),
        jnp.where(low, roll64(tiles[1]) * scale, 0.0),
        tiles[2],
        jnp.where(low, tiles[3] * scale, 0.0),
        jnp.where(low, roll64(tiles[3]), roll64(tiles[4])),
    ]
    for n, part in enumerate(parts):
        out_ref[:, n * 128 : n * 128 + 128] = part.astype(jnp.bfloat16)


def spread_heads(shard):
    return pl.pallas_call(
        spread_kernel,
        out_shape=jax.ShapeDtypeStruct((96, D), jnp.bfloat16),
        compiler_params=limits(60),
        name="spread_heads",
        cost_estimate=COST,
    )(shard)


def qkv_kernel(*refs):
    tok_refs, weight_ref, out_ref = refs[:8], refs[8], refs[9]

    def one(tok_ref):
        out_ref[...] = nn(tok_ref[...], weight_ref[...]).astype(jnp.bfloat16)

    for slot, tok_ref in enumerate(tok_refs):
        pl.when(pl.program_id(0) == slot)(lambda tok_ref=tok_ref: one(tok_ref))


def project(slots, weights):
    return pl.pallas_call(
        qkv_kernel,
        grid=(8,),
        in_specs=[pl.BlockSpec((CHUNK, D), lambda i: (0, 0))] * 8 + [pl.BlockSpec((D, D), lambda i: (0, 0))],
        out_specs=pl.BlockSpec((CHUNK, D), lambda i: (i, 0)),
        out_shape=jax.ShapeDtypeStruct((FULL, D), jnp.bfloat16),
        compiler_params=limits(60),
        name="project",
        cost_estimate=COST,
    )(*slots, weights)


def hide(scores, low, high):
    lane = lax.broadcasted_iota(jnp.int32, scores.shape, 1)
    return jnp.where((lane >= low) & (lane < high), NEGATIVE, scores)


def softmax_rows(scores, part, q):
    if q == 0:
        scores = jnp.where(part == 0, hide(scores, 0, 64), scores)
    if q == 7:
        scores = jnp.where(part == 7, hide(scores, 128, 192), scores)
    top = jnp.max(scores, -1, keepdims=True)
    exponent = jnp.exp(scores - top)
    total = jnp.sum(exponent, -1, keepdims=True)
    return exponent * (1.0 / total)


def attend_kernel(k, tab_ref, qkv_ref, out_ref):
    me = tab_ref[0]

    def step(pair, carry):
        blocks = [(pair * 2 + n, q) for n in range(2) for q in range(8)]
        keys, scores = [], []
        for slot, q in blocks:
            places = block_places(tab_ref, k, (slot ^ me) * 8 + q)
            keys.append(jnp.concatenate([qkv_ref[pl.ds(p, 64), 128:256] for p in places], 0))
            at = pl.multiple_of(slot * CHUNK + q * 64, 64)
            scores.append(nt(qkv_ref[pl.ds(at, 64), 0:128], keys[-1]))
        probs = [
            softmax_rows(score, slot ^ me, q).astype(jnp.bfloat16) for score, (slot, q) in zip(scores, blocks)
        ]
        outs = [nn(prob, key) for prob, key in zip(probs, keys)]
        for n, (slot, q) in enumerate(blocks):
            if q < 4:
                both = jnp.where(lane_low(outs[n].shape), roll64(outs[n]), outs[n + 4])
                out_ref[slot ^ me, q * 64 : q * 64 + 64, :] = both.astype(jnp.bfloat16)
        return carry

    lax.fori_loop(0, 4, step, 0)


def attend(table, qkv):
    return pl.pallas_call(
        lambda *refs: attend_kernel(pl.program_id(0), *refs),
        grid_spec=pltpu.PrefetchScalarGridSpec(
            num_scalar_prefetch=1,
            grid=(3,),
            in_specs=[pl.BlockSpec((FULL, 256), lambda i, t: (0, i))],
            out_specs=pl.BlockSpec((8, 256, 128), lambda i, t: (0, i, 0)),
        ),
        out_shape=jax.ShapeDtypeStruct((8, D, 128), jnp.bfloat16),
        compiler_params=limits(60),
        name="attend",
        cost_estimate=COST,
    )(table, qkv)


def attend_back_kernel(k, tab_ref, qkv_ref, grad_ref, full_ref, pack_ref, acc_ref, shared_ref):
    me = tab_ref[0]
    acc_ref[...] = jnp.zeros_like(acc_ref)
    shared_ref[...] = jnp.zeros_like(shared_ref)

    def step(slot, carry):
        part = slot ^ me
        grads = [None] * 8
        for j in range(4):
            tile = grad_ref[part, j * 64 : j * 64 + 64, :].astype(jnp.float32)
            low_lanes = lane_low(tile.shape)
            grads[j] = jnp.where(low_lanes, 0.0, roll64(tile)).astype(jnp.bfloat16)
            grads[j + 4] = jnp.where(low_lanes, 0.0, tile).astype(jnp.bfloat16)
        places, stacks, keys, both = [], [], [], []
        for q in range(8):
            places.append(block_places(tab_ref, k, part * 8 + q))
            keys.append(jnp.concatenate([qkv_ref[pl.ds(p, 64), 128:256] for p in places[q]], 0))
            at = pl.multiple_of(slot * CHUNK + q * 64, 64)
            stacks.append(jnp.concatenate([qkv_ref[pl.ds(at, 64), 0:128], grads[q]], 0))
            both.append(nt(stacks[q], keys[q]))
        lows, pairs = [], []
        for q in range(8):
            probs, grad_probs = softmax_rows(both[q][:64], part, q), both[q][64:]
            delta = jnp.sum(probs * grad_probs, -1, keepdims=True)
            lows.append((probs * (grad_probs - delta)).astype(jnp.bfloat16))
            pairs.append(jnp.concatenate([lows[q], probs.astype(jnp.bfloat16)], 0))
        queries = []
        for q in range(8):
            grad_query = nn(lows[q], keys[q]) * DH ** (-0.5)
            queries.append(jnp.where(lane_low(grad_query.shape), grad_query, 0.0))
            at = pl.multiple_of(slot * CHUNK + q * 64, 64)
            full_ref[pl.ds(at, 64), 0:128] = queries[q].astype(jnp.bfloat16)
        spreads = [tn(pairs[q], stacks[q]) for q in range(8)]
        shared = spreads[0][384:]
        for q in range(8):
            if q:
                shared = shared + spreads[q][384:]
            for m in range(6):
                acc_ref[pl.ds(places[q][m], 64), :] += spreads[q][m * 64 : m * 64 + 64]
        shared_ref[...] += shared
        for j in range(4):
            packed = queries[j] + roll64(queries[j + 4])
            pack_ref[part, j * 64 : j * 64 + 64, :] = packed.astype(jnp.bfloat16)
        return carry

    lax.fori_loop(0, 8, step, 0)
    for m in range(2):
        block = tab_ref[1 + m]
        at = pl.multiple_of((((block // 8) ^ me) * 8 + block % 8) * 64, 64)
        acc_ref[pl.ds(at, 64), :] += shared_ref[m * 64 : m * 64 + 64]

    def finish(slot, carry):
        at = pl.ds(pl.multiple_of(slot * CHUNK, CHUNK), CHUNK)
        low = acc_ref[at, :].astype(jnp.bfloat16)
        full_ref[at, 128:256] = low
        pack_ref[slot ^ me, 256:768, :] = low
        return carry

    lax.fori_loop(0, 8, finish, 0)


def attend_back(k, table, qkv, grad, row):
    return pl.pallas_call(
        lambda *refs: attend_back_kernel(k, *refs),
        grid_spec=pltpu.PrefetchScalarGridSpec(
            num_scalar_prefetch=1,
            grid=(1,),
            in_specs=[
                pl.BlockSpec((FULL, 256), lambda i, t: (0, k)),
                pl.BlockSpec((8, 256, 128), lambda i, t: (0, row, 0)),
            ],
            out_specs=[
                pl.BlockSpec((FULL, 256), lambda i, t: (0, 0)),
                pl.BlockSpec((8, 768, 128), lambda i, t: (0, 0, 0)),
            ],
            scratch_shapes=[pltpu.VMEM((FULL, 128), jnp.float32), pltpu.VMEM((128, 128), jnp.float32)],
        ),
        out_shape=[
            jax.ShapeDtypeStruct((FULL, 256), jnp.bfloat16),
            jax.ShapeDtypeStruct((8, 768, 128), jnp.bfloat16),
        ],
        compiler_params=limits(60),
        name="attend_back",
        cost_estimate=COST,
    )(table, qkv, grad)


def norm_stats(values):
    center = values - jnp.mean(values, -1, keepdims=True)
    spread = jnp.mean(center * center, -1, keepdims=True)
    scale = lax.rsqrt(spread + EPSILON)
    return center * scale, scale


def halves(first, second):
    low = lane_low(first.shape)
    upper = jnp.where(low, first, roll64(second))
    lower = jnp.where(low, roll64(first), second)
    return upper, lower


def mid_kernel(o_ref, w_ref, tok_ref, par_ref, cat_ref, mid_ref, a2_ref, a2t_ref):
    middle = tok_ref[0].astype(jnp.float32)
    cat_ref[...] = jnp.zeros_like(cat_ref)
    for h in range(4):
        tiles = [o_ref[h, at : at + 256].astype(jnp.float32) for at in (0, 256, 512)]
        upper, lower = halves(tiles[0], tiles[1])
        last_upper, last_lower = halves(tiles[2], jnp.zeros_like(tiles[2]))
        cat_ref[0:256, h * 256 : h * 256 + 128] = upper.astype(jnp.bfloat16)
        cat_ref[256:512, h * 256 : h * 256 + 128] = lower.astype(jnp.bfloat16)
        cat_ref[0:256, h * 256 + 128 : h * 256 + 256] = last_upper.astype(jnp.bfloat16)
        cat_ref[256:512, h * 256 + 128 : h * 256 + 256] = last_lower.astype(jnp.bfloat16)
        middle = middle + nt(cat_ref[:, h * 256 : h * 256 + 256], ordered(w_ref, h))
    mid_ref[0] = middle
    normed, _ = norm_stats(middle)
    low = normed * par_ref[2:3, :] + par_ref[3:4, :]
    a2_ref[...] = low.astype(jnp.bfloat16)
    a2t_ref[...] = low.T.astype(jnp.bfloat16)


def ordered(ref, h):
    return jnp.concatenate([ref[y, h, d] for d in range(ref.shape[2]) for y in range(2)], 0)


def out_weight_spec(dp_size):
    return pl.BlockSpec((2, 4, dp_size, 96, 256), lambda s: (0, 0, 0, 0, 6))


def middle(o_parts, weights, tokens, params):
    seqs = tokens.shape[0]
    rows = pl.BlockSpec((1, CHUNK, D), lambda s: (s, 0, 0))
    return pl.pallas_call(
        mid_kernel,
        grid=(seqs,),
        in_specs=[
            pl.BlockSpec((4, D, 128), lambda s: (s, 0, 0)),
            out_weight_spec(weights.shape[2]), rows, pl.BlockSpec((4, D), lambda s: (0, 0)),
        ],
        out_specs=[
            pl.BlockSpec((CHUNK, 1024), lambda s: (s, 0)), rows,
            pl.BlockSpec((CHUNK, D), lambda s: (s, 0)), pl.BlockSpec((D, CHUNK), lambda s: (0, s)),
        ],
        out_shape=[
            jax.ShapeDtypeStruct((seqs * CHUNK, 1024), jnp.bfloat16),
            jax.ShapeDtypeStruct(tokens.shape, jnp.float32),
            jax.ShapeDtypeStruct((seqs * CHUNK, D), jnp.bfloat16),
            jax.ShapeDtypeStruct((D, seqs * CHUNK), jnp.bfloat16),
        ],
        compiler_params=limits(60),
        name="middle",
        cost_estimate=COST,
    )(o_parts, weights, tokens, params)


def group_of(head, i):
    return head ^ (i % 2 * 2 + 1 - i // 2)


def mlp_kernel(head_ref, a2_ref, a2t_ref, dy_ref, dyt_ref, mid_ref, wu_ref, wd_ref, out_ref, back_ref,
               um_ref, dm_ref, uo_ref, do_ref, g_ref, u_ref, wuo_ref, wdo_ref, wut_ref, wdt_ref, acc_ref):
    step = pl.program_id(0)

    @pl.when(step == 0)
    def _():
        acc_ref[...] = mid_ref[...]
        back_ref[...] = jnp.zeros_like(back_ref)

    wuo_ref[...] = ordered(wu_ref, 0)
    wdo_ref[...] = ordered(wd_ref, 0)
    wut_ref[...] = wuo_ref[...].T
    wdt_ref[...] = wdo_ref[...].T
    rate, cubic = 0.7978845608028654, 0.044715
    rows = [slice(m * 256, m * 256 + 256) for m in range(4)]
    products = lambda m: (nn(a2_ref[rows[m], :], wuo_ref[...]), nn(dy_ref[rows[m], :], wdo_ref[...]))
    ahead = products(0)
    for m in range(4):
        up, grad = ahead
        if m < 3:
            ahead = products(m + 1)
        at = rows[m]
        square = up * up
        bend = jnp.tanh(up * (rate + rate * cubic * square))
        half = 0.5 + 0.5 * bend
        g_ref[at, :] = (up * half).astype(jnp.bfloat16)
        slope = half + (0.5 * up) * (1.0 - bend * bend) * (rate + 3.0 * rate * cubic * square)
        u_ref[at, :] = (grad * slope).astype(jnp.bfloat16)
        acc_ref[at, :] += nn(g_ref[at, :], wdt_ref[...])
        back_ref[at, :] += nn(u_ref[at, :], wut_ref[...])
    up_grad = nn(a2t_ref[...], u_ref[...]).astype(jnp.bfloat16)
    down_grad = nn(dyt_ref[...], g_ref[...]).astype(jnp.bfloat16)

    @pl.when(step < 2)
    def _():
        um_ref[0] = up_grad
        dm_ref[0] = down_grad

    @pl.when(step >= 2)
    def _():
        uo_ref[0] = up_grad
        do_ref[0] = down_grad

    @pl.when(step == 3)
    def _():
        out_ref[...] = acc_ref[...].astype(jnp.bfloat16)


def mlp(head, a2, a2t, dy, dyt, mid, weights):
    tokens = a2.shape[0]
    whole = lambda shape: pl.BlockSpec(shape, lambda i, t: (0, 0))
    weight = lambda part: pl.BlockSpec(
        (2, 1, weights.shape[2], 96, D), lambda i, t: (0, group_of(t[0], i), 0, 0, part)
    )
    theirs = pl.BlockSpec((1, D, D), lambda i, t: (jnp.minimum(i, 1), 0, 0))
    ours = pl.BlockSpec((1, D, D), lambda i, t: (jnp.maximum(i - 2, 0), 0, 0))
    low = jax.ShapeDtypeStruct((2, D, D), jnp.bfloat16)
    return pl.pallas_call(
        mlp_kernel,
        grid_spec=pltpu.PrefetchScalarGridSpec(
            num_scalar_prefetch=1,
            grid=(4,),
            in_specs=[
                whole((tokens, D)), whole((D, tokens)), whole((tokens, D)), whole((D, tokens)), whole((tokens, D)),
                weight(0), weight(1),
            ],
            out_specs=[whole((tokens, D)), whole((tokens, D)), theirs, theirs, ours, ours],
            scratch_shapes=[
                pltpu.VMEM((tokens, D), jnp.bfloat16), pltpu.VMEM((tokens, D), jnp.bfloat16),
                *(pltpu.VMEM((D, D), jnp.bfloat16) for _ in range(4)), pltpu.VMEM((tokens, D), jnp.float32),
            ],
        ),
        out_shape=[
            jax.ShapeDtypeStruct((tokens, D), jnp.bfloat16), jax.ShapeDtypeStruct((tokens, D), jnp.float32),
            low, low, low, low,
        ],
        compiler_params=limits(60),
        name="mlp",
        cost_estimate=COST,
    )(head, a2, a2t, dy, dyt, mid, weights, weights)


def norm_back(grad, values, gain):
    normed, scale = norm_stats(values)
    gain_grad = jnp.sum(grad * normed, 0, keepdims=True)
    shift_grad = jnp.sum(grad, 0, keepdims=True)
    inner = grad * gain
    across = jnp.mean(inner, -1, keepdims=True)
    along = jnp.mean(inner * normed, -1, keepdims=True)
    return scale * (inner - across - normed * along), gain_grad, shift_grad


def mid_back_kernel(b_ref, mid_ref, dy_ref, w_ref, par_ref, grad_ref, low_ref, first_ref, rest_ref, norm_ref):
    grad, gain_grad, shift_grad = norm_back(b_ref[...], mid_ref[0], par_ref[2:3, :])
    total = dy_ref[0].astype(jnp.float32) + grad
    grad_ref[0] = total
    low = total.astype(jnp.bfloat16)
    low_ref[...] = low
    for h in range(4):
        mixed = nn(low, ordered(w_ref, h))
        first, second = halves(mixed[0:256, 0:128], mixed[256:512, 0:128])
        third, _ = halves(mixed[0:256, 128:256], mixed[256:512, 128:256])
        first_ref[h] = first.astype(jnp.bfloat16)
        rest_ref[h, 0:256] = second.astype(jnp.bfloat16)
        rest_ref[h, 256:512] = third.astype(jnp.bfloat16)

    @pl.when(pl.program_id(0) == 0)
    def _():
        norm_ref[...] = jnp.zeros_like(norm_ref)

    norm_ref[0:1, :] += gain_grad
    norm_ref[1:2, :] += shift_grad


def middle_back(back, mid, dy, weights, params):
    seqs = dy.shape[0]
    rows = pl.BlockSpec((1, CHUNK, D), lambda s: (s, 0, 0))
    flat = pl.BlockSpec((CHUNK, D), lambda s: (s, 0))
    return pl.pallas_call(
        mid_back_kernel,
        grid=(seqs,),
        in_specs=[flat, rows, rows, out_weight_spec(weights.shape[2]), pl.BlockSpec((4, D), lambda s: (0, 0))],
        out_specs=[
            rows, flat, pl.BlockSpec((4, 256, 128), lambda s: (s, 0, 0)),
            pl.BlockSpec((4, 512, 128), lambda s: (s, 0, 0)), pl.BlockSpec((8, D), lambda s: (0, 0)),
        ],
        out_shape=[
            jax.ShapeDtypeStruct(dy.shape, jnp.float32),
            jax.ShapeDtypeStruct((seqs * CHUNK, D), jnp.bfloat16),
            jax.ShapeDtypeStruct((8, 256, 128), jnp.bfloat16),
            jax.ShapeDtypeStruct((8, 512, 128), jnp.bfloat16),
            jax.ShapeDtypeStruct((8, D), jnp.float32),
        ],
        compiler_params=limits(60),
        name="middle_back",
        cost_estimate=COST,
    )(back, mid, dy, weights, params)


def out_grad_kernel(head_ref, low_ref, cat_ref, out_ref):
    for h in range(4):
        r = head_ref[0] ^ h
        out_ref[(1 - r % 2) * 2 + r // 2] = tn(low_ref[...], cat_ref[:, h * 256 : h * 256 + 256]).astype(jnp.bfloat16)


def out_weight_grad(head, low, cat):
    return pl.pallas_call(
        out_grad_kernel,
        grid_spec=pltpu.PrefetchScalarGridSpec(
            num_scalar_prefetch=1,
            grid=(1,),
            in_specs=[pl.BlockSpec(low.shape, lambda i, t: (0, 0)), pl.BlockSpec(cat.shape, lambda i, t: (0, 0))],
            out_specs=pl.BlockSpec((4, D, 256), lambda i, t: (0, 0, 0)),
        ),
        out_shape=jax.ShapeDtypeStruct((4, D, 256), jnp.bfloat16),
        compiler_params=limits(60),
        name="out_weight_grad",
        cost_estimate=COST,
    )(head, low, cat)


def merge_heads(queries, pairs):
    low = lane_low(queries[0].shape)
    return [
        jnp.where(low, queries[0], roll64(pairs[0])),
        jnp.where(low, roll64(pairs[0]), roll64(queries[1])),
        pairs[1],
        jnp.where(low, queries[2], roll64(pairs[2])),
        jnp.where(low, roll64(pairs[2]), 0.0),
    ]


def qkv_grad_kernel(*refs):
    tok_refs, full_refs, out_ref, acc_ref = refs[:8], refs[8:11], refs[11], refs[12]
    step = pl.program_id(0)

    @pl.when(step == 0)
    def _():
        acc_ref[...] = jnp.zeros_like(acc_ref)

    def one(tok_ref):
        acc_ref[...] += tn(tok_ref[...], jnp.concatenate([ref[...] for ref in full_refs], 1))

    for slot, tok_ref in enumerate(tok_refs):
        pl.when(step == slot)(lambda tok_ref=tok_ref: one(tok_ref))

    @pl.when(step == 7)
    def _():
        tiles = merge_heads(
            [acc_ref[:, k * 256 : k * 256 + 128] for k in range(3)],
            [acc_ref[:, k * 256 + 128 : k * 256 + 256] for k in range(3)],
        )
        for j, tile in enumerate(tiles):
            out_ref[:, j * 128 : j * 128 + 128] = tile.astype(jnp.bfloat16)


def qkv_weight_grad(slots, fulls):
    return pl.pallas_call(
        qkv_grad_kernel,
        grid=(8,),
        in_specs=[pl.BlockSpec((CHUNK, D), lambda i: (0, 0))] * 8 + [pl.BlockSpec((CHUNK, 256), lambda i: (i, 0))] * 3,
        out_specs=pl.BlockSpec((D, 640), lambda i: (0, 0)),
        out_shape=jax.ShapeDtypeStruct((D, 640), jnp.bfloat16),
        scratch_shapes=[pltpu.VMEM((D, D), jnp.float32)],
        compiler_params=limits(60),
        name="qkv_weight_grad",
        cost_estimate=COST,
    )(*slots, *fulls)


def last_kernel(p0_ref, p1_ref, p2_ref, w_ref, tok_ref, mid_ref, par_ref, out_ref, norm_ref):
    grad = None
    low = lane_low((CHUNK, 128))
    for h in range(4):
        tiles = []
        for ref in (p0_ref, p1_ref, p2_ref):
            both = ref[h, 0:256, :].astype(jnp.float32) * DH**0.5
            tiles.append(jnp.where(low, jnp.concatenate([both, roll64(both)], 0), 0.0).astype(jnp.bfloat16))
            tiles.append(ref[h, 256:768, :])
        part = nt(jnp.concatenate(tiles, 1), w_ref[h])
        grad = part if grad is None else grad + part
    back, gain_grad, shift_grad = norm_back(grad, tok_ref[0].astype(jnp.float32), par_ref[0:1, :])
    out_ref[0] = (mid_ref[0] + back).astype(jnp.bfloat16)

    @pl.when(pl.program_id(0) == 0)
    def _():
        norm_ref[...] = jnp.zeros_like(norm_ref)

    norm_ref[0:1, :] += gain_grad
    norm_ref[1:2, :] += shift_grad


def last(packs, weights, tokens, mid_grad, params):
    seqs = tokens.shape[0]
    piece = pl.BlockSpec((4, 768, 128), lambda s: (s, 0, 0))
    rows = pl.BlockSpec((1, CHUNK, D), lambda s: (s, 0, 0))
    return pl.pallas_call(
        last_kernel,
        grid=(seqs,),
        in_specs=[piece, piece, piece, pl.BlockSpec((4, D, D), lambda s: (0, 0, 0)), rows, rows,
                  pl.BlockSpec((4, D), lambda s: (0, 0))],
        out_specs=[rows, pl.BlockSpec((8, D), lambda s: (0, 0))],
        out_shape=[jax.ShapeDtypeStruct(tokens.shape, jnp.bfloat16), jax.ShapeDtypeStruct((8, D), jnp.float32)],
        compiler_params=limits(60),
        name="last",
        cost_estimate=COST,
    )(*packs, weights, tokens, mid_grad, params)


def step_kernel(factor_ref, *refs):
    factor = factor_ref[0]
    for slot in range(4):
        weight, gradient, first, second, average = (ref[...] for ref in refs[slot * 5 : slot * 5 + 5])
        outs = refs[20 + slot * 5 : 25 + slot * 5]
        new, first, second, average = adamw_moment_update(
            weight, gradient, first, second, average, rates()[slot], factor
        )
        for ref, value in zip(outs, (new, first, second, average, new.astype(jnp.bfloat16))):
            ref[...] = value


def matrix_steps(factor, groups):
    blocks = [pl.BlockSpec((group[0].shape[0] // 3, group[0].shape[1]), lambda i, t: (i, 0)) for group in groups for _ in range(5)]
    shapes = [
        jax.ShapeDtypeStruct(group[0].shape, kind)
        for group in groups
        for kind in (jnp.float32,) * 4 + (jnp.bfloat16,)
    ]
    outs = pl.pallas_call(
        step_kernel,
        grid_spec=pltpu.PrefetchScalarGridSpec(num_scalar_prefetch=1, grid=(3,), in_specs=blocks, out_specs=blocks),
        out_shape=shapes,
        compiler_params=limits(60),
        name="matrix_steps",
        cost_estimate=COST,
    )(factor, *(item for group in groups for item in group))
    return [outs[n * 5 : n * 5 + 5] for n in range(4)]


def gather_heads(mine):
    return lax.all_gather(mine, "head", axis=0)


def pick(values, index, size, axis):
    return lax.dynamic_slice_in_dim(values, index * size, size, axis)


def after(value, *others):
    return lax.optimization_barrier((value, others))[0]


def add_low(left, right):
    return (left.astype(jnp.float32) + right.astype(jnp.float32)).astype(jnp.bfloat16)


def across(values, axes=GROUP):
    return lax.all_to_all(values, axes, 0, 0, tiled=True)


def fast_body(
    tokens, cotangent, rand_blocks, global_blocks, qkv_weight, out_weight, up_weight, down_weight, norm_params,
    qkv_first, out_first, up_first, down_first, norm_first,
    qkv_second, out_second, up_second, down_second, norm_second,
    qkv_average, out_average, up_average, down_average, norm_average,
):
    dp_size = lax.axis_size("dp")
    count = dp_size * 8
    y, head = lax.axis_index("seq"), lax.axis_index("head")
    me = y * 4 + head

    head_word = jnp.reshape(head, (1,)).astype(jnp.int32)

    turned = jnp.stack([pick(tokens, y, 1, 0)[0], pick(tokens, 1 - y, 1, 0)[0]])
    normed = norm_rows(turned.astype(jnp.float32), norm_params[0], norm_params[1]).astype(jnp.bfloat16)
    mine, theirs = normed[0], normed[1]
    beyond = swap(theirs, 4)
    even = [mine, swap(mine, 2), beyond, swap(beyond, 2)]
    odd = [swap(item, 1) for item in even]
    slots = [item for pair in zip(even, odd) for item in pair]

    blank = jnp.zeros((96, 64), jnp.bfloat16)
    rest = (up_weight, down_weight.T, out_weight.T)
    low_rest = jnp.concatenate([item.astype(jnp.bfloat16) for item in rest] + [blank], -1)
    shard = after(spread_heads(qkv_weight), low_rest)
    count_rows = dp_size * 2
    mine_qkv = across(jnp.broadcast_to(shard[None], (count_rows,) + shard.shape), ("dp", "seq")).reshape(D, D)
    along_dp = lax.all_gather(low_rest, "dp", axis=0)
    all_rest = lax.all_gather(after(along_dp, even[1], even[3], mine_qkv), GROUP, axis=0).reshape((2, 4) + along_dp.shape)

    both_rand = jnp.concatenate([rand_blocks.reshape(-1), swap(rand_blocks.reshape(-1), 4)])
    table = jnp.concatenate(
        [jnp.reshape(me, (1,)), global_blocks, jnp.zeros((5,), jnp.int32), both_rand]
    ).astype(jnp.int32)
    qkv = project(slots, mine_qkv)

    o_parts = across(attend(table, qkv))
    mixed, mid, a2, a2t = middle(o_parts, all_rest, tokens, norm_params)
    all_qkv = gather_heads(after(mine_qkv, a2))

    dy = cotangent.reshape(a2.shape)
    block_out, back, up_mate, down_mate, up_own, down_own = mlp(
        head_word, a2, a2t, dy, dy.T, mid.reshape(a2.shape), all_rest
    )
    block_out = block_out.reshape(tokens.shape)
    up_mate, down_mate = swap(up_mate, 1), swap(down_mate, 1)

    mid_grad, low_grad, grad_first, grad_rest, norm_two = middle_back(
        back, mid, cotangent, all_rest, after(norm_params, all_qkv)
    )
    down_mate = after(down_mate, grad_first)
    grad_first, grad_rest = across(grad_first), across(grad_rest)

    fulls, packs = [], []

    def back_step(k, *ahead):
        grad, row = (grad_first, 0) if k == 0 else (grad_rest, k - 1)
        full, pack = attend_back(k, after(table, *ahead), qkv, grad, row)
        fulls.append(full)
        packs.append(across(pack))

    down_both = add_low(down_own, down_mate)
    down_terms = lax.psum_scatter(down_both, "dp", scatter_dimension=1, tiled=True)
    back_step(0, down_both)
    out_terms = out_weight_grad(head_word, after(low_grad, fulls[0], grad_rest), mixed)
    out_mate = swap(out_terms[0:2], 1)
    rest_both = jnp.concatenate([add_low(up_own, after(up_mate, fulls[0])), add_low(out_terms[2:4], out_mate)], -1)
    rest_terms = lax.psum_scatter(rest_both, "dp", scatter_dimension=1, tiled=True)
    back_step(1, fulls[0], rest_both)
    back_step(2, fulls[1], packs[0])
    fulls[2] = after(fulls[2], packs[1])
    wide = qkv_weight_grad(slots, fulls)
    all_terms = jnp.concatenate([after(down_terms, wide), after(rest_terms, wide)], -1)
    shares = across(after(wide, packs[2]).reshape(dp_size * 2, 96, 640), ("dp", "seq"))
    term = lambda over, row: pick(all_terms, row, 96, 1)[over]
    terms = [term(0, y), term(0, 1 - y), term(1, y), term(1, 1 - y)]
    last_params = after(norm_params, *terms)
    terms = [terms[0]] + [swap(item, distance) for item, distance in zip(terms[1:], (4, 2, 6))]
    input_grad, norm_one = last(packs, all_qkv, tokens, mid_grad, last_params)
    qkv_grad = jnp.sum(after(shares, norm_one).astype(jnp.float32), 0)[:, 0:576]
    matrix_grad = sum(item.astype(jnp.float32) for item in after(terms, norm_one))
    down_grad, up_grad, out_grad = matrix_grad[:, 0:D], matrix_grad[:, D : 2 * D], matrix_grad[:, 2 * D : 2 * D + 192]

    reduced = (qkv_grad, out_grad.T, up_grad, down_grad)
    squares = sum((jnp.sum(item * item) for item in reduced))
    shared = jnp.concatenate(
        [norm_one[0:2], norm_two[0:2], jnp.full((1, D), squares), jnp.zeros((3, D), jnp.float32)], 0
    )
    distance = 1
    while distance < count:
        shared = shared + swap_every(shared, distance, count)
        distance *= 2
    norm_grads = shared[0:4]
    grad_norm = jnp.sqrt(shared[4, 0] + jnp.sum(norm_grads * norm_grads))
    factor = jnp.minimum(1.0, CLIP_NORM / (grad_norm + 1e-06))
    groups = (
        (qkv_weight, reduced[0], qkv_first, qkv_second, qkv_average),
        (out_weight, reduced[1], out_first, out_second, out_average),
        (up_weight, reduced[2], up_first, up_second, up_average),
        (down_weight.T, reduced[3], down_first.T, down_second.T, down_average.T),
    )
    stepped = matrix_steps(jnp.reshape(factor, (1,)), groups)
    stepped[3] = [item.T for item in stepped[3]]
    norm_step = adamw_moment_update(
        norm_params, norm_grads, norm_first, norm_second, norm_average, rates()[4], factor
    )
    results = []
    for n in range(4):
        results += [item[n] for item in stepped] + [norm_step[n]]
    copies = [item[4] for item in stepped]
    return (block_out, input_grad, grad_norm, *results, *copies, factor * norm_grads[2:])


def is_fast(mesh):
    sizes = dict(mesh.shape)
    return sizes["seq"] == 2 and sizes["head"] == 4 and sizes["dp"] == 4


def solution(mesh):
    return jax.shard_map(
        fast_body if is_fast(mesh) else body,
        mesh=mesh,
        in_specs=(
            P("dp", ("seq", "head"), None),
            P("dp", ("seq", "head"), None),
            P("head", "seq", None),
            P(),
            P(("dp", "seq"), "head"),
            P("head", ("dp", "seq")),
            P(("dp", "seq"), "head"),
            P("head", ("dp", "seq")),
            P(),
            P(("dp", "seq"), "head"),
            P("head", ("dp", "seq")),
            P(("dp", "seq"), "head"),
            P("head", ("dp", "seq")),
            P(),
            P(("dp", "seq"), "head"),
            P("head", ("dp", "seq")),
            P(("dp", "seq"), "head"),
            P("head", ("dp", "seq")),
            P(),
            P(("dp", "seq"), "head"),
            P("head", ("dp", "seq")),
            P(("dp", "seq"), "head"),
            P("head", ("dp", "seq")),
            P(),
        ),
        out_specs=(
            P("dp", ("seq", "head"), None),
            P("dp", ("seq", "head"), None),
            P(),
            P(("dp", "seq"), "head"),
            P("head", ("dp", "seq")),
            P(("dp", "seq"), "head"),
            P("head", ("dp", "seq")),
            P(),
            P(("dp", "seq"), "head"),
            P("head", ("dp", "seq")),
            P(("dp", "seq"), "head"),
            P("head", ("dp", "seq")),
            P(),
            P(("dp", "seq"), "head"),
            P("head", ("dp", "seq")),
            P(("dp", "seq"), "head"),
            P("head", ("dp", "seq")),
            P(),
            P(("dp", "seq"), "head"),
            P("head", ("dp", "seq")),
            P(("dp", "seq"), "head"),
            P("head", ("dp", "seq")),
            P(),
            P(("dp", "seq"), "head"),
            P("head", ("dp", "seq")),
            P(("dp", "seq"), "head"),
            P("head", ("dp", "seq")),
            P(),
        ),
        check_vma=False,
    )
```

```python
import jax
import jax.numpy as jnp
from jax import lax
from jax.experimental import pallas as pl
from jax.experimental.pallas import tpu as pltpu
from jax.sharding import PartitionSpec as P

D = 768
DH = 64
FF = 3072
BLOCK = 64
STEP = 10


EPSILON = 1e-05
BETA_ONE = 0.9
BETA_TWO = 0.999
DECAY = 0.01
SMALL = 1e-08
CLIP_NORM = 1.0
AVERAGING = 0.999
NEGATIVE = -1e30


def norm_rows(values, gain_row, shift_row):
    center = values - jnp.mean(values, -1, keepdims=True)
    spread = jnp.mean(center * center, -1, keepdims=True)
    return center * lax.rsqrt(spread + EPSILON) * gain_row + shift_row


def key_table(rand_local, global_blocks, first_block, blocks_total):
    head_count, local_blocks = (rand_local.shape[0], rand_local.shape[1])
    places = first_block + jnp.arange(local_blocks, dtype=jnp.int32)
    left_side = jnp.maximum(places - 1, 0)
    right_side = jnp.minimum(places + 1, blocks_total - 1)
    window = jnp.stack([left_side, places, right_side], -1)
    key_index = jnp.concatenate(
        [
            jnp.broadcast_to(window[None], (head_count, local_blocks, 3)),
            rand_local,
            jnp.broadcast_to(global_blocks[None, None], (head_count, local_blocks, 2)),
        ],
        -1,
    )
    column_one = jnp.ones((local_blocks, 1), jnp.float32)
    key_valid = jnp.concatenate(
        [
            (places > 0).astype(jnp.float32)[:, None],
            column_one,
            (places < blocks_total - 1).astype(jnp.float32)[:, None],
            jnp.ones((local_blocks, 5), jnp.float32),
        ],
        -1,
    )
    return (key_index, key_valid)


def gather_rows(values):
    return lax.all_gather(values, "head", axis=1, tiled=True)


def sum_rows(values):
    return lax.psum_scatter(values, "head", scatter_dimension=1, tiled=True)


def contract(left_operand, right_operand):
    return jnp.einsum(
        "enz,enf->zf", left_operand, right_operand, preferred_element_type=jnp.float32
    )


def to_heads(values, head_count):
    seq_count, token_count = (values.shape[0], values.shape[1])
    return jnp.moveaxis(
        values.reshape(seq_count, token_count // BLOCK, BLOCK, head_count, DH), 3, 0
    )


def from_heads(values):
    head_count, seq_count, blocks = (values.shape[0], values.shape[1], values.shape[2])
    return jnp.moveaxis(values, 0, 3).reshape(seq_count, blocks * BLOCK, head_count * DH)


def pick_keys(kv_all, key_index):
    seq_count, token_count = (kv_all.shape[0], kv_all.shape[1])
    head_count = key_index.shape[0]
    blocks = kv_all.reshape(seq_count, token_count // BLOCK, BLOCK, head_count, 2, DH)
    by_head = jnp.moveaxis(blocks, 3, 0)
    return jax.vmap(lambda source, chosen: source[:, chosen])(by_head, key_index)


def scores_of(queries, picked, key_valid):
    raw_scores = jnp.einsum(
        "hsnbe,hsnkce->hsnbkc", queries, picked[..., 0, :], preferred_element_type=jnp.float32
    ) * DH ** (-0.5)
    return jnp.where(key_valid[None, None, :, None, :, None] > 0, raw_scores, NEGATIVE)


def attend_forward(queries, picked, key_valid):
    raw_scores = scores_of(queries, picked, key_valid)
    score_shape = raw_scores.shape
    scores_flat = raw_scores.reshape(score_shape[:4] + (score_shape[4] * score_shape[5],))
    row_max = jnp.max(scores_flat, -1, keepdims=True)
    exponent = jnp.exp(scores_flat - row_max)
    row_total = jnp.sum(exponent, -1, keepdims=True)
    probabilities = (exponent / row_total).astype(jnp.bfloat16).reshape(score_shape)
    output = jnp.einsum(
        "hsnbkc,hsnkce->hsnbe", probabilities, picked[..., 1, :], preferred_element_type=jnp.float32
    )
    return (output, row_max + jnp.log(row_total))


def attend_backward(queries, picked, key_valid, log_total, grad_out):
    raw_scores = scores_of(queries, picked, key_valid)
    score_shape = raw_scores.shape
    scores_flat = raw_scores.reshape(score_shape[:4] + (score_shape[4] * score_shape[5],))
    probabilities = jnp.exp(scores_flat - log_total)
    grad_probs = jnp.einsum(
        "hsnbe,hsnkce->hsnbkc", grad_out, picked[..., 1, :], preferred_element_type=jnp.float32
    ).reshape(scores_flat.shape)
    row_delta = jnp.sum(probabilities * grad_probs, -1, keepdims=True)
    grad_scores = probabilities * (grad_probs - row_delta)
    grad_scores = grad_scores.astype(jnp.bfloat16).reshape(score_shape)
    low_probs = probabilities.astype(jnp.bfloat16).reshape(score_shape)
    grad_query = jnp.einsum(
        "hsnbkc,hsnkce->hsnbe", grad_scores, picked[..., 0, :], preferred_element_type=jnp.float32
    ) * DH ** (-0.5)
    grad_keys = jnp.einsum(
        "hsnbkc,hsnbe->hsnkce", grad_scores, queries, preferred_element_type=jnp.float32
    ) * DH ** (-0.5)
    grad_values = jnp.einsum(
        "hsnbkc,hsnbe->hsnkce", low_probs, grad_out, preferred_element_type=jnp.float32
    )
    return (grad_query, jnp.stack([grad_keys, grad_values], -2), row_delta)


def spread_back(grad_pairs, key_index, seq_count, blocks_total):
    head_count = key_index.shape[0]
    zero_grid = jnp.zeros((head_count, seq_count, blocks_total, BLOCK, 2, DH), jnp.float32)
    filled = jax.vmap(lambda source, chosen, addend: source.at[:, chosen].add(addend))(
        zero_grid, key_index, grad_pairs
    )
    return jnp.moveaxis(filled, 0, 3).reshape(seq_count, blocks_total * BLOCK, head_count * 2 * DH)


def rates():
    return (
        1.5 * D ** (-0.5),
        1.5 * max(1, D // (8 * BLOCK)) ** (-0.5),
        1.5 * D ** (-0.5),
        1.5 * FF ** (-0.5),
        0.5,
    )


def adamw_moment_update(weight, gradient, moment_one, moment_two, average, rate, factor):
    decay_mean = min(AVERAGING, (1.0 + STEP) / (10.0 + STEP))
    clipped = gradient * factor
    first_new = BETA_ONE * moment_one + (1.0 - BETA_ONE) * clipped
    second_new = BETA_TWO * moment_two + (1.0 - BETA_TWO) * clipped * clipped
    update = (
        first_new / (1.0 - BETA_ONE**STEP) / (jnp.sqrt(second_new / (1.0 - BETA_TWO**STEP)) + SMALL)
    )
    weight_new = weight - rate * (update + DECAY * weight)
    average_new = decay_mean * average + (1.0 - decay_mean) * weight_new
    return (weight_new, first_new, second_new, average_new)


def body(
    tokens,
    cotangent,
    rand_blocks,
    global_blocks,
    qkv_weight,
    out_weight,
    up_weight,
    down_weight,
    norm_params,
    qkv_first,
    out_first,
    up_first,
    down_first,
    norm_first,
    qkv_second,
    out_second,
    up_second,
    down_second,
    norm_second,
    qkv_average,
    out_average,
    up_average,
    down_average,
    norm_average,
):
    qkv_low, out_low, up_low, down_low = (
        lax.all_gather(qkv_weight.astype(jnp.bfloat16), ("dp", "seq"), axis=0, tiled=True),
        lax.all_gather(out_weight.astype(jnp.bfloat16), ("dp", "seq"), axis=1, tiled=True),
        lax.all_gather(up_weight.astype(jnp.bfloat16), ("dp", "seq"), axis=0, tiled=True),
        lax.all_gather(down_weight.astype(jnp.bfloat16), ("dp", "seq"), axis=1, tiled=True),
    )
    seq_count = tokens.shape[0]
    head_count = rand_blocks.shape[0]
    local_blocks = rand_blocks.shape[1]
    blocks_total = local_blocks * lax.axis_size("seq")
    first_block = lax.axis_index("seq") * local_blocks
    key_index, key_valid = key_table(rand_blocks, global_blocks, first_block, blocks_total)
    inputs = tokens.astype(jnp.float32)
    full_one = gather_rows(norm_rows(inputs, norm_params[0], norm_params[1]).astype(jnp.bfloat16))
    token_count = full_one.shape[1]
    qkv_all = jnp.dot(full_one, qkv_low, preferred_element_type=jnp.float32).astype(jnp.bfloat16)
    qkv_parts = qkv_all.reshape(seq_count, token_count, head_count, 3, DH)
    kv_local = qkv_parts[:, :, :, 1:, :].reshape(seq_count, token_count, head_count * 2 * DH)
    kv_all = lax.all_gather(kv_local, "seq", axis=1, tiled=True)
    picked = pick_keys(kv_all, key_index)
    queries = to_heads(qkv_parts[:, :, :, 0, :], head_count)
    attended, log_total = attend_forward(queries, picked, key_valid)
    mixed_heads = from_heads(attended.astype(jnp.bfloat16))
    residual = inputs + sum_rows(jnp.dot(mixed_heads, out_low, preferred_element_type=jnp.float32))
    full_two = gather_rows(norm_rows(residual, norm_params[2], norm_params[3]).astype(jnp.bfloat16))
    upward = jnp.dot(full_two, up_low, preferred_element_type=jnp.float32)
    active = jax.nn.gelu(upward).astype(jnp.bfloat16)
    result = residual + sum_rows(jnp.dot(active, down_low, preferred_element_type=jnp.float32))
    block_out = result.astype(jnp.bfloat16)
    grad_top = gather_rows(cotangent)
    grad_down = contract(active, grad_top)
    grad_active = jnp.dot(grad_top, down_low.T, preferred_element_type=jnp.float32)
    _, gelu_back = jax.vjp(jax.nn.gelu, upward)
    grad_upward = gelu_back(grad_active)[0].astype(jnp.bfloat16)
    grad_up = contract(full_two, grad_upward)
    part_two = sum_rows(jnp.dot(grad_upward, up_low.T, preferred_element_type=jnp.float32))
    _, norm_back_two = jax.vjp(norm_rows, residual, norm_params[2], norm_params[3])
    grad_residual_norm, grad_gain_two, grad_shift_two = norm_back_two(part_two)
    grad_residual = cotangent.astype(jnp.float32) + grad_residual_norm
    grad_middle = gather_rows(grad_residual.astype(jnp.bfloat16))
    grad_out = contract(mixed_heads, grad_middle)
    grad_mixed = jnp.dot(grad_middle, out_low.T, preferred_element_type=jnp.float32).astype(
        jnp.bfloat16
    )
    grad_query, grad_pairs, row_delta = attend_backward(
        queries, picked, key_valid, log_total, to_heads(grad_mixed, head_count)
    )
    grad_kv_full = spread_back(grad_pairs, key_index, seq_count, blocks_total)
    grad_kv = lax.psum_scatter(
        grad_kv_full.astype(jnp.bfloat16), "seq", scatter_dimension=1, tiled=True
    ).astype(jnp.float32)
    query_gradient = from_heads(grad_query).reshape(seq_count, token_count, head_count, 1, DH)
    grad_qkv_rows = jnp.concatenate(
        [query_gradient, grad_kv.reshape(seq_count, token_count, head_count, 2, DH)], 3
    )
    grad_qkv_rows = grad_qkv_rows.reshape(seq_count, token_count, head_count * 3 * DH).astype(
        jnp.bfloat16
    )
    grad_qkv = contract(full_one, grad_qkv_rows)
    part_one = sum_rows(jnp.dot(grad_qkv_rows, qkv_low.T, preferred_element_type=jnp.float32))
    _, norm_back_one = jax.vjp(norm_rows, inputs, norm_params[0], norm_params[1])
    grad_input_norm, grad_gain_one, grad_shift_one = norm_back_one(part_one)
    input_grad = (grad_residual + grad_input_norm).astype(jnp.bfloat16)
    grad_norm_local = jnp.stack([grad_gain_one, grad_shift_one, grad_gain_two, grad_shift_two])
    reduced_total = (
        lax.psum_scatter(grad_qkv, ("dp", "seq"), scatter_dimension=0, tiled=True),
        lax.psum_scatter(grad_out, ("dp", "seq"), scatter_dimension=1, tiled=True),
        lax.psum_scatter(grad_up, ("dp", "seq"), scatter_dimension=0, tiled=True),
        lax.psum_scatter(grad_down, ("dp", "seq"), scatter_dimension=1, tiled=True),
    )
    squares = sum((jnp.sum(item * item) for item in reduced_total))
    norm_grads = lax.psum(grad_norm_local, ("dp", "seq", "head"))
    matrix_squares = lax.psum(squares, ("dp", "seq", "head"))
    grad_norm = jnp.sqrt(matrix_squares + jnp.sum(norm_grads * norm_grads))
    factor = jnp.minimum(1.0, CLIP_NORM / (grad_norm + 1e-06))
    weights = (qkv_weight, out_weight, up_weight, down_weight, norm_params)
    gradients = (reduced_total[0], reduced_total[1], reduced_total[2], reduced_total[3], norm_grads)
    firsts = (qkv_first, out_first, up_first, down_first, norm_first)
    seconds = (qkv_second, out_second, up_second, down_second, norm_second)
    averages = (qkv_average, out_average, up_average, down_average, norm_average)
    results = [
        adamw_moment_update(
            weights[slot],
            gradients[slot],
            firsts[slot],
            seconds[slot],
            averages[slot],
            rates()[slot],
            factor,
        )
        for slot in range(5)
    ]
    news = tuple((item[0] for item in results))
    first_news = tuple((item[1] for item in results))
    second_news = tuple((item[2] for item in results))
    average_news = tuple((item[3] for item in results))
    return (
        block_out,
        input_grad,
        grad_norm,
        news[0],
        news[1],
        news[2],
        news[3],
        news[4],
        first_news[0],
        first_news[1],
        first_news[2],
        first_news[3],
        first_news[4],
        second_news[0],
        second_news[1],
        second_news[2],
        second_news[3],
        second_news[4],
        average_news[0],
        average_news[1],
        average_news[2],
        average_news[3],
        average_news[4],
        news[0].astype(jnp.bfloat16),
        news[1].astype(jnp.bfloat16),
        news[2].astype(jnp.bfloat16),
        news[3].astype(jnp.bfloat16),
        factor * norm_grads[2:],
    )


GROUP = ("seq", "head")
EVERY = ("dp", "seq", "head")
FULL = 4096
CHUNK = 512
MB = 1024 * 1024
COST = pl.CostEstimate(flops=10**6, bytes_accessed=10**5, transcendentals=0)


def limits(megabytes):
    return pltpu.CompilerParams(vmem_limit_bytes=megabytes * MB)


def swap(values, distance):
    return lax.ppermute(values, GROUP, [(i, i ^ distance) for i in range(8)])


def swap_every(values, distance, count):
    return lax.ppermute(values, EVERY, [(i, i ^ distance) for i in range(count)])


def nt(left, right):
    return lax.dot_general(left, right, (((1,), (1,)), ((), ())), preferred_element_type=jnp.float32)


def nn(left, right):
    return lax.dot_general(left, right, (((1,), (0,)), ((), ())), preferred_element_type=jnp.float32)


def tn(left, right):
    return lax.dot_general(left, right, (((0,), (0,)), ((), ())), preferred_element_type=jnp.float32)


def lane_low(shape):
    return lax.broadcasted_iota(jnp.int32, shape, len(shape) - 1) < 64


def roll64(values):
    return pltpu.roll(values, 64, 1)


def block_places(tab_ref, k, block):
    me = tab_ref[0]
    part = (block // 32) ^ (me // 4)
    base = 8 + ((part * 3 + k) * 32 + block % 32) * 3
    chosen = [
        jnp.maximum(block - 1, 0),
        block,
        jnp.minimum(block + 1, 63),
        tab_ref[base],
        tab_ref[base + 1],
        tab_ref[base + 2],
        tab_ref[1],
        tab_ref[2],
    ]
    return [pl.multiple_of((((b // 8) ^ me) * 8 + b % 8) * 64, 64) for b in chosen]


def spread_kernel(in_ref, out_ref):
    low = lane_low((96, 128))
    tiles = [in_ref[:, j * 128 : j * 128 + 128] for j in range(4)]
    tiles.append(jnp.concatenate([in_ref[:, 512:576], jnp.zeros((96, 64), jnp.float32)], 1))
    scale = DH ** (-0.5)
    parts = [
        jnp.where(low, tiles[0] * scale, 0.0),
        jnp.where(low, roll64(tiles[0]), roll64(tiles[1])),
        jnp.where(low, roll64(tiles[1]) * scale, 0.0),
        tiles[2],
        jnp.where(low, tiles[3] * scale, 0.0),
        jnp.where(low, roll64(tiles[3]), roll64(tiles[4])),
    ]
    for n, part in enumerate(parts):
        out_ref[:, n * 128 : n * 128 + 128] = part.astype(jnp.bfloat16)


def spread_heads(shard):
    return pl.pallas_call(
        spread_kernel,
        out_shape=jax.ShapeDtypeStruct((96, D), jnp.bfloat16),
        compiler_params=limits(60),
        name="spread_heads",
        cost_estimate=COST,
    )(shard)


def qkv_kernel(*refs):
    tok_refs, weight_ref, out_ref = refs[:8], refs[8], refs[9]

    def one(tok_ref):
        out_ref[...] = nn(tok_ref[...], weight_ref[...]).astype(jnp.bfloat16)

    for slot, tok_ref in enumerate(tok_refs):
        pl.when(pl.program_id(0) == slot)(lambda tok_ref=tok_ref: one(tok_ref))


def project(slots, weights):
    return pl.pallas_call(
        qkv_kernel,
        grid=(8,),
        in_specs=[pl.BlockSpec((CHUNK, D), lambda i: (0, 0))] * 8 + [pl.BlockSpec((D, D), lambda i: (0, 0))],
        out_specs=pl.BlockSpec((CHUNK, D), lambda i: (i, 0)),
        out_shape=jax.ShapeDtypeStruct((FULL, D), jnp.bfloat16),
        compiler_params=limits(60),
        name="project",
        cost_estimate=COST,
    )(*slots, weights)


def hide(scores, low, high):
    lane = lax.broadcasted_iota(jnp.int32, scores.shape, 1)
    return jnp.where((lane >= low) & (lane < high), NEGATIVE, scores)


def softmax_rows(scores, part, q):
    if q == 0:
        scores = jnp.where(part == 0, hide(scores, 0, 64), scores)
    if q == 7:
        scores = jnp.where(part == 7, hide(scores, 128, 192), scores)
    top = jnp.max(scores, -1, keepdims=True)
    exponent = jnp.exp(scores - top)
    total = jnp.sum(exponent, -1, keepdims=True)
    return exponent * (1.0 / total)


def attend_kernel(k, tab_ref, qkv_ref, out_ref):
    me = tab_ref[0]

    def step(pair, carry):
        blocks = [(pair * 2 + n, q) for n in range(2) for q in range(8)]
        keys, scores = [], []
        for slot, q in blocks:
            places = block_places(tab_ref, k, (slot ^ me) * 8 + q)
            keys.append(jnp.concatenate([qkv_ref[pl.ds(p, 64), 128:256] for p in places], 0))
            at = pl.multiple_of(slot * CHUNK + q * 64, 64)
            scores.append(nt(qkv_ref[pl.ds(at, 64), 0:128], keys[-1]))
        probs = [
            softmax_rows(score, slot ^ me, q).astype(jnp.bfloat16) for score, (slot, q) in zip(scores, blocks)
        ]
        outs = [nn(prob, key) for prob, key in zip(probs, keys)]
        for n, (slot, q) in enumerate(blocks):
            if q < 4:
                both = jnp.where(lane_low(outs[n].shape), roll64(outs[n]), outs[n + 4])
                out_ref[slot ^ me, q * 64 : q * 64 + 64, :] = both.astype(jnp.bfloat16)
        return carry

    lax.fori_loop(0, 4, step, 0)


def attend(table, qkv):
    return pl.pallas_call(
        lambda *refs: attend_kernel(pl.program_id(0), *refs),
        grid_spec=pltpu.PrefetchScalarGridSpec(
            num_scalar_prefetch=1,
            grid=(3,),
            in_specs=[pl.BlockSpec((FULL, 256), lambda i, t: (0, i))],
            out_specs=pl.BlockSpec((8, 256, 128), lambda i, t: (0, i, 0)),
        ),
        out_shape=jax.ShapeDtypeStruct((8, D, 128), jnp.bfloat16),
        compiler_params=limits(60),
        name="attend",
        cost_estimate=COST,
    )(table, qkv)


def attend_back_kernel(k, tab_ref, qkv_ref, grad_ref, full_ref, pack_ref, acc_ref, shared_ref):
    me = tab_ref[0]
    acc_ref[...] = jnp.zeros_like(acc_ref)
    shared_ref[...] = jnp.zeros_like(shared_ref)

    def step(slot, carry):
        part = slot ^ me
        grads = [None] * 8
        for j in range(4):
            tile = grad_ref[part, j * 64 : j * 64 + 64, :].astype(jnp.float32)
            low_lanes = lane_low(tile.shape)
            grads[j] = jnp.where(low_lanes, 0.0, roll64(tile)).astype(jnp.bfloat16)
            grads[j + 4] = jnp.where(low_lanes, 0.0, tile).astype(jnp.bfloat16)
        places, stacks, keys, both = [], [], [], []
        for q in range(8):
            places.append(block_places(tab_ref, k, part * 8 + q))
            keys.append(jnp.concatenate([qkv_ref[pl.ds(p, 64), 128:256] for p in places[q]], 0))
            at = pl.multiple_of(slot * CHUNK + q * 64, 64)
            stacks.append(jnp.concatenate([qkv_ref[pl.ds(at, 64), 0:128], grads[q]], 0))
            both.append(nt(stacks[q], keys[q]))
        lows, pairs = [], []
        for q in range(8):
            probs, grad_probs = softmax_rows(both[q][:64], part, q), both[q][64:]
            delta = jnp.sum(probs * grad_probs, -1, keepdims=True)
            lows.append((probs * (grad_probs - delta)).astype(jnp.bfloat16))
            pairs.append(jnp.concatenate([lows[q], probs.astype(jnp.bfloat16)], 0))
        queries = []
        for q in range(8):
            grad_query = nn(lows[q], keys[q]) * DH ** (-0.5)
            queries.append(jnp.where(lane_low(grad_query.shape), grad_query, 0.0))
            at = pl.multiple_of(slot * CHUNK + q * 64, 64)
            full_ref[pl.ds(at, 64), 0:128] = queries[q].astype(jnp.bfloat16)
        spreads = [tn(pairs[q], stacks[q]) for q in range(8)]
        shared = spreads[0][384:]
        for q in range(8):
            if q:
                shared = shared + spreads[q][384:]
            for m in range(6):
                acc_ref[pl.ds(places[q][m], 64), :] += spreads[q][m * 64 : m * 64 + 64]
        shared_ref[...] += shared
        for j in range(4):
            packed = queries[j] + roll64(queries[j + 4])
            pack_ref[part, j * 64 : j * 64 + 64, :] = packed.astype(jnp.bfloat16)
        return carry

    lax.fori_loop(0, 8, step, 0)
    for m in range(2):
        block = tab_ref[1 + m]
        at = pl.multiple_of((((block // 8) ^ me) * 8 + block % 8) * 64, 64)
        acc_ref[pl.ds(at, 64), :] += shared_ref[m * 64 : m * 64 + 64]

    def finish(slot, carry):
        at = pl.ds(pl.multiple_of(slot * CHUNK, CHUNK), CHUNK)
        low = acc_ref[at, :].astype(jnp.bfloat16)
        full_ref[at, 128:256] = low
        pack_ref[slot ^ me, 256:768, :] = low
        return carry

    lax.fori_loop(0, 8, finish, 0)


def attend_back(k, table, qkv, grad, row):
    return pl.pallas_call(
        lambda *refs: attend_back_kernel(k, *refs),
        grid_spec=pltpu.PrefetchScalarGridSpec(
            num_scalar_prefetch=1,
            grid=(1,),
            in_specs=[
                pl.BlockSpec((FULL, 256), lambda i, t: (0, k)),
                pl.BlockSpec((8, 256, 128), lambda i, t: (0, row, 0)),
            ],
            out_specs=[
                pl.BlockSpec((FULL, 256), lambda i, t: (0, 0)),
                pl.BlockSpec((8, 768, 128), lambda i, t: (0, 0, 0)),
            ],
            scratch_shapes=[pltpu.VMEM((FULL, 128), jnp.float32), pltpu.VMEM((128, 128), jnp.float32)],
        ),
        out_shape=[
            jax.ShapeDtypeStruct((FULL, 256), jnp.bfloat16),
            jax.ShapeDtypeStruct((8, 768, 128), jnp.bfloat16),
        ],
        compiler_params=limits(60),
        name="attend_back",
        cost_estimate=COST,
    )(table, qkv, grad)


def norm_stats(values):
    center = values - jnp.mean(values, -1, keepdims=True)
    spread = jnp.mean(center * center, -1, keepdims=True)
    scale = lax.rsqrt(spread + EPSILON)
    return center * scale, scale


def halves(first, second):
    low = lane_low(first.shape)
    upper = jnp.where(low, first, roll64(second))
    lower = jnp.where(low, roll64(first), second)
    return upper, lower


def mid_kernel(o_ref, w_ref, tok_ref, par_ref, cat_ref, mid_ref, a2_ref, a2t_ref):
    middle = tok_ref[0].astype(jnp.float32)
    cat_ref[...] = jnp.zeros_like(cat_ref)
    for h in range(4):
        tiles = [o_ref[h, at : at + 256].astype(jnp.float32) for at in (0, 256, 512)]
        upper, lower = halves(tiles[0], tiles[1])
        last_upper, last_lower = halves(tiles[2], jnp.zeros_like(tiles[2]))
        cat_ref[0:256, h * 256 : h * 256 + 128] = upper.astype(jnp.bfloat16)
        cat_ref[256:512, h * 256 : h * 256 + 128] = lower.astype(jnp.bfloat16)
        cat_ref[0:256, h * 256 + 128 : h * 256 + 256] = last_upper.astype(jnp.bfloat16)
        cat_ref[256:512, h * 256 + 128 : h * 256 + 256] = last_lower.astype(jnp.bfloat16)
        middle = middle + nt(cat_ref[:, h * 256 : h * 256 + 256], ordered(w_ref, h))
    mid_ref[0] = middle
    normed, _ = norm_stats(middle)
    low = normed * par_ref[2:3, :] + par_ref[3:4, :]
    a2_ref[...] = low.astype(jnp.bfloat16)
    a2t_ref[...] = low.T.astype(jnp.bfloat16)


def ordered(ref, h):
    return jnp.concatenate([ref[y, h, d] for d in range(ref.shape[2]) for y in range(2)], 0)


def out_weight_spec(dp_size):
    return pl.BlockSpec((2, 4, dp_size, 96, 256), lambda s: (0, 0, 0, 0, 6))


def middle(o_parts, weights, tokens, params):
    seqs = tokens.shape[0]
    rows = pl.BlockSpec((1, CHUNK, D), lambda s: (s, 0, 0))
    return pl.pallas_call(
        mid_kernel,
        grid=(seqs,),
        in_specs=[
            pl.BlockSpec((4, D, 128), lambda s: (s, 0, 0)),
            out_weight_spec(weights.shape[2]), rows, pl.BlockSpec((4, D), lambda s: (0, 0)),
        ],
        out_specs=[
            pl.BlockSpec((CHUNK, 1024), lambda s: (s, 0)), rows,
            pl.BlockSpec((CHUNK, D), lambda s: (s, 0)), pl.BlockSpec((D, CHUNK), lambda s: (0, s)),
        ],
        out_shape=[
            jax.ShapeDtypeStruct((seqs * CHUNK, 1024), jnp.bfloat16),
            jax.ShapeDtypeStruct(tokens.shape, jnp.float32),
            jax.ShapeDtypeStruct((seqs * CHUNK, D), jnp.bfloat16),
            jax.ShapeDtypeStruct((D, seqs * CHUNK), jnp.bfloat16),
        ],
        compiler_params=limits(60),
        name="middle",
        cost_estimate=COST,
    )(o_parts, weights, tokens, params)


def group_of(head, i):
    return head ^ (i % 2 * 2 + 1 - i // 2)


def mlp_kernel(head_ref, a2_ref, a2t_ref, dy_ref, dyt_ref, mid_ref, wu_ref, wd_ref, out_ref, back_ref,
               um_ref, dm_ref, uo_ref, do_ref, g_ref, u_ref, wuo_ref, wdo_ref, wut_ref, wdt_ref, acc_ref):
    step = pl.program_id(0)

    @pl.when(step == 0)
    def _():
        acc_ref[...] = mid_ref[...]
        back_ref[...] = jnp.zeros_like(back_ref)

    wuo_ref[...] = ordered(wu_ref, 0)
    wdo_ref[...] = ordered(wd_ref, 0)
    wut_ref[...] = wuo_ref[...].T
    wdt_ref[...] = wdo_ref[...].T
    rate, cubic = 0.7978845608028654, 0.044715
    rows = [slice(m * 256, m * 256 + 256) for m in range(4)]
    products = lambda m: (nn(a2_ref[rows[m], :], wuo_ref[...]), nn(dy_ref[rows[m], :], wdo_ref[...]))
    ahead = products(0)
    for m in range(4):
        up, grad = ahead
        if m < 3:
            ahead = products(m + 1)
        at = rows[m]
        square = up * up
        bend = jnp.tanh(up * (rate + rate * cubic * square))
        half = 0.5 + 0.5 * bend
        g_ref[at, :] = (up * half).astype(jnp.bfloat16)
        slope = half + (0.5 * up) * (1.0 - bend * bend) * (rate + 3.0 * rate * cubic * square)
        u_ref[at, :] = (grad * slope).astype(jnp.bfloat16)
        acc_ref[at, :] += nn(g_ref[at, :], wdt_ref[...])
        back_ref[at, :] += nn(u_ref[at, :], wut_ref[...])
    up_grad = nn(a2t_ref[...], u_ref[...]).astype(jnp.bfloat16)
    down_grad = nn(dyt_ref[...], g_ref[...]).astype(jnp.bfloat16)

    @pl.when(step < 2)
    def _():
        um_ref[0] = up_grad
        dm_ref[0] = down_grad

    @pl.when(step >= 2)
    def _():
        uo_ref[0] = up_grad
        do_ref[0] = down_grad

    @pl.when(step == 3)
    def _():
        out_ref[...] = acc_ref[...].astype(jnp.bfloat16)


def mlp(head, a2, a2t, dy, dyt, mid, weights):
    tokens = a2.shape[0]
    whole = lambda shape: pl.BlockSpec(shape, lambda i, t: (0, 0))
    weight = lambda part: pl.BlockSpec(
        (2, 1, weights.shape[2], 96, D), lambda i, t: (0, group_of(t[0], i), 0, 0, part)
    )
    theirs = pl.BlockSpec((1, D, D), lambda i, t: (jnp.minimum(i, 1), 0, 0))
    ours = pl.BlockSpec((1, D, D), lambda i, t: (jnp.maximum(i - 2, 0), 0, 0))
    low = jax.ShapeDtypeStruct((2, D, D), jnp.bfloat16)
    return pl.pallas_call(
        mlp_kernel,
        grid_spec=pltpu.PrefetchScalarGridSpec(
            num_scalar_prefetch=1,
            grid=(4,),
            in_specs=[
                whole((tokens, D)), whole((D, tokens)), whole((tokens, D)), whole((D, tokens)), whole((tokens, D)),
                weight(0), weight(1),
            ],
            out_specs=[whole((tokens, D)), whole((tokens, D)), theirs, theirs, ours, ours],
            scratch_shapes=[
                pltpu.VMEM((tokens, D), jnp.bfloat16), pltpu.VMEM((tokens, D), jnp.bfloat16),
                *(pltpu.VMEM((D, D), jnp.bfloat16) for _ in range(4)), pltpu.VMEM((tokens, D), jnp.float32),
            ],
        ),
        out_shape=[
            jax.ShapeDtypeStruct((tokens, D), jnp.bfloat16), jax.ShapeDtypeStruct((tokens, D), jnp.float32),
            low, low, low, low,
        ],
        compiler_params=limits(60),
        name="mlp",
        cost_estimate=COST,
    )(head, a2, a2t, dy, dyt, mid, weights, weights)


def norm_back(grad, values, gain):
    normed, scale = norm_stats(values)
    gain_grad = jnp.sum(grad * normed, 0, keepdims=True)
    shift_grad = jnp.sum(grad, 0, keepdims=True)
    inner = grad * gain
    across = jnp.mean(inner, -1, keepdims=True)
    along = jnp.mean(inner * normed, -1, keepdims=True)
    return scale * (inner - across - normed * along), gain_grad, shift_grad


def mid_back_kernel(b_ref, mid_ref, dy_ref, w_ref, par_ref, grad_ref, low_ref, first_ref, rest_ref, norm_ref):
    grad, gain_grad, shift_grad = norm_back(b_ref[...], mid_ref[0], par_ref[2:3, :])
    total = dy_ref[0].astype(jnp.float32) + grad
    grad_ref[0] = total
    low = total.astype(jnp.bfloat16)
    low_ref[...] = low
    for h in range(4):
        mixed = nn(low, ordered(w_ref, h))
        first, second = halves(mixed[0:256, 0:128], mixed[256:512, 0:128])
        third, _ = halves(mixed[0:256, 128:256], mixed[256:512, 128:256])
        first_ref[h] = first.astype(jnp.bfloat16)
        rest_ref[h, 0:256] = second.astype(jnp.bfloat16)
        rest_ref[h, 256:512] = third.astype(jnp.bfloat16)

    @pl.when(pl.program_id(0) == 0)
    def _():
        norm_ref[...] = jnp.zeros_like(norm_ref)

    norm_ref[0:1, :] += gain_grad
    norm_ref[1:2, :] += shift_grad


def middle_back(back, mid, dy, weights, params):
    seqs = dy.shape[0]
    rows = pl.BlockSpec((1, CHUNK, D), lambda s: (s, 0, 0))
    flat = pl.BlockSpec((CHUNK, D), lambda s: (s, 0))
    return pl.pallas_call(
        mid_back_kernel,
        grid=(seqs,),
        in_specs=[flat, rows, rows, out_weight_spec(weights.shape[2]), pl.BlockSpec((4, D), lambda s: (0, 0))],
        out_specs=[
            rows, flat, pl.BlockSpec((4, 256, 128), lambda s: (s, 0, 0)),
            pl.BlockSpec((4, 512, 128), lambda s: (s, 0, 0)), pl.BlockSpec((8, D), lambda s: (0, 0)),
        ],
        out_shape=[
            jax.ShapeDtypeStruct(dy.shape, jnp.float32),
            jax.ShapeDtypeStruct((seqs * CHUNK, D), jnp.bfloat16),
            jax.ShapeDtypeStruct((8, 256, 128), jnp.bfloat16),
            jax.ShapeDtypeStruct((8, 512, 128), jnp.bfloat16),
            jax.ShapeDtypeStruct((8, D), jnp.float32),
        ],
        compiler_params=limits(60),
        name="middle_back",
        cost_estimate=COST,
    )(back, mid, dy, weights, params)


def out_grad_kernel(head_ref, low_ref, cat_ref, out_ref):
    for h in range(4):
        r = head_ref[0] ^ h
        out_ref[(1 - r % 2) * 2 + r // 2] = tn(low_ref[...], cat_ref[:, h * 256 : h * 256 + 256]).astype(jnp.bfloat16)


def out_weight_grad(head, low, cat):
    return pl.pallas_call(
        out_grad_kernel,
        grid_spec=pltpu.PrefetchScalarGridSpec(
            num_scalar_prefetch=1,
            grid=(1,),
            in_specs=[pl.BlockSpec(low.shape, lambda i, t: (0, 0)), pl.BlockSpec(cat.shape, lambda i, t: (0, 0))],
            out_specs=pl.BlockSpec((4, D, 256), lambda i, t: (0, 0, 0)),
        ),
        out_shape=jax.ShapeDtypeStruct((4, D, 256), jnp.bfloat16),
        compiler_params=limits(60),
        name="out_weight_grad",
        cost_estimate=COST,
    )(head, low, cat)


def merge_heads(queries, pairs):
    low = lane_low(queries[0].shape)
    return [
        jnp.where(low, queries[0], roll64(pairs[0])),
        jnp.where(low, roll64(pairs[0]), roll64(queries[1])),
        pairs[1],
        jnp.where(low, queries[2], roll64(pairs[2])),
        jnp.where(low, roll64(pairs[2]), 0.0),
    ]


def qkv_grad_kernel(*refs):
    tok_refs, full_refs, out_ref, acc_ref = refs[:8], refs[8:11], refs[11], refs[12]
    step = pl.program_id(0)

    @pl.when(step == 0)
    def _():
        acc_ref[...] = jnp.zeros_like(acc_ref)

    def one(tok_ref):
        acc_ref[...] += tn(tok_ref[...], jnp.concatenate([ref[...] for ref in full_refs], 1))

    for slot, tok_ref in enumerate(tok_refs):
        pl.when(step == slot)(lambda tok_ref=tok_ref: one(tok_ref))

    @pl.when(step == 7)
    def _():
        tiles = merge_heads(
            [acc_ref[:, k * 256 : k * 256 + 128] for k in range(3)],
            [acc_ref[:, k * 256 + 128 : k * 256 + 256] for k in range(3)],
        )
        for j, tile in enumerate(tiles):
            out_ref[:, j * 128 : j * 128 + 128] = tile.astype(jnp.bfloat16)


def qkv_weight_grad(slots, fulls):
    return pl.pallas_call(
        qkv_grad_kernel,
        grid=(8,),
        in_specs=[pl.BlockSpec((CHUNK, D), lambda i: (0, 0))] * 8 + [pl.BlockSpec((CHUNK, 256), lambda i: (i, 0))] * 3,
        out_specs=pl.BlockSpec((D, 640), lambda i: (0, 0)),
        out_shape=jax.ShapeDtypeStruct((D, 640), jnp.bfloat16),
        scratch_shapes=[pltpu.VMEM((D, D), jnp.float32)],
        compiler_params=limits(60),
        name="qkv_weight_grad",
        cost_estimate=COST,
    )(*slots, *fulls)


def back_product(pack_refs, w_ref):
    grad = None
    low = lane_low((CHUNK, 128))
    for h in range(4):
        tiles = []
        for ref in pack_refs:
            both = ref[h, 0:256, :].astype(jnp.float32) * DH**0.5
            tiles.append(jnp.where(low, jnp.concatenate([both, roll64(both)], 0), 0.0).astype(jnp.bfloat16))
            tiles.append(ref[h, 256:768, :])
        part = nt(jnp.concatenate(tiles, 1), w_ref[h])
        grad = part if grad is None else grad + part
    return grad


def part_kernel(p0_ref, p1_ref, w_ref, out_ref):
    out_ref[...] = back_product((p0_ref, p1_ref), w_ref)


def last_kernel(p2_ref, w_ref, part_ref, tok_ref, mid_ref, par_ref, out_ref, norm_ref):
    grad = part_ref[...] + back_product((p2_ref,), w_ref)
    back, gain_grad, shift_grad = norm_back(grad, tok_ref[0].astype(jnp.float32), par_ref[0:1, :])
    out_ref[0] = (mid_ref[0] + back).astype(jnp.bfloat16)

    @pl.when(pl.program_id(0) == 0)
    def _():
        norm_ref[...] = jnp.zeros_like(norm_ref)

    norm_ref[0:1, :] += gain_grad
    norm_ref[1:2, :] += shift_grad


def last_part(first, second, weights):
    seqs = 2
    piece = pl.BlockSpec((4, 768, 128), lambda s: (s, 0, 0))
    return pl.pallas_call(
        part_kernel,
        grid=(seqs,),
        in_specs=[piece, piece, pl.BlockSpec((4, D, 512), lambda s: (0, 0, 0))],
        out_specs=pl.BlockSpec((CHUNK, D), lambda s: (s, 0)),
        out_shape=jax.ShapeDtypeStruct((seqs * CHUNK, D), jnp.float32),
        compiler_params=limits(60),
        name="last_part",
        cost_estimate=COST,
    )(first, second, weights)


def last(pack, part, weights, tokens, mid_grad, params):
    seqs = tokens.shape[0]
    piece = pl.BlockSpec((4, 768, 128), lambda s: (s, 0, 0))
    rows = pl.BlockSpec((1, CHUNK, D), lambda s: (s, 0, 0))
    flat = pl.BlockSpec((CHUNK, D), lambda s: (s, 0))
    return pl.pallas_call(
        last_kernel,
        grid=(seqs,),
        in_specs=[piece, pl.BlockSpec((4, D, 256), lambda s: (0, 0, 2)), flat, rows, rows,
                  pl.BlockSpec((4, D), lambda s: (0, 0))],
        out_specs=[rows, pl.BlockSpec((8, D), lambda s: (0, 0))],
        out_shape=[jax.ShapeDtypeStruct(tokens.shape, jnp.bfloat16), jax.ShapeDtypeStruct((8, D), jnp.float32)],
        compiler_params=limits(60),
        name="last",
        cost_estimate=COST,
    )(pack, weights, part, tokens, mid_grad, params)


def step_kernel(factor_ref, *refs):
    factor = factor_ref[0]
    for slot in range(4):
        weight, gradient, first, second, average = (ref[...] for ref in refs[slot * 5 : slot * 5 + 5])
        outs = refs[20 + slot * 5 : 25 + slot * 5]
        new, first, second, average = adamw_moment_update(
            weight, gradient, first, second, average, rates()[slot], factor
        )
        for ref, value in zip(outs, (new, first, second, average, new.astype(jnp.bfloat16))):
            ref[...] = value


def matrix_steps(factor, groups):
    blocks = [pl.BlockSpec((group[0].shape[0] // 3, group[0].shape[1]), lambda i, t: (i, 0)) for group in groups for _ in range(5)]
    shapes = [
        jax.ShapeDtypeStruct(group[0].shape, kind)
        for group in groups
        for kind in (jnp.float32,) * 4 + (jnp.bfloat16,)
    ]
    outs = pl.pallas_call(
        step_kernel,
        grid_spec=pltpu.PrefetchScalarGridSpec(num_scalar_prefetch=1, grid=(3,), in_specs=blocks, out_specs=blocks),
        out_shape=shapes,
        compiler_params=limits(60),
        name="matrix_steps",
        cost_estimate=COST,
    )(factor, *(item for group in groups for item in group))
    return [outs[n * 5 : n * 5 + 5] for n in range(4)]


def gather_heads(mine):
    return lax.all_gather(mine, "head", axis=0)


def pick(values, index, size, axis):
    return lax.dynamic_slice_in_dim(values, index * size, size, axis)


def after(value, *others):
    return lax.optimization_barrier((value, others))[0]


def add_low(left, right):
    return (left.astype(jnp.float32) + right.astype(jnp.float32)).astype(jnp.bfloat16)


def across(values, axes=GROUP):
    return lax.all_to_all(values, axes, 0, 0, tiled=True)


def fast_body(
    tokens, cotangent, rand_blocks, global_blocks, qkv_weight, out_weight, up_weight, down_weight, norm_params,
    qkv_first, out_first, up_first, down_first, norm_first,
    qkv_second, out_second, up_second, down_second, norm_second,
    qkv_average, out_average, up_average, down_average, norm_average,
):
    dp_size = lax.axis_size("dp")
    count = dp_size * 8
    y, head = lax.axis_index("seq"), lax.axis_index("head")
    me = y * 4 + head

    head_word = jnp.reshape(head, (1,)).astype(jnp.int32)

    turned = jnp.stack([pick(tokens, y, 1, 0)[0], pick(tokens, 1 - y, 1, 0)[0]])
    normed = norm_rows(turned.astype(jnp.float32), norm_params[0], norm_params[1]).astype(jnp.bfloat16)
    mine, theirs = normed[0], normed[1]
    beyond = swap(theirs, 4)
    even = [mine, swap(mine, 2), beyond, swap(beyond, 2)]
    odd = [swap(item, 1) for item in even]
    slots = [item for pair in zip(even, odd) for item in pair]

    blank = jnp.zeros((96, 64), jnp.bfloat16)
    rest = (up_weight, down_weight.T, out_weight.T)
    low_rest = jnp.concatenate([item.astype(jnp.bfloat16) for item in rest] + [blank], -1)
    shard = after(spread_heads(qkv_weight), low_rest)
    count_rows = dp_size * 2
    mine_qkv = across(jnp.broadcast_to(shard[None], (count_rows,) + shard.shape), ("dp", "seq")).reshape(D, D)
    along_dp = lax.all_gather(low_rest, "dp", axis=0)
    all_rest = lax.all_gather(after(along_dp, even[1], even[3], mine_qkv), GROUP, axis=0).reshape((2, 4) + along_dp.shape)

    both_rand = jnp.concatenate([rand_blocks.reshape(-1), swap(rand_blocks.reshape(-1), 4)])
    table = jnp.concatenate(
        [jnp.reshape(me, (1,)), global_blocks, jnp.zeros((5,), jnp.int32), both_rand]
    ).astype(jnp.int32)
    qkv = project(slots, mine_qkv)

    o_parts = across(attend(table, qkv))
    mixed, mid, a2, a2t = middle(o_parts, all_rest, tokens, norm_params)
    all_qkv = gather_heads(after(mine_qkv, a2))

    dy = cotangent.reshape(a2.shape)
    block_out, back, up_mate, down_mate, up_own, down_own = mlp(
        head_word, a2, a2t, dy, dy.T, mid.reshape(a2.shape), all_rest
    )
    block_out = block_out.reshape(tokens.shape)
    up_mate, down_mate = swap(up_mate, 1), swap(down_mate, 1)

    mid_grad, low_grad, grad_first, grad_rest, norm_two = middle_back(
        back, mid, cotangent, all_rest, after(norm_params, all_qkv)
    )
    down_mate = after(down_mate, grad_first)
    grad_first, grad_rest = across(grad_first), across(grad_rest)

    fulls, packs = [], []

    def back_step(k, *ahead):
        grad, row = (grad_first, 0) if k == 0 else (grad_rest, k - 1)
        full, pack = attend_back(k, after(table, *ahead), qkv, grad, row)
        fulls.append(full)
        packs.append(across(pack))

    down_both = add_low(down_own, down_mate)
    down_terms = lax.psum_scatter(down_both, "dp", scatter_dimension=1, tiled=True)
    back_step(0, down_both)
    out_terms = out_weight_grad(head_word, low_grad, mixed)
    out_mate = swap(after(out_terms[0:2], fulls[0], grad_rest), 1)
    rest_both = jnp.concatenate([add_low(up_own, after(up_mate, fulls[0])), add_low(out_terms[2:4], out_mate)], -1)
    rest_terms = lax.psum_scatter(rest_both, "dp", scatter_dimension=1, tiled=True)
    back_step(1, fulls[0], rest_both)
    back_step(2, fulls[1], packs[0])
    part = last_part(packs[0], packs[1], all_qkv)
    fulls[2] = after(fulls[2], part)
    wide = qkv_weight_grad(slots, fulls)
    all_terms = jnp.concatenate([after(down_terms, wide), after(rest_terms, wide)], -1)
    shares = across(after(wide, packs[2]).reshape(dp_size * 2, 96, 640), ("dp", "seq"))
    term = lambda over, row: pick(all_terms, row, 96, 1)[over]
    terms = [term(0, y), term(0, 1 - y), term(1, y), term(1, 1 - y)]
    last_params = after(norm_params, *terms)
    terms = [terms[0]] + [swap(item, distance) for item, distance in zip(terms[1:], (4, 2, 6))]
    input_grad, norm_one = last(packs[2], part, all_qkv, tokens, mid_grad, last_params)
    qkv_grad = jnp.sum(after(shares, norm_one).astype(jnp.float32), 0)[:, 0:576]
    matrix_grad = sum(item.astype(jnp.float32) for item in after(terms, norm_one))
    down_grad, up_grad, out_grad = matrix_grad[:, 0:D], matrix_grad[:, D : 2 * D], matrix_grad[:, 2 * D : 2 * D + 192]

    reduced = (qkv_grad, out_grad.T, up_grad, down_grad)
    squares = sum((jnp.sum(item * item) for item in reduced))
    shared = jnp.concatenate(
        [norm_one[0:2], norm_two[0:2], jnp.full((1, D), squares), jnp.zeros((3, D), jnp.float32)], 0
    )
    distance = 1
    while distance < count:
        shared = shared + swap_every(shared, distance, count)
        distance *= 2
    norm_grads = shared[0:4]
    grad_norm = jnp.sqrt(shared[4, 0] + jnp.sum(norm_grads * norm_grads))
    factor = jnp.minimum(1.0, CLIP_NORM / (grad_norm + 1e-06))
    groups = (
        (qkv_weight, reduced[0], qkv_first, qkv_second, qkv_average),
        (out_weight, reduced[1], out_first, out_second, out_average),
        (up_weight, reduced[2], up_first, up_second, up_average),
        (down_weight.T, reduced[3], down_first.T, down_second.T, down_average.T),
    )
    stepped = matrix_steps(jnp.reshape(factor, (1,)), groups)
    stepped[3] = [item.T for item in stepped[3]]
    norm_step = adamw_moment_update(
        norm_params, norm_grads, norm_first, norm_second, norm_average, rates()[4], factor
    )
    results = []
    for n in range(4):
        results += [item[n] for item in stepped] + [norm_step[n]]
    copies = [item[4] for item in stepped]
    return (block_out, input_grad, grad_norm, *results, *copies, factor * norm_grads[2:])


def is_fast(mesh):
    sizes = dict(mesh.shape)
    return sizes["seq"] == 2 and sizes["head"] == 4 and sizes["dp"] == 4


def solution(mesh):
    return jax.shard_map(
        fast_body if is_fast(mesh) else body,
        mesh=mesh,
        in_specs=(
            P("dp", ("seq", "head"), None),
            P("dp", ("seq", "head"), None),
            P("head", "seq", None),
            P(),
            P(("dp", "seq"), "head"),
            P("head", ("dp", "seq")),
            P(("dp", "seq"), "head"),
            P("head", ("dp", "seq")),
            P(),
            P(("dp", "seq"), "head"),
            P("head", ("dp", "seq")),
            P(("dp", "seq"), "head"),
            P("head", ("dp", "seq")),
            P(),
            P(("dp", "seq"), "head"),
            P("head", ("dp", "seq")),
            P(("dp", "seq"), "head"),
            P("head", ("dp", "seq")),
            P(),
            P(("dp", "seq"), "head"),
            P("head", ("dp", "seq")),
            P(("dp", "seq"), "head"),
            P("head", ("dp", "seq")),
            P(),
        ),
        out_specs=(
            P("dp", ("seq", "head"), None),
            P("dp", ("seq", "head"), None),
            P(),
            P(("dp", "seq"), "head"),
            P("head", ("dp", "seq")),
            P(("dp", "seq"), "head"),
            P("head", ("dp", "seq")),
            P(),
            P(("dp", "seq"), "head"),
            P("head", ("dp", "seq")),
            P(("dp", "seq"), "head"),
            P("head", ("dp", "seq")),
            P(),
            P(("dp", "seq"), "head"),
            P("head", ("dp", "seq")),
            P(("dp", "seq"), "head"),
            P("head", ("dp", "seq")),
            P(),
            P(("dp", "seq"), "head"),
            P("head", ("dp", "seq")),
            P(("dp", "seq"), "head"),
            P("head", ("dp", "seq")),
            P(),
            P(("dp", "seq"), "head"),
            P("head", ("dp", "seq")),
            P(("dp", "seq"), "head"),
            P("head", ("dp", "seq")),
            P(),
        ),
        check_vma=False,
    )
```
